32 devices in a mesh: lat: 2 (over y), ma: 16 (over z, x, core).
Axes of the slice: x: 2, y: 2, z: 4, core: 2. Of those that a mesh axis runs over, the one named last changes fastest.
Arguments:
- inputs: float32 [2, 384, 32, 73], P(None, 'ma', 'lat'), may hold values from -5 to 5
- targets: float32 [2, 2, 384, 32, 73], P(None, None, 'ma', 'lat'), may hold values from -5 to 5
- mask: int32 [2, 384, 32], P(None, 'ma', 'lat'), may hold values 0 or 1
- var_weight: int32 [73], replicated, may hold values from 1 to 4
- step_count: int32 [1], replicated, may hold values from 2 to 20
- spec_w: float32 [3, 96, 2, 256, 256], P(None, 'ma', None, None, 'lat'), may hold values from -1 to 1
- spec_m: float32 [3, 96, 2, 256, 256], P(None, 'ma', None, None, 'lat'), may hold values from -1.335144e-05 to 1.335144e-05
- spec_v: float32 [3, 96, 2, 256, 256], P(None, 'ma', None, None, 'lat'), may hold values from 6.481165e-14 to 2.592466e-13
- encdec_w: float32 [2, 73, 256], replicated, may hold values from -0.5 to 0.5
- encdec_m: float32 [2, 73, 256], replicated, may hold values from -1.335144e-05 to 1.335144e-05
- encdec_v: float32 [2, 73, 256], replicated, may hold values from 6.481165e-14 to 2.592466e-13
- mlp_w: float32 [3, 2, 256, 512], replicated, may hold values from -0.375 to 0.375
- mlp_m: float32 [3, 2, 256, 512], replicated, may hold values from -1.335144e-05 to 1.335144e-05
- mlp_v: float32 [3, 2, 256, 512], replicated, may hold values from 6.481165e-14 to 2.592466e-13
- gain_w: float32 [3, 256], replicated, may hold values from 0.5 to 1.5
- gain_m: float32 [3, 256], replicated, may hold values from -1.335144e-05 to 1.335144e-05
- gain_v: float32 [3, 256], replicated, may hold values from 6.481165e-14 to 2.592466e-13
Outputs:
- loss: float32 [], replicated
- grad_norm: float32 [], replicated
- matrix_norms: float32 [14, 2], replicated
- spec_new: float32 [3, 96, 2, 256, 256], P(None, 'ma', None, None, 'lat')
- spec_m_new: float32 [3, 96, 2, 256, 256], P(None, 'ma', None, None, 'lat')
- spec_v_new: float32 [3, 96, 2, 256, 256], P(None, 'ma', None, None, 'lat')
- spec_low: bfloat16 [3, 96, 2, 256, 256], P(None, 'ma', None, None, 'lat')
- encdec_new: float32 [2, 73, 256], replicated
- encdec_m_new: float32 [2, 73, 256], replicated
- encdec_v_new: float32 [2, 73, 256], replicated
- encdec_low: bfloat16 [2, 73, 256], replicated
- mlp_new: float32 [3, 2, 256, 512], replicated
- mlp_m_new: float32 [3, 2, 256, 512], replicated
- mlp_v_new: float32 [3, 2, 256, 512], replicated
- mlp_low: bfloat16 [3, 2, 256, 512], replicated
- gain_new: float32 [3, 256], replicated
- gain_m_new: float32 [3, 256], replicated
- gain_v_new: float32 [3, 256], replicated
- gain_low: bfloat16 [3, 256], replicated
The draws below stay inside these ranges and needn't reach their ends.
All inputs are finite; a program needn't handle non-finite values. No bound on the sum of `mask` on one device may be relied on, other than what follows from the above.
Results may differ from the reference program's by a relative error of at most 0.011.
Values may be sent and summed in bfloat16 or wider, within the bound.
A program may use at most 256 MiB of HBM per device.

```python
import math
import jax
import jax.numpy as jnp
from jax import lax

E = 256
F = 512
C = 73
L = 96
NLON = 384
NB = 3
ROLL = 2
BATCH = 2
NLAT = 32
NPARAM = 38573312


def shared_field(key):
    normal_key = jax.random.fold_in(key, 0)
    shape = (BATCH, NLON, NLAT, C)
    normal_part = jax.random.normal(normal_key, shape, jnp.float32)
    return normal_part


def draw_inputs(key, part):
    normal_part = shared_field(key)
    field = normal_part
    return jnp.clip(field, -5.0, 5.0)


def draw_targets(key, part):
    normal_part = shared_field(key)
    key = jax.random.fold_in(key, 23)
    shape = (BATCH, NLON, NLAT, C)
    state = jnp.clip(normal_part, -5.0, 5.0)
    sections = []
    for section_idx in range(ROLL):
        step_key = jax.random.fold_in(key, section_idx)
        innovation = jax.random.normal(step_key, shape, jnp.float32)
        state = jnp.clip(0.9 * state + 0.45 * innovation, -5.0, 5.0)
        sections.append(state)
    return jnp.stack(sections, 0)


def place_ends(entries, own_key, least, high):
    longest = entries.shape.index(max(entries.shape))
    spots = []
    for shift in (0, 1):
        where = [jax.random.randint(jax.random.fold_in(own_key, axis), (), 0, length) for axis, length in enumerate(entries.shape)]
        where[longest] = (where[longest] + shift) % entries.shape[longest]
        spots.append(tuple(where))
    return entries.at[spots[0]].set(least).at[spots[1]].set(high)


def steps_of(rng, extent, shards, least, high):
    def one(dim, shards_of):
        heights = jax.random.uniform(jax.random.fold_in(jax.random.fold_in(rng, 6), dim), (shards_of,), jnp.float32, least / len(shards), high / len(shards))
        return jnp.repeat(jnp.exp(heights), extent[dim] // shards_of).reshape((-1,) + (1,) * (len(extent) - dim - 1))

    factor_of = one(*shards[0])
    for cut in shards[1:]:
        factor_of = factor_of * one(*cut)
    return factor_of


def bell_draw(key, dims, spread, bound, pieces=(), held_as=jnp.bfloat16):
    array = spread * jax.random.normal(key, dims, jnp.float32)
    if pieces:
        array = array * steps_of(key, dims, pieces, -0.22, 0.18)
    return jnp.clip(array, -bound, bound).astype(held_as)


def setup_inputs(seed: int = 0) -> dict:
    arg_keys = jax.random.split(jax.random.key(seed), 18)
    return {
        "inputs": draw_inputs(jax.random.fold_in(arg_keys[17], 71), 0),
        "targets": draw_targets(jax.random.fold_in(arg_keys[17], 71), 0),
        "mask": place_ends((jax.random.randint(arg_keys[2], (BATCH, NLON, NLAT), 0, 8) < 7).astype(jnp.int32), jax.random.fold_in(arg_keys[2], 1), 0, 1),
        "var_weight": place_ends(jax.random.randint(arg_keys[3], (C,), 1, 5), jax.random.fold_in(arg_keys[3], 1), 1, 4).astype(jnp.int32),
        "step_count": jax.random.randint(arg_keys[4], (1,), 2, 21).astype(jnp.int32),
        "spec_w": bell_draw(arg_keys[5], (NB, L, 2, E, E), (E // 8) ** -0.5, 1.0, ((1, 16), (4, 2)), jnp.float32),
        "spec_m": bell_draw(arg_keys[6], (NB, L, 2, E, E), (0.005556 / NPARAM ** 0.5), 1.33514404296875e-05, ((1, 16), (4, 2)), jnp.float32),
        "spec_v": jnp.clip(jnp.exp(math.log(2.592465901240376e-13) - 1.3862944 * jax.random.uniform(arg_keys[7], (NB, L, 2, E, E), jnp.float32) ** steps_of(arg_keys[7], (NB, L, 2, E, E), ((1, 16), (4, 2)), -0.2, 0.2)), 6.48116475310094e-14, 2.592465901240376e-13),
        "encdec_w": bell_draw(arg_keys[8], (2, C, E), ((C + E) // 2) ** -0.5, 0.5, (), jnp.float32),
        "encdec_m": bell_draw(arg_keys[9], (2, C, E), (0.005556 / NPARAM ** 0.5), 1.33514404296875e-05, (), jnp.float32),
        "encdec_v": jnp.clip(jnp.exp(jax.random.uniform(arg_keys[10], (2, C, E), jnp.float32, math.log(6.48116475310094e-14), math.log(2.592465901240376e-13))), 6.48116475310094e-14, 2.592465901240376e-13),
        "mlp_w": bell_draw(arg_keys[11], (NB, 2, E, F), E ** -0.5, 0.375, (), jnp.float32),
        "mlp_m": bell_draw(arg_keys[12], (NB, 2, E, F), (0.005556 / NPARAM ** 0.5), 1.33514404296875e-05, (), jnp.float32),
        "mlp_v": jnp.clip(jnp.exp(jax.random.uniform(arg_keys[13], (NB, 2, E, F), jnp.float32, math.log(6.48116475310094e-14), math.log(2.592465901240376e-13))), 6.48116475310094e-14, 2.592465901240376e-13),
        "gain_w": jnp.clip(1.0 + 0.1 * jax.random.normal(arg_keys[14], (NB, E), jnp.float32), 0.5, 1.5),
        "gain_m": bell_draw(arg_keys[15], (NB, E), (0.005556 / NPARAM ** 0.5), 1.33514404296875e-05, (), jnp.float32),
        "gain_v": jnp.clip(jnp.exp(jax.random.uniform(arg_keys[16], (NB, E), jnp.float32, math.log(6.48116475310094e-14), math.log(2.592465901240376e-13))), 6.48116475310094e-14, 2.592465901240376e-13),
    }


@jax.custom_vjp
def low(v):
    return lax.optimization_barrier(v.astype(jnp.bfloat16)).astype(jnp.float32)

@jax.custom_vjp
def low_back(v):
    return v

def low_keep(v):
    return (low(v), None)

def low_pass(kept, grad):
    return (grad,)

def back_keep(v):
    return (v, None)

def back_low(kept, grad):
    return (low(grad),)
low.defvjp(low_keep, low_pass)
low_back.defvjp(back_keep, back_low)
beta_first = 0.9
beta_second = 0.999
adam_eps = 1e-08
weight_decay = 0.01
learn_rate = 0.4
clip_norm = 0.05
norm_eps = 1e-05

def contract(form, left, right):
    return jnp.einsum(form, left, right, precision=lax.Precision.HIGHEST)

def legendre(orders, angles):
    cosines = jnp.cos(angles)[None, :]
    sines = jnp.sin(angles)[None, :]
    order_col = orders[:, None]
    log_start = 0.5 * (jnp.log((2.0 * order_col + 1.0) / (4.0 * math.pi)) + lax.lgamma(2.0 * order_col + 1.0) - 2.0 * lax.lgamma(order_col + 1.0) - order_col * math.log(4.0)) + order_col * jnp.log(sines)
    starting = jnp.exp(log_start)

    def advance(carry, degree):
        previous, earlier = carry
        upper = jnp.maximum(degree * degree - order_col * order_col, 1.0)
        factor = jnp.sqrt(jnp.maximum(4.0 * degree * degree - 1.0, 1.0) / upper)
        lower = jnp.maximum((degree - 1.0) ** 2 - order_col * order_col, 0.0)
        shrink = jnp.sqrt(lower / jnp.maximum(4.0 * (degree - 1.0) ** 2 - 1.0, 1.0))
        stepped = factor * (cosines * previous - shrink * earlier)
        second = jnp.sqrt(2.0 * order_col + 3.0) * cosines * starting
        value = jnp.where(degree < order_col, 0.0, jnp.where(degree == order_col, starting, jnp.where(degree == order_col + 1.0, second, stepped)))
        return ((value, previous), value)
    zero_rows = jnp.zeros_like(starting)
    unused, table = lax.scan(advance, (zero_rows, zero_rows), jnp.arange(L, dtype=jnp.float32))
    return table

def dft_tables(orders, count_lon):
    phases = orders[:, None] * jnp.arange(count_lon, dtype=jnp.int32)[None, :] % count_lon
    phase = phases.astype(jnp.float32) * (2.0 * math.pi / count_lon)
    cosines = jnp.cos(phase)
    sines = jnp.sin(phase)
    number = orders.shape[0]
    forward = jnp.stack([cosines, -sines], 1).reshape(2 * number, count_lon)
    factor = jnp.where(orders == 0, 1.0, 2.0)[:, None] / math.sqrt(2.0 * math.pi)
    inverse = jnp.stack([factor * cosines, -factor * sines], 1).reshape(2 * number, count_lon).T
    return (forward, inverse)

def adaptive(weight, first, second, grad, step_float):
    first_new = beta_first * first + (1.0 - beta_first) * grad
    second_new = beta_second * second + (1.0 - beta_second) * grad * grad
    direction = first_new / (1.0 - beta_first ** step_float) / (jnp.sqrt(second_new / (1.0 - beta_second ** step_float)) + adam_eps) + weight_decay * weight
    return (first_new, second_new, direction)

def lamb_dense(weight, first, second, grad, step_float, groups):
    first_new, second_new, direction = adaptive(weight, first, second, grad, step_float)
    flat_weight = weight.reshape(groups, -1)
    flat_dir = direction.reshape(groups, -1)
    weight_norm = jnp.sqrt(lax.optimization_barrier(jnp.sum(flat_weight * flat_weight, 1)))
    dir_norm = jnp.sqrt(lax.optimization_barrier(jnp.sum(flat_dir * flat_dir, 1)))
    trust = weight_norm / (dir_norm + 1e-06)
    new_weight = (flat_weight - learn_rate * trust[:, None] * flat_dir).reshape(weight.shape)
    return (new_weight, first_new, second_new, jnp.stack([weight_norm, dir_norm], 1))

def layer_norm(hidden, gain_vec):
    centre = lax.optimization_barrier(jnp.mean(hidden, -1, keepdims=True))
    centred = hidden - centre
    inv_std = lax.rsqrt(lax.optimization_barrier(jnp.mean(centred * centred, -1, keepdims=True)) + norm_eps)
    return centred * inv_std * gain_vec

def forward_model(state, params, tables):
    spec, encdec, mlp, gains = params
    fwd_four, inv_four, fwd_leg, inv_leg = tables
    hidden = low_back(contract('jic,ce->jie', low(state), low(encdec[0])))
    for block_idx in range(NB):
        normed = low(layer_norm(hidden, gains[block_idx]))
        spec_rows = low_back(low(contract('kj,jie->kie', fwd_four, normed)))
        paired = spec_rows.reshape(L, 2, NLAT, E)
        coeffs = low(contract('lmi,mpie->lmpe', fwd_leg, paired))
        weight = low(spec[block_idx])
        real_w = weight[:, 0]
        imag_w = weight[:, 1]
        mixed_real = contract('lme,leo->lmo', coeffs[:, :, 0], real_w) - contract('lme,leo->lmo', coeffs[:, :, 1], imag_w)
        mixed_imag = contract('lme,leo->lmo', coeffs[:, :, 0], imag_w) + contract('lme,leo->lmo', coeffs[:, :, 1], real_w)
        mixed = low_back(low(jnp.stack([mixed_real, mixed_imag], 2)))
        spec_out = low_back(low(contract('lmi,lmpo->mpio', inv_leg, mixed).reshape(2 * L, NLAT, E)))
        filtered = low_back(contract('jk,kie->jie', inv_four, spec_out))
        merged = hidden + filtered
        pre_act = low_back(contract('jie,ef->jif', low(merged), low(mlp[block_idx, 0])))
        gelu_out = low(jax.nn.gelu(pre_act))
        hidden = merged + low_back(contract('jif,ef->jie', gelu_out, low(mlp[block_idx, 1])))
    return state + low_back(contract('jie,ce->jic', low(hidden), low(encdec[1])))

def total_loss(params, inputs, targets, pixel_weight, tables):
    state = inputs
    total = jnp.zeros((), jnp.float32)
    for section_idx in range(ROLL):
        prediction = forward_model(state, params, tables)
        misfit = prediction - targets[section_idx]
        total = total + jnp.sum(pixel_weight * misfit * misfit)
        state = prediction
    return total / (BATCH * NLON * NLAT * C)

def reference(inputs, targets, mask, var_weight, step_count, spec_w, spec_m, spec_v, encdec_w, encdec_m, encdec_v, mlp_w, mlp_m, mlp_v, gain_w, gain_m, gain_v):
    angles = (jnp.arange(NLAT, dtype=jnp.float32) + 0.5) * (math.pi / NLAT)
    orders = jnp.arange(L, dtype=jnp.int32)
    table = legendre(orders.astype(jnp.float32), angles)
    quadrature = jnp.sin(angles) * (math.sqrt(2.0 * math.pi) / NLON * math.pi / NLAT)
    fwd_four, inv_four = dft_tables(orders, NLON)
    tables = (low(fwd_four), low(inv_four), low(table * quadrature[None, None, :]), low(table))
    sines = jnp.sin(angles)
    area = sines / jnp.mean(sines)
    params = (spec_w, encdec_w, mlp_w, gain_w)
    item_targets = jnp.transpose(targets, (1, 0, 2, 3, 4))

    def one_item(carry, item):
        loss_sum, grad_sum = carry
        item_in, item_tgt, item_mask = item
        pixel_weight = area[None, :, None] * var_weight.astype(jnp.float32)[None, None, :] * item_mask.astype(jnp.float32)[:, :, None]

        def objective(values):
            return total_loss(values, item_in, item_tgt, pixel_weight, tables)
        loss_item, pullback = jax.vjp(objective, params)
        grads_item = pullback(jnp.ones((), jnp.float32))[0]
        return ((loss_sum + loss_item, jax.tree.map(jnp.add, grad_sum, grads_item)), None)
    start = (jnp.zeros((), jnp.float32), jax.tree.map(jnp.zeros_like, params))
    (loss_value, grads), unused = lax.scan(one_item, start, (inputs, item_targets, mask))
    square = jnp.zeros((), jnp.float32)
    for grad in grads:
        square = square + jnp.sum(grad * grad)
    grad_norm = jnp.sqrt(square)
    scale = clip_norm / jnp.maximum(grad_norm, clip_norm)
    step_float = step_count[0].astype(jnp.float32)
    spec_new, spec_m_new, spec_v_new, spec_norms = lamb_dense(spec_w, spec_m, spec_v, grads[0] * scale, step_float, NB)
    encdec_new, encdec_m_new, encdec_v_new, encdec_norms = lamb_dense(encdec_w, encdec_m, encdec_v, grads[1] * scale, step_float, 2)
    mlp_new, mlp_m_new, mlp_v_new, mlp_norms = lamb_dense(mlp_w, mlp_m, mlp_v, grads[2] * scale, step_float, 2 * NB)
    gain_new, gain_m_new, gain_v_new, gain_norms = lamb_dense(gain_w, gain_m, gain_v, grads[3] * scale, step_float, NB)
    matrix_norms = jnp.concatenate([spec_norms, encdec_norms, mlp_norms, gain_norms], 0)
    return (loss_value, grad_norm, matrix_norms, spec_new, spec_m_new, spec_v_new, spec_new.astype(jnp.bfloat16), encdec_new, encdec_m_new, encdec_v_new, encdec_new.astype(jnp.bfloat16), mlp_new, mlp_m_new, mlp_v_new, mlp_new.astype(jnp.bfloat16), gain_new, gain_m_new, gain_v_new, gain_new.astype(jnp.bfloat16))
```

```python
import functools
import math

import jax
import jax.numpy as jnp
import ml_dtypes
import numpy as np
from jax import lax
from jax.experimental import pallas as pl
from jax.experimental.pallas import tpu as pltpu
from jax.sharding import PartitionSpec as P

E = 256
C = 73
L = 96
NB = 3
ROLL = 2


beta_first = 0.9
beta_second = 0.999
adam_eps = 1e-08
weight_decay = 0.01
learn_rate = 0.4
clip_norm = 0.05
norm_eps = 1e-05


def legendre(orders, angles):
    cosines = jnp.cos(angles)[None, :]
    sines = jnp.sin(angles)[None, :]
    order_col = orders[:, None]
    log_start = 0.5 * (
        jnp.log((2.0 * order_col + 1.0) / (4.0 * math.pi))
        + lax.lgamma(2.0 * order_col + 1.0)
        - 2.0 * lax.lgamma(order_col + 1.0)
        - order_col * math.log(4.0)
    ) + order_col * jnp.log(sines)
    starting = jnp.exp(log_start)

    def advance(carry, degree):
        previous, earlier = carry
        upper = jnp.maximum(degree * degree - order_col * order_col, 1.0)
        factor = jnp.sqrt(jnp.maximum(4.0 * degree * degree - 1.0, 1.0) / upper)
        lower = jnp.maximum((degree - 1.0) ** 2 - order_col * order_col, 0.0)
        shrink = jnp.sqrt(lower / jnp.maximum(4.0 * (degree - 1.0) ** 2 - 1.0, 1.0))
        stepped = factor * (cosines * previous - shrink * earlier)
        second = jnp.sqrt(2.0 * order_col + 3.0) * cosines * starting
        value = jnp.where(
            degree < order_col,
            0.0,
            jnp.where(
                degree == order_col, starting, jnp.where(degree == order_col + 1.0, second, stepped)
            ),
        )
        return ((value, previous), value)

    zero_rows = jnp.zeros_like(starting)
    unused, table = lax.scan(advance, (zero_rows, zero_rows), jnp.arange(L, dtype=jnp.float32))
    return table


def dft_tables(orders, count_lon):
    phases = orders[:, None] * jnp.arange(count_lon, dtype=jnp.int32)[None, :] % count_lon
    phase = phases.astype(jnp.float32) * (2.0 * math.pi / count_lon)
    cosines = jnp.cos(phase)
    sines = jnp.sin(phase)
    number = orders.shape[0]
    forward = jnp.stack([cosines, -sines], 1).reshape(2 * number, count_lon)
    factor = jnp.where(orders == 0, 1.0, 2.0)[:, None] / math.sqrt(2.0 * math.pi)
    inverse = jnp.stack([factor * cosines, -factor * sines], 1).reshape(2 * number, count_lon).T
    return (forward, inverse)


def adaptive(weight, first, second, grad, step_float):
    first_new = beta_first * first + (1.0 - beta_first) * grad
    second_new = beta_second * second + (1.0 - beta_second) * grad * grad
    direction = (
        first_new
        / (1.0 - beta_first**step_float)
        / (jnp.sqrt(second_new / (1.0 - beta_second**step_float)) + adam_eps)
        + weight_decay * weight
    )
    return (first_new, second_new, direction)


def lamb_dense(weight, first, second, grad, step_float, groups):
    first_new, second_new, direction = adaptive(weight, first, second, grad, step_float)
    flat_weight = weight.reshape(groups, -1)
    flat_dir = direction.reshape(groups, -1)
    weight_norm = jnp.sqrt(jnp.sum(flat_weight * flat_weight, 1))
    dir_norm = jnp.sqrt(jnp.sum(flat_dir * flat_dir, 1))
    trust = weight_norm / (dir_norm + 1e-06)
    new_weight = (flat_weight - learn_rate * trust[:, None] * flat_dir).reshape(weight.shape)
    return (new_weight, first_new, second_new, jnp.stack([weight_norm, dir_norm], 1))


def norm_forward(hidden, gain_vec):
    centre = jnp.mean(hidden, -1, keepdims=True)
    centred = hidden - centre
    inv_std = lax.rsqrt(jnp.mean(centred * centred, -1, keepdims=True) + norm_eps)
    normal = centred * inv_std
    return ((normal * gain_vec).astype(jnp.bfloat16), normal, inv_std)


def norm_backward(d_normed, normal, inv_std, gain_vec):
    scaled = d_normed * gain_vec
    d_gain = jnp.sum(d_normed * normal, axis=(0, 1, 2))
    d_hidden = inv_std * (
        scaled
        - jnp.mean(scaled, -1, keepdims=True)
        - normal * jnp.mean(scaled * normal, -1, keepdims=True)
    )
    return (d_hidden, d_gain)


def mlp_forward(merged, weights):
    merged_low = merged.astype(jnp.bfloat16)
    pre_act = jnp.einsum(
        "jibe,ef->jibf", merged_low, weights[0], preferred_element_type=jnp.float32
    )
    gelu_out = jax.nn.gelu(pre_act).astype(jnp.bfloat16)
    hidden = merged + jnp.einsum(
        "jibf,ef->jibe", gelu_out, weights[1], preferred_element_type=jnp.float32
    )
    return (hidden, (merged_low, pre_act, gelu_out))


def mlp_backward(d_hidden, stored, weights):
    merged_low, pre_act, gelu_out = stored
    d_branch = d_hidden.astype(jnp.bfloat16)
    d_gelu = jnp.einsum("jibe,ef->jibf", d_branch, weights[1], preferred_element_type=jnp.float32)
    unused, pullback = jax.vjp(jax.nn.gelu, pre_act)
    d_pre = pullback(d_gelu)[0].astype(jnp.bfloat16)
    grad_out = jnp.einsum("jibf,jibe->ef", gelu_out, d_branch, preferred_element_type=jnp.float32)
    grad_in = jnp.einsum("jibe,jibf->ef", merged_low, d_pre, preferred_element_type=jnp.float32)
    d_merged = d_hidden + jnp.einsum(
        "jibf,ef->jibe", d_pre, weights[0], preferred_element_type=jnp.float32
    )
    return (d_merged, jnp.stack([grad_in, grad_out], 0))


def general(
    inputs,
    targets,
    mask,
    var_weight,
    step_count,
    spec_w,
    spec_m,
    spec_v,
    encdec_w,
    encdec_m,
    encdec_v,
    mlp_w,
    mlp_m,
    mlp_v,
    gain_w,
    gain_m,
    gain_v,
):
    n_ma = lax.axis_size("ma")
    n_lat = lax.axis_size("lat")
    ma_pos = lax.axis_index("ma")
    lat_pos = lax.axis_index("lat")
    batch = inputs.shape[0]
    lon_loc = inputs.shape[1]
    lat_loc = inputs.shape[2]
    nlon_all = lon_loc * n_ma
    nlat_all = lat_loc * n_lat
    orders_loc = L // n_ma
    angles = (jnp.arange(nlat_all, dtype=jnp.float32) + 0.5) * (math.pi / nlat_all)
    local_orders = ma_pos * orders_loc + jnp.arange(orders_loc, dtype=jnp.int32)
    table = legendre(local_orders.astype(jnp.float32), angles)
    quadrature = jnp.sin(angles) * (math.sqrt(2.0 * math.pi) / nlon_all * math.pi / nlat_all)
    fwd_leg = (table * quadrature[None, None, :]).astype(jnp.bfloat16)
    inv_leg = table.astype(jnp.bfloat16)
    fwd_table, inv_table = dft_tables(jnp.arange(L, dtype=jnp.int32), nlon_all)
    fwd_four = fwd_table.astype(jnp.bfloat16)
    inv_four = inv_table.astype(jnp.bfloat16)
    fwd_back = fwd_four.T
    inv_back = inv_four.T
    sines = jnp.sin(angles)
    area = sines / jnp.mean(sines)
    area_rows = lax.dynamic_slice_in_dim(area, lat_pos * lat_loc, lat_loc)
    mask_grid = jnp.transpose(mask, (1, 2, 0)).astype(jnp.float32)
    pixel_weight = (
        area_rows[None, :, None, None]
        * var_weight.astype(jnp.float32)[None, None, None, :]
        * mask_grid[:, :, :, None]
    )
    grid_targets = jnp.transpose(targets, (0, 2, 3, 1, 4))
    denom = float(batch * nlon_all * nlat_all * C)

    def apply_table(table_full, block_in):
        whole_out = jnp.einsum(
            "ok,kibe->oibe",
            table_full,
            lax.all_to_all(block_in, "ma", split_axis=3, concat_axis=0, tiled=True),
            preferred_element_type=jnp.float32,
        )
        return lax.all_to_all(
            whole_out.astype(jnp.bfloat16), "ma", split_axis=0, concat_axis=3, tiled=True
        ).astype(whole_out.dtype)

    def spectral_backward(d_filtered, owned, weight_blk):
        d_rows = apply_table(inv_back, d_filtered.astype(jnp.bfloat16)).astype(jnp.bfloat16)
        d_spec = lax.all_to_all(d_rows, "lat", split_axis=3, concat_axis=1, tiled=True)
        out_width = d_spec.shape[3]
        d_mixed = jnp.einsum(
            "lmi,mpibo->lmpbo",
            inv_leg,
            d_spec.reshape(orders_loc, 2, nlat_all, batch, out_width),
            preferred_element_type=jnp.float32,
        ).astype(jnp.bfloat16)
        d_own = lax.all_to_all(d_mixed, "ma", split_axis=0, concat_axis=1, tiled=True)
        real_w = weight_blk[:, 0]
        imag_w = weight_blk[:, 1]
        d_real = d_own[:, :, 0]
        d_imag = d_own[:, :, 1]
        d_coef_real = jnp.einsum(
            "lmbo,leo->lmbe", d_real, real_w, preferred_element_type=jnp.float32
        ) + jnp.einsum("lmbo,leo->lmbe", d_imag, imag_w, preferred_element_type=jnp.float32)
        d_coef_imag = jnp.einsum(
            "lmbo,leo->lmbe", d_imag, real_w, preferred_element_type=jnp.float32
        ) - jnp.einsum("lmbo,leo->lmbe", d_real, imag_w, preferred_element_type=jnp.float32)
        grad_real = jnp.einsum(
            "lmbe,lmbo->leo", owned[:, :, 0], d_real, preferred_element_type=jnp.float32
        ) + jnp.einsum("lmbe,lmbo->leo", owned[:, :, 1], d_imag, preferred_element_type=jnp.float32)
        grad_imag = jnp.einsum(
            "lmbe,lmbo->leo", owned[:, :, 0], d_imag, preferred_element_type=jnp.float32
        ) - jnp.einsum("lmbe,lmbo->leo", owned[:, :, 1], d_real, preferred_element_type=jnp.float32)
        d_owned = jnp.stack([d_coef_real, d_coef_imag], 2)
        d_coeffs = lax.all_to_all(
            d_owned.astype(jnp.bfloat16), "ma", split_axis=1, concat_axis=0, tiled=True
        ).astype(d_owned.dtype)
        d_full = jnp.einsum(
            "lmi,lmpbe->mpibe",
            fwd_leg.astype(jnp.float32),
            d_coeffs,
            precision=lax.Precision.HIGHEST,
        ).reshape(2 * orders_loc, nlat_all, batch, E)
        d_spec_rows = lax.psum_scatter(
            d_full.astype(jnp.bfloat16), "lat", scatter_dimension=1, tiled=True
        )
        return (apply_table(fwd_back, d_spec_rows), jnp.stack([grad_real, grad_imag], 1))

    spec_bf = spec_w.astype(jnp.bfloat16)
    encdec_bf = encdec_w.astype(jnp.bfloat16)
    mlp_bf = mlp_w.astype(jnp.bfloat16)

    def model_backward(d_pred, stored):
        state_low, hidden_low, records = stored
        d_dec = d_pred.astype(jnp.bfloat16)
        grad_dec = jnp.einsum(
            "jibe,jibc->ce", hidden_low, d_dec, preferred_element_type=jnp.float32
        )
        d_hidden = jnp.einsum(
            "jibc,ce->jibe", d_dec, encdec_bf[1], preferred_element_type=jnp.float32
        )
        spec_grads = [None] * NB
        mlp_grads = [None] * NB
        gain_grads = [None] * NB
        for block_idx in reversed(range(NB)):
            normal, inv_std, owned, mlp_kept = records[block_idx]
            d_merged, mlp_grads[block_idx] = mlp_backward(d_hidden, mlp_kept, mlp_bf[block_idx])
            d_normed, spec_grads[block_idx] = spectral_backward(d_merged, owned, spec_bf[block_idx])
            d_norm_in, gain_grads[block_idx] = norm_backward(
                d_normed, normal, inv_std, gain_w[block_idx]
            )
            d_hidden = d_merged + d_norm_in
        d_enc = d_hidden.astype(jnp.bfloat16)
        grad_enc = jnp.einsum("jibc,jibe->ce", state_low, d_enc, preferred_element_type=jnp.float32)
        d_state = d_pred + jnp.einsum(
            "jibe,ce->jibc", d_enc, encdec_bf[0], preferred_element_type=jnp.float32
        )
        return (
            d_state,
            (
                jnp.stack([grad_enc, grad_dec], 0),
                jnp.stack(spec_grads, 0),
                jnp.stack(mlp_grads, 0),
                jnp.stack(gain_grads, 0),
            ),
        )

    state = jnp.transpose(inputs, (1, 2, 0, 3))
    history = []
    loss_part = jnp.zeros((), jnp.float32)
    for section_idx in range(ROLL):
        model_state_low = state.astype(jnp.bfloat16)
        hidden = jnp.einsum(
            "jibc,ce->jibe", model_state_low, encdec_bf[0], preferred_element_type=jnp.float32
        )
        model_records = []
        for model_block_idx in range(NB):
            model_normed, model_normal, model_inv_std = norm_forward(
                hidden, gain_w[model_block_idx]
            )
            spectral_weight_blk = spec_bf[model_block_idx]
            spec_rows = apply_table(fwd_four, model_normed).astype(jnp.bfloat16)
            piece = lax.all_gather(spec_rows, "lat", axis=1, tiled=True)
            row_width = piece.shape[1]
            paired = piece.reshape(orders_loc, 2, row_width, piece.shape[2], piece.shape[3])
            coeffs = jnp.einsum(
                "lmi,mpibe->lmpbe", fwd_leg, paired, preferred_element_type=jnp.float32
            ).astype(jnp.bfloat16)
            spectral_owned = lax.all_to_all(coeffs, "ma", split_axis=0, concat_axis=1, tiled=True)
            spectral_real_w = spectral_weight_blk[:, 0]
            spectral_imag_w = spectral_weight_blk[:, 1]
            mixed_real = jnp.einsum(
                "lmbe,leo->lmbo",
                spectral_owned[:, :, 0],
                spectral_real_w,
                preferred_element_type=jnp.float32,
            ) - jnp.einsum(
                "lmbe,leo->lmbo",
                spectral_owned[:, :, 1],
                spectral_imag_w,
                preferred_element_type=jnp.float32,
            )
            mixed_imag = jnp.einsum(
                "lmbe,leo->lmbo",
                spectral_owned[:, :, 0],
                spectral_imag_w,
                preferred_element_type=jnp.float32,
            ) + jnp.einsum(
                "lmbe,leo->lmbo",
                spectral_owned[:, :, 1],
                spectral_real_w,
                preferred_element_type=jnp.float32,
            )
            mixed_owned = jnp.stack([mixed_real, mixed_imag], 2).astype(jnp.bfloat16)
            mixed = lax.all_to_all(mixed_owned, "ma", split_axis=1, concat_axis=0, tiled=True)
            spec_out = jnp.einsum(
                "lmi,lmpbo->mpibo", inv_leg, mixed, preferred_element_type=jnp.float32
            )
            spec_out = spec_out.astype(jnp.bfloat16).reshape(
                2 * orders_loc, nlat_all, batch, mixed.shape[4]
            )
            rows_out = lax.all_to_all(spec_out, "lat", split_axis=1, concat_axis=3, tiled=True)
            filtered = apply_table(inv_four, rows_out)
            hidden, model_mlp_kept = mlp_forward(hidden + filtered, mlp_bf[model_block_idx])
            model_records.append((model_normal, model_inv_std, spectral_owned, model_mlp_kept))
        model_hidden_low = hidden.astype(jnp.bfloat16)
        prediction = state + jnp.einsum(
            "jibe,ce->jibc", model_hidden_low, encdec_bf[1], preferred_element_type=jnp.float32
        )
        prediction, stored = (prediction, (model_state_low, model_hidden_low, model_records))
        misfit = prediction - grid_targets[section_idx]
        loss_part = loss_part + jnp.sum(pixel_weight * misfit * misfit) / denom
        history.append((stored, misfit))
        state = prediction
    d_state = jnp.zeros_like(state)
    totals = None
    for section_idx in reversed(range(ROLL)):
        stored, misfit = history[section_idx]
        d_pred = 2.0 * pixel_weight * misfit / denom + d_state
        d_state, section_grads = model_backward(d_pred, stored)
        totals = section_grads if totals is None else jax.tree.map(jnp.add, totals, section_grads)
    grad_encdec, spec_grad, grad_mlp, grad_gain = totals
    grad_encdec, grad_mlp, grad_gain, loss_value, spec_square, weight_square = lax.psum(
        (
            grad_encdec,
            grad_mlp,
            grad_gain,
            loss_part,
            jnp.sum(spec_grad * spec_grad),
            jnp.sum(spec_w * spec_w, axis=(1, 2, 3, 4)),
        ),
        ("lat", "ma"),
    )
    total_square = (
        spec_square
        + jnp.sum(grad_encdec * grad_encdec)
        + jnp.sum(grad_mlp * grad_mlp)
        + jnp.sum(grad_gain * grad_gain)
    )
    grad_norm = jnp.sqrt(total_square)
    scale = clip_norm / jnp.maximum(grad_norm, clip_norm)
    step_float = step_count[0].astype(jnp.float32)
    spec_m_new, spec_v_new, direction = adaptive(
        spec_w, spec_m, spec_v, spec_grad * scale, step_float
    )
    dir_square = lax.psum(jnp.sum(direction * direction, axis=(1, 2, 3, 4)), ("lat", "ma"))
    weight_norm = jnp.sqrt(weight_square)
    dir_norm = jnp.sqrt(dir_square)
    trust = weight_norm / (dir_norm + 1e-06)
    spec_new = spec_w - learn_rate * trust[:, None, None, None, None] * direction
    encdec_new, encdec_m_new, encdec_v_new, encdec_norms = lamb_dense(
        encdec_w, encdec_m, encdec_v, grad_encdec * scale, step_float, 2
    )
    mlp_new, mlp_m_new, mlp_v_new, mlp_norms = lamb_dense(
        mlp_w, mlp_m, mlp_v, grad_mlp * scale, step_float, 2 * NB
    )
    gain_new, gain_m_new, gain_v_new, gain_norms = lamb_dense(
        gain_w, gain_m, gain_v, grad_gain * scale, step_float, NB
    )
    matrix_norms = jnp.concatenate(
        [jnp.stack([weight_norm, dir_norm], 1), encdec_norms, mlp_norms, gain_norms], 0
    )
    return (
        loss_value,
        grad_norm,
        matrix_norms,
        spec_new,
        spec_m_new,
        spec_v_new,
        spec_new.astype(jnp.bfloat16),
        encdec_new,
        encdec_m_new,
        encdec_v_new,
        encdec_new.astype(jnp.bfloat16),
        mlp_new,
        mlp_m_new,
        mlp_v_new,
        mlp_new.astype(jnp.bfloat16),
        gain_new,
        gain_m_new,
        gain_v_new,
        gain_new.astype(jnp.bfloat16),
    )


RANKS = 16
ORDS = L // RANKS
SLOTS = 8
F32 = jnp.float32
BF16 = jnp.bfloat16


def legendre_f64(nlat):
    theta = (np.arange(nlat) + 0.5) * (math.pi / nlat)
    cosines, sines = np.cos(theta), np.sin(theta)
    table = np.zeros((L, L, nlat))
    for m in range(L):
        log_start = 0.5 * (
            math.log((2.0 * m + 1.0) / (4.0 * math.pi))
            + math.lgamma(2.0 * m + 1.0)
            - 2.0 * math.lgamma(m + 1.0)
            - m * math.log(4.0)
        ) + m * np.log(sines)
        table[m, m] = np.exp(log_start)
        if m + 1 < L:
            table[m + 1, m] = math.sqrt(2.0 * m + 3.0) * cosines * table[m, m]
        for k in range(m + 2, L):
            factor = math.sqrt((4.0 * k * k - 1.0) / (k * k - m * m))
            shrink = math.sqrt(((k - 1.0) ** 2 - m * m) / (4.0 * (k - 1.0) ** 2 - 1.0))
            table[k, m] = factor * (cosines * table[k - 1, m] - shrink * table[k - 2, m])
    return table, sines


def low_np(array):
    return array.astype(np.float32).astype(ml_dtypes.bfloat16)


def slot_map():
    degree = np.full((RANKS, 3, SLOTS), -1)
    order = np.full((RANKS, SLOTS), -1)
    for d in range(RANKS):
        y, w, xc = d // 8, (d // 4) % 2, d % 4
        lo, hi = 4 * w + xc, 4 * (3 - w) + xc
        n_lo, n_hi = (6 * lo + 5) // RANKS + 1, (6 * hi + 5) // RANKS + 1
        for group, first, count in ((hi, 0, n_hi), (lo, SLOTS - n_lo, n_lo)):
            for r in range(count):
                order[d, first + r] = r
                for t in range(3):
                    degree[d, t, first + r] = 6 * group + 3 * y + t
    return degree, order


def make_tables(nlat, nlon):
    table, sines = legendre_f64(nlat)
    quadrature = sines * (math.sqrt(2.0 * math.pi) / nlon * math.pi / nlat)
    fwd_leg = np.asarray(low_np(table * quadrature[None, None, :]))
    inv_leg = np.asarray(low_np(table))
    degree, order = slot_map()
    shape = (RANKS, RANKS, 3, 2, SLOTS, RANKS, ORDS, 2, 2)
    fwd = np.zeros(shape, ml_dtypes.bfloat16)
    inv = np.zeros(shape, ml_dtypes.bfloat16)
    for g in range(RANKS):
        for d in range(RANKS):
            for slot in range(SLOTS):
                r = order[d, slot]
                if r < 0:
                    continue
                for t in range(3):
                    k, m = degree[d, t, slot], g + RANKS * r
                    for p in range(2):
                        fwd[g, d, t, p, slot, :, r, p, :] = fwd_leg[k, m].reshape(RANKS, 2)
                        inv[g, d, t, p, slot, :, r, p, :] = inv_leg[k, m].reshape(RANKS, 2)
    rows = RANKS * 3 * 2 * SLOTS
    cols = RANKS * ORDS * 2 * 2
    fwd = fwd.reshape(RANKS, rows, cols)
    inv = inv.reshape(RANKS, rows, cols).transpose(0, 2, 1)
    phase = 2.0 * math.pi * (np.arange(L)[:, None] * np.arange(nlon)[None, :] % nlon) / nlon
    scale = np.where(np.arange(L) == 0, 1.0, 2.0)[:, None] / math.sqrt(2.0 * math.pi)
    four = low_np(np.stack([np.cos(phase), -np.sin(phase)], 1))
    back = low_np(np.stack([scale * np.cos(phase), -scale * np.sin(phase)], 1))
    def wide(small):
        out = np.zeros((RANKS, ORDS, 2, 2, 2, nlon), ml_dtypes.bfloat16)
        ordered = small.reshape(ORDS, RANKS, 2, nlon).transpose(1, 0, 2, 3)
        for il in range(2):
            out[:, :, :, il, il, :] = ordered
        return out.reshape(cols, 2 * nlon)
    return fwd, np.ascontiguousarray(inv), wide(four), np.ascontiguousarray(wide(back).T)


def place():
    ma = lax.axis_index("ma")
    y = lax.axis_index("lat")
    z = ma // 4
    zh = z // 2
    w = z + zh * (3 - 2 * z)
    return zh, y, w, 8 * y + 4 * w + ma % 4


def device_of(zh, q):
    w = (q // 4) % 2
    z = w + zh * (3 - 2 * w)
    return {"lat": q // 8, "ma": 4 * z + q % 4}


def enter(zh, q):
    barrier = pltpu.get_barrier_semaphore()

    def greet(s, carry):
        pl.semaphore_signal(
            barrier, inc=1, device_id=device_of(zh, (q + s) % RANKS), device_id_type=pl.DeviceIdType.MESH
        )
        return carry

    lax.fori_loop(1, RANKS, greet, 0)
    pl.semaphore_wait(barrier, RANKS - 1)


def exchange(send, recv, send_sem, recv_sem, zh, q):
    pltpu.make_async_copy(send.at[q], recv.at[q], recv_sem).start()

    def push(s, carry):
        d = (q + s) % RANKS
        pltpu.make_async_remote_copy(
            src_ref=send.at[d],
            dst_ref=recv.at[q],
            send_sem=send_sem,
            recv_sem=recv_sem,
            device_id=device_of(zh, d),
            device_id_type=pl.DeviceIdType.MESH,
        ).start()
        return carry

    lax.fori_loop(1, RANKS, push, 0)
    pltpu.make_async_copy(send, recv, recv_sem).wait()
    rest = pl.ds(0, RANKS - 1)
    pltpu.make_async_copy(send.at[rest], recv.at[rest], send_sem).wait()


def nn(a, b):
    return lax.dot_general(a, b, (((1,), (0,)), ((), ())), preferred_element_type=F32)


def nt(a, b):
    return lax.dot_general(a, b, (((1,), (1,)), ((), ())), preferred_element_type=F32)


def tn(a, b):
    return lax.dot_general(a, b, (((0,), (0,)), ((), ())), preferred_element_type=F32)


def piece_of(kind, half, zh, y):
    return 2 - 2 * ((kind + zh) % 2) + (half + y) % 2


def weight_of(w_ref, kind, t, part, zh, y):
    return jnp.concatenate(
        [w_ref[piece_of(kind, half, zh, y), t, part] for half in range(2)], axis=1
    )


def hi_rows(w):
    slot = lax.broadcasted_iota(jnp.int32, (RANKS * 2 * SLOTS, 1), 0) % SLOTS
    return slot < 6 - w


GELU_A = math.sqrt(2.0 / math.pi)
GELU_B = 0.044715


def normal_of(hidden):
    centre = jnp.mean(hidden, -1, keepdims=True)
    centred = hidden - centre
    inv_std = lax.rsqrt(jnp.mean(centred * centred, -1, keepdims=True) + norm_eps)
    return centred * inv_std, inv_std


def rows_loop(total, step, body):
    def one(k, carry):
        body(pl.ds(pl.multiple_of(k * step, step), step))
        return carry

    lax.fori_loop(0, total // step, one, 0)


def block_fwd(h_ref, gain_ref, ftx, pfx, pix, itx, w_ref, w0, w1, h_out, v_low, a_own,
              u_buf, s_send, s_recv, a_send, b_recv, send_sem, recv_sem):
    zh, y, w, q = place()
    enter(zh, q)
    pixels, chans = h_ref.shape
    gain = gain_ref[...]

    def norm_rows(rows):
        normal, unused = normal_of(h_ref[rows, :])
        u_buf[rows, :] = (normal * gain).astype(BF16)

    rows_loop(pixels, 128, norm_rows)
    s_send[...] = nn(ftx[...], u_buf[...]).astype(BF16).reshape(s_send.shape)
    exchange(s_send, s_recv, send_sem.at[0], recv_sem.at[0], zh, q)
    a_send[...] = nn(pfx[...], s_recv[...].reshape(pix.shape[0], chans)).astype(BF16).reshape(a_send.shape)
    exchange(a_send, a_own, send_sem.at[1], recv_sem.at[1], zh, q)
    hi = hi_rows(w)
    for t in range(3):
        coef = a_own[:, t].reshape(RANKS * 2 * SLOTS, chans)

        def times(part):
            return jnp.where(
                hi,
                nn(coef, weight_of(w_ref, 0, t, part, zh, y)),
                nn(coef, weight_of(w_ref, 1, t, part, zh, y)),
            ).reshape(RANKS, 2, SLOTS, chans)

        by_real, by_imag = times(0), times(1)
        mixed = jnp.stack(
            [by_real[:, 0] - by_imag[:, 1], by_real[:, 1] + by_imag[:, 0]], 1
        )
        a_send[:, t] = mixed.reshape(RANKS, 2 * SLOTS, chans).astype(BF16)
    exchange(a_send, b_recv, send_sem.at[2], recv_sem.at[2], zh, q)
    s_send[...] = nn(pix[...], b_recv[...].reshape(pfx.shape[0], chans)).astype(BF16).reshape(s_send.shape)
    exchange(s_send, s_recv, send_sem.at[3], recv_sem.at[3], zh, q)
    spectrum = s_recv[...].reshape(pix.shape[0], chans)

    def mlp_rows(rows):
        merged = h_ref[rows, :] + nn(itx[rows, :], spectrum)
        merged_low = merged.astype(BF16)
        v_low[rows, :] = merged_low
        pre = nn(merged_low, w0[...])
        act = (0.5 * pre * (1.0 + jnp.tanh(GELU_A * (pre + GELU_B * pre * pre * pre)))).astype(BF16)
        h_out[rows, :] = merged + nt(act, w1[...])

    rows_loop(pixels, 256, mlp_rows)


def block_bwd(dh_ref, h_ref, v_low, a_own, gain_ref, itxt, pixt, pfxt, ftxt, w_ref, w0, w1,
              dh_out, dw_out, dmlp, dgain,
              dv_buf, dv_low, y_send, y_recv, b_send, b_recv, c_recv, send_sem, recv_sem):
    zh, y, w, q = place()
    enter(zh, q)
    pixels, chans = h_ref.shape
    gain = gain_ref[...]
    dmlp[...] = jnp.zeros_like(dmlp)
    dgain[...] = jnp.zeros_like(dgain)

    def mlp_rows(rows):
        d_hidden = dh_ref[rows, :]
        d_branch = d_hidden.astype(BF16)
        merged_low = v_low[rows, :]
        pre = nn(merged_low, w0[...])
        tan = jnp.tanh(GELU_A * (pre + GELU_B * pre * pre * pre))
        act = (0.5 * pre * (1.0 + tan)).astype(BF16)
        slope = 0.5 * (1.0 + tan) + 0.5 * pre * (1.0 - tan * tan) * (GELU_A * (1.0 + 3.0 * GELU_B * pre * pre))
        d_pre = (nn(d_branch, w1[...]) * slope).astype(BF16)
        dmlp[0] += tn(merged_low, d_pre)
        dmlp[1] += tn(d_branch, act)
        d_merged = d_hidden + nt(d_pre, w0[...])
        dv_buf[rows, :] = d_merged
        dv_low[rows, :] = d_merged.astype(BF16)

    rows_loop(pixels, 256, mlp_rows)
    y_send[...] = nn(itxt[...], dv_low[...]).astype(BF16).reshape(y_send.shape)
    exchange(y_send, y_recv, send_sem.at[0], recv_sem.at[0], zh, q)
    b_send[...] = nn(pixt[...], y_recv[...].reshape(itxt.shape[0], chans)).astype(BF16).reshape(b_send.shape)
    exchange(b_send, b_recv, send_sem.at[1], recv_sem.at[1], zh, q)
    hi = hi_rows(w)
    for t in range(3):
        rows = RANKS * 2 * SLOTS
        d_mixed = b_recv[:, t].reshape(rows, chans)
        wide = d_mixed.astype(F32).reshape(RANKS, 2, SLOTS, chans)
        turned = jnp.stack([wide[:, 1], -wide[:, 0]], 1).reshape(rows, chans).astype(BF16)

        def times(part):
            return jnp.where(
                hi,
                nt(d_mixed, weight_of(w_ref, 0, t, part, zh, y)),
                nt(d_mixed, weight_of(w_ref, 1, t, part, zh, y)),
            ).reshape(RANKS, 2, SLOTS, chans)

        by_real, by_imag = times(0), times(1)
        d_coef = jnp.stack([by_real[:, 0] + by_imag[:, 1], by_real[:, 1] - by_imag[:, 0]], 1)
        b_send[:, t] = d_coef.reshape(RANKS, 2 * SLOTS, chans).astype(BF16)
        coef = a_own[:, t].reshape(rows, chans).astype(F32)
        for kind in range(2):
            keep = hi if kind == 0 else jnp.logical_not(hi)
            kept = jnp.where(keep, coef, 0.0).astype(BF16)
            for part, other in enumerate((d_mixed, turned)):
                grad = tn(kept, other)
                for half in range(2):
                    width = chans // 2
                    dw_out[piece_of(kind, half, zh, y), t, part] = grad[:, half * width : (half + 1) * width]
    exchange(b_send, c_recv, send_sem.at[2], recv_sem.at[2], zh, q)
    y_send[...] = nn(pfxt[...], c_recv[...].reshape(pixt.shape[0], chans)).astype(BF16).reshape(y_send.shape)
    exchange(y_send, y_recv, send_sem.at[3], recv_sem.at[3], zh, q)
    spectrum = y_recv[...].reshape(itxt.shape[0], chans)

    def norm_rows(rows):
        normal, inv_std = normal_of(h_ref[rows, :])
        d_normed = nn(ftxt[rows, :], spectrum)
        scaled = d_normed * gain
        dgain[...] += jnp.sum(d_normed * normal, axis=0, keepdims=True)
        d_norm_in = inv_std * (
            scaled
            - jnp.mean(scaled, -1, keepdims=True)
            - normal * jnp.mean(scaled * normal, -1, keepdims=True)
        )
        dh_out[rows, :] = dv_buf[rows, :] + d_norm_in

    rows_loop(pixels, 256, norm_rows)


VMEM = pltpu.VMEM
PARTS = (RANKS, 3, 2 * SLOTS)


def call_fwd(hidden, gain, tables, pieces, mlp):
    pixels, chans = hidden.shape
    narrow = VMEM((RANKS, 4 * ORDS, chans), BF16)
    wide = VMEM((*PARTS, chans), BF16)
    return pl.pallas_call(
        block_fwd,
        out_shape=(
            jax.ShapeDtypeStruct((pixels, chans), F32),
            jax.ShapeDtypeStruct((pixels, chans), BF16),
            jax.ShapeDtypeStruct((*PARTS, chans), BF16),
        ),
        in_specs=[pl.BlockSpec(memory_space=VMEM)] * 9,
        out_specs=[pl.BlockSpec(memory_space=VMEM)] * 3,
        scratch_shapes=[
            VMEM((pixels, chans), BF16),
            narrow,
            narrow,
            wide,
            wide,
            pltpu.SemaphoreType.DMA((4,)),
            pltpu.SemaphoreType.DMA((4,)),
        ],
        compiler_params=pltpu.CompilerParams(
            collective_id=0, has_side_effects=True, vmem_limit_bytes=48 << 20
        ),
    )(hidden, gain[None], *tables, pieces, mlp[0], mlp[1])


def call_bwd(d_hidden, hidden, merged_low, owned, gain, tables, pieces, mlp):
    pixels, chans = hidden.shape
    narrow = VMEM((RANKS, 4 * ORDS, chans), BF16)
    wide = VMEM((*PARTS, chans), BF16)
    return pl.pallas_call(
        block_bwd,
        out_shape=(
            jax.ShapeDtypeStruct((pixels, chans), F32),
            jax.ShapeDtypeStruct(pieces.shape, F32),
            jax.ShapeDtypeStruct(mlp.shape, F32),
            jax.ShapeDtypeStruct((1, chans), F32),
        ),
        in_specs=[pl.BlockSpec(memory_space=VMEM)] * 12,
        out_specs=[pl.BlockSpec(memory_space=VMEM)] * 4,
        scratch_shapes=[
            VMEM((pixels, chans), F32),
            VMEM((pixels, chans), BF16),
            narrow,
            narrow,
            wide,
            wide,
            wide,
            pltpu.SemaphoreType.DMA((4,)),
            pltpu.SemaphoreType.DMA((4,)),
        ],
        compiler_params=pltpu.CompilerParams(
            collective_id=1, has_side_effects=True, vmem_limit_bytes=48 << 20
        ),
    )(d_hidden, hidden, merged_low, owned, gain[None], *tables, pieces, mlp[0], mlp[1])


def regroup(field):
    extra = field.shape[3:]
    items, lon, lat = field.shape[:3]
    pairs = lat // 2
    chunks = jnp.moveaxis(field.reshape(items, lon, pairs, 2, *extra), 1, 3)
    chunks = jnp.concatenate([chunks[0], jnp.roll(chunks[1], pairs // 2, 0)], 0)
    swapped = lax.all_to_all(chunks, "ma", split_axis=0, concat_axis=0, tiled=True)
    return jnp.moveaxis(swapped, 1, 0).reshape(2 * lon * lax.axis_size("ma"), *extra)


def partners(kind):
    pairs = []
    for y in range(2):
        for ma in range(16):
            other_y = 1 - y if kind in (1, 3) else y
            other_ma = 4 * (3 - ma // 4) + ma % 4 if kind in (2, 3) else ma
            pairs.append((16 * y + ma, 16 * other_y + other_ma))
    return pairs


def send_to(kind, array):
    return lax.ppermute(array, ("lat", "ma"), partners(kind))


def special(
    inputs,
    targets,
    mask,
    var_weight,
    step_count,
    spec_w,
    spec_m,
    spec_v,
    encdec_w,
    encdec_m,
    encdec_v,
    mlp_w,
    mlp_m,
    mlp_v,
    gain_w,
    gain_m,
    gain_v,
):
    zh, y, w, q = place()
    batch = inputs.shape[0]
    nlon = inputs.shape[1] * lax.axis_size("ma")
    nlat = inputs.shape[2] * lax.axis_size("lat")
    fwd_leg, inv_leg, fwd_four, inv_four = make_tables(nlat, nlon)
    pfx = lax.dynamic_index_in_dim(jnp.asarray(fwd_leg), q, 0, keepdims=False)
    pix = lax.dynamic_index_in_dim(jnp.asarray(inv_leg), q, 0, keepdims=False)
    ftx, itx = jnp.asarray(fwd_four), jnp.asarray(inv_four)
    fwd_tables = (ftx, pfx, pix, itx)
    bwd_tables = (itx.T, pix.T, pfx.T, ftx.T)
    denom = float(batch * nlon * nlat * C)

    encdec_bf = encdec_w.astype(BF16)
    mlp_bf = mlp_w.astype(BF16)
    state = regroup(inputs)

    third = spec_w.shape[1] // 2
    low = spec_w.astype(BF16)
    pieces = []
    for block in range(NB):
        mine = lax.dynamic_slice_in_dim(low[block], third * y, third, 0)
        other = lax.dynamic_slice_in_dim(low[block], third * (1 - y), third, 0)
        pieces.append(
            jnp.stack([mine, send_to(1, other), send_to(2, mine), send_to(3, other)], 0)
        )

    angles = (jnp.arange(nlat, dtype=F32) + 0.5) * (math.pi / nlat)
    sines = jnp.sin(angles)
    area = lax.dynamic_slice_in_dim(sines / jnp.mean(sines), 2 * q, 2)
    rest = jnp.concatenate(
        [targets[0], targets[1], mask.astype(F32)[..., None]], -1
    )
    rest = regroup(rest)
    goals = (rest[:, :C], rest[:, C : 2 * C])
    pixel_weight = (
        jnp.repeat(area, nlon)[:, None] * rest[:, 2 * C :] * var_weight.astype(F32)[None, :]
    )

    kept = []
    loss_part = jnp.zeros((), F32)
    for step in range(ROLL):
        state_low = state.astype(BF16)
        hidden = nn(state_low, encdec_bf[0])
        records = []
        for block in range(NB):
            out, merged_low, owned = call_fwd(hidden, gain_w[block], fwd_tables, pieces[block], mlp_bf[block])
            records.append((hidden, merged_low, owned))
            hidden = out
        hidden_low = hidden.astype(BF16)
        state = state + nt(hidden_low, encdec_bf[1])
        misfit = state - goals[step]
        loss_part = loss_part + jnp.sum(pixel_weight * misfit * misfit) / denom
        kept.append((state_low, hidden_low, records, misfit))

    spec_sum = [None] * NB
    mlp_sum = [None] * NB
    gain_sum = [None] * NB
    encdec_sum = None
    d_state = None

    def plus(total, term):
        return term if total is None else total + term

    for step in reversed(range(ROLL)):
        state_low, hidden_low, records, misfit = kept[step]
        d_pred = plus(d_state, 2.0 * pixel_weight * misfit / denom)
        d_dec = d_pred.astype(BF16)
        grad_dec = tn(d_dec, hidden_low)
        d_hidden = nn(d_dec, encdec_bf[1])
        for block in reversed(range(NB)):
            hidden, merged_low, owned = records[block]
            d_hidden, dw, dmlp, dgain = call_bwd(
                d_hidden, hidden, merged_low, owned, gain_w[block], bwd_tables, pieces[block], mlp_bf[block]
            )
            spec_sum[block] = plus(spec_sum[block], dw)
            mlp_sum[block] = plus(mlp_sum[block], dmlp)
            gain_sum[block] = plus(gain_sum[block], dgain[0])
        d_enc = d_hidden.astype(BF16)
        encdec_sum = plus(encdec_sum, jnp.stack([tn(state_low, d_enc), grad_dec], 0))
        if step:
            d_state = d_pred + nt(d_enc, encdec_bf[0])

    spec_grad = []
    for block in range(NB):
        total = spec_sum[block]
        sent = total[1:].astype(BF16)
        near, far, cross = send_to(1, sent[0]), send_to(2, sent[1]), send_to(3, sent[2])
        same = total[0] + far.astype(F32)
        other = near.astype(F32) + cross.astype(F32)
        spec_grad.append(jnp.where(y == 0, jnp.concatenate([same, other], 0), jnp.concatenate([other, same], 0)))
    spec_grad = jnp.stack(spec_grad, 0)
    grad_encdec, grad_mlp, grad_gain, loss_value, spec_square, weight_square = lax.psum(
        (
            encdec_sum,
            jnp.stack(mlp_sum, 0),
            jnp.stack(gain_sum, 0),
            loss_part,
            jnp.sum(spec_grad * spec_grad),
            jnp.sum(spec_w * spec_w, axis=(1, 2, 3, 4)),
        ),
        ("lat", "ma"),
    )
    total_square = (
        spec_square
        + jnp.sum(grad_encdec * grad_encdec)
        + jnp.sum(grad_mlp * grad_mlp)
        + jnp.sum(grad_gain * grad_gain)
    )
    grad_norm = jnp.sqrt(total_square)
    scale = clip_norm / jnp.maximum(grad_norm, clip_norm)
    step_float = step_count[0].astype(jnp.float32)
    spec_m_new, spec_v_new, direction = adaptive(
        spec_w, spec_m, spec_v, spec_grad * scale, step_float
    )
    dir_square = lax.psum(jnp.sum(direction * direction, axis=(1, 2, 3, 4)), ("lat", "ma"))
    weight_norm = jnp.sqrt(weight_square)
    dir_norm = jnp.sqrt(dir_square)
    trust = weight_norm / (dir_norm + 1e-06)
    spec_new = spec_w - learn_rate * trust[:, None, None, None, None] * direction
    encdec_new, encdec_m_new, encdec_v_new, encdec_norms = lamb_dense(
        encdec_w, encdec_m, encdec_v, grad_encdec * scale, step_float, 2
    )
    mlp_new, mlp_m_new, mlp_v_new, mlp_norms = lamb_dense(
        mlp_w, mlp_m, mlp_v, grad_mlp * scale, step_float, 2 * NB
    )
    gain_new, gain_m_new, gain_v_new, gain_norms = lamb_dense(
        gain_w, gain_m, gain_v, grad_gain * scale, step_float, NB
    )
    matrix_norms = jnp.concatenate(
        [jnp.stack([weight_norm, dir_norm], 1), encdec_norms, mlp_norms, gain_norms], 0
    )
    return (
        loss_value,
        grad_norm,
        matrix_norms,
        spec_new,
        spec_m_new,
        spec_v_new,
        spec_new.astype(jnp.bfloat16),
        encdec_new,
        encdec_m_new,
        encdec_v_new,
        encdec_new.astype(jnp.bfloat16),
        mlp_new,
        mlp_m_new,
        mlp_v_new,
        mlp_new.astype(jnp.bfloat16),
        gain_new,
        gain_m_new,
        gain_v_new,
        gain_new.astype(jnp.bfloat16),
    )


def local(mesh, *args):
    inputs, spec_w = args[0], args[5]
    lat = inputs.shape[2] * mesh.shape["lat"]
    fits = (
        dict(mesh.shape) == {"lat": 2, "ma": RANKS}
        and inputs.shape[0] == 2
        and lat == 2 * RANKS
        and spec_w.shape[1] * RANKS == L
    )
    return (special if fits else general)(*args)


def solution(mesh):
    placed = (
        P(None, "ma", "lat", None),
        P(None, None, "ma", "lat", None),
        P(None, "ma", "lat"),
        P(),
        P(),
        P(None, "ma", None, None, "lat"),
        P(None, "ma", None, None, "lat"),
        P(None, "ma", None, None, "lat"),
        P(),
        P(),
        P(),
        P(),
        P(),
        P(),
        P(),
        P(),
        P(),
    )
    return jax.shard_map(
        functools.partial(local, mesh),
        mesh=mesh,
        in_specs=placed,
        out_specs=(
            P(),
            P(),
            P(),
            P(None, "ma", None, None, "lat"),
            P(None, "ma", None, None, "lat"),
            P(None, "ma", None, None, "lat"),
            P(None, "ma", None, None, "lat"),
            P(),
            P(),
            P(),
            P(),
            P(),
            P(),
            P(),
            P(),
            P(),
            P(),
            P(),
            P(),
        ),
        check_vma=False,
    )
```

```python
import functools
import math

import jax
import jax.numpy as jnp
import ml_dtypes
import numpy as np
from jax import lax
from jax.experimental import pallas as pl
from jax.experimental.pallas import tpu as pltpu
from jax.sharding import PartitionSpec as P

E = 256
C = 73
L = 96
NB = 3
ROLL = 2


beta_first = 0.9
beta_second = 0.999
adam_eps = 1e-08
weight_decay = 0.01
learn_rate = 0.4
clip_norm = 0.05
norm_eps = 1e-05


def legendre(orders, angles):
    cosines = jnp.cos(angles)[None, :]
    sines = jnp.sin(angles)[None, :]
    order_col = orders[:, None]
    log_start = 0.5 * (
        jnp.log((2.0 * order_col + 1.0) / (4.0 * math.pi))
        + lax.lgamma(2.0 * order_col + 1.0)
        - 2.0 * lax.lgamma(order_col + 1.0)
        - order_col * math.log(4.0)
    ) + order_col * jnp.log(sines)
    starting = jnp.exp(log_start)

    def advance(carry, degree):
        previous, earlier = carry
        upper = jnp.maximum(degree * degree - order_col * order_col, 1.0)
        factor = jnp.sqrt(jnp.maximum(4.0 * degree * degree - 1.0, 1.0) / upper)
        lower = jnp.maximum((degree - 1.0) ** 2 - order_col * order_col, 0.0)
        shrink = jnp.sqrt(lower / jnp.maximum(4.0 * (degree - 1.0) ** 2 - 1.0, 1.0))
        stepped = factor * (cosines * previous - shrink * earlier)
        second = jnp.sqrt(2.0 * order_col + 3.0) * cosines * starting
        value = jnp.where(
            degree < order_col,
            0.0,
            jnp.where(
                degree == order_col, starting, jnp.where(degree == order_col + 1.0, second, stepped)
            ),
        )
        return ((value, previous), value)

    zero_rows = jnp.zeros_like(starting)
    unused, table = lax.scan(advance, (zero_rows, zero_rows), jnp.arange(L, dtype=jnp.float32))
    return table


def dft_tables(orders, count_lon):
    phases = orders[:, None] * jnp.arange(count_lon, dtype=jnp.int32)[None, :] % count_lon
    phase = phases.astype(jnp.float32) * (2.0 * math.pi / count_lon)
    cosines = jnp.cos(phase)
    sines = jnp.sin(phase)
    number = orders.shape[0]
    forward = jnp.stack([cosines, -sines], 1).reshape(2 * number, count_lon)
    factor = jnp.where(orders == 0, 1.0, 2.0)[:, None] / math.sqrt(2.0 * math.pi)
    inverse = jnp.stack([factor * cosines, -factor * sines], 1).reshape(2 * number, count_lon).T
    return (forward, inverse)


def adaptive(weight, first, second, grad, step_float):
    first_new = beta_first * first + (1.0 - beta_first) * grad
    second_new = beta_second * second + (1.0 - beta_second) * grad * grad
    direction = (
        first_new
        / (1.0 - beta_first**step_float)
        / (jnp.sqrt(second_new / (1.0 - beta_second**step_float)) + adam_eps)
        + weight_decay * weight
    )
    return (first_new, second_new, direction)


def lamb_dense(weight, first, second, grad, step_float, groups):
    first_new, second_new, direction = adaptive(weight, first, second, grad, step_float)
    flat_weight = weight.reshape(groups, -1)
    flat_dir = direction.reshape(groups, -1)
    weight_norm = jnp.sqrt(jnp.sum(flat_weight * flat_weight, 1))
    dir_norm = jnp.sqrt(jnp.sum(flat_dir * flat_dir, 1))
    trust = weight_norm / (dir_norm + 1e-06)
    new_weight = (flat_weight - learn_rate * trust[:, None] * flat_dir).reshape(weight.shape)
    return (new_weight, first_new, second_new, jnp.stack([weight_norm, dir_norm], 1))


def norm_forward(hidden, gain_vec):
    centre = jnp.mean(hidden, -1, keepdims=True)
    centred = hidden - centre
    inv_std = lax.rsqrt(jnp.mean(centred * centred, -1, keepdims=True) + norm_eps)
    normal = centred * inv_std
    return ((normal * gain_vec).astype(jnp.bfloat16), normal, inv_std)


def norm_backward(d_normed, normal, inv_std, gain_vec):
    scaled = d_normed * gain_vec
    d_gain = jnp.sum(d_normed * normal, axis=(0, 1, 2))
    d_hidden = inv_std * (
        scaled
        - jnp.mean(scaled, -1, keepdims=True)
        - normal * jnp.mean(scaled * normal, -1, keepdims=True)
    )
    return (d_hidden, d_gain)


def mlp_forward(merged, weights):
    merged_low = merged.astype(jnp.bfloat16)
    pre_act = jnp.einsum(
        "jibe,ef->jibf", merged_low, weights[0], preferred_element_type=jnp.float32
    )
    gelu_out = jax.nn.gelu(pre_act).astype(jnp.bfloat16)
    hidden = merged + jnp.einsum(
        "jibf,ef->jibe", gelu_out, weights[1], preferred_element_type=jnp.float32
    )
    return (hidden, (merged_low, pre_act, gelu_out))


def mlp_backward(d_hidden, stored, weights):
    merged_low, pre_act, gelu_out = stored
    d_branch = d_hidden.astype(jnp.bfloat16)
    d_gelu = jnp.einsum("jibe,ef->jibf", d_branch, weights[1], preferred_element_type=jnp.float32)
    unused, pullback = jax.vjp(jax.nn.gelu, pre_act)
    d_pre = pullback(d_gelu)[0].astype(jnp.bfloat16)
    grad_out = jnp.einsum("jibf,jibe->ef", gelu_out, d_branch, preferred_element_type=jnp.float32)
    grad_in = jnp.einsum("jibe,jibf->ef", merged_low, d_pre, preferred_element_type=jnp.float32)
    d_merged = d_hidden + jnp.einsum(
        "jibf,ef->jibe", d_pre, weights[0], preferred_element_type=jnp.float32
    )
    return (d_merged, jnp.stack([grad_in, grad_out], 0))


def general(
    inputs,
    targets,
    mask,
    var_weight,
    step_count,
    spec_w,
    spec_m,
    spec_v,
    encdec_w,
    encdec_m,
    encdec_v,
    mlp_w,
    mlp_m,
    mlp_v,
    gain_w,
    gain_m,
    gain_v,
):
    n_ma = lax.axis_size("ma")
    n_lat = lax.axis_size("lat")
    ma_pos = lax.axis_index("ma")
    lat_pos = lax.axis_index("lat")
    batch = inputs.shape[0]
    lon_loc = inputs.shape[1]
    lat_loc = inputs.shape[2]
    nlon_all = lon_loc * n_ma
    nlat_all = lat_loc * n_lat
    orders_loc = L // n_ma
    angles = (jnp.arange(nlat_all, dtype=jnp.float32) + 0.5) * (math.pi / nlat_all)
    local_orders = ma_pos * orders_loc + jnp.arange(orders_loc, dtype=jnp.int32)
    table = legendre(local_orders.astype(jnp.float32), angles)
    quadrature = jnp.sin(angles) * (math.sqrt(2.0 * math.pi) / nlon_all * math.pi / nlat_all)
    fwd_leg = (table * quadrature[None, None, :]).astype(jnp.bfloat16)
    inv_leg = table.astype(jnp.bfloat16)
    fwd_table, inv_table = dft_tables(jnp.arange(L, dtype=jnp.int32), nlon_all)
    fwd_four = fwd_table.astype(jnp.bfloat16)
    inv_four = inv_table.astype(jnp.bfloat16)
    fwd_back = fwd_four.T
    inv_back = inv_four.T
    sines = jnp.sin(angles)
    area = sines / jnp.mean(sines)
    area_rows = lax.dynamic_slice_in_dim(area, lat_pos * lat_loc, lat_loc)
    mask_grid = jnp.transpose(mask, (1, 2, 0)).astype(jnp.float32)
    pixel_weight = (
        area_rows[None, :, None, None]
        * var_weight.astype(jnp.float32)[None, None, None, :]
        * mask_grid[:, :, :, None]
    )
    grid_targets = jnp.transpose(targets, (0, 2, 3, 1, 4))
    denom = float(batch * nlon_all * nlat_all * C)

    def apply_table(table_full, block_in):
        whole_out = jnp.einsum(
            "ok,kibe->oibe",
            table_full,
            lax.all_to_all(block_in, "ma", split_axis=3, concat_axis=0, tiled=True),
            preferred_element_type=jnp.float32,
        )
        return lax.all_to_all(
            whole_out.astype(jnp.bfloat16), "ma", split_axis=0, concat_axis=3, tiled=True
        ).astype(whole_out.dtype)

    def spectral_backward(d_filtered, owned, weight_blk):
        d_rows = apply_table(inv_back, d_filtered.astype(jnp.bfloat16)).astype(jnp.bfloat16)
        d_spec = lax.all_to_all(d_rows, "lat", split_axis=3, concat_axis=1, tiled=True)
        out_width = d_spec.shape[3]
        d_mixed = jnp.einsum(
            "lmi,mpibo->lmpbo",
            inv_leg,
            d_spec.reshape(orders_loc, 2, nlat_all, batch, out_width),
            preferred_element_type=jnp.float32,
        ).astype(jnp.bfloat16)
        d_own = lax.all_to_all(d_mixed, "ma", split_axis=0, concat_axis=1, tiled=True)
        real_w = weight_blk[:, 0]
        imag_w = weight_blk[:, 1]
        d_real = d_own[:, :, 0]
        d_imag = d_own[:, :, 1]
        d_coef_real = jnp.einsum(
            "lmbo,leo->lmbe", d_real, real_w, preferred_element_type=jnp.float32
        ) + jnp.einsum("lmbo,leo->lmbe", d_imag, imag_w, preferred_element_type=jnp.float32)
        d_coef_imag = jnp.einsum(
            "lmbo,leo->lmbe", d_imag, real_w, preferred_element_type=jnp.float32
        ) - jnp.einsum("lmbo,leo->lmbe", d_real, imag_w, preferred_element_type=jnp.float32)
        grad_real = jnp.einsum(
            "lmbe,lmbo->leo", owned[:, :, 0], d_real, preferred_element_type=jnp.float32
        ) + jnp.einsum("lmbe,lmbo->leo", owned[:, :, 1], d_imag, preferred_element_type=jnp.float32)
        grad_imag = jnp.einsum(
            "lmbe,lmbo->leo", owned[:, :, 0], d_imag, preferred_element_type=jnp.float32
        ) - jnp.einsum("lmbe,lmbo->leo", owned[:, :, 1], d_real, preferred_element_type=jnp.float32)
        d_owned = jnp.stack([d_coef_real, d_coef_imag], 2)
        d_coeffs = lax.all_to_all(
            d_owned.astype(jnp.bfloat16), "ma", split_axis=1, concat_axis=0, tiled=True
        ).astype(d_owned.dtype)
        d_full = jnp.einsum(
            "lmi,lmpbe->mpibe",
            fwd_leg.astype(jnp.float32),
            d_coeffs,
            precision=lax.Precision.HIGHEST,
        ).reshape(2 * orders_loc, nlat_all, batch, E)
        d_spec_rows = lax.psum_scatter(
            d_full.astype(jnp.bfloat16), "lat", scatter_dimension=1, tiled=True
        )
        return (apply_table(fwd_back, d_spec_rows), jnp.stack([grad_real, grad_imag], 1))

    spec_bf = spec_w.astype(jnp.bfloat16)
    encdec_bf = encdec_w.astype(jnp.bfloat16)
    mlp_bf = mlp_w.astype(jnp.bfloat16)

    def model_backward(d_pred, stored):
        state_low, hidden_low, records = stored
        d_dec = d_pred.astype(jnp.bfloat16)
        grad_dec = jnp.einsum(
            "jibe,jibc->ce", hidden_low, d_dec, preferred_element_type=jnp.float32
        )
        d_hidden = jnp.einsum(
            "jibc,ce->jibe", d_dec, encdec_bf[1], preferred_element_type=jnp.float32
        )
        spec_grads = [None] * NB
        mlp_grads = [None] * NB
        gain_grads = [None] * NB
        for block_idx in reversed(range(NB)):
            normal, inv_std, owned, mlp_kept = records[block_idx]
            d_merged, mlp_grads[block_idx] = mlp_backward(d_hidden, mlp_kept, mlp_bf[block_idx])
            d_normed, spec_grads[block_idx] = spectral_backward(d_merged, owned, spec_bf[block_idx])
            d_norm_in, gain_grads[block_idx] = norm_backward(
                d_normed, normal, inv_std, gain_w[block_idx]
            )
            d_hidden = d_merged + d_norm_in
        d_enc = d_hidden.astype(jnp.bfloat16)
        grad_enc = jnp.einsum("jibc,jibe->ce", state_low, d_enc, preferred_element_type=jnp.float32)
        d_state = d_pred + jnp.einsum(
            "jibe,ce->jibc", d_enc, encdec_bf[0], preferred_element_type=jnp.float32
        )
        return (
            d_state,
            (
                jnp.stack([grad_enc, grad_dec], 0),
                jnp.stack(spec_grads, 0),
                jnp.stack(mlp_grads, 0),
                jnp.stack(gain_grads, 0),
            ),
        )

    state = jnp.transpose(inputs, (1, 2, 0, 3))
    history = []
    loss_part = jnp.zeros((), jnp.float32)
    for section_idx in range(ROLL):
        model_state_low = state.astype(jnp.bfloat16)
        hidden = jnp.einsum(
            "jibc,ce->jibe", model_state_low, encdec_bf[0], preferred_element_type=jnp.float32
        )
        model_records = []
        for model_block_idx in range(NB):
            model_normed, model_normal, model_inv_std = norm_forward(
                hidden, gain_w[model_block_idx]
            )
            spectral_weight_blk = spec_bf[model_block_idx]
            spec_rows = apply_table(fwd_four, model_normed).astype(jnp.bfloat16)
            piece = lax.all_gather(spec_rows, "lat", axis=1, tiled=True)
            row_width = piece.shape[1]
            paired = piece.reshape(orders_loc, 2, row_width, piece.shape[2], piece.shape[3])
            coeffs = jnp.einsum(
                "lmi,mpibe->lmpbe", fwd_leg, paired, preferred_element_type=jnp.float32
            ).astype(jnp.bfloat16)
            spectral_owned = lax.all_to_all(coeffs, "ma", split_axis=0, concat_axis=1, tiled=True)
            spectral_real_w = spectral_weight_blk[:, 0]
            spectral_imag_w = spectral_weight_blk[:, 1]
            mixed_real = jnp.einsum(
                "lmbe,leo->lmbo",
                spectral_owned[:, :, 0],
                spectral_real_w,
                preferred_element_type=jnp.float32,
            ) - jnp.einsum(
                "lmbe,leo->lmbo",
                spectral_owned[:, :, 1],
                spectral_imag_w,
                preferred_element_type=jnp.float32,
            )
            mixed_imag = jnp.einsum(
                "lmbe,leo->lmbo",
                spectral_owned[:, :, 0],
                spectral_imag_w,
                preferred_element_type=jnp.float32,
            ) + jnp.einsum(
                "lmbe,leo->lmbo",
                spectral_owned[:, :, 1],
                spectral_real_w,
                preferred_element_type=jnp.float32,
            )
            mixed_owned = jnp.stack([mixed_real, mixed_imag], 2).astype(jnp.bfloat16)
            mixed = lax.all_to_all(mixed_owned, "ma", split_axis=1, concat_axis=0, tiled=True)
            spec_out = jnp.einsum(
                "lmi,lmpbo->mpibo", inv_leg, mixed, preferred_element_type=jnp.float32
            )
            spec_out = spec_out.astype(jnp.bfloat16).reshape(
                2 * orders_loc, nlat_all, batch, mixed.shape[4]
            )
            rows_out = lax.all_to_all(spec_out, "lat", split_axis=1, concat_axis=3, tiled=True)
            filtered = apply_table(inv_four, rows_out)
            hidden, model_mlp_kept = mlp_forward(hidden + filtered, mlp_bf[model_block_idx])
            model_records.append((model_normal, model_inv_std, spectral_owned, model_mlp_kept))
        model_hidden_low = hidden.astype(jnp.bfloat16)
        prediction = state + jnp.einsum(
            "jibe,ce->jibc", model_hidden_low, encdec_bf[1], preferred_element_type=jnp.float32
        )
        prediction, stored = (prediction, (model_state_low, model_hidden_low, model_records))
        misfit = prediction - grid_targets[section_idx]
        loss_part = loss_part + jnp.sum(pixel_weight * misfit * misfit) / denom
        history.append((stored, misfit))
        state = prediction
    d_state = jnp.zeros_like(state)
    totals = None
    for section_idx in reversed(range(ROLL)):
        stored, misfit = history[section_idx]
        d_pred = 2.0 * pixel_weight * misfit / denom + d_state
        d_state, section_grads = model_backward(d_pred, stored)
        totals = section_grads if totals is None else jax.tree.map(jnp.add, totals, section_grads)
    grad_encdec, spec_grad, grad_mlp, grad_gain = totals
    grad_encdec, grad_mlp, grad_gain, loss_value, spec_square, weight_square = lax.psum(
        (
            grad_encdec,
            grad_mlp,
            grad_gain,
            loss_part,
            jnp.sum(spec_grad * spec_grad),
            jnp.sum(spec_w * spec_w, axis=(1, 2, 3, 4)),
        ),
        ("lat", "ma"),
    )
    total_square = (
        spec_square
        + jnp.sum(grad_encdec * grad_encdec)
        + jnp.sum(grad_mlp * grad_mlp)
        + jnp.sum(grad_gain * grad_gain)
    )
    grad_norm = jnp.sqrt(total_square)
    scale = clip_norm / jnp.maximum(grad_norm, clip_norm)
    step_float = step_count[0].astype(jnp.float32)
    spec_m_new, spec_v_new, direction = adaptive(
        spec_w, spec_m, spec_v, spec_grad * scale, step_float
    )
    dir_square = lax.psum(jnp.sum(direction * direction, axis=(1, 2, 3, 4)), ("lat", "ma"))
    weight_norm = jnp.sqrt(weight_square)
    dir_norm = jnp.sqrt(dir_square)
    trust = weight_norm / (dir_norm + 1e-06)
    spec_new = spec_w - learn_rate * trust[:, None, None, None, None] * direction
    encdec_new, encdec_m_new, encdec_v_new, encdec_norms = lamb_dense(
        encdec_w, encdec_m, encdec_v, grad_encdec * scale, step_float, 2
    )
    mlp_new, mlp_m_new, mlp_v_new, mlp_norms = lamb_dense(
        mlp_w, mlp_m, mlp_v, grad_mlp * scale, step_float, 2 * NB
    )
    gain_new, gain_m_new, gain_v_new, gain_norms = lamb_dense(
        gain_w, gain_m, gain_v, grad_gain * scale, step_float, NB
    )
    matrix_norms = jnp.concatenate(
        [jnp.stack([weight_norm, dir_norm], 1), encdec_norms, mlp_norms, gain_norms], 0
    )
    return (
        loss_value,
        grad_norm,
        matrix_norms,
        spec_new,
        spec_m_new,
        spec_v_new,
        spec_new.astype(jnp.bfloat16),
        encdec_new,
        encdec_m_new,
        encdec_v_new,
        encdec_new.astype(jnp.bfloat16),
        mlp_new,
        mlp_m_new,
        mlp_v_new,
        mlp_new.astype(jnp.bfloat16),
        gain_new,
        gain_m_new,
        gain_v_new,
        gain_new.astype(jnp.bfloat16),
    )


RANKS = 16
ORDS = L // RANKS
SLOTS = 8
F32 = jnp.float32
BF16 = jnp.bfloat16


def legendre_f64(nlat):
    theta = (np.arange(nlat) + 0.5) * (math.pi / nlat)
    cosines, sines = np.cos(theta), np.sin(theta)
    table = np.zeros((L, L, nlat))
    for m in range(L):
        log_start = 0.5 * (
            math.log((2.0 * m + 1.0) / (4.0 * math.pi))
            + math.lgamma(2.0 * m + 1.0)
            - 2.0 * math.lgamma(m + 1.0)
            - m * math.log(4.0)
        ) + m * np.log(sines)
        table[m, m] = np.exp(log_start)
        if m + 1 < L:
            table[m + 1, m] = math.sqrt(2.0 * m + 3.0) * cosines * table[m, m]
        for k in range(m + 2, L):
            factor = math.sqrt((4.0 * k * k - 1.0) / (k * k - m * m))
            shrink = math.sqrt(((k - 1.0) ** 2 - m * m) / (4.0 * (k - 1.0) ** 2 - 1.0))
            table[k, m] = factor * (cosines * table[k - 1, m] - shrink * table[k - 2, m])
    return table, sines


def low_np(array):
    return array.astype(np.float32).astype(ml_dtypes.bfloat16)


def slot_map():
    degree = np.full((RANKS, 3, SLOTS), -1)
    order = np.full((RANKS, SLOTS), -1)
    for d in range(RANKS):
        y, w, xc = d // 8, (d // 4) % 2, d % 4
        lo, hi = 4 * w + xc, 4 * (3 - w) + xc
        n_lo, n_hi = (6 * lo + 5) // RANKS + 1, (6 * hi + 5) // RANKS + 1
        for group, first, count in ((hi, 0, n_hi), (lo, SLOTS - n_lo, n_lo)):
            for r in range(count):
                order[d, first + r] = r
                for t in range(3):
                    degree[d, t, first + r] = 6 * group + 3 * y + t
    return degree, order


def make_tables(nlat, nlon):
    table, sines = legendre_f64(nlat)
    quadrature = sines * (math.sqrt(2.0 * math.pi) / nlon * math.pi / nlat)
    fwd_leg = np.asarray(low_np(table * quadrature[None, None, :]))
    inv_leg = np.asarray(low_np(table))
    degree, order = slot_map()
    shape = (RANKS, RANKS, 3, 2, SLOTS, RANKS, ORDS, 2, 2)
    fwd = np.zeros(shape, ml_dtypes.bfloat16)
    inv = np.zeros(shape, ml_dtypes.bfloat16)
    for g in range(RANKS):
        for d in range(RANKS):
            for slot in range(SLOTS):
                r = order[d, slot]
                if r < 0:
                    continue
                for t in range(3):
                    k, m = degree[d, t, slot], g + RANKS * r
                    for p in range(2):
                        fwd[g, d, t, p, slot, :, r, p, :] = fwd_leg[k, m].reshape(RANKS, 2)
                        inv[g, d, t, p, slot, :, r, p, :] = inv_leg[k, m].reshape(RANKS, 2)
    rows = RANKS * 3 * 2 * SLOTS
    cols = RANKS * ORDS * 2 * 2
    fwd = fwd.reshape(RANKS, rows, cols)
    inv = inv.reshape(RANKS, rows, cols)
    phase = 2.0 * math.pi * (np.arange(L)[:, None] * np.arange(nlon)[None, :] % nlon) / nlon
    scale = np.where(np.arange(L) == 0, 1.0, 2.0)[:, None] / math.sqrt(2.0 * math.pi)
    four = low_np(np.stack([np.cos(phase), -np.sin(phase)], 1))
    back = low_np(np.stack([scale * np.cos(phase), -scale * np.sin(phase)], 1))
    def wide(small):
        out = np.zeros((RANKS, ORDS, 2, 2, 2, nlon), ml_dtypes.bfloat16)
        ordered = small.reshape(ORDS, RANKS, 2, nlon).transpose(1, 0, 2, 3)
        for il in range(2):
            out[:, :, :, il, il, :] = ordered
        return out.reshape(cols, 2 * nlon)

    def turn(array):
        return np.ascontiguousarray(np.swapaxes(array, -1, -2))

    four, back = wide(four), wide(back)
    return (fwd, turn(inv), turn(fwd), inv), (four, turn(back), turn(four), back)


def place():
    ma = lax.axis_index("ma")
    y = lax.axis_index("lat")
    z = ma // 4
    zh = z // 2
    w = z + zh * (3 - 2 * z)
    return zh, y, w, 8 * y + 4 * w + ma % 4


def device_of(zh, q):
    w = (q // 4) % 2
    z = w + zh * (3 - 2 * w)
    return {"lat": q // 8, "ma": 4 * z + q % 4}


def nn(a, b):
    return lax.dot_general(a, b, (((1,), (0,)), ((), ())), preferred_element_type=F32)


def nt(a, b):
    return lax.dot_general(a, b, (((1,), (1,)), ((), ())), preferred_element_type=F32)


def tn(a, b):
    return lax.dot_general(a, b, (((0,), (0,)), ((), ())), preferred_element_type=F32)


def piece_of(kind, half, zh, y):
    return 2 - 2 * ((kind + zh) % 2) + (half + y) % 2


def weight_of(w_all, block, kind, t, part, zh, y):
    return jnp.concatenate(
        [w_all[block, piece_of(kind, half, zh, y), t, part] for half in range(2)], axis=1
    )


def hi_rows(w):
    slot = lax.broadcasted_iota(jnp.int32, (RANKS * 2 * SLOTS, 1), 0) % SLOTS
    return slot < 6 - w


GELU_A = math.sqrt(2.0 / math.pi)
GELU_B = 0.044715


def normal_of(hidden):
    centre = jnp.mean(hidden, -1, keepdims=True)
    centred = hidden - centre
    inv_std = lax.rsqrt(jnp.mean(centred * centred, -1, keepdims=True) + norm_eps)
    return centred * inv_std, inv_std


def rows_loop(total, step, body):
    def one(k, carry):
        body(pl.ds(pl.multiple_of(k * step, step), step))
        return carry

    lax.fori_loop(0, total // step, one, 0)


MESH = pl.DeviceIdType.MESH
LANES = 128
MASK_LANE = LANES - 1


def greet_all():
    barrier = pltpu.get_barrier_semaphore()
    me = 2 * RANKS // 2 * lax.axis_index("lat") + lax.axis_index("ma")

    def greet(s, carry):
        other = (me + s) % (2 * RANKS)
        pl.semaphore_signal(
            barrier, inc=1, device_id={"lat": other // RANKS, "ma": other % RANKS}, device_id_type=MESH
        )
        return carry

    lax.fori_loop(1, 2 * RANKS, greet, 0)
    pl.semaphore_wait(barrier, 2 * RANKS - 1)


def remote(src, dst, send_sem, recv_sem, device):
    return pltpu.make_async_remote_copy(
        src_ref=src,
        dst_ref=dst,
        send_sem=send_sem,
        recv_sem=recv_sem,
        device_id=device,
        device_id_type=MESH,
    )


def bytes_wait(ref, sem):
    pltpu.make_async_copy(ref, ref, sem).wait()


def push_blocks(source_of, landing, send_sem, recv_sem, zh, q):
    pltpu.make_async_copy(source_of(q), landing, recv_sem).start()

    def push(s, carry):
        d = (q + s) % RANKS
        remote(source_of(d), landing, send_sem, recv_sem, device_of(zh, d)).start()
        return carry

    lax.fori_loop(1, RANKS, push, 0)


def exchange_start(send, recv, send_sem, recv_sem, zh, q):
    push_blocks(lambda d: send.at[d], recv.at[q], send_sem, recv_sem, zh, q)


def exchange_wait(send, recv, send_sem, recv_sem):
    bytes_wait(recv, recv_sem)
    bytes_wait(send.at[pl.ds(0, RANKS - 1)], send_sem)


def exchange(send, recv, send_sem, recv_sem, zh, q):
    exchange_start(send, recv, send_sem, recv_sem, zh, q)
    exchange_wait(send, recv, send_sem, recv_sem)


def lane_sums(array):
    return jnp.sum(array.reshape(-1, LANES), axis=0, keepdims=True)


def train(
    x_chunks, t_chunks, spec_w, mlp_w, r0, r1, r2, r3, f0, f1, f2, f3,
    encdec, gain, area, var_row,
    g_spec, g_mlp, g_small, scalars,
    pfx, pix, pfxt, pixt, ftx, itx, ftxt, itxt, w_all, w_other, mlp_bf, mlp_stage, code_bf,
    x_recv, goals, weight, x_low, misfit, d_state, h_all, hid_low, v_low, u_buf, dv_buf, dh_buf,
    n_send, s_recv, y_recv, w_send, b_recv, a_own, d_mix,
    dwf, dw_send, dw_recv, dw_own, dmlp, rs_send, rs_recv, mir_send, mir_recv, ag_src,
    d_small, d_gain, sm_send, sm_recv, sm_mir_send, sm_mir_recv, sm_src, scal, scal_recv,
    load_sem, stage_sem, once_send, once_recv, w_send_sem, w_recv_sem, x_send, x_recv_sem,
    g_send_sem, g_recv_sem, rs_sem, mir_send_sem, mir_recv_sem, ag_send_sem, ag_recv_sem, sm_sem,
):
    zh, y, w, q = place()
    ma = lax.axis_index("ma")
    xc = ma % 4
    mirror_ma = 4 * (3 - ma // 4) + xc
    near, far, cross = {"lat": 1 - y, "ma": ma}, {"lat": y, "ma": mirror_ma}, {"lat": 1 - y, "ma": mirror_ma}
    pixels, chans = dh_buf.shape
    spectra = pix.shape[0]
    triples = pfx.shape[0]
    third = 3

    loads = [
        pltpu.make_async_copy(src.at[q], dst, load_sem.at[k])
        for k, (src, dst) in enumerate(((r0, pfx), (r1, pix), (r2, pfxt), (r3, pixt)))
    ] + [
        pltpu.make_async_copy(src, dst, load_sem.at[4 + k])
        for k, (src, dst) in enumerate(((f0, ftx), (f1, itx), (f2, ftxt), (f3, itxt)))
    ]
    stage = dwf

    class SpecLoad:
        def __init__(self, b):
            self.copies = [
                pltpu.make_async_copy(
                    spec_w.at[b, pl.ds(third * k, third)], stage.at[2 * (b % 2) + k], stage_sem.at[2 * b + k]
                )
                for k in range(2)
            ]

        def start(self):
            for copy in self.copies:
                copy.start()

        def wait(self):
            for copy in self.copies:
                copy.wait()

    spec_loads = [SpecLoad(b) for b in range(NB)]
    mlp_loads = [pltpu.make_async_copy(mlp_w.at[b], mlp_stage.at[b % 2], stage_sem.at[2 * NB + b]) for b in range(NB)]
    spec_loads[0].start()
    spec_loads[1].start()
    loads[4].start()
    loads[0].start()
    scal[...] = jnp.zeros_like(scal)
    d_small[...] = jnp.zeros_like(d_small)
    d_gain[...] = jnp.zeros_like(d_gain)
    d_state[...] = jnp.zeros_like(d_state)
    code_bf[...] = encdec[...].astype(BF16)
    greet_all()

    def chunk_to(chunks, landing, sems):
        pltpu.make_async_copy(chunks.at[ma], landing, sems[1]).start()

        def push(s, carry):
            other = (ma + s) % RANKS
            remote(chunks.at[other], landing, sems[0], sems[1], {"lat": y, "ma": other}).start()
            return carry

        lax.fori_loop(1, RANKS, push, 0)

    chunk_to(x_chunks, x_recv.at[:, ma], (once_send.at[0], once_recv.at[0]))

    for b in range(NB):
        spec_loads[b].wait()
        for t in range(third):
            for own, target in ((y, w_all.at[b, 0]), (1 - y, w_other.at[b])):
                value = stage[2 * (b % 2) + own, t]
                scal[2 + b : 3 + b] += lane_sums(value * value)
                target[t] = value.astype(BF16)
        if b + 2 < NB:
            spec_loads[b + 2].start()
        sems = (w_send_sem.at[b], w_recv_sem.at[b])
        remote(w_other.at[b], w_all.at[b, 3], *sems, cross).start()
        remote(w_all.at[b, 0], w_all.at[b, 2], *sems, far).start()
        remote(w_other.at[b], w_all.at[b, 1], *sems, near).start()
        if b == 0:
            mlp_loads[0].start()
            mlp_loads[1].start()
            for k in (1, 2, 3, 5, 6, 7):
                loads[k].start()
    chunk_to(t_chunks, goals.at[:, :, ma], (once_send.at[1], once_recv.at[1]))
    for b in range(NB):
        mlp_loads[b].wait()
        mlp_bf[b] = mlp_stage[b % 2].astype(BF16)
        if b + 2 < NB:
            mlp_loads[b + 2].start()
    for copy in loads:
        copy.wait()
    bytes_wait(x_recv, once_recv.at[0])
    bytes_wait(x_chunks.at[pl.ds(0, RANKS - 1)], once_send.at[0])

    hi = hi_rows(w)
    rows_mix = RANKS * 2 * SLOTS

    def mixed_by(source, product, block, t, part):
        return jnp.where(
            hi,
            product(source, weight_of(w_all, block, 0, t, part, zh, y)),
            product(source, weight_of(w_all, block, 1, t, part, zh, y)),
        ).reshape(RANKS, 2, SLOTS, chans)

    def narrow(value):
        return value.astype(BF16).reshape(n_send.shape)

    def broad(value):
        return value.astype(BF16).reshape(w_send.shape)

    def fwd_block(step, block):
        slot, idx = 4 * step + block, NB * step + block
        gain_row = gain[block]

        def norm_rows(rows):
            normal, unused = normal_of(h_all[slot, rows, :])
            u_buf[rows, :] = (normal * gain_row).astype(BF16)

        rows_loop(pixels, 128, norm_rows)
        n_send[...] = narrow(nn(ftx[...], u_buf[...]))
        exchange(n_send, s_recv, x_send.at[0], x_recv_sem.at[0], zh, q)
        w_send[...] = broad(nn(pfx[...], s_recv[...].reshape(spectra, chans)))
        exchange(w_send, a_own.at[idx], x_send.at[1], x_recv_sem.at[1], zh, q)

        @pl.when(step == 0)
        def _():
            bytes_wait(w_all.at[block, pl.ds(1, 3)], w_recv_sem.at[block])

        for t in range(3):
            coef = a_own[idx, :, t].reshape(rows_mix, chans)
            by_real, by_imag = (mixed_by(coef, nn, block, t, part) for part in range(2))
            mixed = jnp.stack([by_real[:, 0] - by_imag[:, 1], by_real[:, 1] + by_imag[:, 0]], 1)
            w_send[:, t] = mixed.reshape(RANKS, 2 * SLOTS, chans).astype(BF16)
        exchange(w_send, b_recv, x_send.at[2], x_recv_sem.at[2], zh, q)
        n_send[...] = narrow(nn(pix[...], b_recv[...].reshape(triples, chans)))
        exchange(n_send, y_recv, x_send.at[3], x_recv_sem.at[3], zh, q)
        spectrum = y_recv[...].reshape(spectra, chans)

        def mlp_rows(rows):
            merged = h_all[slot, rows, :] + nn(itx[rows, :], spectrum)
            merged_low = merged.astype(BF16)
            v_low[idx, rows, :] = merged_low
            pre = nn(merged_low, mlp_bf[block, 0])
            act = (0.5 * pre * (1.0 + jnp.tanh(GELU_A * (pre + GELU_B * pre * pre * pre)))).astype(BF16)
            h_all[slot + 1, rows, :] = merged + nt(act, mlp_bf[block, 1])

        rows_loop(pixels, 256, mlp_rows)

    denom = float(pixels * RANKS * C * 2)

    def fwd_step(step, carry):
        state = x_recv[...].reshape(pixels, LANES)
        state_low = state.astype(BF16)
        x_low[step] = state_low
        h_all[4 * step] = nn(state_low, code_bf[0])

        def one(block, inner):
            fwd_block(step, block)
            return inner

        lax.fori_loop(0, NB, one, 0)
        hidden_low = h_all[4 * step + 3].astype(BF16)
        hid_low[step] = hidden_low
        prediction = state + nt(hidden_low, code_bf[1])
        x_recv[...] = prediction.reshape(x_recv.shape)

        @pl.when(step == 0)
        def _():
            bytes_wait(goals, once_recv.at[1])
            bytes_wait(t_chunks.at[pl.ds(0, RANKS - 1)], once_send.at[1])
            for il in range(2):
                valid = goals[0, il].reshape(pixels // 2, LANES)[:, MASK_LANE:]
                rows = slice(il * pixels // 2, (il + 1) * pixels // 2)
                weight[rows, :] = valid * (area[il] * var_row[...])

        miss = prediction - goals[step].reshape(pixels, LANES)
        weighted = weight[...] * miss
        scal[0:1] += lane_sums(weighted * miss / denom)
        misfit[step] = 2.0 * weighted / denom
        return carry

    lax.fori_loop(0, ROLL, fwd_step, 0)
    for b in range(NB):
        bytes_wait(w_all.at[b, pl.ds(1, 3)], w_send_sem.at[b])

    def settle(block):
        bytes_wait(dw_recv.at[block], g_recv_sem.at[block])
        for t in range(third):
            for own, one, two in (
                (y, dw_own[block, t], dw_recv[block, 1, t]),
                (1 - y, dw_recv[block, 0, t], dw_recv[block, 2, t]),
            ):
                total = one.astype(F32) + two.astype(F32)
                scal[1:2] += lane_sums(total * total)
                g_spec[block, third * own + t] = total

    def bwd_block(lap, step, block):
        slot, idx = 4 * step + block, NB * step + block
        gain_row = gain[block]

        @pl.when(lap == 0)
        def _():
            dmlp[block] = jnp.zeros(dmlp.shape[1:], F32)

        def mlp_rows(rows):
            d_hidden = dh_buf[rows, :]
            d_branch = d_hidden.astype(BF16)
            merged_low = v_low[idx, rows, :]
            pre = nn(merged_low, mlp_bf[block, 0])
            tan = jnp.tanh(GELU_A * (pre + GELU_B * pre * pre * pre))
            act = (0.5 * pre * (1.0 + tan)).astype(BF16)
            slope = 0.5 * (1.0 + tan) + 0.5 * pre * (1.0 - tan * tan) * (
                GELU_A * (1.0 + 3.0 * GELU_B * pre * pre)
            )
            d_pre = (nn(d_branch, mlp_bf[block, 1]) * slope).astype(BF16)
            dmlp[block, 0] += tn(merged_low, d_pre)
            dmlp[block, 1] += tn(d_branch, act)
            d_merged = d_hidden + nt(d_pre, mlp_bf[block, 0])
            dv_buf[rows, :] = d_merged
            u_buf[rows, :] = d_merged.astype(BF16)

        rows_loop(pixels, 256, mlp_rows)
        n_send[...] = narrow(nn(itxt[...], u_buf[...]))
        exchange_start(n_send, s_recv, x_send.at[4], x_recv_sem.at[4], zh, q)

        @pl.when(lap == 1)
        def _():
            rs_send[...] = dmlp[block].astype(BF16).reshape(rs_send.shape)
            exchange_start(rs_send, rs_recv, rs_sem.at[0], rs_sem.at[1], zh, q)

        exchange_wait(n_send, s_recv, x_send.at[4], x_recv_sem.at[4])
        w_send[...] = broad(nn(pixt[...], s_recv[...].reshape(spectra, chans)))
        which = NB * lap + block
        exchange_start(w_send, d_mix.at[which], x_send.at[5], x_recv_sem.at[5], zh, q)

        @pl.when(lap == 1)
        def _():
            exchange_wait(rs_send, rs_recv, rs_sem.at[0], rs_sem.at[1])
            share = rs_recv[0].astype(F32)
            for k in range(1, RANKS):
                share = share + rs_recv[k].astype(F32)
            mir_send[block] = share
            remote(mir_send.at[block], mir_recv.at[block], mir_send_sem.at[block], mir_recv_sem.at[block], far).start()

        exchange_wait(w_send, d_mix.at[which], x_send.at[5], x_recv_sem.at[5])

        def turned_of(d_mixed):
            wide = d_mixed.astype(F32).reshape(RANKS, 2, SLOTS, chans)
            return jnp.stack([wide[:, 1], -wide[:, 0]], 1).reshape(rows_mix, chans).astype(BF16)

        for t in range(3):
            d_mixed = d_mix[which, :, t].reshape(rows_mix, chans)
            by_real, by_imag = (mixed_by(d_mixed, nt, block, t, part) for part in range(2))
            d_coef = jnp.stack([by_real[:, 0] + by_imag[:, 1], by_real[:, 1] - by_imag[:, 0]], 1)
            w_send[:, t] = d_coef.reshape(RANKS, 2 * SLOTS, chans).astype(BF16)
        exchange_start(w_send, b_recv, x_send.at[6], x_recv_sem.at[6], zh, q)

        @pl.when(lap == 1)
        def _():
            for t in range(3):
                others = []
                for turn in range(ROLL):
                    d_mixed = d_mix[NB * turn + block, :, t].reshape(rows_mix, chans)
                    others.append((d_mixed, turned_of(d_mixed)))
                for kind in range(2):
                    keep = hi if kind == 0 else jnp.logical_not(hi)
                    kept = [
                        jnp.where(
                            keep, a_own[NB * (1 - turn) + block, :, t].reshape(rows_mix, chans).astype(F32), 0.0
                        ).astype(BF16)
                        for turn in range(ROLL)
                    ]
                    for part in range(2):
                        grad = tn(kept[0], others[0][part]) + tn(kept[1], others[1][part])
                        for half in range(2):
                            dwf[piece_of(kind, half, zh, y), t, part] = grad[
                                :, half * LANES : (half + 1) * LANES
                            ]
            dw_own[block] = dwf[0]
            for k in range(3):
                dw_send[block, k] = dwf[1 + k].astype(BF16)
            sems = (g_send_sem.at[block], g_recv_sem.at[block])
            remote(dw_send.at[block, 2], dw_recv.at[block, 2], *sems, cross).start()
            remote(dw_send.at[block, 1], dw_recv.at[block, 1], *sems, far).start()
            remote(dw_send.at[block, 0], dw_recv.at[block, 0], *sems, near).start()
            bytes_wait(mir_recv.at[block], mir_recv_sem.at[block])
            total = mir_send[block] + mir_recv[block]
            scal[1:2] += 0.5 * lane_sums(total * total)
            ag_src[block] = total.astype(BF16)
            push_blocks(lambda d: ag_src.at[block], g_mlp.at[block, q], ag_send_sem.at[block], ag_recv_sem.at[block], zh, q)

        exchange_wait(w_send, b_recv, x_send.at[6], x_recv_sem.at[6])
        n_send[...] = narrow(nn(pfxt[...], b_recv[...].reshape(triples, chans)))
        exchange(n_send, y_recv, x_send.at[7], x_recv_sem.at[7], zh, q)
        spectrum = y_recv[...].reshape(spectra, chans)

        def norm_rows(rows):
            normal, inv_std = normal_of(h_all[slot, rows, :])
            d_normed = nn(ftxt[rows, :], spectrum)
            scaled = d_normed * gain_row
            d_gain[block] += jnp.sum(d_normed * normal, axis=0, keepdims=True)
            d_norm_in = inv_std * (
                scaled
                - jnp.mean(scaled, -1, keepdims=True)
                - normal * jnp.mean(scaled * normal, -1, keepdims=True)
            )
            dh_buf[rows, :] = dv_buf[rows, :] + d_norm_in

        rows_loop(pixels, 256, norm_rows)

        @pl.when(jnp.logical_and(lap == 1, block < NB - 1))
        def _():
            settle(block + 1)

    def bwd_step(lap, carry):
        step = ROLL - 1 - lap
        d_pred = misfit[step] + d_state[...]
        d_dec = d_pred.astype(BF16)
        d_small[LANES:] += tn(d_dec, hid_low[step])
        dh_buf[...] = nn(d_dec, code_bf[1])

        def one(k, inner):
            bwd_block(lap, step, NB - 1 - k)
            return inner

        lax.fori_loop(0, NB, one, 0)
        d_enc = dh_buf[...].astype(BF16)
        d_small[:LANES] += tn(x_low[step], d_enc)

        @pl.when(lap == 0)
        def _():
            d_state[...] = d_pred + nt(d_enc, code_bf[0])

        return carry

    lax.fori_loop(0, ROLL, bwd_step, 0)

    for b in range(NB):
        d_small[LANES - NB + b : LANES - NB + b + 1] = d_gain[b]
    sm_send[...] = d_small[...].reshape(sm_send.shape)
    exchange(sm_send, sm_recv, sm_sem.at[0], sm_sem.at[1], zh, q)
    share = sm_recv[0]
    for k in range(1, RANKS):
        share = share + sm_recv[k]
    sm_mir_send[...] = share
    swap = remote(sm_mir_send, sm_mir_recv, sm_sem.at[2], sm_sem.at[3], far)
    swap.start()
    swap.wait()
    total = sm_mir_send[...] + sm_mir_recv[...]
    scal[1:2] += 0.5 * lane_sums(total * total)
    sm_src[...] = total
    push_blocks(lambda d: sm_src, g_small.at[q], sm_sem.at[4], sm_sem.at[5], zh, q)
    settle(0)

    me = RANKS * y + ma
    pltpu.make_async_copy(scal, scal_recv.at[me], sm_sem.at[7]).start()

    def spread(s, carry):
        other = (me + s) % (2 * RANKS)
        remote(
            scal, scal_recv.at[me], sm_sem.at[6], sm_sem.at[7], {"lat": other // RANKS, "ma": other % RANKS}
        ).start()
        return carry

    lax.fori_loop(1, 2 * RANKS, spread, 0)
    bytes_wait(g_small, sm_sem.at[5])
    bytes_wait(g_small.at[pl.ds(0, RANKS - 1)], sm_sem.at[4])
    for b in range(NB):
        bytes_wait(g_mlp.at[b], ag_recv_sem.at[b])
        bytes_wait(g_mlp.at[b, pl.ds(0, RANKS - 1)], ag_send_sem.at[b])
        bytes_wait(mir_send.at[b], mir_send_sem.at[b])
        bytes_wait(dw_send.at[b], g_send_sem.at[b])
    bytes_wait(scal_recv, sm_sem.at[7])
    bytes_wait(scal_recv.at[pl.ds(0, 2 * RANKS - 1)], sm_sem.at[6])
    total = scal_recv[0]
    for k in range(1, 2 * RANKS):
        total = total + scal_recv[k]
    scalars[...] = total


def call_train(x_chunks, t_chunks, spec_w, mlp_w, tables, encdec, gain, area, var_row):
    vmem = pltpu.VMEM
    dma = pltpu.SemaphoreType.DMA
    lon = x_chunks.shape[2]
    pixels, chans = 2 * RANKS * lon, gain.shape[-1]
    third = spec_w.shape[1] // 2
    triple = (third, 2, chans, LANES)
    narrow, wide = (RANKS, 4 * ORDS, chans), (RANKS, 3, 2 * SLOTS, chans)
    triples, spectra = RANKS * 6 * SLOTS, RANKS * 4 * ORDS
    mlp_shape = mlp_w.shape[1:]
    chunk = (mlp_shape[0] * mlp_shape[1] // RANKS, mlp_shape[2])
    small = (2 * LANES // RANKS, chans)
    b16 = lambda *shape: vmem(shape, BF16)
    f32 = lambda *shape: vmem(shape, F32)
    everywhere = pl.BlockSpec(memory_space=pl.ANY)
    inside = pl.BlockSpec(memory_space=vmem)
    return pl.pallas_call(
        train,
        out_shape=(
            jax.ShapeDtypeStruct(spec_w.shape, F32),
            jax.ShapeDtypeStruct((NB, RANKS, *chunk), BF16),
            jax.ShapeDtypeStruct((RANKS, *small), F32),
            jax.ShapeDtypeStruct((8, LANES), F32),
        ),
        in_specs=[everywhere] * 12 + [inside] * 4,
        out_specs=[inside] * 4,
        scratch_shapes=[
            b16(triples, spectra), b16(spectra, triples), b16(spectra, triples), b16(triples, spectra),
            b16(spectra, pixels), b16(pixels, spectra), b16(pixels, spectra), b16(spectra, pixels),
            b16(NB, 4, *triple), b16(NB, *triple), b16(*mlp_w.shape), f32(2, *mlp_shape),
            b16(*encdec.shape),
            f32(2, RANKS, lon, LANES), f32(ROLL, 2, RANKS, lon, LANES), f32(pixels, LANES), b16(ROLL, pixels, LANES),
            f32(ROLL, pixels, LANES), f32(pixels, LANES), f32(4 * ROLL, pixels, chans), b16(ROLL, pixels, chans),
            b16(NB * ROLL, pixels, chans), b16(pixels, chans), f32(pixels, chans), f32(pixels, chans),
            b16(*narrow), b16(*narrow), b16(*narrow), b16(*wide), b16(*wide), b16(NB * ROLL, *wide), b16(NB * ROLL, *wide),
            f32(4, *triple), b16(NB, 3, *triple), b16(NB, 3, *triple), f32(NB, *triple), f32(NB, *mlp_shape),
            b16(RANKS, *chunk), b16(RANKS, *chunk), f32(NB, *chunk), f32(NB, *chunk), b16(NB, *chunk),
            f32(2 * LANES, chans), f32(NB, 1, chans), f32(RANKS, *small), f32(RANKS, *small), f32(*small), f32(*small),
            f32(*small), f32(8, LANES), f32(2 * RANKS, 8, LANES),
            dma((8,)), dma((3 * NB,)), dma((2,)), dma((2,)), dma((NB,)), dma((NB,)), dma((8,)), dma((8,)),
            dma((NB,)), dma((NB,)), dma((2,)), dma((NB,)), dma((NB,)), dma((NB,)), dma((NB,)), dma((8,)),
        ],
        compiler_params=pltpu.CompilerParams(
            collective_id=0, has_side_effects=True, vmem_limit_bytes=61 << 20
        ),
    )(x_chunks, t_chunks, spec_w, mlp_w, *tables, encdec, gain, area, var_row)


def sum_all(value_ref, out_ref, recv, send_sem, recv_sem):
    greet_all()
    me = RANKS * lax.axis_index("lat") + lax.axis_index("ma")
    pltpu.make_async_copy(value_ref, recv.at[me], recv_sem).start()

    def spread(s, carry):
        other = (me + s) % (2 * RANKS)
        remote(value_ref, recv.at[me], send_sem, recv_sem, {"lat": other // RANKS, "ma": other % RANKS}).start()
        return carry

    lax.fori_loop(1, 2 * RANKS, spread, 0)
    bytes_wait(recv, recv_sem)
    bytes_wait(recv.at[pl.ds(0, 2 * RANKS - 1)], send_sem)
    total = recv[0]
    for k in range(1, 2 * RANKS):
        total = total + recv[k]
    out_ref[...] = total


def call_sum(value):
    inside = pl.BlockSpec(memory_space=pltpu.VMEM)
    return pl.pallas_call(
        sum_all,
        out_shape=jax.ShapeDtypeStruct(value.shape, F32),
        in_specs=[inside],
        out_specs=inside,
        scratch_shapes=[
            pltpu.VMEM((2 * RANKS, *value.shape), F32),
            pltpu.SemaphoreType.DMA,
            pltpu.SemaphoreType.DMA,
        ],
        compiler_params=pltpu.CompilerParams(collective_id=1, has_side_effects=True),
    )(value)


def chunks_of(field):
    items, lon, lat, width = field.shape
    pairs = lat // 2
    chunks = jnp.moveaxis(field.reshape(items, lon, pairs, 2, width), 1, 3)
    return jnp.concatenate([chunks[0], jnp.roll(chunks[1], pairs // 2, 0)], 0)


def special(
    inputs,
    targets,
    mask,
    var_weight,
    step_count,
    spec_w,
    spec_m,
    spec_v,
    encdec_w,
    encdec_m,
    encdec_v,
    mlp_w,
    mlp_m,
    mlp_v,
    gain_w,
    gain_m,
    gain_v,
):
    zh, y, w, q = place()
    nlon = inputs.shape[1] * lax.axis_size("ma")
    nlat = inputs.shape[2] * lax.axis_size("lat")
    ranked, common = make_tables(nlat, nlon)
    tables = tuple(jnp.asarray(t) for t in (*ranked, *common))
    spare = LANES - C
    x_chunks = chunks_of(jnp.pad(inputs, ((0, 0),) * 3 + ((0, spare),)))
    masks = jnp.broadcast_to(mask.astype(F32)[None, ..., None], (*targets.shape[:-1], 1))
    goal = jnp.concatenate([targets, jnp.zeros((*targets.shape[:-1], spare - 1), F32), masks], -1)
    t_chunks = jnp.stack([chunks_of(goal[0]), chunks_of(goal[1])], 1)
    angles = (jnp.arange(nlat, dtype=F32) + 0.5) * (math.pi / nlat)
    sines = jnp.sin(angles)
    area = lax.dynamic_slice_in_dim(sines / jnp.mean(sines), 2 * q, 2)
    area = jnp.broadcast_to(area[:, None, None], (2, 1, LANES))
    var_row = jnp.pad(var_weight.astype(F32), (0, spare))[None]
    encdec = jnp.pad(encdec_w, ((0, 0), (0, spare), (0, 0)))
    spec_grad, mlp_sum, small_sum, scalars = call_train(
        x_chunks, t_chunks, spec_w, mlp_w, tables, encdec, gain_w[:, None], area, var_row
    )
    grad_mlp = mlp_sum.reshape(mlp_w.shape).astype(F32)
    small_sum = small_sum.reshape(2, LANES, E)
    grad_encdec = small_sum[:, :C]
    grad_gain = small_sum[0, LANES - NB :]
    sums = jnp.sum(scalars, 1)
    loss_value = sums[0]
    weight_square = sums[2 : 2 + NB]
    grad_norm = jnp.sqrt(sums[1])
    scale = clip_norm / jnp.maximum(grad_norm, clip_norm)
    step_float = step_count[0].astype(F32)
    spec_m_new, spec_v_new, direction = adaptive(
        spec_w, spec_m, spec_v, spec_grad * scale, step_float
    )
    dir_part = jnp.sum(direction * direction, axis=(1, 2, 3))
    dir_square = jnp.sum(call_sum(jnp.pad(dir_part, ((0, 8 - NB), (0, 0)))), 1)[:NB]
    weight_norm = jnp.sqrt(weight_square)
    dir_norm = jnp.sqrt(dir_square)
    trust = weight_norm / (dir_norm + 1e-06)
    spec_new = spec_w - learn_rate * trust[:, None, None, None, None] * direction
    encdec_new, encdec_m_new, encdec_v_new, encdec_norms = lamb_dense(
        encdec_w, encdec_m, encdec_v, grad_encdec * scale, step_float, 2
    )
    mlp_new, mlp_m_new, mlp_v_new, mlp_norms = lamb_dense(
        mlp_w, mlp_m, mlp_v, grad_mlp * scale, step_float, 2 * NB
    )
    gain_new, gain_m_new, gain_v_new, gain_norms = lamb_dense(
        gain_w, gain_m, gain_v, grad_gain * scale, step_float, NB
    )
    matrix_norms = jnp.concatenate(
        [jnp.stack([weight_norm, dir_norm], 1), encdec_norms, mlp_norms, gain_norms], 0
    )
    return (
        loss_value,
        grad_norm,
        matrix_norms,
        spec_new,
        spec_m_new,
        spec_v_new,
        spec_new.astype(jnp.bfloat16),
        encdec_new,
        encdec_m_new,
        encdec_v_new,
        encdec_new.astype(jnp.bfloat16),
        mlp_new,
        mlp_m_new,
        mlp_v_new,
        mlp_new.astype(jnp.bfloat16),
        gain_new,
        gain_m_new,
        gain_v_new,
        gain_new.astype(jnp.bfloat16),
    )


def local(mesh, *args):
    inputs, spec_w = args[0], args[5]
    lat = inputs.shape[2] * mesh.shape["lat"]
    fits = (
        dict(mesh.shape) == {"lat": 2, "ma": RANKS}
        and inputs.shape[0] == 2
        and lat == 2 * RANKS
        and spec_w.shape[1] * RANKS == L
    )
    return (special if fits else general)(*args)


def solution(mesh):
    placed = (
        P(None, "ma", "lat", None),
        P(None, None, "ma", "lat", None),
        P(None, "ma", "lat"),
        P(),
        P(),
        P(None, "ma", None, None, "lat"),
        P(None, "ma", None, None, "lat"),
        P(None, "ma", None, None, "lat"),
        P(),
        P(),
        P(),
        P(),
        P(),
        P(),
        P(),
        P(),
        P(),
    )
    return jax.shard_map(
        functools.partial(local, mesh),
        mesh=mesh,
        in_specs=placed,
        out_specs=(
            P(),
            P(),
            P(),
            P(None, "ma", None, None, "lat"),
            P(None, "ma", None, None, "lat"),
            P(None, "ma", None, None, "lat"),
            P(None, "ma", None, None, "lat"),
            P(),
            P(),
            P(),
            P(),
            P(),
            P(),
            P(),
            P(),
            P(),
            P(),
            P(),
            P(),
        ),
        check_vma=False,
    )
```

```python
import functools
import math

import jax
import jax.numpy as jnp
import ml_dtypes
import numpy as np
from jax import lax
from jax.experimental import pallas as pl
from jax.experimental.pallas import tpu as pltpu
from jax.sharding import PartitionSpec as P

E = 256
C = 73
L = 96
NB = 3
ROLL = 2


beta_first = 0.9
beta_second = 0.999
adam_eps = 1e-08
weight_decay = 0.01
learn_rate = 0.4
clip_norm = 0.05
norm_eps = 1e-05


def legendre(orders, angles):
    cosines = jnp.cos(angles)[None, :]
    sines = jnp.sin(angles)[None, :]
    order_col = orders[:, None]
    log_start = 0.5 * (
        jnp.log((2.0 * order_col + 1.0) / (4.0 * math.pi))
        + lax.lgamma(2.0 * order_col + 1.0)
        - 2.0 * lax.lgamma(order_col + 1.0)
        - order_col * math.log(4.0)
    ) + order_col * jnp.log(sines)
    starting = jnp.exp(log_start)

    def advance(carry, degree):
        previous, earlier = carry
        upper = jnp.maximum(degree * degree - order_col * order_col, 1.0)
        factor = jnp.sqrt(jnp.maximum(4.0 * degree * degree - 1.0, 1.0) / upper)
        lower = jnp.maximum((degree - 1.0) ** 2 - order_col * order_col, 0.0)
        shrink = jnp.sqrt(lower / jnp.maximum(4.0 * (degree - 1.0) ** 2 - 1.0, 1.0))
        stepped = factor * (cosines * previous - shrink * earlier)
        second = jnp.sqrt(2.0 * order_col + 3.0) * cosines * starting
        value = jnp.where(
            degree < order_col,
            0.0,
            jnp.where(
                degree == order_col, starting, jnp.where(degree == order_col + 1.0, second, stepped)
            ),
        )
        return ((value, previous), value)

    zero_rows = jnp.zeros_like(starting)
    unused, table = lax.scan(advance, (zero_rows, zero_rows), jnp.arange(L, dtype=jnp.float32))
    return table


def dft_tables(orders, count_lon):
    phases = orders[:, None] * jnp.arange(count_lon, dtype=jnp.int32)[None, :] % count_lon
    phase = phases.astype(jnp.float32) * (2.0 * math.pi / count_lon)
    cosines = jnp.cos(phase)
    sines = jnp.sin(phase)
    number = orders.shape[0]
    forward = jnp.stack([cosines, -sines], 1).reshape(2 * number, count_lon)
    factor = jnp.where(orders == 0, 1.0, 2.0)[:, None] / math.sqrt(2.0 * math.pi)
    inverse = jnp.stack([factor * cosines, -factor * sines], 1).reshape(2 * number, count_lon).T
    return (forward, inverse)


def adaptive(weight, first, second, grad, step_float):
    first_new = beta_first * first + (1.0 - beta_first) * grad
    second_new = beta_second * second + (1.0 - beta_second) * grad * grad
    direction = (
        first_new
        / (1.0 - beta_first**step_float)
        / (jnp.sqrt(second_new / (1.0 - beta_second**step_float)) + adam_eps)
        + weight_decay * weight
    )
    return (first_new, second_new, direction)


def lamb_dense(weight, first, second, grad, step_float, groups):
    first_new, second_new, direction = adaptive(weight, first, second, grad, step_float)
    flat_weight = weight.reshape(groups, -1)
    flat_dir = direction.reshape(groups, -1)
    weight_norm = jnp.sqrt(jnp.sum(flat_weight * flat_weight, 1))
    dir_norm = jnp.sqrt(jnp.sum(flat_dir * flat_dir, 1))
    trust = weight_norm / (dir_norm + 1e-06)
    new_weight = (flat_weight - learn_rate * trust[:, None] * flat_dir).reshape(weight.shape)
    return (new_weight, first_new, second_new, jnp.stack([weight_norm, dir_norm], 1))


def norm_forward(hidden, gain_vec):
    centre = jnp.mean(hidden, -1, keepdims=True)
    centred = hidden - centre
    inv_std = lax.rsqrt(jnp.mean(centred * centred, -1, keepdims=True) + norm_eps)
    normal = centred * inv_std
    return ((normal * gain_vec).astype(jnp.bfloat16), normal, inv_std)


def norm_backward(d_normed, normal, inv_std, gain_vec):
    scaled = d_normed * gain_vec
    d_gain = jnp.sum(d_normed * normal, axis=(0, 1, 2))
    d_hidden = inv_std * (
        scaled
        - jnp.mean(scaled, -1, keepdims=True)
        - normal * jnp.mean(scaled * normal, -1, keepdims=True)
    )
    return (d_hidden, d_gain)


def mlp_forward(merged, weights):
    merged_low = merged.astype(jnp.bfloat16)
    pre_act = jnp.einsum(
        "jibe,ef->jibf", merged_low, weights[0], preferred_element_type=jnp.float32
    )
    gelu_out = jax.nn.gelu(pre_act).astype(jnp.bfloat16)
    hidden = merged + jnp.einsum(
        "jibf,ef->jibe", gelu_out, weights[1], preferred_element_type=jnp.float32
    )
    return (hidden, (merged_low, pre_act, gelu_out))


def mlp_backward(d_hidden, stored, weights):
    merged_low, pre_act, gelu_out = stored
    d_branch = d_hidden.astype(jnp.bfloat16)
    d_gelu = jnp.einsum("jibe,ef->jibf", d_branch, weights[1], preferred_element_type=jnp.float32)
    unused, pullback = jax.vjp(jax.nn.gelu, pre_act)
    d_pre = pullback(d_gelu)[0].astype(jnp.bfloat16)
    grad_out = jnp.einsum("jibf,jibe->ef", gelu_out, d_branch, preferred_element_type=jnp.float32)
    grad_in = jnp.einsum("jibe,jibf->ef", merged_low, d_pre, preferred_element_type=jnp.float32)
    d_merged = d_hidden + jnp.einsum(
        "jibf,ef->jibe", d_pre, weights[0], preferred_element_type=jnp.float32
    )
    return (d_merged, jnp.stack([grad_in, grad_out], 0))


def general(
    inputs,
    targets,
    mask,
    var_weight,
    step_count,
    spec_w,
    spec_m,
    spec_v,
    encdec_w,
    encdec_m,
    encdec_v,
    mlp_w,
    mlp_m,
    mlp_v,
    gain_w,
    gain_m,
    gain_v,
):
    n_ma = lax.axis_size("ma")
    n_lat = lax.axis_size("lat")
    ma_pos = lax.axis_index("ma")
    lat_pos = lax.axis_index("lat")
    batch = inputs.shape[0]
    lon_loc = inputs.shape[1]
    lat_loc = inputs.shape[2]
    nlon_all = lon_loc * n_ma
    nlat_all = lat_loc * n_lat
    orders_loc = L // n_ma
    angles = (jnp.arange(nlat_all, dtype=jnp.float32) + 0.5) * (math.pi / nlat_all)
    local_orders = ma_pos * orders_loc + jnp.arange(orders_loc, dtype=jnp.int32)
    table = legendre(local_orders.astype(jnp.float32), angles)
    quadrature = jnp.sin(angles) * (math.sqrt(2.0 * math.pi) / nlon_all * math.pi / nlat_all)
    fwd_leg = (table * quadrature[None, None, :]).astype(jnp.bfloat16)
    inv_leg = table.astype(jnp.bfloat16)
    fwd_table, inv_table = dft_tables(jnp.arange(L, dtype=jnp.int32), nlon_all)
    fwd_four = fwd_table.astype(jnp.bfloat16)
    inv_four = inv_table.astype(jnp.bfloat16)
    fwd_back = fwd_four.T
    inv_back = inv_four.T
    sines = jnp.sin(angles)
    area = sines / jnp.mean(sines)
    area_rows = lax.dynamic_slice_in_dim(area, lat_pos * lat_loc, lat_loc)
    mask_grid = jnp.transpose(mask, (1, 2, 0)).astype(jnp.float32)
    pixel_weight = (
        area_rows[None, :, None, None]
        * var_weight.astype(jnp.float32)[None, None, None, :]
        * mask_grid[:, :, :, None]
    )
    grid_targets = jnp.transpose(targets, (0, 2, 3, 1, 4))
    denom = float(batch * nlon_all * nlat_all * C)

    def apply_table(table_full, block_in):
        whole_out = jnp.einsum(
            "ok,kibe->oibe",
            table_full,
            lax.all_to_all(block_in, "ma", split_axis=3, concat_axis=0, tiled=True),
            preferred_element_type=jnp.float32,
        )
        return lax.all_to_all(
            whole_out.astype(jnp.bfloat16), "ma", split_axis=0, concat_axis=3, tiled=True
        ).astype(whole_out.dtype)

    def spectral_backward(d_filtered, owned, weight_blk):
        d_rows = apply_table(inv_back, d_filtered.astype(jnp.bfloat16)).astype(jnp.bfloat16)
        d_spec = lax.all_to_all(d_rows, "lat", split_axis=3, concat_axis=1, tiled=True)
        out_width = d_spec.shape[3]
        d_mixed = jnp.einsum(
            "lmi,mpibo->lmpbo",
            inv_leg,
            d_spec.reshape(orders_loc, 2, nlat_all, batch, out_width),
            preferred_element_type=jnp.float32,
        ).astype(jnp.bfloat16)
        d_own = lax.all_to_all(d_mixed, "ma", split_axis=0, concat_axis=1, tiled=True)
        real_w = weight_blk[:, 0]
        imag_w = weight_blk[:, 1]
        d_real = d_own[:, :, 0]
        d_imag = d_own[:, :, 1]
        d_coef_real = jnp.einsum(
            "lmbo,leo->lmbe", d_real, real_w, preferred_element_type=jnp.float32
        ) + jnp.einsum("lmbo,leo->lmbe", d_imag, imag_w, preferred_element_type=jnp.float32)
        d_coef_imag = jnp.einsum(
            "lmbo,leo->lmbe", d_imag, real_w, preferred_element_type=jnp.float32
        ) - jnp.einsum("lmbo,leo->lmbe", d_real, imag_w, preferred_element_type=jnp.float32)
        grad_real = jnp.einsum(
            "lmbe,lmbo->leo", owned[:, :, 0], d_real, preferred_element_type=jnp.float32
        ) + jnp.einsum("lmbe,lmbo->leo", owned[:, :, 1], d_imag, preferred_element_type=jnp.float32)
        grad_imag = jnp.einsum(
            "lmbe,lmbo->leo", owned[:, :, 0], d_imag, preferred_element_type=jnp.float32
        ) - jnp.einsum("lmbe,lmbo->leo", owned[:, :, 1], d_real, preferred_element_type=jnp.float32)
        d_owned = jnp.stack([d_coef_real, d_coef_imag], 2)
        d_coeffs = lax.all_to_all(
            d_owned.astype(jnp.bfloat16), "ma", split_axis=1, concat_axis=0, tiled=True
        ).astype(d_owned.dtype)
        d_full = jnp.einsum(
            "lmi,lmpbe->mpibe",
            fwd_leg.astype(jnp.float32),
            d_coeffs,
            precision=lax.Precision.HIGHEST,
        ).reshape(2 * orders_loc, nlat_all, batch, E)
        d_spec_rows = lax.psum_scatter(
            d_full.astype(jnp.bfloat16), "lat", scatter_dimension=1, tiled=True
        )
        return (apply_table(fwd_back, d_spec_rows), jnp.stack([grad_real, grad_imag], 1))

    spec_bf = spec_w.astype(jnp.bfloat16)
    encdec_bf = encdec_w.astype(jnp.bfloat16)
    mlp_bf = mlp_w.astype(jnp.bfloat16)

    def model_backward(d_pred, stored):
        state_low, hidden_low, records = stored
        d_dec = d_pred.astype(jnp.bfloat16)
        grad_dec = jnp.einsum(
            "jibe,jibc->ce", hidden_low, d_dec, preferred_element_type=jnp.float32
        )
        d_hidden = jnp.einsum(
            "jibc,ce->jibe", d_dec, encdec_bf[1], preferred_element_type=jnp.float32
        )
        spec_grads = [None] * NB
        mlp_grads = [None] * NB
        gain_grads = [None] * NB
        for block_idx in reversed(range(NB)):
            normal, inv_std, owned, mlp_kept = records[block_idx]
            d_merged, mlp_grads[block_idx] = mlp_backward(d_hidden, mlp_kept, mlp_bf[block_idx])
            d_normed, spec_grads[block_idx] = spectral_backward(d_merged, owned, spec_bf[block_idx])
            d_norm_in, gain_grads[block_idx] = norm_backward(
                d_normed, normal, inv_std, gain_w[block_idx]
            )
            d_hidden = d_merged + d_norm_in
        d_enc = d_hidden.astype(jnp.bfloat16)
        grad_enc = jnp.einsum("jibc,jibe->ce", state_low, d_enc, preferred_element_type=jnp.float32)
        d_state = d_pred + jnp.einsum(
            "jibe,ce->jibc", d_enc, encdec_bf[0], preferred_element_type=jnp.float32
        )
        return (
            d_state,
            (
                jnp.stack([grad_enc, grad_dec], 0),
                jnp.stack(spec_grads, 0),
                jnp.stack(mlp_grads, 0),
                jnp.stack(gain_grads, 0),
            ),
        )

    state = jnp.transpose(inputs, (1, 2, 0, 3))
    history = []
    loss_part = jnp.zeros((), jnp.float32)
    for section_idx in range(ROLL):
        model_state_low = state.astype(jnp.bfloat16)
        hidden = jnp.einsum(
            "jibc,ce->jibe", model_state_low, encdec_bf[0], preferred_element_type=jnp.float32
        )
        model_records = []
        for model_block_idx in range(NB):
            model_normed, model_normal, model_inv_std = norm_forward(
                hidden, gain_w[model_block_idx]
            )
            spectral_weight_blk = spec_bf[model_block_idx]
            spec_rows = apply_table(fwd_four, model_normed).astype(jnp.bfloat16)
            piece = lax.all_gather(spec_rows, "lat", axis=1, tiled=True)
            row_width = piece.shape[1]
            paired = piece.reshape(orders_loc, 2, row_width, piece.shape[2], piece.shape[3])
            coeffs = jnp.einsum(
                "lmi,mpibe->lmpbe", fwd_leg, paired, preferred_element_type=jnp.float32
            ).astype(jnp.bfloat16)
            spectral_owned = lax.all_to_all(coeffs, "ma", split_axis=0, concat_axis=1, tiled=True)
            spectral_real_w = spectral_weight_blk[:, 0]
            spectral_imag_w = spectral_weight_blk[:, 1]
            mixed_real = jnp.einsum(
                "lmbe,leo->lmbo",
                spectral_owned[:, :, 0],
                spectral_real_w,
                preferred_element_type=jnp.float32,
            ) - jnp.einsum(
                "lmbe,leo->lmbo",
                spectral_owned[:, :, 1],
                spectral_imag_w,
                preferred_element_type=jnp.float32,
            )
            mixed_imag = jnp.einsum(
                "lmbe,leo->lmbo",
                spectral_owned[:, :, 0],
                spectral_imag_w,
                preferred_element_type=jnp.float32,
            ) + jnp.einsum(
                "lmbe,leo->lmbo",
                spectral_owned[:, :, 1],
                spectral_real_w,
                preferred_element_type=jnp.float32,
            )
            mixed_owned = jnp.stack([mixed_real, mixed_imag], 2).astype(jnp.bfloat16)
            mixed = lax.all_to_all(mixed_owned, "ma", split_axis=1, concat_axis=0, tiled=True)
            spec_out = jnp.einsum(
                "lmi,lmpbo->mpibo", inv_leg, mixed, preferred_element_type=jnp.float32
            )
            spec_out = spec_out.astype(jnp.bfloat16).reshape(
                2 * orders_loc, nlat_all, batch, mixed.shape[4]
            )
            rows_out = lax.all_to_all(spec_out, "lat", split_axis=1, concat_axis=3, tiled=True)
            filtered = apply_table(inv_four, rows_out)
            hidden, model_mlp_kept = mlp_forward(hidden + filtered, mlp_bf[model_block_idx])
            model_records.append((model_normal, model_inv_std, spectral_owned, model_mlp_kept))
        model_hidden_low = hidden.astype(jnp.bfloat16)
        prediction = state + jnp.einsum(
            "jibe,ce->jibc", model_hidden_low, encdec_bf[1], preferred_element_type=jnp.float32
        )
        prediction, stored = (prediction, (model_state_low, model_hidden_low, model_records))
        misfit = prediction - grid_targets[section_idx]
        loss_part = loss_part + jnp.sum(pixel_weight * misfit * misfit) / denom
        history.append((stored, misfit))
        state = prediction
    d_state = jnp.zeros_like(state)
    totals = None
    for section_idx in reversed(range(ROLL)):
        stored, misfit = history[section_idx]
        d_pred = 2.0 * pixel_weight * misfit / denom + d_state
        d_state, section_grads = model_backward(d_pred, stored)
        totals = section_grads if totals is None else jax.tree.map(jnp.add, totals, section_grads)
    grad_encdec, spec_grad, grad_mlp, grad_gain = totals
    grad_encdec, grad_mlp, grad_gain, loss_value, spec_square, weight_square = lax.psum(
        (
            grad_encdec,
            grad_mlp,
            grad_gain,
            loss_part,
            jnp.sum(spec_grad * spec_grad),
            jnp.sum(spec_w * spec_w, axis=(1, 2, 3, 4)),
        ),
        ("lat", "ma"),
    )
    total_square = (
        spec_square
        + jnp.sum(grad_encdec * grad_encdec)
        + jnp.sum(grad_mlp * grad_mlp)
        + jnp.sum(grad_gain * grad_gain)
    )
    grad_norm = jnp.sqrt(total_square)
    scale = clip_norm / jnp.maximum(grad_norm, clip_norm)
    step_float = step_count[0].astype(jnp.float32)
    spec_m_new, spec_v_new, direction = adaptive(
        spec_w, spec_m, spec_v, spec_grad * scale, step_float
    )
    dir_square = lax.psum(jnp.sum(direction * direction, axis=(1, 2, 3, 4)), ("lat", "ma"))
    weight_norm = jnp.sqrt(weight_square)
    dir_norm = jnp.sqrt(dir_square)
    trust = weight_norm / (dir_norm + 1e-06)
    spec_new = spec_w - learn_rate * trust[:, None, None, None, None] * direction
    encdec_new, encdec_m_new, encdec_v_new, encdec_norms = lamb_dense(
        encdec_w, encdec_m, encdec_v, grad_encdec * scale, step_float, 2
    )
    mlp_new, mlp_m_new, mlp_v_new, mlp_norms = lamb_dense(
        mlp_w, mlp_m, mlp_v, grad_mlp * scale, step_float, 2 * NB
    )
    gain_new, gain_m_new, gain_v_new, gain_norms = lamb_dense(
        gain_w, gain_m, gain_v, grad_gain * scale, step_float, NB
    )
    matrix_norms = jnp.concatenate(
        [jnp.stack([weight_norm, dir_norm], 1), encdec_norms, mlp_norms, gain_norms], 0
    )
    return (
        loss_value,
        grad_norm,
        matrix_norms,
        spec_new,
        spec_m_new,
        spec_v_new,
        spec_new.astype(jnp.bfloat16),
        encdec_new,
        encdec_m_new,
        encdec_v_new,
        encdec_new.astype(jnp.bfloat16),
        mlp_new,
        mlp_m_new,
        mlp_v_new,
        mlp_new.astype(jnp.bfloat16),
        gain_new,
        gain_m_new,
        gain_v_new,
        gain_new.astype(jnp.bfloat16),
    )


RANKS = 16
ORDS = L // RANKS
SLOTS = 8
F32 = jnp.float32
BF16 = jnp.bfloat16


def legendre_f64(nlat):
    theta = (np.arange(nlat) + 0.5) * (math.pi / nlat)
    cosines, sines = np.cos(theta), np.sin(theta)
    table = np.zeros((L, L, nlat))
    for m in range(L):
        log_start = 0.5 * (
            math.log((2.0 * m + 1.0) / (4.0 * math.pi))
            + math.lgamma(2.0 * m + 1.0)
            - 2.0 * math.lgamma(m + 1.0)
            - m * math.log(4.0)
        ) + m * np.log(sines)
        table[m, m] = np.exp(log_start)
        if m + 1 < L:
            table[m + 1, m] = math.sqrt(2.0 * m + 3.0) * cosines * table[m, m]
        for k in range(m + 2, L):
            factor = math.sqrt((4.0 * k * k - 1.0) / (k * k - m * m))
            shrink = math.sqrt(((k - 1.0) ** 2 - m * m) / (4.0 * (k - 1.0) ** 2 - 1.0))
            table[k, m] = factor * (cosines * table[k - 1, m] - shrink * table[k - 2, m])
    return table, sines


def low_np(array):
    return array.astype(np.float32).astype(ml_dtypes.bfloat16)


def slot_map():
    degree = np.full((RANKS, 3, SLOTS), -1)
    order = np.full((RANKS, SLOTS), -1)
    for d in range(RANKS):
        y, w, xc = d // 8, (d // 4) % 2, d % 4
        lo, hi = 4 * w + xc, 4 * (3 - w) + xc
        n_lo, n_hi = (6 * lo + 5) // RANKS + 1, (6 * hi + 5) // RANKS + 1
        for group, first, count in ((hi, 0, n_hi), (lo, SLOTS - n_lo, n_lo)):
            for r in range(count):
                order[d, first + r] = r
                for t in range(3):
                    degree[d, t, first + r] = 6 * group + 3 * y + t
    return degree, order


def make_tables(nlat, nlon):
    table, sines = legendre_f64(nlat)
    quadrature = sines * (math.sqrt(2.0 * math.pi) / nlon * math.pi / nlat)
    fwd_leg = np.asarray(low_np(table * quadrature[None, None, :]))
    inv_leg = np.asarray(low_np(table))
    degree, order = slot_map()
    shape = (RANKS, RANKS, 3, 2, SLOTS, RANKS, ORDS, 2, 2)
    fwd = np.zeros(shape, ml_dtypes.bfloat16)
    inv = np.zeros(shape, ml_dtypes.bfloat16)
    for g in range(RANKS):
        for d in range(RANKS):
            for slot in range(SLOTS):
                r = order[d, slot]
                if r < 0:
                    continue
                for t in range(3):
                    k, m = degree[d, t, slot], g + RANKS * r
                    for p in range(2):
                        fwd[g, d, t, p, slot, :, r, p, :] = fwd_leg[k, m].reshape(RANKS, 2)
                        inv[g, d, t, p, slot, :, r, p, :] = inv_leg[k, m].reshape(RANKS, 2)
    rows = RANKS * 3 * 2 * SLOTS
    cols = RANKS * ORDS * 2 * 2
    fwd = fwd.reshape(RANKS, rows, cols)
    inv = inv.reshape(RANKS, rows, cols)
    phase = 2.0 * math.pi * (np.arange(L)[:, None] * np.arange(nlon)[None, :] % nlon) / nlon
    scale = np.where(np.arange(L) == 0, 1.0, 2.0)[:, None] / math.sqrt(2.0 * math.pi)
    four = low_np(np.stack([np.cos(phase), -np.sin(phase)], 1))
    back = low_np(np.stack([scale * np.cos(phase), -scale * np.sin(phase)], 1))
    def wide(small):
        out = np.zeros((RANKS, ORDS, 2, 2, 2, nlon), ml_dtypes.bfloat16)
        ordered = small.reshape(ORDS, RANKS, 2, nlon).transpose(1, 0, 2, 3)
        for il in range(2):
            out[:, :, :, il, il, :] = ordered
        return out.reshape(cols, 2 * nlon)

    def turn(array):
        return np.ascontiguousarray(np.swapaxes(array, -1, -2))

    four, back = wide(four), wide(back)
    return (fwd, turn(inv), turn(fwd), inv), (four, turn(back), turn(four), back)


def place():
    ma = lax.axis_index("ma")
    y = lax.axis_index("lat")
    z = ma // 4
    zh = z // 2
    w = z + zh * (3 - 2 * z)
    return zh, y, w, 8 * y + 4 * w + ma % 4


def device_of(zh, q):
    w = (q // 4) % 2
    z = w + zh * (3 - 2 * w)
    return {"lat": q // 8, "ma": 4 * z + q % 4}


def nn(a, b):
    return lax.dot_general(a, b, (((1,), (0,)), ((), ())), preferred_element_type=F32)


def nt(a, b):
    return lax.dot_general(a, b, (((1,), (1,)), ((), ())), preferred_element_type=F32)


def tn(a, b):
    return lax.dot_general(a, b, (((0,), (0,)), ((), ())), preferred_element_type=F32)


def piece_of(kind, half, zh, y):
    return 2 - 2 * ((kind + zh) % 2) + (half + y) % 2


def weight_of(w_all, block, kind, t, part, zh, y):
    return jnp.concatenate(
        [w_all[block, piece_of(kind, half, zh, y), t, part] for half in range(2)], axis=1
    )


def hi_rows(w):
    slot = lax.broadcasted_iota(jnp.int32, (RANKS * 2 * SLOTS, 1), 0) % SLOTS
    return slot < 6 - w


GELU_A = math.sqrt(2.0 / math.pi)
GELU_B = 0.044715


def normal_of(hidden):
    centre = jnp.mean(hidden, -1, keepdims=True)
    centred = hidden - centre
    inv_std = lax.rsqrt(jnp.mean(centred * centred, -1, keepdims=True) + norm_eps)
    return centred * inv_std, inv_std


def rows_loop(total, step, body):
    def one(k, carry):
        body(pl.ds(pl.multiple_of(k * step, step), step))
        return carry

    lax.fori_loop(0, total // step, one, 0)


MESH = pl.DeviceIdType.MESH
LANES = 128
MASK_LANE = LANES - 1


def greet_all():
    barrier = pltpu.get_barrier_semaphore()
    me = 2 * RANKS // 2 * lax.axis_index("lat") + lax.axis_index("ma")

    def greet(s, carry):
        other = (me + s) % (2 * RANKS)
        pl.semaphore_signal(
            barrier, inc=1, device_id={"lat": other // RANKS, "ma": other % RANKS}, device_id_type=MESH
        )
        return carry

    lax.fori_loop(1, 2 * RANKS, greet, 0)
    pl.semaphore_wait(barrier, 2 * RANKS - 1)


def remote(src, dst, send_sem, recv_sem, device):
    return pltpu.make_async_remote_copy(
        src_ref=src,
        dst_ref=dst,
        send_sem=send_sem,
        recv_sem=recv_sem,
        device_id=device,
        device_id_type=MESH,
    )


def bytes_wait(ref, sem):
    pltpu.make_async_copy(ref, ref, sem).wait()


def flip(value, bits, span):
    out, unit = 0, 1
    while unit < span:
        digit = (value // unit) % 2
        out = out + unit * (1 - digit if bits // unit % 2 else digit)
        unit *= 2
    return out


def peers_of(zh, q):
    ranks = [flip(q, s, RANKS) for s in range(RANKS - 1, 0, -1)]
    return [(d, device_of(zh, d)) for d in ranks]


def push_blocks(source_of, landing, send_sem, recv_sem, peers, q):
    for d, device in peers:
        remote(source_of(d), landing, send_sem, recv_sem, device).start()
    pltpu.make_async_copy(source_of(q), landing, recv_sem).start()


def exchange_start(send, recv, send_sem, recv_sem, peers, q):
    push_blocks(lambda d: send.at[d], recv.at[q], send_sem, recv_sem, peers, q)


def exchange_wait(send, recv, send_sem, recv_sem):
    bytes_wait(recv, recv_sem)
    bytes_wait(send.at[pl.ds(0, RANKS - 1)], send_sem)


def exchange(send, recv, send_sem, recv_sem, peers, q):
    exchange_start(send, recv, send_sem, recv_sem, peers, q)
    exchange_wait(send, recv, send_sem, recv_sem)


def lane_sums(array):
    return jnp.sum(array.reshape(-1, LANES), axis=0, keepdims=True)


def train(
    x_chunks, t_chunks, spec_w, mlp_w, r0, r1, r2, r3, f0, f1, f2, f3,
    encdec, gain, area, var_row,
    g_spec, g_mlp, g_small, scalars,
    pfx, pix, pfxt, pixt, ftx, itx, ftxt, itxt, w_all, w_other, mlp_bf, mlp_stage, code_bf,
    x_recv, goals, weight, x_low, misfit, d_state, h_all, hid_low, v_low, u_buf, dv_buf, dh_buf,
    n_send, s_recv, y_recv, w_send, b_recv, a_own, d_mix,
    dwf, dw_send, dw_recv, dw_own, dmlp, rs_send, rs_recv, mir_send, mir_recv, ag_src,
    d_small, d_gain, sm_send, sm_recv, sm_mir_send, sm_mir_recv, sm_src, scal, scal_recv,
    load_sem, stage_sem, once_send, once_recv, w_send_sem, w_recv_sem, x_send, x_recv_sem,
    g_send_sem, g_recv_sem, rs_sem, mir_send_sem, mir_recv_sem, ag_send_sem, ag_recv_sem, sm_sem,
):
    zh, y, w, q = place()
    peers = peers_of(zh, q)
    ma = lax.axis_index("ma")
    xc = ma % 4
    mirror_ma = 4 * (3 - ma // 4) + xc
    near, far, cross = {"lat": 1 - y, "ma": ma}, {"lat": y, "ma": mirror_ma}, {"lat": 1 - y, "ma": mirror_ma}
    pixels, chans = dh_buf.shape
    spectra = pix.shape[0]
    triples = pfx.shape[0]
    third = 3

    loads = [
        pltpu.make_async_copy(src.at[q], dst, load_sem.at[k])
        for k, (src, dst) in enumerate(((r0, pfx), (r1, pix), (r2, pfxt), (r3, pixt)))
    ] + [
        pltpu.make_async_copy(src, dst, load_sem.at[4 + k])
        for k, (src, dst) in enumerate(((f0, ftx), (f1, itx), (f2, ftxt), (f3, itxt)))
    ]
    stage = dwf

    class SpecLoad:
        def __init__(self, b):
            self.copies = [
                pltpu.make_async_copy(
                    spec_w.at[b, pl.ds(third * k, third)], stage.at[2 * (b % 2) + k], stage_sem.at[2 * b + k]
                )
                for k in range(2)
            ]

        def start(self):
            for copy in self.copies:
                copy.start()

        def wait(self):
            for copy in self.copies:
                copy.wait()

    spec_loads = [SpecLoad(b) for b in range(NB)]
    mlp_loads = [pltpu.make_async_copy(mlp_w.at[b], mlp_stage.at[b % 2], stage_sem.at[2 * NB + b]) for b in range(NB)]
    spec_loads[0].start()
    spec_loads[1].start()
    loads[4].start()
    loads[0].start()
    scal[...] = jnp.zeros_like(scal)
    d_small[...] = jnp.zeros_like(d_small)
    d_gain[...] = jnp.zeros_like(d_gain)
    d_state[...] = jnp.zeros_like(d_state)
    code_bf[...] = encdec[...].astype(BF16)
    greet_all()

    def chunk_to(chunks, landing, sems):
        for bits in range(RANKS - 1, 0, -1):
            other = flip(ma, bits, RANKS)
            remote(chunks.at[other], landing, sems[0], sems[1], {"lat": y, "ma": other}).start()
        pltpu.make_async_copy(chunks.at[ma], landing, sems[1]).start()

    chunk_to(x_chunks, x_recv.at[:, ma], (once_send.at[0], once_recv.at[0]))

    def weights_out(b, where, triple):
        source, piece, device = {
            "near": (w_other, 1, near), "far": (w_all.at[:, 0], 2, far), "cross": (w_other, 3, cross)
        }[where]
        for t in triple:
            remote(source.at[b, t], w_all.at[b, piece, t], w_send_sem.at[b], w_recv_sem.at[b], device).start()

    for b in range(NB):
        spec_loads[b].wait()
        for t in range(third):
            for own, target in ((y, w_all.at[b, 0]), (1 - y, w_other.at[b])):
                value = stage[2 * (b % 2) + own, t]
                scal[2 + b : 3 + b] += lane_sums(value * value)
                target[t] = value.astype(BF16)
        if b + 2 < NB:
            spec_loads[b + 2].start()
        if b == 0:
            weights_out(0, "far", range(third))
            weights_out(0, "cross", range(third))
            weights_out(0, "near", range(third))
            mlp_loads[0].start()
            mlp_loads[1].start()
            for k in (1, 2, 3, 5, 6, 7):
                loads[k].start()
    for b in range(NB):
        mlp_loads[b].wait()
        mlp_bf[b] = mlp_stage[b % 2].astype(BF16)
        if b + 2 < NB:
            mlp_loads[b + 2].start()
    for copy in loads:
        copy.wait()
    bytes_wait(x_recv, once_recv.at[0])
    bytes_wait(x_chunks.at[pl.ds(0, RANKS - 1)], once_send.at[0])

    hi = hi_rows(w)
    rows_mix = RANKS * 2 * SLOTS

    def mixed_by(source, product, block, t, part):
        return jnp.where(
            hi,
            product(source, weight_of(w_all, block, 0, t, part, zh, y)),
            product(source, weight_of(w_all, block, 1, t, part, zh, y)),
        ).reshape(RANKS, 2, SLOTS, chans)

    def narrow(value):
        return value.astype(BF16).reshape(n_send.shape)

    def broad(value):
        return value.astype(BF16).reshape(w_send.shape)

    def fwd_block(step, block):
        slot, idx = 4 * step + block, NB * step + block
        gain_row = gain[block]

        def norm_rows(rows):
            normal, unused = normal_of(h_all[slot, rows, :])
            u_buf[rows, :] = (normal * gain_row).astype(BF16)

        rows_loop(pixels, 128, norm_rows)
        n_send[...] = narrow(nn(ftx[...], u_buf[...]))
        exchange_start(n_send, s_recv, x_send.at[0], x_recv_sem.at[0], peers, q)

        @pl.when(jnp.logical_and(step == 0, block > 0))
        def _():
            weights_out(block, "near", (2,))

        @pl.when(jnp.logical_and(step == 1, block == 0))
        def _():
            chunk_to(t_chunks.at[1], goals.at[1, :, ma], (once_send.at[2], once_recv.at[2]))

        exchange_wait(n_send, s_recv, x_send.at[0], x_recv_sem.at[0])
        w_send[...] = broad(nn(pfx[...], s_recv[...].reshape(spectra, chans)))
        exchange_start(w_send, a_own.at[idx], x_send.at[1], x_recv_sem.at[1], peers, q)

        @pl.when(jnp.logical_and(step == 0, block < NB - 1))
        def _():
            weights_out(block + 1, "far", (0, 1))

        @pl.when(jnp.logical_and(step == 0, block == NB - 1))
        def _():
            chunk_to(t_chunks.at[0], goals.at[0, :, ma], (once_send.at[1], once_recv.at[1]))

        exchange_wait(w_send, a_own.at[idx], x_send.at[1], x_recv_sem.at[1])

        @pl.when(step == 0)
        def _():
            bytes_wait(w_all.at[block, pl.ds(1, 3)], w_recv_sem.at[block])

        for t in range(3):
            coef = a_own[idx, :, t].reshape(rows_mix, chans)
            by_real, by_imag = (mixed_by(coef, nn, block, t, part) for part in range(2))
            mixed = jnp.stack([by_real[:, 0] - by_imag[:, 1], by_real[:, 1] + by_imag[:, 0]], 1)
            w_send[:, t] = mixed.reshape(RANKS, 2 * SLOTS, chans).astype(BF16)
        exchange_start(w_send, b_recv, x_send.at[2], x_recv_sem.at[2], peers, q)

        @pl.when(jnp.logical_and(step == 0, block < NB - 1))
        def _():
            weights_out(block + 1, "far", (2,))
            weights_out(block + 1, "cross", (0,))
            weights_out(block + 1, "near", (0,))

        exchange_wait(w_send, b_recv, x_send.at[2], x_recv_sem.at[2])
        n_send[...] = narrow(nn(pix[...], b_recv[...].reshape(triples, chans)))
        exchange_start(n_send, y_recv, x_send.at[3], x_recv_sem.at[3], peers, q)

        @pl.when(jnp.logical_and(step == 0, block < NB - 1))
        def _():
            weights_out(block + 1, "cross", (1, 2))
            weights_out(block + 1, "near", (1,))

        exchange_wait(n_send, y_recv, x_send.at[3], x_recv_sem.at[3])
        spectrum = y_recv[...].reshape(spectra, chans)

        def mlp_rows(rows):
            merged = h_all[slot, rows, :] + nn(itx[rows, :], spectrum)
            merged_low = merged.astype(BF16)
            v_low[idx, rows, :] = merged_low
            pre = nn(merged_low, mlp_bf[block, 0])
            act = (0.5 * pre * (1.0 + jnp.tanh(GELU_A * (pre + GELU_B * pre * pre * pre)))).astype(BF16)
            h_all[slot + 1, rows, :] = merged + nt(act, mlp_bf[block, 1])

        rows_loop(pixels, 256, mlp_rows)

    denom = float(pixels * RANKS * C * 2)

    def fwd_step(step, carry):
        state = x_recv[...].reshape(pixels, LANES)
        state_low = state.astype(BF16)
        x_low[step] = state_low
        h_all[4 * step] = nn(state_low, code_bf[0])

        def one(block, inner):
            fwd_block(step, block)
            return inner

        lax.fori_loop(0, NB, one, 0)
        hidden_low = h_all[4 * step + 3].astype(BF16)
        hid_low[step] = hidden_low
        prediction = state + nt(hidden_low, code_bf[1])
        x_recv[...] = prediction.reshape(x_recv.shape)

        @pl.when(step == 0)
        def _():
            bytes_wait(goals.at[0], once_recv.at[1])
            bytes_wait(t_chunks.at[0, pl.ds(0, RANKS - 1)], once_send.at[1])
            for il in range(2):
                valid = goals[0, il].reshape(pixels // 2, LANES)[:, MASK_LANE:]
                rows = slice(il * pixels // 2, (il + 1) * pixels // 2)
                weight[rows, :] = valid * (area[il] * var_row[...])

        @pl.when(step == 1)
        def _():
            bytes_wait(goals.at[1], once_recv.at[2])
            bytes_wait(t_chunks.at[1, pl.ds(0, RANKS - 1)], once_send.at[2])

        miss = prediction - goals[step].reshape(pixels, LANES)
        weighted = weight[...] * miss
        scal[0:1] += lane_sums(weighted * miss / denom)
        misfit[step] = 2.0 * weighted / denom
        return carry

    lax.fori_loop(0, ROLL, fwd_step, 0)
    for b in range(NB):
        bytes_wait(w_all.at[b, pl.ds(1, 3)], w_send_sem.at[b])

    def settle(block):
        bytes_wait(dw_recv.at[block], g_recv_sem.at[block])
        for t in range(third):
            for own, one, two in (
                (y, dw_own[block, t], dw_recv[block, 1, t]),
                (1 - y, dw_recv[block, 0, t], dw_recv[block, 2, t]),
            ):
                total = one.astype(F32) + two.astype(F32)
                scal[1:2] += lane_sums(total * total)
                g_spec[block, third * own + t] = total

    def shares_start(block):
        rs_send[...] = dmlp[block].astype(BF16).reshape(rs_send.shape)
        exchange_start(rs_send, rs_recv, rs_sem.at[0], rs_sem.at[1], peers, q)

    def shares_finish(block):
        exchange_wait(rs_send, rs_recv, rs_sem.at[0], rs_sem.at[1])
        share = rs_recv[0].astype(F32)
        for k in range(1, RANKS):
            share = share + rs_recv[k].astype(F32)
        mir_send[block] = share
        remote(mir_send.at[block], mir_recv.at[block], mir_send_sem.at[block], mir_recv_sem.at[block], far).start()

    def shares_spread(block):
        bytes_wait(mir_recv.at[block], mir_recv_sem.at[block])
        total = mir_send[block] + mir_recv[block]
        scal[1:2] += 0.5 * lane_sums(total * total)
        ag_src[block] = total.astype(BF16)
        push_blocks(
            lambda d: ag_src.at[block], g_mlp.at[block, q], ag_send_sem.at[block], ag_recv_sem.at[block], peers, q
        )

    def grads_out(b, where, triple):
        piece, device = {"near": (0, near), "far": (1, far), "cross": (2, cross)}[where]
        for t in triple:
            remote(
                dw_send.at[b, piece, t], dw_recv.at[b, piece, t], g_send_sem.at[b], g_recv_sem.at[b], device
            ).start()

    def bwd_block(lap, step, block):
        early = jnp.logical_and(lap == 1, block > 0)
        later = jnp.logical_and(lap == 1, block < NB - 1)
        slot, idx = 4 * step + block, NB * step + block
        gain_row = gain[block]

        @pl.when(lap == 0)
        def _():
            dmlp[block] = jnp.zeros(dmlp.shape[1:], F32)

        def mlp_rows(rows):
            d_hidden = dh_buf[rows, :]
            d_branch = d_hidden.astype(BF16)
            merged_low = v_low[idx, rows, :]
            pre = nn(merged_low, mlp_bf[block, 0])
            tan = jnp.tanh(GELU_A * (pre + GELU_B * pre * pre * pre))
            act = (0.5 * pre * (1.0 + tan)).astype(BF16)
            slope = 0.5 * (1.0 + tan) + 0.5 * pre * (1.0 - tan * tan) * (
                GELU_A * (1.0 + 3.0 * GELU_B * pre * pre)
            )
            d_pre = (nn(d_branch, mlp_bf[block, 1]) * slope).astype(BF16)
            dmlp[block, 0] += tn(merged_low, d_pre)
            dmlp[block, 1] += tn(d_branch, act)
            d_merged = d_hidden + nt(d_pre, mlp_bf[block, 0])
            dv_buf[rows, :] = d_merged
            u_buf[rows, :] = d_merged.astype(BF16)

        rows_loop(pixels, 256, mlp_rows)
        n_send[...] = narrow(nn(itxt[...], u_buf[...]))
        exchange_start(n_send, s_recv, x_send.at[4], x_recv_sem.at[4], peers, q)

        @pl.when(later)
        def _():
            grads_out(block + 1, "cross", (1,))
            grads_out(block + 1, "near", (1,))

        exchange_wait(n_send, s_recv, x_send.at[4], x_recv_sem.at[4])
        w_send[...] = broad(nn(pixt[...], s_recv[...].reshape(spectra, chans)))
        which = NB * lap + block
        exchange_start(w_send, d_mix.at[which], x_send.at[5], x_recv_sem.at[5], peers, q)

        @pl.when(jnp.logical_and(lap == 1, block < NB - 1))
        def _():
            grads_out(block + 1, "cross", (2,))
            grads_out(block + 1, "near", (2,))
            shares_finish(block + 1)

        exchange_wait(w_send, d_mix.at[which], x_send.at[5], x_recv_sem.at[5])

        def turned_of(d_mixed):
            wide = d_mixed.astype(F32).reshape(RANKS, 2, SLOTS, chans)
            return jnp.stack([wide[:, 1], -wide[:, 0]], 1).reshape(rows_mix, chans).astype(BF16)

        for t in range(3):
            d_mixed = d_mix[which, :, t].reshape(rows_mix, chans)
            by_real, by_imag = (mixed_by(d_mixed, nt, block, t, part) for part in range(2))
            d_coef = jnp.stack([by_real[:, 0] + by_imag[:, 1], by_real[:, 1] - by_imag[:, 0]], 1)
            w_send[:, t] = d_coef.reshape(RANKS, 2 * SLOTS, chans).astype(BF16)
        exchange_start(w_send, b_recv, x_send.at[6], x_recv_sem.at[6], peers, q)

        @pl.when(lap == 1)
        def _():
            for t in range(3):
                others = []
                for turn in range(ROLL):
                    d_mixed = d_mix[NB * turn + block, :, t].reshape(rows_mix, chans)
                    others.append((d_mixed, turned_of(d_mixed)))
                for kind in range(2):
                    keep = hi if kind == 0 else jnp.logical_not(hi)
                    kept = [
                        jnp.where(
                            keep, a_own[NB * (1 - turn) + block, :, t].reshape(rows_mix, chans).astype(F32), 0.0
                        ).astype(BF16)
                        for turn in range(ROLL)
                    ]
                    for part in range(2):
                        grad = tn(kept[0], others[0][part]) + tn(kept[1], others[1][part])
                        for half in range(2):
                            dwf[piece_of(kind, half, zh, y), t, part] = grad[
                                :, half * LANES : (half + 1) * LANES
                            ]
            dw_own[block] = dwf[0]
            for k in range(3):
                dw_send[block, k] = dwf[1 + k].astype(BF16)

            grads_out(block, "far", (0, 1))

        @pl.when(jnp.logical_and(lap == 1, block == 0))
        def _():
            grads_out(block, "far", (2,))
            grads_out(block, "cross", range(third))

        exchange_wait(w_send, b_recv, x_send.at[6], x_recv_sem.at[6])
        n_send[...] = narrow(nn(pfxt[...], b_recv[...].reshape(triples, chans)))
        exchange_start(n_send, y_recv, x_send.at[7], x_recv_sem.at[7], peers, q)

        @pl.when(early)
        def _():
            grads_out(block, "far", (2,))
            grads_out(block, "cross", (0,))
            grads_out(block, "near", (0,))

        @pl.when(jnp.logical_and(lap == 1, block == 0))
        def _():
            grads_out(block, "near", range(third))

        exchange_wait(n_send, y_recv, x_send.at[7], x_recv_sem.at[7])

        @pl.when(lap == 1)
        def _():
            shares_start(block)

        spectrum = y_recv[...].reshape(spectra, chans)

        def norm_rows(rows):
            normal, inv_std = normal_of(h_all[slot, rows, :])
            d_normed = nn(ftxt[rows, :], spectrum)
            scaled = d_normed * gain_row
            d_gain[block] += jnp.sum(d_normed * normal, axis=0, keepdims=True)
            d_norm_in = inv_std * (
                scaled
                - jnp.mean(scaled, -1, keepdims=True)
                - normal * jnp.mean(scaled * normal, -1, keepdims=True)
            )
            dh_buf[rows, :] = dv_buf[rows, :] + d_norm_in

        rows_loop(pixels, 256, norm_rows)

        @pl.when(jnp.logical_and(lap == 1, block < NB - 1))
        def _():
            settle(block + 1)

    def bwd_step(lap, carry):
        step = ROLL - 1 - lap
        d_pred = misfit[step] + d_state[...]
        d_dec = d_pred.astype(BF16)
        d_small[LANES:] += tn(d_dec, hid_low[step])
        dh_buf[...] = nn(d_dec, code_bf[1])

        def one(k, inner):
            bwd_block(lap, step, NB - 1 - k)
            return inner

        lax.fori_loop(0, NB, one, 0)
        d_enc = dh_buf[...].astype(BF16)
        d_small[:LANES] += tn(x_low[step], d_enc)

        @pl.when(lap == 0)
        def _():
            d_state[...] = d_pred + nt(d_enc, code_bf[0])

        return carry

    lax.fori_loop(0, ROLL, bwd_step, 0)

    for b in range(NB):
        d_small[LANES - NB + b : LANES - NB + b + 1] = d_gain[b]
    sm_send[...] = d_small[...].reshape(sm_send.shape)
    exchange_start(sm_send, sm_recv, sm_sem.at[0], sm_sem.at[1], peers, q)
    for b in range(NB - 1, 0, -1):
        shares_spread(b)
    shares_finish(0)
    exchange_wait(sm_send, sm_recv, sm_sem.at[0], sm_sem.at[1])
    share = sm_recv[0]
    for k in range(1, RANKS):
        share = share + sm_recv[k]
    sm_mir_send[...] = share
    swap = remote(sm_mir_send, sm_mir_recv, sm_sem.at[2], sm_sem.at[3], far)
    swap.start()
    swap.wait()
    total = sm_mir_send[...] + sm_mir_recv[...]
    scal[1:2] += 0.5 * lane_sums(total * total)
    sm_src[...] = total
    push_blocks(lambda d: sm_src, g_small.at[q], sm_sem.at[4], sm_sem.at[5], peers, q)
    shares_spread(0)
    settle(0)

    me = RANKS * y + ma
    pltpu.make_async_copy(scal, scal_recv.at[me], sm_sem.at[7]).start()

    def spread(s, carry):
        other = (me + s) % (2 * RANKS)
        remote(
            scal, scal_recv.at[me], sm_sem.at[6], sm_sem.at[7], {"lat": other // RANKS, "ma": other % RANKS}
        ).start()
        return carry

    lax.fori_loop(1, 2 * RANKS, spread, 0)
    bytes_wait(g_small, sm_sem.at[5])
    bytes_wait(g_small.at[pl.ds(0, RANKS - 1)], sm_sem.at[4])
    for b in range(NB):
        bytes_wait(g_mlp.at[b], ag_recv_sem.at[b])
        bytes_wait(g_mlp.at[b, pl.ds(0, RANKS - 1)], ag_send_sem.at[b])
        bytes_wait(mir_send.at[b], mir_send_sem.at[b])
        bytes_wait(dw_send.at[b], g_send_sem.at[b])
    bytes_wait(scal_recv, sm_sem.at[7])
    bytes_wait(scal_recv.at[pl.ds(0, 2 * RANKS - 1)], sm_sem.at[6])
    total = scal_recv[0]
    for k in range(1, 2 * RANKS):
        total = total + scal_recv[k]
    scalars[...] = total


def call_train(x_chunks, t_chunks, spec_w, mlp_w, tables, encdec, gain, area, var_row):
    vmem = pltpu.VMEM
    dma = pltpu.SemaphoreType.DMA
    lon = x_chunks.shape[2]
    pixels, chans = 2 * RANKS * lon, gain.shape[-1]
    third = spec_w.shape[1] // 2
    triple = (third, 2, chans, LANES)
    narrow, wide = (RANKS, 4 * ORDS, chans), (RANKS, 3, 2 * SLOTS, chans)
    triples, spectra = RANKS * 6 * SLOTS, RANKS * 4 * ORDS
    mlp_shape = mlp_w.shape[1:]
    chunk = (mlp_shape[0] * mlp_shape[1] // RANKS, mlp_shape[2])
    small = (2 * LANES // RANKS, chans)
    b16 = lambda *shape: vmem(shape, BF16)
    f32 = lambda *shape: vmem(shape, F32)
    everywhere = pl.BlockSpec(memory_space=pl.ANY)
    inside = pl.BlockSpec(memory_space=vmem)
    return pl.pallas_call(
        train,
        out_shape=(
            jax.ShapeDtypeStruct(spec_w.shape, F32),
            jax.ShapeDtypeStruct((NB, RANKS, *chunk), BF16),
            jax.ShapeDtypeStruct((RANKS, *small), F32),
            jax.ShapeDtypeStruct((8, LANES), F32),
        ),
        in_specs=[everywhere] * 12 + [inside] * 4,
        out_specs=[inside] * 4,
        scratch_shapes=[
            b16(triples, spectra), b16(spectra, triples), b16(spectra, triples), b16(triples, spectra),
            b16(spectra, pixels), b16(pixels, spectra), b16(pixels, spectra), b16(spectra, pixels),
            b16(NB, 4, *triple), b16(NB, *triple), b16(*mlp_w.shape), f32(2, *mlp_shape),
            b16(*encdec.shape),
            f32(2, RANKS, lon, LANES), f32(ROLL, 2, RANKS, lon, LANES), f32(pixels, LANES), b16(ROLL, pixels, LANES),
            f32(ROLL, pixels, LANES), f32(pixels, LANES), f32(4 * ROLL, pixels, chans), b16(ROLL, pixels, chans),
            b16(NB * ROLL, pixels, chans), b16(pixels, chans), f32(pixels, chans), f32(pixels, chans),
            b16(*narrow), b16(*narrow), b16(*narrow), b16(*wide), b16(*wide), b16(NB * ROLL, *wide), b16(NB * ROLL, *wide),
            f32(4, *triple), b16(NB, 3, *triple), b16(NB, 3, *triple), f32(NB, *triple), f32(NB, *mlp_shape),
            b16(RANKS, *chunk), b16(RANKS, *chunk), f32(NB, *chunk), f32(NB, *chunk), b16(NB, *chunk),
            f32(2 * LANES, chans), f32(NB, 1, chans), f32(RANKS, *small), f32(RANKS, *small), f32(*small), f32(*small),
            f32(*small), f32(8, LANES), f32(2 * RANKS, 8, LANES),
            dma((8,)), dma((3 * NB,)), dma((3,)), dma((3,)), dma((NB,)), dma((NB,)), dma((8,)), dma((8,)),
            dma((NB,)), dma((NB,)), dma((2,)), dma((NB,)), dma((NB,)), dma((NB,)), dma((NB,)), dma((8,)),
        ],
        compiler_params=pltpu.CompilerParams(
            collective_id=0, has_side_effects=True, vmem_limit_bytes=61 << 20
        ),
    )(x_chunks, t_chunks, spec_w, mlp_w, *tables, encdec, gain, area, var_row)


def sum_all(value_ref, out_ref, recv, send_sem, recv_sem):
    greet_all()
    me = RANKS * lax.axis_index("lat") + lax.axis_index("ma")
    pltpu.make_async_copy(value_ref, recv.at[me], recv_sem).start()

    def spread(s, carry):
        other = (me + s) % (2 * RANKS)
        remote(value_ref, recv.at[me], send_sem, recv_sem, {"lat": other // RANKS, "ma": other % RANKS}).start()
        return carry

    lax.fori_loop(1, 2 * RANKS, spread, 0)
    bytes_wait(recv, recv_sem)
    bytes_wait(recv.at[pl.ds(0, 2 * RANKS - 1)], send_sem)
    total = recv[0]
    for k in range(1, 2 * RANKS):
        total = total + recv[k]
    out_ref[...] = total


def call_sum(value):
    inside = pl.BlockSpec(memory_space=pltpu.VMEM)
    return pl.pallas_call(
        sum_all,
        out_shape=jax.ShapeDtypeStruct(value.shape, F32),
        in_specs=[inside],
        out_specs=inside,
        scratch_shapes=[
            pltpu.VMEM((2 * RANKS, *value.shape), F32),
            pltpu.SemaphoreType.DMA,
            pltpu.SemaphoreType.DMA,
        ],
        compiler_params=pltpu.CompilerParams(collective_id=1, has_side_effects=True),
    )(value)


def chunks_of(field):
    items, lon, lat, width = field.shape
    pairs = lat // 2
    chunks = jnp.moveaxis(field.reshape(items, lon, pairs, 2, width), 1, 3)
    return jnp.concatenate([chunks[0], jnp.roll(chunks[1], pairs // 2, 0)], 0)


def special(
    inputs,
    targets,
    mask,
    var_weight,
    step_count,
    spec_w,
    spec_m,
    spec_v,
    encdec_w,
    encdec_m,
    encdec_v,
    mlp_w,
    mlp_m,
    mlp_v,
    gain_w,
    gain_m,
    gain_v,
):
    zh, y, w, q = place()
    nlon = inputs.shape[1] * lax.axis_size("ma")
    nlat = inputs.shape[2] * lax.axis_size("lat")
    ranked, common = make_tables(nlat, nlon)
    tables = tuple(jnp.asarray(t) for t in (*ranked, *common))
    spare = LANES - C
    x_chunks = chunks_of(jnp.pad(inputs, ((0, 0),) * 3 + ((0, spare),)))
    masks = jnp.broadcast_to(mask.astype(F32)[None, ..., None], (*targets.shape[:-1], 1))
    goal = jnp.concatenate([targets, jnp.zeros((*targets.shape[:-1], spare - 1), F32), masks], -1)
    t_chunks = jnp.stack([chunks_of(goal[0]), chunks_of(goal[1])], 0)
    angles = (jnp.arange(nlat, dtype=F32) + 0.5) * (math.pi / nlat)
    sines = jnp.sin(angles)
    area = lax.dynamic_slice_in_dim(sines / jnp.mean(sines), 2 * q, 2)
    area = jnp.broadcast_to(area[:, None, None], (2, 1, LANES))
    var_row = jnp.pad(var_weight.astype(F32), (0, spare))[None]
    encdec = jnp.pad(encdec_w, ((0, 0), (0, spare), (0, 0)))
    spec_grad, mlp_sum, small_sum, scalars = call_train(
        x_chunks, t_chunks, spec_w, mlp_w, tables, encdec, gain_w[:, None], area, var_row
    )
    grad_mlp = mlp_sum.reshape(mlp_w.shape).astype(F32)
    small_sum = small_sum.reshape(2, LANES, E)
    grad_encdec = small_sum[:, :C]
    grad_gain = small_sum[0, LANES - NB :]
    sums = jnp.sum(scalars, 1)
    loss_value = sums[0]
    weight_square = sums[2 : 2 + NB]
    grad_norm = jnp.sqrt(sums[1])
    scale = clip_norm / jnp.maximum(grad_norm, clip_norm)
    step_float = step_count[0].astype(F32)
    spec_m_new, spec_v_new, direction = adaptive(
        spec_w, spec_m, spec_v, spec_grad * scale, step_float
    )
    dir_part = jnp.sum(direction * direction, axis=(1, 2, 3))
    dir_square = jnp.sum(call_sum(jnp.pad(dir_part, ((0, 8 - NB), (0, 0)))), 1)[:NB]
    weight_norm = jnp.sqrt(weight_square)
    dir_norm = jnp.sqrt(dir_square)
    trust = weight_norm / (dir_norm + 1e-06)
    spec_new = spec_w - learn_rate * trust[:, None, None, None, None] * direction
    encdec_new, encdec_m_new, encdec_v_new, encdec_norms = lamb_dense(
        encdec_w, encdec_m, encdec_v, grad_encdec * scale, step_float, 2
    )
    mlp_new, mlp_m_new, mlp_v_new, mlp_norms = lamb_dense(
        mlp_w, mlp_m, mlp_v, grad_mlp * scale, step_float, 2 * NB
    )
    gain_new, gain_m_new, gain_v_new, gain_norms = lamb_dense(
        gain_w, gain_m, gain_v, grad_gain * scale, step_float, NB
    )
    matrix_norms = jnp.concatenate(
        [jnp.stack([weight_norm, dir_norm], 1), encdec_norms, mlp_norms, gain_norms], 0
    )
    return (
        loss_value,
        grad_norm,
        matrix_norms,
        spec_new,
        spec_m_new,
        spec_v_new,
        spec_new.astype(jnp.bfloat16),
        encdec_new,
        encdec_m_new,
        encdec_v_new,
        encdec_new.astype(jnp.bfloat16),
        mlp_new,
        mlp_m_new,
        mlp_v_new,
        mlp_new.astype(jnp.bfloat16),
        gain_new,
        gain_m_new,
        gain_v_new,
        gain_new.astype(jnp.bfloat16),
    )


def local(mesh, *args):
    inputs, spec_w = args[0], args[5]
    lat = inputs.shape[2] * mesh.shape["lat"]
    fits = (
        dict(mesh.shape) == {"lat": 2, "ma": RANKS}
        and inputs.shape[0] == 2
        and lat == 2 * RANKS
        and spec_w.shape[1] * RANKS == L
    )
    return (special if fits else general)(*args)


def solution(mesh):
    placed = (
        P(None, "ma", "lat", None),
        P(None, None, "ma", "lat", None),
        P(None, "ma", "lat"),
        P(),
        P(),
        P(None, "ma", None, None, "lat"),
        P(None, "ma", None, None, "lat"),
        P(None, "ma", None, None, "lat"),
        P(),
        P(),
        P(),
        P(),
        P(),
        P(),
        P(),
        P(),
        P(),
    )
    return jax.shard_map(
        functools.partial(local, mesh),
        mesh=mesh,
        in_specs=placed,
        out_specs=(
            P(),
            P(),
            P(),
            P(None, "ma", None, None, "lat"),
            P(None, "ma", None, None, "lat"),
            P(None, "ma", None, None, "lat"),
            P(None, "ma", None, None, "lat"),
            P(),
            P(),
            P(),
            P(),
            P(),
            P(),
            P(),
            P(),
            P(),
            P(),
            P(),
            P(),
        ),
        check_vma=False,
    )
```

```python
import functools
import math

import jax
import jax.numpy as jnp
import ml_dtypes
import numpy as np
from jax import lax
from jax.experimental import pallas as pl
from jax.experimental.pallas import tpu as pltpu
from jax.sharding import PartitionSpec as P

E = 256
C = 73
L = 96
NB = 3
ROLL = 2


beta_first = 0.9
beta_second = 0.999
adam_eps = 1e-08
weight_decay = 0.01
learn_rate = 0.4
clip_norm = 0.05
norm_eps = 1e-05


def legendre(orders, angles):
    cosines = jnp.cos(angles)[None, :]
    sines = jnp.sin(angles)[None, :]
    order_col = orders[:, None]
    log_start = 0.5 * (
        jnp.log((2.0 * order_col + 1.0) / (4.0 * math.pi))
        + lax.lgamma(2.0 * order_col + 1.0)
        - 2.0 * lax.lgamma(order_col + 1.0)
        - order_col * math.log(4.0)
    ) + order_col * jnp.log(sines)
    starting = jnp.exp(log_start)

    def advance(carry, degree):
        previous, earlier = carry
        upper = jnp.maximum(degree * degree - order_col * order_col, 1.0)
        factor = jnp.sqrt(jnp.maximum(4.0 * degree * degree - 1.0, 1.0) / upper)
        lower = jnp.maximum((degree - 1.0) ** 2 - order_col * order_col, 0.0)
        shrink = jnp.sqrt(lower / jnp.maximum(4.0 * (degree - 1.0) ** 2 - 1.0, 1.0))
        stepped = factor * (cosines * previous - shrink * earlier)
        second = jnp.sqrt(2.0 * order_col + 3.0) * cosines * starting
        value = jnp.where(
            degree < order_col,
            0.0,
            jnp.where(
                degree == order_col, starting, jnp.where(degree == order_col + 1.0, second, stepped)
            ),
        )
        return ((value, previous), value)

    zero_rows = jnp.zeros_like(starting)
    unused, table = lax.scan(advance, (zero_rows, zero_rows), jnp.arange(L, dtype=jnp.float32))
    return table


def dft_tables(orders, count_lon):
    phases = orders[:, None] * jnp.arange(count_lon, dtype=jnp.int32)[None, :] % count_lon
    phase = phases.astype(jnp.float32) * (2.0 * math.pi / count_lon)
    cosines = jnp.cos(phase)
    sines = jnp.sin(phase)
    number = orders.shape[0]
    forward = jnp.stack([cosines, -sines], 1).reshape(2 * number, count_lon)
    factor = jnp.where(orders == 0, 1.0, 2.0)[:, None] / math.sqrt(2.0 * math.pi)
    inverse = jnp.stack([factor * cosines, -factor * sines], 1).reshape(2 * number, count_lon).T
    return (forward, inverse)


def adaptive(weight, first, second, grad, step_float):
    first_new = beta_first * first + (1.0 - beta_first) * grad
    second_new = beta_second * second + (1.0 - beta_second) * grad * grad
    direction = (
        first_new
        / (1.0 - beta_first**step_float)
        / (jnp.sqrt(second_new / (1.0 - beta_second**step_float)) + adam_eps)
        + weight_decay * weight
    )
    return (first_new, second_new, direction)


def lamb_dense(weight, first, second, grad, step_float, groups):
    first_new, second_new, direction = adaptive(weight, first, second, grad, step_float)
    flat_weight = weight.reshape(groups, -1)
    flat_dir = direction.reshape(groups, -1)
    weight_norm = jnp.sqrt(jnp.sum(flat_weight * flat_weight, 1))
    dir_norm = jnp.sqrt(jnp.sum(flat_dir * flat_dir, 1))
    trust = weight_norm / (dir_norm + 1e-06)
    new_weight = (flat_weight - learn_rate * trust[:, None] * flat_dir).reshape(weight.shape)
    return (new_weight, first_new, second_new, jnp.stack([weight_norm, dir_norm], 1))


def norm_forward(hidden, gain_vec):
    centre = jnp.mean(hidden, -1, keepdims=True)
    centred = hidden - centre
    inv_std = lax.rsqrt(jnp.mean(centred * centred, -1, keepdims=True) + norm_eps)
    normal = centred * inv_std
    return ((normal * gain_vec).astype(jnp.bfloat16), normal, inv_std)


def norm_backward(d_normed, normal, inv_std, gain_vec):
    scaled = d_normed * gain_vec
    d_gain = jnp.sum(d_normed * normal, axis=(0, 1, 2))
    d_hidden = inv_std * (
        scaled
        - jnp.mean(scaled, -1, keepdims=True)
        - normal * jnp.mean(scaled * normal, -1, keepdims=True)
    )
    return (d_hidden, d_gain)


def mlp_forward(merged, weights):
    merged_low = merged.astype(jnp.bfloat16)
    pre_act = jnp.einsum(
        "jibe,ef->jibf", merged_low, weights[0], preferred_element_type=jnp.float32
    )
    gelu_out = jax.nn.gelu(pre_act).astype(jnp.bfloat16)
    hidden = merged + jnp.einsum(
        "jibf,ef->jibe", gelu_out, weights[1], preferred_element_type=jnp.float32
    )
    return (hidden, (merged_low, pre_act, gelu_out))


def mlp_backward(d_hidden, stored, weights):
    merged_low, pre_act, gelu_out = stored
    d_branch = d_hidden.astype(jnp.bfloat16)
    d_gelu = jnp.einsum("jibe,ef->jibf", d_branch, weights[1], preferred_element_type=jnp.float32)
    unused, pullback = jax.vjp(jax.nn.gelu, pre_act)
    d_pre = pullback(d_gelu)[0].astype(jnp.bfloat16)
    grad_out = jnp.einsum("jibf,jibe->ef", gelu_out, d_branch, preferred_element_type=jnp.float32)
    grad_in = jnp.einsum("jibe,jibf->ef", merged_low, d_pre, preferred_element_type=jnp.float32)
    d_merged = d_hidden + jnp.einsum(
        "jibf,ef->jibe", d_pre, weights[0], preferred_element_type=jnp.float32
    )
    return (d_merged, jnp.stack([grad_in, grad_out], 0))


def general(
    inputs,
    targets,
    mask,
    var_weight,
    step_count,
    spec_w,
    spec_m,
    spec_v,
    encdec_w,
    encdec_m,
    encdec_v,
    mlp_w,
    mlp_m,
    mlp_v,
    gain_w,
    gain_m,
    gain_v,
):
    n_ma = lax.axis_size("ma")
    n_lat = lax.axis_size("lat")
    ma_pos = lax.axis_index("ma")
    lat_pos = lax.axis_index("lat")
    batch = inputs.shape[0]
    lon_loc = inputs.shape[1]
    lat_loc = inputs.shape[2]
    nlon_all = lon_loc * n_ma
    nlat_all = lat_loc * n_lat
    orders_loc = L // n_ma
    angles = (jnp.arange(nlat_all, dtype=jnp.float32) + 0.5) * (math.pi / nlat_all)
    local_orders = ma_pos * orders_loc + jnp.arange(orders_loc, dtype=jnp.int32)
    table = legendre(local_orders.astype(jnp.float32), angles)
    quadrature = jnp.sin(angles) * (math.sqrt(2.0 * math.pi) / nlon_all * math.pi / nlat_all)
    fwd_leg = (table * quadrature[None, None, :]).astype(jnp.bfloat16)
    inv_leg = table.astype(jnp.bfloat16)
    fwd_table, inv_table = dft_tables(jnp.arange(L, dtype=jnp.int32), nlon_all)
    fwd_four = fwd_table.astype(jnp.bfloat16)
    inv_four = inv_table.astype(jnp.bfloat16)
    fwd_back = fwd_four.T
    inv_back = inv_four.T
    sines = jnp.sin(angles)
    area = sines / jnp.mean(sines)
    area_rows = lax.dynamic_slice_in_dim(area, lat_pos * lat_loc, lat_loc)
    mask_grid = jnp.transpose(mask, (1, 2, 0)).astype(jnp.float32)
    pixel_weight = (
        area_rows[None, :, None, None]
        * var_weight.astype(jnp.float32)[None, None, None, :]
        * mask_grid[:, :, :, None]
    )
    grid_targets = jnp.transpose(targets, (0, 2, 3, 1, 4))
    denom = float(batch * nlon_all * nlat_all * C)

    def apply_table(table_full, block_in):
        whole_out = jnp.einsum(
            "ok,kibe->oibe",
            table_full,
            lax.all_to_all(block_in, "ma", split_axis=3, concat_axis=0, tiled=True),
            preferred_element_type=jnp.float32,
        )
        return lax.all_to_all(
            whole_out.astype(jnp.bfloat16), "ma", split_axis=0, concat_axis=3, tiled=True
        ).astype(whole_out.dtype)

    def spectral_backward(d_filtered, owned, weight_blk):
        d_rows = apply_table(inv_back, d_filtered.astype(jnp.bfloat16)).astype(jnp.bfloat16)
        d_spec = lax.all_to_all(d_rows, "lat", split_axis=3, concat_axis=1, tiled=True)
        out_width = d_spec.shape[3]
        d_mixed = jnp.einsum(
            "lmi,mpibo->lmpbo",
            inv_leg,
            d_spec.reshape(orders_loc, 2, nlat_all, batch, out_width),
            preferred_element_type=jnp.float32,
        ).astype(jnp.bfloat16)
        d_own = lax.all_to_all(d_mixed, "ma", split_axis=0, concat_axis=1, tiled=True)
        real_w = weight_blk[:, 0]
        imag_w = weight_blk[:, 1]
        d_real = d_own[:, :, 0]
        d_imag = d_own[:, :, 1]
        d_coef_real = jnp.einsum(
            "lmbo,leo->lmbe", d_real, real_w, preferred_element_type=jnp.float32
        ) + jnp.einsum("lmbo,leo->lmbe", d_imag, imag_w, preferred_element_type=jnp.float32)
        d_coef_imag = jnp.einsum(
            "lmbo,leo->lmbe", d_imag, real_w, preferred_element_type=jnp.float32
        ) - jnp.einsum("lmbo,leo->lmbe", d_real, imag_w, preferred_element_type=jnp.float32)
        grad_real = jnp.einsum(
            "lmbe,lmbo->leo", owned[:, :, 0], d_real, preferred_element_type=jnp.float32
        ) + jnp.einsum("lmbe,lmbo->leo", owned[:, :, 1], d_imag, preferred_element_type=jnp.float32)
        grad_imag = jnp.einsum(
            "lmbe,lmbo->leo", owned[:, :, 0], d_imag, preferred_element_type=jnp.float32
        ) - jnp.einsum("lmbe,lmbo->leo", owned[:, :, 1], d_real, preferred_element_type=jnp.float32)
        d_owned = jnp.stack([d_coef_real, d_coef_imag], 2)
        d_coeffs = lax.all_to_all(
            d_owned.astype(jnp.bfloat16), "ma", split_axis=1, concat_axis=0, tiled=True
        ).astype(d_owned.dtype)
        d_full = jnp.einsum(
            "lmi,lmpbe->mpibe",
            fwd_leg.astype(jnp.float32),
            d_coeffs,
            precision=lax.Precision.HIGHEST,
        ).reshape(2 * orders_loc, nlat_all, batch, E)
        d_spec_rows = lax.psum_scatter(
            d_full.astype(jnp.bfloat16), "lat", scatter_dimension=1, tiled=True
        )
        return (apply_table(fwd_back, d_spec_rows), jnp.stack([grad_real, grad_imag], 1))

    spec_bf = spec_w.astype(jnp.bfloat16)
    encdec_bf = encdec_w.astype(jnp.bfloat16)
    mlp_bf = mlp_w.astype(jnp.bfloat16)

    def model_backward(d_pred, stored):
        state_low, hidden_low, records = stored
        d_dec = d_pred.astype(jnp.bfloat16)
        grad_dec = jnp.einsum(
            "jibe,jibc->ce", hidden_low, d_dec, preferred_element_type=jnp.float32
        )
        d_hidden = jnp.einsum(
            "jibc,ce->jibe", d_dec, encdec_bf[1], preferred_element_type=jnp.float32
        )
        spec_grads = [None] * NB
        mlp_grads = [None] * NB
        gain_grads = [None] * NB
        for block_idx in reversed(range(NB)):
            normal, inv_std, owned, mlp_kept = records[block_idx]
            d_merged, mlp_grads[block_idx] = mlp_backward(d_hidden, mlp_kept, mlp_bf[block_idx])
            d_normed, spec_grads[block_idx] = spectral_backward(d_merged, owned, spec_bf[block_idx])
            d_norm_in, gain_grads[block_idx] = norm_backward(
                d_normed, normal, inv_std, gain_w[block_idx]
            )
            d_hidden = d_merged + d_norm_in
        d_enc = d_hidden.astype(jnp.bfloat16)
        grad_enc = jnp.einsum("jibc,jibe->ce", state_low, d_enc, preferred_element_type=jnp.float32)
        d_state = d_pred + jnp.einsum(
            "jibe,ce->jibc", d_enc, encdec_bf[0], preferred_element_type=jnp.float32
        )
        return (
            d_state,
            (
                jnp.stack([grad_enc, grad_dec], 0),
                jnp.stack(spec_grads, 0),
                jnp.stack(mlp_grads, 0),
                jnp.stack(gain_grads, 0),
            ),
        )

    state = jnp.transpose(inputs, (1, 2, 0, 3))
    history = []
    loss_part = jnp.zeros((), jnp.float32)
    for section_idx in range(ROLL):
        model_state_low = state.astype(jnp.bfloat16)
        hidden = jnp.einsum(
            "jibc,ce->jibe", model_state_low, encdec_bf[0], preferred_element_type=jnp.float32
        )
        model_records = []
        for model_block_idx in range(NB):
            model_normed, model_normal, model_inv_std = norm_forward(
                hidden, gain_w[model_block_idx]
            )
            spectral_weight_blk = spec_bf[model_block_idx]
            spec_rows = apply_table(fwd_four, model_normed).astype(jnp.bfloat16)
            piece = lax.all_gather(spec_rows, "lat", axis=1, tiled=True)
            row_width = piece.shape[1]
            paired = piece.reshape(orders_loc, 2, row_width, piece.shape[2], piece.shape[3])
            coeffs = jnp.einsum(
                "lmi,mpibe->lmpbe", fwd_leg, paired, preferred_element_type=jnp.float32
            ).astype(jnp.bfloat16)
            spectral_owned = lax.all_to_all(coeffs, "ma", split_axis=0, concat_axis=1, tiled=True)
            spectral_real_w = spectral_weight_blk[:, 0]
            spectral_imag_w = spectral_weight_blk[:, 1]
            mixed_real = jnp.einsum(
                "lmbe,leo->lmbo",
                spectral_owned[:, :, 0],
                spectral_real_w,
                preferred_element_type=jnp.float32,
            ) - jnp.einsum(
                "lmbe,leo->lmbo",
                spectral_owned[:, :, 1],
                spectral_imag_w,
                preferred_element_type=jnp.float32,
            )
            mixed_imag = jnp.einsum(
                "lmbe,leo->lmbo",
                spectral_owned[:, :, 0],
                spectral_imag_w,
                preferred_element_type=jnp.float32,
            ) + jnp.einsum(
                "lmbe,leo->lmbo",
                spectral_owned[:, :, 1],
                spectral_real_w,
                preferred_element_type=jnp.float32,
            )
            mixed_owned = jnp.stack([mixed_real, mixed_imag], 2).astype(jnp.bfloat16)
            mixed = lax.all_to_all(mixed_owned, "ma", split_axis=1, concat_axis=0, tiled=True)
            spec_out = jnp.einsum(
                "lmi,lmpbo->mpibo", inv_leg, mixed, preferred_element_type=jnp.float32
            )
            spec_out = spec_out.astype(jnp.bfloat16).reshape(
                2 * orders_loc, nlat_all, batch, mixed.shape[4]
            )
            rows_out = lax.all_to_all(spec_out, "lat", split_axis=1, concat_axis=3, tiled=True)
            filtered = apply_table(inv_four, rows_out)
            hidden, model_mlp_kept = mlp_forward(hidden + filtered, mlp_bf[model_block_idx])
            model_records.append((model_normal, model_inv_std, spectral_owned, model_mlp_kept))
        model_hidden_low = hidden.astype(jnp.bfloat16)
        prediction = state + jnp.einsum(
            "jibe,ce->jibc", model_hidden_low, encdec_bf[1], preferred_element_type=jnp.float32
        )
        prediction, stored = (prediction, (model_state_low, model_hidden_low, model_records))
        misfit = prediction - grid_targets[section_idx]
        loss_part = loss_part + jnp.sum(pixel_weight * misfit * misfit) / denom
        history.append((stored, misfit))
        state = prediction
    d_state = jnp.zeros_like(state)
    totals = None
    for section_idx in reversed(range(ROLL)):
        stored, misfit = history[section_idx]
        d_pred = 2.0 * pixel_weight * misfit / denom + d_state
        d_state, section_grads = model_backward(d_pred, stored)
        totals = section_grads if totals is None else jax.tree.map(jnp.add, totals, section_grads)
    grad_encdec, spec_grad, grad_mlp, grad_gain = totals
    grad_encdec, grad_mlp, grad_gain, loss_value, spec_square, weight_square = lax.psum(
        (
            grad_encdec,
            grad_mlp,
            grad_gain,
            loss_part,
            jnp.sum(spec_grad * spec_grad),
            jnp.sum(spec_w * spec_w, axis=(1, 2, 3, 4)),
        ),
        ("lat", "ma"),
    )
    total_square = (
        spec_square
        + jnp.sum(grad_encdec * grad_encdec)
        + jnp.sum(grad_mlp * grad_mlp)
        + jnp.sum(grad_gain * grad_gain)
    )
    grad_norm = jnp.sqrt(total_square)
    scale = clip_norm / jnp.maximum(grad_norm, clip_norm)
    step_float = step_count[0].astype(jnp.float32)
    spec_m_new, spec_v_new, direction = adaptive(
        spec_w, spec_m, spec_v, spec_grad * scale, step_float
    )
    dir_square = lax.psum(jnp.sum(direction * direction, axis=(1, 2, 3, 4)), ("lat", "ma"))
    weight_norm = jnp.sqrt(weight_square)
    dir_norm = jnp.sqrt(dir_square)
    trust = weight_norm / (dir_norm + 1e-06)
    spec_new = spec_w - learn_rate * trust[:, None, None, None, None] * direction
    encdec_new, encdec_m_new, encdec_v_new, encdec_norms = lamb_dense(
        encdec_w, encdec_m, encdec_v, grad_encdec * scale, step_float, 2
    )
    mlp_new, mlp_m_new, mlp_v_new, mlp_norms = lamb_dense(
        mlp_w, mlp_m, mlp_v, grad_mlp * scale, step_float, 2 * NB
    )
    gain_new, gain_m_new, gain_v_new, gain_norms = lamb_dense(
        gain_w, gain_m, gain_v, grad_gain * scale, step_float, NB
    )
    matrix_norms = jnp.concatenate(
        [jnp.stack([weight_norm, dir_norm], 1), encdec_norms, mlp_norms, gain_norms], 0
    )
    return (
        loss_value,
        grad_norm,
        matrix_norms,
        spec_new,
        spec_m_new,
        spec_v_new,
        spec_new.astype(jnp.bfloat16),
        encdec_new,
        encdec_m_new,
        encdec_v_new,
        encdec_new.astype(jnp.bfloat16),
        mlp_new,
        mlp_m_new,
        mlp_v_new,
        mlp_new.astype(jnp.bfloat16),
        gain_new,
        gain_m_new,
        gain_v_new,
        gain_new.astype(jnp.bfloat16),
    )


RANKS = 16
ORDS = L // RANKS
SLOTS = 8
F32 = jnp.float32
BF16 = jnp.bfloat16


def legendre_f64(nlat):
    theta = (np.arange(nlat) + 0.5) * (math.pi / nlat)
    cosines, sines = np.cos(theta), np.sin(theta)
    table = np.zeros((L, L, nlat))
    for m in range(L):
        log_start = 0.5 * (
            math.log((2.0 * m + 1.0) / (4.0 * math.pi))
            + math.lgamma(2.0 * m + 1.0)
            - 2.0 * math.lgamma(m + 1.0)
            - m * math.log(4.0)
        ) + m * np.log(sines)
        table[m, m] = np.exp(log_start)
        if m + 1 < L:
            table[m + 1, m] = math.sqrt(2.0 * m + 3.0) * cosines * table[m, m]
        for k in range(m + 2, L):
            factor = math.sqrt((4.0 * k * k - 1.0) / (k * k - m * m))
            shrink = math.sqrt(((k - 1.0) ** 2 - m * m) / (4.0 * (k - 1.0) ** 2 - 1.0))
            table[k, m] = factor * (cosines * table[k - 1, m] - shrink * table[k - 2, m])
    return table, sines


def low_np(array):
    return array.astype(np.float32).astype(ml_dtypes.bfloat16)


def slot_map():
    degree = np.full((RANKS, 3, SLOTS), -1)
    order = np.full((RANKS, SLOTS), -1)
    for d in range(RANKS):
        y, w, xc = d // 8, (d // 4) % 2, d % 4
        lo, hi = 4 * w + xc, 4 * (3 - w) + xc
        n_lo, n_hi = (6 * lo + 5) // RANKS + 1, (6 * hi + 5) // RANKS + 1
        for group, first, count in ((hi, 0, n_hi), (lo, SLOTS - n_lo, n_lo)):
            for r in range(count):
                order[d, first + r] = r
                for t in range(3):
                    degree[d, t, first + r] = 6 * group + 3 * y + t
    return degree, order


def make_tables(nlat, nlon):
    table, sines = legendre_f64(nlat)
    quadrature = sines * (math.sqrt(2.0 * math.pi) / nlon * math.pi / nlat)
    fwd_leg = np.asarray(low_np(table * quadrature[None, None, :]))
    inv_leg = np.asarray(low_np(table))
    degree, order = slot_map()
    shape = (RANKS, RANKS, 3, 2, SLOTS, RANKS, ORDS, 2, 2)
    fwd = np.zeros(shape, ml_dtypes.bfloat16)
    inv = np.zeros(shape, ml_dtypes.bfloat16)
    for g in range(RANKS):
        for d in range(RANKS):
            for slot in range(SLOTS):
                r = order[d, slot]
                if r < 0:
                    continue
                for t in range(3):
                    k, m = degree[d, t, slot], g + RANKS * r
                    for p in range(2):
                        fwd[g, d, t, p, slot, :, r, p, :] = fwd_leg[k, m].reshape(RANKS, 2)
                        inv[g, d, t, p, slot, :, r, p, :] = inv_leg[k, m].reshape(RANKS, 2)
    rows = RANKS * 3 * 2 * SLOTS
    cols = RANKS * ORDS * 2 * 2
    fwd = fwd.reshape(RANKS, rows, cols)
    inv = inv.reshape(RANKS, rows, cols)
    phase = 2.0 * math.pi * (np.arange(L)[:, None] * np.arange(nlon)[None, :] % nlon) / nlon
    scale = np.where(np.arange(L) == 0, 1.0, 2.0)[:, None] / math.sqrt(2.0 * math.pi)
    four = low_np(np.stack([np.cos(phase), -np.sin(phase)], 1))
    back = low_np(np.stack([scale * np.cos(phase), -scale * np.sin(phase)], 1))
    def wide(small):
        out = np.zeros((RANKS, ORDS, 2, 2, 2, nlon), ml_dtypes.bfloat16)
        ordered = small.reshape(ORDS, RANKS, 2, nlon).transpose(1, 0, 2, 3)
        for il in range(2):
            out[:, :, :, il, il, :] = ordered
        return out.reshape(cols, 2 * nlon)

    def turn(array):
        return np.ascontiguousarray(np.swapaxes(array, -1, -2))

    four, back = wide(four), wide(back)
    return (fwd, turn(inv), turn(fwd), inv), (four, turn(back), turn(four), back)


def place():
    ma = lax.axis_index("ma")
    y = lax.axis_index("lat")
    z = ma // 4
    zh = z // 2
    w = z + zh * (3 - 2 * z)
    return zh, y, w, 8 * y + 4 * w + ma % 4


def device_of(zh, q):
    w = (q // 4) % 2
    z = w + zh * (3 - 2 * w)
    return {"lat": q // 8, "ma": 4 * z + q % 4}


def nn(a, b):
    return lax.dot_general(a, b, (((1,), (0,)), ((), ())), preferred_element_type=F32)


def nt(a, b):
    return lax.dot_general(a, b, (((1,), (1,)), ((), ())), preferred_element_type=F32)


def tn(a, b):
    return lax.dot_general(a, b, (((0,), (0,)), ((), ())), preferred_element_type=F32)


def piece_of(kind, half, zh, y):
    return 2 - 2 * ((kind + zh) % 2) + (half + y) % 2


def weight_of(w_all, block, kind, t, part, zh, y):
    return jnp.concatenate(
        [w_all[block, piece_of(kind, half, zh, y), t, part] for half in range(2)], axis=1
    )


def hi_rows(w):
    slot = lax.broadcasted_iota(jnp.int32, (RANKS * 2 * SLOTS, 1), 0) % SLOTS
    return slot < 6 - w


GELU_A = math.sqrt(2.0 / math.pi)
GELU_B = 0.044715


def normal_of(hidden):
    centre = jnp.mean(hidden, -1, keepdims=True)
    centred = hidden - centre
    inv_std = lax.rsqrt(jnp.mean(centred * centred, -1, keepdims=True) + norm_eps)
    return centred * inv_std, inv_std


def rows_loop(total, step, body):
    def one(k, carry):
        body(pl.ds(pl.multiple_of(k * step, step), step))
        return carry

    lax.fori_loop(0, total // step, one, 0)


MESH = pl.DeviceIdType.MESH
LANES = 128
MASK_LANE = LANES - 1
VAR_ROW, FIRST_ROW, SECOND_ROW = 124, 123, 122


def greet_all(between=None):
    barrier = pltpu.get_barrier_semaphore()
    me = 2 * RANKS // 2 * lax.axis_index("lat") + lax.axis_index("ma")

    def greet(s, carry):
        other = (me + s) % (2 * RANKS)
        pl.semaphore_signal(
            barrier, inc=1, device_id={"lat": other // RANKS, "ma": other % RANKS}, device_id_type=MESH
        )
        return carry

    lax.fori_loop(1, 2 * RANKS, greet, 0)
    if between is not None:
        between()
    pl.semaphore_wait(barrier, 2 * RANKS - 1)


def remote(src, dst, send_sem, recv_sem, device):
    return pltpu.make_async_remote_copy(
        src_ref=src,
        dst_ref=dst,
        send_sem=send_sem,
        recv_sem=recv_sem,
        device_id=device,
        device_id_type=MESH,
    )


def bytes_wait(ref, sem):
    pltpu.make_async_copy(ref, ref, sem).wait()


def flip(value, bits, span):
    out, unit = 0, 1
    while unit < span:
        digit = (value // unit) % 2
        out = out + unit * (1 - digit if bits // unit % 2 else digit)
        unit *= 2
    return out


def peers_of(zh, q):
    ranks = [flip(q, s, RANKS) for s in range(RANKS - 1, 0, -1)]
    return [(d, device_of(zh, d)) for d in ranks]


def push_blocks(source_of, landing, send_sem, recv_sem, peers, q):
    for d, device in peers:
        remote(source_of(d), landing, send_sem, recv_sem, device).start()
    pltpu.make_async_copy(source_of(q), landing, recv_sem).start()


def exchange_start(send, recv, send_sem, recv_sem, peers, q):
    push_blocks(lambda d: send.at[d], recv.at[q], send_sem, recv_sem, peers, q)


def exchange_wait(send, recv, send_sem, recv_sem):
    bytes_wait(recv, recv_sem)
    bytes_wait(send.at[pl.ds(0, RANKS - 1)], send_sem)


def exchange(send, recv, send_sem, recv_sem, peers, q):
    exchange_start(send, recv, send_sem, recv_sem, peers, q)
    exchange_wait(send, recv, send_sem, recv_sem)


def lane_sums(array):
    return jnp.sum(array.reshape(-1, LANES), axis=0, keepdims=True)


def train(
    xb_chunks, x_chunks, t_chunks, spec_w, spec_m, spec_v, mlp_w, mlp_m, mlp_v, r0, r1, r2, r3, f0, f1, f2, f3,
    small, area,
    g_spec, g_mlp, g_small, scalars,
    pfx, pix, pfxt, pixt, ftx, itx, ftxt, itxt, w_all, mlp_bf, mlp_stage, code_bf,
    x_recv, goals, weight, x_low, misfit, d_state, h_all, hid_low, v_low, u_buf, dv_buf, dh_buf,
    n_send, s_recv, y_recv, w_send, b_recv, a_own, d_mix,
    dwf, dw_send, dw_recv, dw_own, dmlp, rs_send, rs_recv, mir_send, mir_recv, ag_src,
    d_small, d_gain, sm_send, sm_recv, sm_mir_send, sm_mir_recv, sm_src, scal, scal_recv,
    ml_buf, dirs, dirs_recv,
    load_sem, stage_sem, once_send, once_recv, w_send_sem, w_recv_sem, x_send, x_recv_sem,
    g_send_sem, g_recv_sem, rs_sem, mir_send_sem, mir_recv_sem, ag_send_sem, ag_recv_sem, sm_sem,
    lamb_sem, ml_sem,
):
    zh, y, w, q = place()
    peers = peers_of(zh, q)
    ma = lax.axis_index("ma")
    xc = ma % 4
    mirror_ma = 4 * (3 - ma // 4) + xc
    near, far, cross = {"lat": 1 - y, "ma": ma}, {"lat": y, "ma": mirror_ma}, {"lat": 1 - y, "ma": mirror_ma}
    pixels, chans = dh_buf.shape
    spectra = pix.shape[0]
    triples = pfx.shape[0]
    third = 3

    loads = [
        pltpu.make_async_copy(src.at[q], dst, load_sem.at[k])
        for k, (src, dst) in enumerate(((r0, pfx), (r1, pix), (r2, pfxt), (r3, pixt)))
    ] + [
        pltpu.make_async_copy(src, dst, load_sem.at[4 + k])
        for k, (src, dst) in enumerate(((f0, ftx), (f1, itx), (f2, ftxt), (f3, itxt)))
    ]
    stage = dwf

    class SpecLoad:
        def __init__(self, b):
            self.copies = [
                pltpu.make_async_copy(
                    spec_w.at[b, pl.ds(third * k, third)], stage.at[2 * (b % 2) + k], stage_sem.at[2 * b + k]
                )
                for k in range(2)
            ]

        def start(self):
            for copy in self.copies:
                copy.start()

        def wait(self):
            for copy in self.copies:
                copy.wait()

    spec_loads = [SpecLoad(b) for b in range(NB)]
    mlp_loads = [pltpu.make_async_copy(mlp_w.at[b], mlp_stage.at[b % 2], stage_sem.at[2 * NB + b]) for b in range(NB)]
    spec_loads[0].start()
    spec_loads[1].start()
    loads[4].start()
    scal[...] = jnp.zeros_like(scal)
    d_small[...] = jnp.zeros_like(d_small)
    d_gain[...] = jnp.zeros_like(d_gain)
    d_state[...] = jnp.zeros_like(d_state)
    dirs[...] = jnp.zeros_like(dirs)
    kept_rows = lax.broadcasted_iota(jnp.int32, (LANES, 1), 0) < C
    for k in range(2):
        code_bf[k] = jnp.where(kept_rows, small[k], 0.0).astype(BF16)

    def chunk_to(chunks, landing, sems):
        for bits in range(RANKS - 1, 0, -1):
            other = flip(ma, bits, RANKS)
            remote(chunks.at[other], landing, sems[0], sems[1], {"lat": y, "ma": other}).start()
        pltpu.make_async_copy(chunks.at[ma], landing, sems[1]).start()

    def weights_out(b, where, triple):
        source, piece, device = {
            "near": (dw_send, 1, near), "far": (w_all, 2, far), "cross": (dw_send, 3, cross)
        }[where]
        for t in triple:
            remote(source.at[b, 0, t], w_all.at[b, piece, t], w_send_sem.at[b], w_recv_sem.at[b], device).start()

    def cast_weights(b):
        spec_loads[b].wait()
        for t in range(third):
            for own, target in ((y, w_all.at[b, 0]), (1 - y, dw_send.at[b, 0])):
                value = stage[2 * (b % 2) + own, t]
                scal[2 + b : 3 + b] += lane_sums(value * value)
                target[t] = value.astype(BF16)
        if b + 2 < NB:
            spec_loads[b + 2].start()

    def first_weights():
        cast_weights(0)
        loads[0].start()
        mlp_loads[0].start()
        mlp_loads[1].start()
        for k in (1, 2, 3, 5, 6, 7):
            loads[k].start()

    greet_all(first_weights)
    chunk_to(xb_chunks, x_low.at[0, :, ma], (once_send.at[0], once_recv.at[0]))
    weights_out(0, "far", range(third))
    weights_out(0, "cross", range(third))
    weights_out(0, "near", range(third))
    for b in range(1, NB):
        cast_weights(b)
    for b in range(NB):
        mlp_loads[b].wait()
        mlp_bf[b] = mlp_stage[b % 2].astype(BF16)
        if b + 2 < NB:
            mlp_loads[b + 2].start()
    for copy in loads:
        copy.wait()
    share_rows = pl.ds(pl.multiple_of((q % (RANKS // 2)) * ml_buf.shape[2], ml_buf.shape[2]), ml_buf.shape[2])
    ml_loads = [
        pltpu.make_async_copy(array.at[b, q // (RANKS // 2), share_rows], ml_buf.at[k, b], ml_sem)
        for k, array in enumerate((mlp_w, mlp_m, mlp_v))
        for b in range(NB)
    ]
    for copy in ml_loads:
        copy.start()
    bytes_wait(x_low.at[0], once_recv.at[0])
    bytes_wait(xb_chunks.at[pl.ds(0, RANKS - 1)], once_send.at[0])

    hi = hi_rows(w)
    rows_mix = RANKS * 2 * SLOTS

    def mixed_by(source, product, block, t, part):
        return jnp.where(
            hi,
            product(source, weight_of(w_all, block, 0, t, part, zh, y)),
            product(source, weight_of(w_all, block, 1, t, part, zh, y)),
        ).reshape(RANKS, 2, SLOTS, chans)

    def narrow(value):
        return value.astype(BF16).reshape(n_send.shape)

    def broad(value):
        return value.astype(BF16).reshape(w_send.shape)

    def fwd_block(step, block):
        slot, idx = 4 * step + block, NB * step + block
        gain_row = small[0, pl.ds(LANES - NB + block, 1), :]

        def norm_rows(rows):
            normal, unused = normal_of(h_all[slot, rows, :])
            u_buf[rows, :] = (normal * gain_row).astype(BF16)

        rows_loop(pixels, 256, norm_rows)
        n_send[...] = narrow(nn(ftx[...], u_buf[...]))
        exchange_start(n_send, s_recv, x_send.at[0], x_recv_sem.at[0], peers, q)

        @pl.when(jnp.logical_and(step == 0, block > 0))
        def _():
            weights_out(block, "near", (2,))

        @pl.when(jnp.logical_and(step == 1, block == 0))
        def _():
            chunk_to(t_chunks.at[1], goals.at[1, :, ma], (once_send.at[2], once_recv.at[2]))

        exchange_wait(n_send, s_recv, x_send.at[0], x_recv_sem.at[0])
        w_send[...] = broad(nn(pfx[...], s_recv[...].reshape(spectra, chans)))
        exchange_start(w_send, a_own.at[idx], x_send.at[1], x_recv_sem.at[1], peers, q)

        @pl.when(jnp.logical_and(step == 0, block < NB - 1))
        def _():
            weights_out(block + 1, "far", (0, 1))

        @pl.when(jnp.logical_and(step == 0, block == NB - 1))
        def _():
            chunk_to(x_chunks, x_recv.at[:, ma], (once_send.at[3], once_recv.at[3]))
            chunk_to(t_chunks.at[0], goals.at[0, :, ma], (once_send.at[1], once_recv.at[1]))

        exchange_wait(w_send, a_own.at[idx], x_send.at[1], x_recv_sem.at[1])

        @pl.when(step == 0)
        def _():
            bytes_wait(w_all.at[block, pl.ds(1, 3)], w_recv_sem.at[block])

        for t in range(3):
            coef = a_own[idx, :, t].reshape(rows_mix, chans)
            by_real, by_imag = (mixed_by(coef, nn, block, t, part) for part in range(2))
            mixed = jnp.stack([by_real[:, 0] - by_imag[:, 1], by_real[:, 1] + by_imag[:, 0]], 1)
            w_send[:, t] = mixed.reshape(RANKS, 2 * SLOTS, chans).astype(BF16)
        exchange_start(w_send, b_recv, x_send.at[2], x_recv_sem.at[2], peers, q)

        @pl.when(jnp.logical_and(step == 0, block < NB - 1))
        def _():
            weights_out(block + 1, "far", (2,))
            weights_out(block + 1, "cross", (0,))
            weights_out(block + 1, "near", (0,))

        exchange_wait(w_send, b_recv, x_send.at[2], x_recv_sem.at[2])
        n_send[...] = narrow(nn(pix[...], b_recv[...].reshape(triples, chans)))
        exchange_start(n_send, y_recv, x_send.at[3], x_recv_sem.at[3], peers, q)

        @pl.when(jnp.logical_and(step == 0, block < NB - 1))
        def _():
            weights_out(block + 1, "cross", (1, 2))
            weights_out(block + 1, "near", (1,))

        exchange_wait(n_send, y_recv, x_send.at[3], x_recv_sem.at[3])
        spectrum = y_recv[...].reshape(spectra, chans)

        def mlp_rows(rows):
            merged = h_all[slot, rows, :] + nn(itx[rows, :], spectrum)
            merged_low = merged.astype(BF16)
            v_low[idx, rows, :] = merged_low
            pre = nn(merged_low, mlp_bf[block, 0])
            act = (0.5 * pre * (1.0 + jnp.tanh(GELU_A * (pre + GELU_B * pre * pre * pre)))).astype(BF16)
            h_all[slot + 1, rows, :] = merged + nt(act, mlp_bf[block, 1])

        rows_loop(pixels, 256, mlp_rows)

    denom = float(pixels * RANKS * C * 2)

    def fwd_step(step, carry):
        h_all[4 * step] = nn(x_low[step].reshape(pixels, LANES), code_bf[0])

        def one(block, inner):
            fwd_block(step, block)
            return inner

        lax.fori_loop(0, NB, one, 0)
        hidden_low = h_all[4 * step + 3].astype(BF16)
        hid_low[step] = hidden_low
        delta = nt(hidden_low, code_bf[1])

        @pl.when(step == 0)
        def _():
            bytes_wait(x_recv, once_recv.at[3])
            bytes_wait(x_chunks.at[pl.ds(0, RANKS - 1)], once_send.at[3])
            bytes_wait(goals.at[0], once_recv.at[1])
            bytes_wait(t_chunks.at[0, pl.ds(0, RANKS - 1)], once_send.at[1])
            for il in range(2):
                valid = goals[0, il].reshape(pixels // 2, LANES)[:, MASK_LANE:]
                rows = slice(il * pixels // 2, (il + 1) * pixels // 2)
                weight[rows, :] = valid * (area[q, il] * small[1, VAR_ROW : VAR_ROW + 1, :LANES])

        @pl.when(step == 1)
        def _():
            bytes_wait(goals.at[1], once_recv.at[2])
            bytes_wait(t_chunks.at[1, pl.ds(0, RANKS - 1)], once_send.at[2])

        prediction = x_recv[...].reshape(pixels, LANES) + delta
        x_recv[...] = prediction.reshape(x_recv.shape)

        @pl.when(step == 0)
        def _():
            x_low[1] = prediction.astype(BF16).reshape(x_low.shape[1:])

        miss = prediction - goals[step].reshape(pixels, LANES)
        weighted = weight[...] * miss
        scal[0:1] += lane_sums(weighted * miss / denom)
        misfit[step] = 2.0 * weighted / denom
        return carry

    lax.fori_loop(0, ROLL, fwd_step, 0)
    for b in range(NB):
        bytes_wait(w_all.at[b, pl.ds(1, 3)], w_send_sem.at[b])

    def settle(block):
        bytes_wait(dw_recv.at[block], g_recv_sem.at[block])
        for t in range(third):
            for own, one, two in (
                (y, dw_own[block, t], dw_recv[block, 1, t]),
                (1 - y, dw_recv[block, 0, t], dw_recv[block, 2, t]),
            ):
                total = one.astype(F32) + two.astype(F32)
                scal[1:2] += lane_sums(total * total)
                g_spec[block, third * own + t] = total

    def shares_start(block):
        rs_send[...] = dmlp[block].astype(BF16).reshape(rs_send.shape)
        exchange_start(rs_send, rs_recv, rs_sem.at[0], rs_sem.at[1], peers, q)

    def shares_finish(block):
        exchange_wait(rs_send, rs_recv, rs_sem.at[0], rs_sem.at[1])
        share = rs_recv[0].astype(F32)
        for k in range(1, RANKS):
            share = share + rs_recv[k].astype(F32)
        mir_send[block] = share
        remote(mir_send.at[block], mir_recv.at[block], mir_send_sem.at[block], mir_recv_sem.at[block], far).start()

    def shares_spread(block):
        bytes_wait(mir_recv.at[block], mir_recv_sem.at[block])
        total = mir_send[block] + mir_recv[block]
        scal[1:2] += 0.5 * lane_sums(total * total)
        ag_src[block] = total.astype(BF16)
        push_blocks(
            lambda d: ag_src.at[block], g_mlp.at[block, q], ag_send_sem.at[block], ag_recv_sem.at[block], peers, q
        )

    def grads_out(b, where, triple):
        piece, device = {"near": (0, near), "far": (1, far), "cross": (2, cross)}[where]
        for t in triple:
            remote(
                dw_send.at[b, piece, t], dw_recv.at[b, piece, t], g_send_sem.at[b], g_recv_sem.at[b], device
            ).start()

    def bwd_block(lap, step, block):
        early = jnp.logical_and(lap == 1, block > 0)
        later = jnp.logical_and(lap == 1, block < NB - 1)
        slot, idx = 4 * step + block, NB * step + block
        gain_row = small[0, pl.ds(LANES - NB + block, 1), :]

        @pl.when(lap == 0)
        def _():
            dmlp[block] = jnp.zeros(dmlp.shape[1:], F32)

        def mlp_rows(rows):
            d_hidden = dh_buf[rows, :]
            d_branch = d_hidden.astype(BF16)
            merged_low = v_low[idx, rows, :]
            pre = nn(merged_low, mlp_bf[block, 0])
            tan = jnp.tanh(GELU_A * (pre + GELU_B * pre * pre * pre))
            act = (0.5 * pre * (1.0 + tan)).astype(BF16)
            slope = 0.5 * (1.0 + tan) + 0.5 * pre * (1.0 - tan * tan) * (
                GELU_A * (1.0 + 3.0 * GELU_B * pre * pre)
            )
            d_pre = (nn(d_branch, mlp_bf[block, 1]) * slope).astype(BF16)
            dmlp[block, 0] += tn(merged_low, d_pre)
            dmlp[block, 1] += tn(d_branch, act)
            d_merged = d_hidden + nt(d_pre, mlp_bf[block, 0])
            dv_buf[rows, :] = d_merged
            u_buf[rows, :] = d_merged.astype(BF16)

        rows_loop(pixels, 256, mlp_rows)
        n_send[...] = narrow(nn(itxt[...], u_buf[...]))
        exchange_start(n_send, s_recv, x_send.at[4], x_recv_sem.at[4], peers, q)

        @pl.when(later)
        def _():
            grads_out(block + 1, "cross", (1,))
            grads_out(block + 1, "near", (1,))
            shares_finish(block + 1)

        exchange_wait(n_send, s_recv, x_send.at[4], x_recv_sem.at[4])
        w_send[...] = broad(nn(pixt[...], s_recv[...].reshape(spectra, chans)))
        which = NB * lap + block
        exchange_start(w_send, d_mix.at[which], x_send.at[5], x_recv_sem.at[5], peers, q)

        @pl.when(jnp.logical_and(lap == 1, block < NB - 1))
        def _():
            grads_out(block + 1, "cross", (2,))
            grads_out(block + 1, "near", (2,))

        exchange_wait(w_send, d_mix.at[which], x_send.at[5], x_recv_sem.at[5])

        def turned_of(d_mixed):
            wide = d_mixed.astype(F32).reshape(RANKS, 2, SLOTS, chans)
            return jnp.stack([wide[:, 1], -wide[:, 0]], 1).reshape(rows_mix, chans).astype(BF16)

        for t in range(3):
            d_mixed = d_mix[which, :, t].reshape(rows_mix, chans)
            by_real, by_imag = (mixed_by(d_mixed, nt, block, t, part) for part in range(2))
            d_coef = jnp.stack([by_real[:, 0] + by_imag[:, 1], by_real[:, 1] - by_imag[:, 0]], 1)
            w_send[:, t] = d_coef.reshape(RANKS, 2 * SLOTS, chans).astype(BF16)
        exchange_start(w_send, b_recv, x_send.at[6], x_recv_sem.at[6], peers, q)

        @pl.when(jnp.logical_and(lap == 1, block == 0))
        def _():
            shares_start(block)

        @pl.when(lap == 1)
        def _():
            for t in range(3):
                others = []
                for turn in range(ROLL):
                    d_mixed = d_mix[NB * turn + block, :, t].reshape(rows_mix, chans)
                    others.append((d_mixed, turned_of(d_mixed)))
                for kind in range(2):
                    keep = hi if kind == 0 else jnp.logical_not(hi)
                    kept = [
                        jnp.where(
                            keep, a_own[NB * (1 - turn) + block, :, t].reshape(rows_mix, chans).astype(F32), 0.0
                        ).astype(BF16)
                        for turn in range(ROLL)
                    ]
                    for part in range(2):
                        grad = tn(kept[0], others[0][part]) + tn(kept[1], others[1][part])
                        for half in range(2):
                            dwf[piece_of(kind, half, zh, y), t, part] = grad[
                                :, half * LANES : (half + 1) * LANES
                            ]
            dw_own[block] = dwf[0]
            for k in range(3):
                dw_send[block, k] = dwf[1 + k].astype(BF16)

            grads_out(block, "far", (0, 1))

        @pl.when(jnp.logical_and(lap == 1, block == 0))
        def _():
            grads_out(block, "far", (2,))

        exchange_wait(w_send, b_recv, x_send.at[6], x_recv_sem.at[6])
        n_send[...] = narrow(nn(pfxt[...], b_recv[...].reshape(triples, chans)))
        exchange_start(n_send, y_recv, x_send.at[7], x_recv_sem.at[7], peers, q)

        @pl.when(early)
        def _():
            grads_out(block, "far", (2,))
            grads_out(block, "cross", (0,))
            grads_out(block, "near", (0,))

        @pl.when(jnp.logical_and(lap == 1, block == 0))
        def _():
            grads_out(block, "near", range(third))

        exchange_wait(n_send, y_recv, x_send.at[7], x_recv_sem.at[7])

        @pl.when(early)
        def _():
            shares_start(block)

        @pl.when(jnp.logical_and(lap == 1, block == 0))
        def _():
            shares_finish(block)

        spectrum = y_recv[...].reshape(spectra, chans)

        def norm_rows(rows):
            normal, inv_std = normal_of(h_all[slot, rows, :])
            d_normed = nn(ftxt[rows, :], spectrum)
            scaled = d_normed * gain_row
            d_gain[block] += jnp.sum(d_normed * normal, axis=0, keepdims=True)
            d_norm_in = inv_std * (
                scaled
                - jnp.mean(scaled, -1, keepdims=True)
                - normal * jnp.mean(scaled * normal, -1, keepdims=True)
            )
            dh_buf[rows, :] = dv_buf[rows, :] + d_norm_in

        rows_loop(pixels, 256, norm_rows)

        @pl.when(jnp.logical_and(lap == 1, block < NB - 1))
        def _():
            settle(block + 1)

    def bwd_step(lap, carry):
        step = ROLL - 1 - lap
        d_pred = misfit[step] + d_state[...]
        d_dec = d_pred.astype(BF16)
        d_small[LANES:] += tn(d_dec, hid_low[step])
        dh_buf[...] = nn(d_dec, code_bf[1])

        def one(k, inner):
            bwd_block(lap, step, NB - 1 - k)
            return inner

        lax.fori_loop(0, NB, one, 0)
        d_enc = dh_buf[...].astype(BF16)
        d_small[:LANES] += tn(x_low[step].reshape(pixels, LANES), d_enc)

        @pl.when(lap == 0)
        def _():
            d_state[...] = d_pred + nt(d_enc, code_bf[0])

        return carry

    lax.fori_loop(0, ROLL, bwd_step, 0)

    for b in range(NB):
        d_small[LANES - NB + b : LANES - NB + b + 1] = d_gain[b]
    sm_send[...] = d_small[...].reshape(sm_send.shape)
    exchange_start(sm_send, sm_recv, sm_sem.at[0], sm_sem.at[1], peers, q)
    for b in range(NB - 1, 0, -1):
        shares_spread(b)
    exchange_wait(sm_send, sm_recv, sm_sem.at[0], sm_sem.at[1])
    share = sm_recv[0]
    for k in range(1, RANKS):
        share = share + sm_recv[k]
    sm_mir_send[...] = share
    swap = remote(sm_mir_send, sm_mir_recv, sm_sem.at[2], sm_sem.at[3], far)
    swap.start()
    grads_out(0, "cross", range(third))
    swap.wait()
    total = sm_mir_send[...] + sm_mir_recv[...]
    scal[1:2] += 0.5 * lane_sums(total * total)
    sm_src[...] = total
    push_blocks(lambda d: sm_src, g_small.at[q], sm_sem.at[4], sm_sem.at[5], peers, q)
    shares_spread(0)
    settle(0)

    me = RANKS * y + ma
    sets = ((dwf.at[0], dwf.at[1], dwf.at[2]), (dwf.at[3], dw_own.at[0], dw_own.at[1]))

    def unit_loads(u):
        part = pl.ds(third * (u % 2), third)
        return [
            pltpu.make_async_copy(array.at[u // 2, part], buffer, lamb_sem.at[u % 2, k])
            for k, (array, buffer) in enumerate(zip((spec_w, spec_m, spec_v), sets[u % 2]))
        ]

    for u in range(2):
        for copy in unit_loads(u):
            copy.start()

    def spread_start(value, landing, sems):
        def spread(s, carry):
            other = (me + s) % (2 * RANKS)
            remote(
                value, landing.at[me], sems[0], sems[1], {"lat": other // RANKS, "ma": other % RANKS}
            ).start()
            return carry

        lax.fori_loop(1, 2 * RANKS, spread, 0)
        pltpu.make_async_copy(value, landing.at[me], sems[1]).start()

    def spread_total(landing, sems):
        bytes_wait(landing, sems[1])
        bytes_wait(landing.at[pl.ds(0, 2 * RANKS - 1)], sems[0])
        total = landing[0]
        for k in range(1, 2 * RANKS):
            total = total + landing[k]
        return jnp.broadcast_to(jnp.sum(total, axis=1, keepdims=True), total.shape)

    first_sems, second_sems = (sm_sem.at[6], sm_sem.at[7]), (sm_sem.at[8], sm_sem.at[9])
    spread_start(scal, scal_recv, first_sems)
    for copy in ml_loads:
        copy.wait()
    total = spread_total(scal_recv, first_sems)
    scalars[:8] = total

    scale = clip_norm / jnp.maximum(jnp.sqrt(total[1:2, :1]), clip_norm)
    first_inv = 1.0 / small[1, FIRST_ROW : FIRST_ROW + 1, :1]
    second_inv = 1.0 / small[1, SECOND_ROW : SECOND_ROW + 1, :1]

    def direction_of(weight_old, first, second, grad):
        grad = grad * scale
        first_new = (beta_first * first + (1.0 - beta_first) * grad) * first_inv
        second_new = (beta_second * second + (1.0 - beta_second) * grad * grad) * second_inv
        return first_new / (jnp.sqrt(second_new) + adam_eps) + weight_decay * weight_old

    for u in range(2 * NB):
        for copy in unit_loads(u):
            copy.wait()
        w_buf, m_buf, v_buf = sets[u % 2]

        def one_degree(t, carry, u=u, w_buf=w_buf, m_buf=m_buf, v_buf=v_buf):
            for part in range(2):
                step_dir = direction_of(
                    w_buf[t, part], m_buf[t, part], v_buf[t, part], g_spec[u // 2, third * (u % 2) + t, part]
                )
                dirs[u // 2 : u // 2 + 1] += lane_sums(step_dir * step_dir)
            return carry

        lax.fori_loop(0, third, one_degree, 0)
        if u + 2 < 2 * NB:
            for copy in unit_loads(u + 2):
                copy.start()
    for b in range(NB):
        old = ml_buf[0, b]
        step_dir = direction_of(old, ml_buf[1, b], ml_buf[2, b], ag_src[b].astype(F32))
        row = NB + 2 * b + q // (RANKS // 2)
        for place_row, value in ((row, step_dir), (row + 2 * NB, old)):
            squares = value * value
            lanes = sum(squares[:, k * LANES : (k + 1) * LANES] for k in range(squares.shape[1] // LANES))
            dirs[pl.ds(place_row, 1), :] += 0.5 * jnp.sum(lanes, axis=0, keepdims=True)
    spread_start(dirs, dirs_recv, second_sems)

    bytes_wait(g_small, sm_sem.at[5])
    bytes_wait(g_small.at[pl.ds(0, RANKS - 1)], sm_sem.at[4])
    for b in range(NB):
        bytes_wait(g_mlp.at[b], ag_recv_sem.at[b])
        bytes_wait(g_mlp.at[b, pl.ds(0, RANKS - 1)], ag_send_sem.at[b])
        bytes_wait(mir_send.at[b], mir_send_sem.at[b])
        bytes_wait(dw_send.at[b], g_send_sem.at[b])
    scalars[8:] = spread_total(dirs_recv, second_sems)


def call_train(chunks, weights, tables, small_in, area):
    vmem = pltpu.VMEM
    dma = pltpu.SemaphoreType.DMA
    spec_w, mlp_w = weights[0], weights[3]
    lon = chunks[0].shape[2]
    pixels, chans = 2 * RANKS * lon, small_in.shape[-1]
    third = spec_w.shape[1] // 2
    triple = (third, 2, chans, LANES)
    narrow, wide = (RANKS, 4 * ORDS, chans), (RANKS, 3, 2 * SLOTS, chans)
    triples, spectra = RANKS * 6 * SLOTS, RANKS * 4 * ORDS
    mlp_shape = mlp_w.shape[1:]
    chunk = (mlp_shape[0] * mlp_shape[1] // RANKS, mlp_shape[2])
    small = (2 * LANES // RANKS, chans)
    b16 = lambda *shape: vmem(shape, BF16)
    f32 = lambda *shape: vmem(shape, F32)
    everywhere = pl.BlockSpec(memory_space=pl.ANY)
    inside = pl.BlockSpec(memory_space=vmem)
    return pl.pallas_call(
        train,
        out_shape=(
            jax.ShapeDtypeStruct(spec_w.shape, F32),
            jax.ShapeDtypeStruct((NB, RANKS, *chunk), BF16),
            jax.ShapeDtypeStruct((RANKS, *small), F32),
            jax.ShapeDtypeStruct((24, LANES), F32),
        ),
        in_specs=[everywhere] * 17 + [inside] * 2,
        out_specs=[inside] * 4,
        scratch_shapes=[
            b16(triples, spectra), b16(spectra, triples), b16(spectra, triples), b16(triples, spectra),
            b16(spectra, pixels), b16(pixels, spectra), b16(pixels, spectra), b16(spectra, pixels),
            b16(NB, 4, *triple), b16(*mlp_w.shape), f32(2, *mlp_shape),
            b16(*small_in.shape),
            f32(2, RANKS, lon, LANES), f32(ROLL, 2, RANKS, lon, LANES), f32(pixels, LANES), b16(ROLL, 2, RANKS, lon, LANES),
            f32(ROLL, pixels, LANES), f32(pixels, LANES), f32(4 * ROLL, pixels, chans), b16(ROLL, pixels, chans),
            b16(NB * ROLL, pixels, chans), b16(pixels, chans), f32(pixels, chans), f32(pixels, chans),
            b16(*narrow), b16(*narrow), b16(*narrow), b16(*wide), b16(*wide), b16(NB * ROLL, *wide), b16(NB * ROLL, *wide),
            f32(4, *triple), b16(NB, 3, *triple), b16(NB, 3, *triple), f32(NB, *triple), f32(NB, *mlp_shape),
            b16(RANKS, *chunk), b16(RANKS, *chunk), f32(NB, *chunk), f32(NB, *chunk), b16(NB, *chunk),
            f32(2 * LANES, chans), f32(NB, 1, chans), f32(RANKS, *small), f32(RANKS, *small), f32(*small), f32(*small),
            f32(*small), f32(8, LANES), f32(2 * RANKS, 8, LANES),
            f32(3, NB, *chunk), f32(16, LANES), f32(2 * RANKS, 16, LANES),
            dma((8,)), dma((3 * NB,)), dma((4,)), dma((4,)), dma((NB,)), dma((NB,)), dma((8,)), dma((8,)),
            dma((NB,)), dma((NB,)), dma((2,)), dma((NB,)), dma((NB,)), dma((NB,)), dma((NB,)), dma((10,)),
            dma((2, 3)), dma,
        ],
        compiler_params=pltpu.CompilerParams(
            collective_id=0, has_side_effects=True, vmem_limit_bytes=61 << 20
        ),
    )(*chunks, *weights, *tables, small_in, area)


def chunks_of(field):
    items, lon, lat, width = field.shape
    pairs = lat // 2
    chunks = jnp.moveaxis(field.reshape(items, lon, pairs, 2, width), 1, 3)
    return jnp.concatenate([chunks[0], jnp.roll(chunks[1], pairs // 2, 0)], 0)


def special(
    inputs,
    targets,
    mask,
    var_weight,
    step_count,
    spec_w,
    spec_m,
    spec_v,
    encdec_w,
    encdec_m,
    encdec_v,
    mlp_w,
    mlp_m,
    mlp_v,
    gain_w,
    gain_m,
    gain_v,
):
    zh, y, w, q = place()
    nlon = inputs.shape[1] * lax.axis_size("ma")
    nlat = inputs.shape[2] * lax.axis_size("lat")
    ranked, common = make_tables(nlat, nlon)
    tables = tuple(jnp.asarray(t) for t in (*ranked, *common))
    spare = LANES - C
    x_chunks = chunks_of(jnp.pad(inputs, ((0, 0),) * 3 + ((0, spare),)))
    masks = jnp.broadcast_to(mask.astype(F32)[None, ..., None], (*targets.shape[:-1], 1))
    goal = jnp.concatenate([targets, jnp.zeros((*targets.shape[:-1], spare - 1), F32), masks], -1)
    t_chunks = jnp.stack([chunks_of(goal[0]), chunks_of(goal[1])], 0)
    sines = np.sin((np.arange(nlat) + 0.5) * (math.pi / nlat))
    area = np.repeat((sines / np.mean(sines)).astype(np.float32).reshape(RANKS, 2, 1, 1), LANES, 3)
    step_float = step_count[0].astype(F32)
    fixes = jnp.stack([1.0 - beta_second**step_float, 1.0 - beta_first**step_float])
    var_row = jnp.pad(var_weight.astype(F32), (0, E - C))[None]
    small_in = jnp.stack(
        [
            jnp.concatenate([encdec_w[0], jnp.zeros((LANES - NB - C, E), F32), gain_w], 0),
            jnp.concatenate(
                [
                    encdec_w[1],
                    jnp.zeros((SECOND_ROW - C, E), F32),
                    jnp.broadcast_to(fixes[:, None], (2, E)),
                    var_row,
                    jnp.zeros((LANES - 1 - VAR_ROW, E), F32),
                ],
                0,
            ),
        ]
    )
    spec_grad, mlp_sum, small_sum, sums = call_train(
        (x_chunks.astype(BF16), x_chunks, t_chunks),
        (spec_w, spec_m, spec_v, mlp_w, mlp_m, mlp_v),
        tables,
        small_in,
        jnp.asarray(area),
    )
    grad_mlp = mlp_sum.reshape(mlp_w.shape).astype(F32)
    small_sum = small_sum.reshape(2, LANES, E)
    grad_encdec = small_sum[:, :C]
    grad_gain = small_sum[0, LANES - NB :]
    sums = sums[:, 0]
    loss_value = sums[0]
    weight_square = sums[2 : 2 + NB]
    grad_norm = jnp.sqrt(sums[1])
    scale = clip_norm / jnp.maximum(grad_norm, clip_norm)
    spec_m_new, spec_v_new, direction = adaptive(
        spec_w, spec_m, spec_v, spec_grad * scale, step_float
    )
    dir_square = sums[8 : 8 + NB]
    weight_norm = jnp.sqrt(weight_square)
    dir_norm = jnp.sqrt(dir_square)
    trust = weight_norm / (dir_norm + 1e-06)
    spec_new = spec_w - learn_rate * trust[:, None, None, None, None] * direction
    encdec_new, encdec_m_new, encdec_v_new, encdec_norms = lamb_dense(
        encdec_w, encdec_m, encdec_v, grad_encdec * scale, step_float, 2
    )
    mlp_m_new, mlp_v_new, mlp_dir = adaptive(mlp_w, mlp_m, mlp_v, grad_mlp * scale, step_float)
    mlp_dir_norm = jnp.sqrt(sums[8 + NB : 8 + 3 * NB])
    mlp_weight_norm = jnp.sqrt(sums[8 + 3 * NB : 8 + 5 * NB])
    mlp_trust = (mlp_weight_norm / (mlp_dir_norm + 1e-06)).reshape(NB, 2, 1, 1)
    mlp_new = mlp_w - learn_rate * mlp_trust * mlp_dir
    mlp_norms = jnp.stack([mlp_weight_norm, mlp_dir_norm], 1)
    gain_new, gain_m_new, gain_v_new, gain_norms = lamb_dense(
        gain_w, gain_m, gain_v, grad_gain * scale, step_float, NB
    )
    matrix_norms = jnp.concatenate(
        [jnp.stack([weight_norm, dir_norm], 1), encdec_norms, mlp_norms, gain_norms], 0
    )
    return (
        loss_value,
        grad_norm,
        matrix_norms,
        spec_new,
        spec_m_new,
        spec_v_new,
        spec_new.astype(jnp.bfloat16),
        encdec_new,
        encdec_m_new,
        encdec_v_new,
        encdec_new.astype(jnp.bfloat16),
        mlp_new,
        mlp_m_new,
        mlp_v_new,
        mlp_new.astype(jnp.bfloat16),
        gain_new,
        gain_m_new,
        gain_v_new,
        gain_new.astype(jnp.bfloat16),
    )


def local(mesh, *args):
    inputs, spec_w = args[0], args[5]
    lat = inputs.shape[2] * mesh.shape["lat"]
    fits = (
        dict(mesh.shape) == {"lat": 2, "ma": RANKS}
        and inputs.shape[0] == 2
        and lat == 2 * RANKS
        and spec_w.shape[1] * RANKS == L
    )
    return (special if fits else general)(*args)


def solution(mesh):
    placed = (
        P(None, "ma", "lat", None),
        P(None, None, "ma", "lat", None),
        P(None, "ma", "lat"),
        P(),
        P(),
        P(None, "ma", None, None, "lat"),
        P(None, "ma", None, None, "lat"),
        P(None, "ma", None, None, "lat"),
        P(),
        P(),
        P(),
        P(),
        P(),
        P(),
        P(),
        P(),
        P(),
    )
    return jax.shard_map(
        functools.partial(local, mesh),
        mesh=mesh,
        in_specs=placed,
        out_specs=(
            P(),
            P(),
            P(),
            P(None, "ma", None, None, "lat"),
            P(None, "ma", None, None, "lat"),
            P(None, "ma", None, None, "lat"),
            P(None, "ma", None, None, "lat"),
            P(),
            P(),
            P(),
            P(),
            P(),
            P(),
            P(),
            P(),
            P(),
            P(),
            P(),
            P(),
        ),
        check_vma=False,
    )
```

```python
import functools
import math

import jax
import jax.numpy as jnp
import ml_dtypes
import numpy as np
from jax import lax
from jax.experimental import pallas as pl
from jax.experimental.pallas import tpu as pltpu
from jax.sharding import PartitionSpec as P

E = 256
C = 73
L = 96
NB = 3
ROLL = 2


beta_first = 0.9
beta_second = 0.999
adam_eps = 1e-08
weight_decay = 0.01
learn_rate = 0.4
clip_norm = 0.05
norm_eps = 1e-05


def legendre(orders, angles):
    cosines = jnp.cos(angles)[None, :]
    sines = jnp.sin(angles)[None, :]
    order_col = orders[:, None]
    log_start = 0.5 * (
        jnp.log((2.0 * order_col + 1.0) / (4.0 * math.pi))
        + lax.lgamma(2.0 * order_col + 1.0)
        - 2.0 * lax.lgamma(order_col + 1.0)
        - order_col * math.log(4.0)
    ) + order_col * jnp.log(sines)
    starting = jnp.exp(log_start)

    def advance(carry, degree):
        previous, earlier = carry
        upper = jnp.maximum(degree * degree - order_col * order_col, 1.0)
        factor = jnp.sqrt(jnp.maximum(4.0 * degree * degree - 1.0, 1.0) / upper)
        lower = jnp.maximum((degree - 1.0) ** 2 - order_col * order_col, 0.0)
        shrink = jnp.sqrt(lower / jnp.maximum(4.0 * (degree - 1.0) ** 2 - 1.0, 1.0))
        stepped = factor * (cosines * previous - shrink * earlier)
        second = jnp.sqrt(2.0 * order_col + 3.0) * cosines * starting
        value = jnp.where(
            degree < order_col,
            0.0,
            jnp.where(
                degree == order_col, starting, jnp.where(degree == order_col + 1.0, second, stepped)
            ),
        )
        return ((value, previous), value)

    zero_rows = jnp.zeros_like(starting)
    unused, table = lax.scan(advance, (zero_rows, zero_rows), jnp.arange(L, dtype=jnp.float32))
    return table


def dft_tables(orders, count_lon):
    phases = orders[:, None] * jnp.arange(count_lon, dtype=jnp.int32)[None, :] % count_lon
    phase = phases.astype(jnp.float32) * (2.0 * math.pi / count_lon)
    cosines = jnp.cos(phase)
    sines = jnp.sin(phase)
    number = orders.shape[0]
    forward = jnp.stack([cosines, -sines], 1).reshape(2 * number, count_lon)
    factor = jnp.where(orders == 0, 1.0, 2.0)[:, None] / math.sqrt(2.0 * math.pi)
    inverse = jnp.stack([factor * cosines, -factor * sines], 1).reshape(2 * number, count_lon).T
    return (forward, inverse)


def adaptive(weight, first, second, grad, step_float):
    first_new = beta_first * first + (1.0 - beta_first) * grad
    second_new = beta_second * second + (1.0 - beta_second) * grad * grad
    direction = (
        first_new
        / (1.0 - beta_first**step_float)
        / (jnp.sqrt(second_new / (1.0 - beta_second**step_float)) + adam_eps)
        + weight_decay * weight
    )
    return (first_new, second_new, direction)


def lamb_dense(weight, first, second, grad, step_float, groups):
    first_new, second_new, direction = adaptive(weight, first, second, grad, step_float)
    flat_weight = weight.reshape(groups, -1)
    flat_dir = direction.reshape(groups, -1)
    weight_norm = jnp.sqrt(jnp.sum(flat_weight * flat_weight, 1))
    dir_norm = jnp.sqrt(jnp.sum(flat_dir * flat_dir, 1))
    trust = weight_norm / (dir_norm + 1e-06)
    new_weight = (flat_weight - learn_rate * trust[:, None] * flat_dir).reshape(weight.shape)
    return (new_weight, first_new, second_new, jnp.stack([weight_norm, dir_norm], 1))


def norm_forward(hidden, gain_vec):
    centre = jnp.mean(hidden, -1, keepdims=True)
    centred = hidden - centre
    inv_std = lax.rsqrt(jnp.mean(centred * centred, -1, keepdims=True) + norm_eps)
    normal = centred * inv_std
    return ((normal * gain_vec).astype(jnp.bfloat16), normal, inv_std)


def norm_backward(d_normed, normal, inv_std, gain_vec):
    scaled = d_normed * gain_vec
    d_gain = jnp.sum(d_normed * normal, axis=(0, 1, 2))
    d_hidden = inv_std * (
        scaled
        - jnp.mean(scaled, -1, keepdims=True)
        - normal * jnp.mean(scaled * normal, -1, keepdims=True)
    )
    return (d_hidden, d_gain)


def mlp_forward(merged, weights):
    merged_low = merged.astype(jnp.bfloat16)
    pre_act = jnp.einsum(
        "jibe,ef->jibf", merged_low, weights[0], preferred_element_type=jnp.float32
    )
    gelu_out = jax.nn.gelu(pre_act).astype(jnp.bfloat16)
    hidden = merged + jnp.einsum(
        "jibf,ef->jibe", gelu_out, weights[1], preferred_element_type=jnp.float32
    )
    return (hidden, (merged_low, pre_act, gelu_out))


def mlp_backward(d_hidden, stored, weights):
    merged_low, pre_act, gelu_out = stored
    d_branch = d_hidden.astype(jnp.bfloat16)
    d_gelu = jnp.einsum("jibe,ef->jibf", d_branch, weights[1], preferred_element_type=jnp.float32)
    unused, pullback = jax.vjp(jax.nn.gelu, pre_act)
    d_pre = pullback(d_gelu)[0].astype(jnp.bfloat16)
    grad_out = jnp.einsum("jibf,jibe->ef", gelu_out, d_branch, preferred_element_type=jnp.float32)
    grad_in = jnp.einsum("jibe,jibf->ef", merged_low, d_pre, preferred_element_type=jnp.float32)
    d_merged = d_hidden + jnp.einsum(
        "jibf,ef->jibe", d_pre, weights[0], preferred_element_type=jnp.float32
    )
    return (d_merged, jnp.stack([grad_in, grad_out], 0))


def general(
    inputs,
    targets,
    mask,
    var_weight,
    step_count,
    spec_w,
    spec_m,
    spec_v,
    encdec_w,
    encdec_m,
    encdec_v,
    mlp_w,
    mlp_m,
    mlp_v,
    gain_w,
    gain_m,
    gain_v,
):
    n_ma = lax.axis_size("ma")
    n_lat = lax.axis_size("lat")
    ma_pos = lax.axis_index("ma")
    lat_pos = lax.axis_index("lat")
    batch = inputs.shape[0]
    lon_loc = inputs.shape[1]
    lat_loc = inputs.shape[2]
    nlon_all = lon_loc * n_ma
    nlat_all = lat_loc * n_lat
    orders_loc = L // n_ma
    angles = (jnp.arange(nlat_all, dtype=jnp.float32) + 0.5) * (math.pi / nlat_all)
    local_orders = ma_pos * orders_loc + jnp.arange(orders_loc, dtype=jnp.int32)
    table = legendre(local_orders.astype(jnp.float32), angles)
    quadrature = jnp.sin(angles) * (math.sqrt(2.0 * math.pi) / nlon_all * math.pi / nlat_all)
    fwd_leg = (table * quadrature[None, None, :]).astype(jnp.bfloat16)
    inv_leg = table.astype(jnp.bfloat16)
    fwd_table, inv_table = dft_tables(jnp.arange(L, dtype=jnp.int32), nlon_all)
    fwd_four = fwd_table.astype(jnp.bfloat16)
    inv_four = inv_table.astype(jnp.bfloat16)
    fwd_back = fwd_four.T
    inv_back = inv_four.T
    sines = jnp.sin(angles)
    area = sines / jnp.mean(sines)
    area_rows = lax.dynamic_slice_in_dim(area, lat_pos * lat_loc, lat_loc)
    mask_grid = jnp.transpose(mask, (1, 2, 0)).astype(jnp.float32)
    pixel_weight = (
        area_rows[None, :, None, None]
        * var_weight.astype(jnp.float32)[None, None, None, :]
        * mask_grid[:, :, :, None]
    )
    grid_targets = jnp.transpose(targets, (0, 2, 3, 1, 4))
    denom = float(batch * nlon_all * nlat_all * C)

    def apply_table(table_full, block_in):
        whole_out = jnp.einsum(
            "ok,kibe->oibe",
            table_full,
            lax.all_to_all(block_in, "ma", split_axis=3, concat_axis=0, tiled=True),
            preferred_element_type=jnp.float32,
        )
        return lax.all_to_all(
            whole_out.astype(jnp.bfloat16), "ma", split_axis=0, concat_axis=3, tiled=True
        ).astype(whole_out.dtype)

    def spectral_backward(d_filtered, owned, weight_blk):
        d_rows = apply_table(inv_back, d_filtered.astype(jnp.bfloat16)).astype(jnp.bfloat16)
        d_spec = lax.all_to_all(d_rows, "lat", split_axis=3, concat_axis=1, tiled=True)
        out_width = d_spec.shape[3]
        d_mixed = jnp.einsum(
            "lmi,mpibo->lmpbo",
            inv_leg,
            d_spec.reshape(orders_loc, 2, nlat_all, batch, out_width),
            preferred_element_type=jnp.float32,
        ).astype(jnp.bfloat16)
        d_own = lax.all_to_all(d_mixed, "ma", split_axis=0, concat_axis=1, tiled=True)
        real_w = weight_blk[:, 0]
        imag_w = weight_blk[:, 1]
        d_real = d_own[:, :, 0]
        d_imag = d_own[:, :, 1]
        d_coef_real = jnp.einsum(
            "lmbo,leo->lmbe", d_real, real_w, preferred_element_type=jnp.float32
        ) + jnp.einsum("lmbo,leo->lmbe", d_imag, imag_w, preferred_element_type=jnp.float32)
        d_coef_imag = jnp.einsum(
            "lmbo,leo->lmbe", d_imag, real_w, preferred_element_type=jnp.float32
        ) - jnp.einsum("lmbo,leo->lmbe", d_real, imag_w, preferred_element_type=jnp.float32)
        grad_real = jnp.einsum(
            "lmbe,lmbo->leo", owned[:, :, 0], d_real, preferred_element_type=jnp.float32
        ) + jnp.einsum("lmbe,lmbo->leo", owned[:, :, 1], d_imag, preferred_element_type=jnp.float32)
        grad_imag = jnp.einsum(
            "lmbe,lmbo->leo", owned[:, :, 0], d_imag, preferred_element_type=jnp.float32
        ) - jnp.einsum("lmbe,lmbo->leo", owned[:, :, 1], d_real, preferred_element_type=jnp.float32)
        d_owned = jnp.stack([d_coef_real, d_coef_imag], 2)
        d_coeffs = lax.all_to_all(
            d_owned.astype(jnp.bfloat16), "ma", split_axis=1, concat_axis=0, tiled=True
        ).astype(d_owned.dtype)
        d_full = jnp.einsum(
            "lmi,lmpbe->mpibe",
            fwd_leg.astype(jnp.float32),
            d_coeffs,
            precision=lax.Precision.HIGHEST,
        ).reshape(2 * orders_loc, nlat_all, batch, E)
        d_spec_rows = lax.psum_scatter(
            d_full.astype(jnp.bfloat16), "lat", scatter_dimension=1, tiled=True
        )
        return (apply_table(fwd_back, d_spec_rows), jnp.stack([grad_real, grad_imag], 1))

    spec_bf = spec_w.astype(jnp.bfloat16)
    encdec_bf = encdec_w.astype(jnp.bfloat16)
    mlp_bf = mlp_w.astype(jnp.bfloat16)

    def model_backward(d_pred, stored):
        state_low, hidden_low, records = stored
        d_dec = d_pred.astype(jnp.bfloat16)
        grad_dec = jnp.einsum(
            "jibe,jibc->ce", hidden_low, d_dec, preferred_element_type=jnp.float32
        )
        d_hidden = jnp.einsum(
            "jibc,ce->jibe", d_dec, encdec_bf[1], preferred_element_type=jnp.float32
        )
        spec_grads = [None] * NB
        mlp_grads = [None] * NB
        gain_grads = [None] * NB
        for block_idx in reversed(range(NB)):
            normal, inv_std, owned, mlp_kept = records[block_idx]
            d_merged, mlp_grads[block_idx] = mlp_backward(d_hidden, mlp_kept, mlp_bf[block_idx])
            d_normed, spec_grads[block_idx] = spectral_backward(d_merged, owned, spec_bf[block_idx])
            d_norm_in, gain_grads[block_idx] = norm_backward(
                d_normed, normal, inv_std, gain_w[block_idx]
            )
            d_hidden = d_merged + d_norm_in
        d_enc = d_hidden.astype(jnp.bfloat16)
        grad_enc = jnp.einsum("jibc,jibe->ce", state_low, d_enc, preferred_element_type=jnp.float32)
        d_state = d_pred + jnp.einsum(
            "jibe,ce->jibc", d_enc, encdec_bf[0], preferred_element_type=jnp.float32
        )
        return (
            d_state,
            (
                jnp.stack([grad_enc, grad_dec], 0),
                jnp.stack(spec_grads, 0),
                jnp.stack(mlp_grads, 0),
                jnp.stack(gain_grads, 0),
            ),
        )

    state = jnp.transpose(inputs, (1, 2, 0, 3))
    history = []
    loss_part = jnp.zeros((), jnp.float32)
    for section_idx in range(ROLL):
        model_state_low = state.astype(jnp.bfloat16)
        hidden = jnp.einsum(
            "jibc,ce->jibe", model_state_low, encdec_bf[0], preferred_element_type=jnp.float32
        )
        model_records = []
        for model_block_idx in range(NB):
            model_normed, model_normal, model_inv_std = norm_forward(
                hidden, gain_w[model_block_idx]
            )
            spectral_weight_blk = spec_bf[model_block_idx]
            spec_rows = apply_table(fwd_four, model_normed).astype(jnp.bfloat16)
            piece = lax.all_gather(spec_rows, "lat", axis=1, tiled=True)
            row_width = piece.shape[1]
            paired = piece.reshape(orders_loc, 2, row_width, piece.shape[2], piece.shape[3])
            coeffs = jnp.einsum(
                "lmi,mpibe->lmpbe", fwd_leg, paired, preferred_element_type=jnp.float32
            ).astype(jnp.bfloat16)
            spectral_owned = lax.all_to_all(coeffs, "ma", split_axis=0, concat_axis=1, tiled=True)
            spectral_real_w = spectral_weight_blk[:, 0]
            spectral_imag_w = spectral_weight_blk[:, 1]
            mixed_real = jnp.einsum(
                "lmbe,leo->lmbo",
                spectral_owned[:, :, 0],
                spectral_real_w,
                preferred_element_type=jnp.float32,
            ) - jnp.einsum(
                "lmbe,leo->lmbo",
                spectral_owned[:, :, 1],
                spectral_imag_w,
                preferred_element_type=jnp.float32,
            )
            mixed_imag = jnp.einsum(
                "lmbe,leo->lmbo",
                spectral_owned[:, :, 0],
                spectral_imag_w,
                preferred_element_type=jnp.float32,
            ) + jnp.einsum(
                "lmbe,leo->lmbo",
                spectral_owned[:, :, 1],
                spectral_real_w,
                preferred_element_type=jnp.float32,
            )
            mixed_owned = jnp.stack([mixed_real, mixed_imag], 2).astype(jnp.bfloat16)
            mixed = lax.all_to_all(mixed_owned, "ma", split_axis=1, concat_axis=0, tiled=True)
            spec_out = jnp.einsum(
                "lmi,lmpbo->mpibo", inv_leg, mixed, preferred_element_type=jnp.float32
            )
            spec_out = spec_out.astype(jnp.bfloat16).reshape(
                2 * orders_loc, nlat_all, batch, mixed.shape[4]
            )
            rows_out = lax.all_to_all(spec_out, "lat", split_axis=1, concat_axis=3, tiled=True)
            filtered = apply_table(inv_four, rows_out)
            hidden, model_mlp_kept = mlp_forward(hidden + filtered, mlp_bf[model_block_idx])
            model_records.append((model_normal, model_inv_std, spectral_owned, model_mlp_kept))
        model_hidden_low = hidden.astype(jnp.bfloat16)
        prediction = state + jnp.einsum(
            "jibe,ce->jibc", model_hidden_low, encdec_bf[1], preferred_element_type=jnp.float32
        )
        prediction, stored = (prediction, (model_state_low, model_hidden_low, model_records))
        misfit = prediction - grid_targets[section_idx]
        loss_part = loss_part + jnp.sum(pixel_weight * misfit * misfit) / denom
        history.append((stored, misfit))
        state = prediction
    d_state = jnp.zeros_like(state)
    totals = None
    for section_idx in reversed(range(ROLL)):
        stored, misfit = history[section_idx]
        d_pred = 2.0 * pixel_weight * misfit / denom + d_state
        d_state, section_grads = model_backward(d_pred, stored)
        totals = section_grads if totals is None else jax.tree.map(jnp.add, totals, section_grads)
    grad_encdec, spec_grad, grad_mlp, grad_gain = totals
    grad_encdec, grad_mlp, grad_gain, loss_value, spec_square, weight_square = lax.psum(
        (
            grad_encdec,
            grad_mlp,
            grad_gain,
            loss_part,
            jnp.sum(spec_grad * spec_grad),
            jnp.sum(spec_w * spec_w, axis=(1, 2, 3, 4)),
        ),
        ("lat", "ma"),
    )
    total_square = (
        spec_square
        + jnp.sum(grad_encdec * grad_encdec)
        + jnp.sum(grad_mlp * grad_mlp)
        + jnp.sum(grad_gain * grad_gain)
    )
    grad_norm = jnp.sqrt(total_square)
    scale = clip_norm / jnp.maximum(grad_norm, clip_norm)
    step_float = step_count[0].astype(jnp.float32)
    spec_m_new, spec_v_new, direction = adaptive(
        spec_w, spec_m, spec_v, spec_grad * scale, step_float
    )
    dir_square = lax.psum(jnp.sum(direction * direction, axis=(1, 2, 3, 4)), ("lat", "ma"))
    weight_norm = jnp.sqrt(weight_square)
    dir_norm = jnp.sqrt(dir_square)
    trust = weight_norm / (dir_norm + 1e-06)
    spec_new = spec_w - learn_rate * trust[:, None, None, None, None] * direction
    encdec_new, encdec_m_new, encdec_v_new, encdec_norms = lamb_dense(
        encdec_w, encdec_m, encdec_v, grad_encdec * scale, step_float, 2
    )
    mlp_new, mlp_m_new, mlp_v_new, mlp_norms = lamb_dense(
        mlp_w, mlp_m, mlp_v, grad_mlp * scale, step_float, 2 * NB
    )
    gain_new, gain_m_new, gain_v_new, gain_norms = lamb_dense(
        gain_w, gain_m, gain_v, grad_gain * scale, step_float, NB
    )
    matrix_norms = jnp.concatenate(
        [jnp.stack([weight_norm, dir_norm], 1), encdec_norms, mlp_norms, gain_norms], 0
    )
    return (
        loss_value,
        grad_norm,
        matrix_norms,
        spec_new,
        spec_m_new,
        spec_v_new,
        spec_new.astype(jnp.bfloat16),
        encdec_new,
        encdec_m_new,
        encdec_v_new,
        encdec_new.astype(jnp.bfloat16),
        mlp_new,
        mlp_m_new,
        mlp_v_new,
        mlp_new.astype(jnp.bfloat16),
        gain_new,
        gain_m_new,
        gain_v_new,
        gain_new.astype(jnp.bfloat16),
    )


RANKS = 16
ORDS = L // RANKS
SLOTS = 8
F32 = jnp.float32
BF16 = jnp.bfloat16


def legendre_f64(nlat):
    theta = (np.arange(nlat) + 0.5) * (math.pi / nlat)
    cosines, sines = np.cos(theta), np.sin(theta)
    table = np.zeros((L, L, nlat))
    for m in range(L):
        log_start = 0.5 * (
            math.log((2.0 * m + 1.0) / (4.0 * math.pi))
            + math.lgamma(2.0 * m + 1.0)
            - 2.0 * math.lgamma(m + 1.0)
            - m * math.log(4.0)
        ) + m * np.log(sines)
        table[m, m] = np.exp(log_start)
        if m + 1 < L:
            table[m + 1, m] = math.sqrt(2.0 * m + 3.0) * cosines * table[m, m]
        for k in range(m + 2, L):
            factor = math.sqrt((4.0 * k * k - 1.0) / (k * k - m * m))
            shrink = math.sqrt(((k - 1.0) ** 2 - m * m) / (4.0 * (k - 1.0) ** 2 - 1.0))
            table[k, m] = factor * (cosines * table[k - 1, m] - shrink * table[k - 2, m])
    return table, sines


def low_np(array):
    return array.astype(np.float32).astype(ml_dtypes.bfloat16)


def slot_map():
    degree = np.full((RANKS, 3, SLOTS), -1)
    order = np.full((RANKS, SLOTS), -1)
    for d in range(RANKS):
        y, w, xc = d // 8, (d // 4) % 2, d % 4
        lo, hi = 4 * w + xc, 4 * (3 - w) + xc
        n_lo, n_hi = (6 * lo + 5) // RANKS + 1, (6 * hi + 5) // RANKS + 1
        for group, first, count in ((hi, 0, n_hi), (lo, SLOTS - n_lo, n_lo)):
            for r in range(count):
                order[d, first + r] = r
                for t in range(3):
                    degree[d, t, first + r] = 6 * group + 3 * y + t
    return degree, order


def make_tables(nlat, nlon):
    table, sines = legendre_f64(nlat)
    quadrature = sines * (math.sqrt(2.0 * math.pi) / nlon * math.pi / nlat)
    fwd_leg = np.asarray(low_np(table * quadrature[None, None, :]))
    inv_leg = np.asarray(low_np(table))
    degree, order = slot_map()
    shape = (RANKS, RANKS, 3, 2, SLOTS, RANKS, ORDS, 2, 2)
    fwd = np.zeros(shape, ml_dtypes.bfloat16)
    inv = np.zeros(shape, ml_dtypes.bfloat16)
    for g in range(RANKS):
        for d in range(RANKS):
            for slot in range(SLOTS):
                r = order[d, slot]
                if r < 0:
                    continue
                for t in range(3):
                    k, m = degree[d, t, slot], g + RANKS * r
                    for p in range(2):
                        fwd[g, d, t, p, slot, :, r, p, :] = fwd_leg[k, m].reshape(RANKS, 2)
                        inv[g, d, t, p, slot, :, r, p, :] = inv_leg[k, m].reshape(RANKS, 2)
    rows = RANKS * 3 * 2 * SLOTS
    cols = RANKS * ORDS * 2 * 2
    fwd = fwd.reshape(RANKS, rows, cols)
    inv = inv.reshape(RANKS, rows, cols)
    phase = 2.0 * math.pi * (np.arange(L)[:, None] * np.arange(nlon)[None, :] % nlon) / nlon
    scale = np.where(np.arange(L) == 0, 1.0, 2.0)[:, None] / math.sqrt(2.0 * math.pi)
    four = low_np(np.stack([np.cos(phase), -np.sin(phase)], 1))
    back = low_np(np.stack([scale * np.cos(phase), -scale * np.sin(phase)], 1))
    def wide(small):
        out = np.zeros((RANKS, ORDS, 2, 2, 2, nlon), ml_dtypes.bfloat16)
        ordered = small.reshape(ORDS, RANKS, 2, nlon).transpose(1, 0, 2, 3)
        for il in range(2):
            out[:, :, :, il, il, :] = ordered
        return out.reshape(cols, 2 * nlon)

    def turn(array):
        return np.ascontiguousarray(np.swapaxes(array, -1, -2))

    four, back = wide(four), wide(back)
    return (fwd, turn(inv), turn(fwd), inv), (four, turn(back), turn(four), back)


def place():
    ma = lax.axis_index("ma")
    y = lax.axis_index("lat")
    z = ma // 4
    zh = z // 2
    w = z + zh * (3 - 2 * z)
    return zh, y, w, 8 * y + 4 * w + ma % 4


def device_of(zh, q):
    w = (q // 4) % 2
    z = w + zh * (3 - 2 * w)
    return {"lat": q // 8, "ma": 4 * z + q % 4}


def nn(a, b):
    return lax.dot_general(a, b, (((1,), (0,)), ((), ())), preferred_element_type=F32)


def nt(a, b):
    return lax.dot_general(a, b, (((1,), (1,)), ((), ())), preferred_element_type=F32)


def tn(a, b):
    return lax.dot_general(a, b, (((0,), (0,)), ((), ())), preferred_element_type=F32)


def piece_of(kind, half, zh, y):
    return 2 - 2 * ((kind + zh) % 2) + (half + y) % 2


def weight_of(w_all, block, kind, t, part, zh, y):
    return jnp.concatenate(
        [w_all[block, piece_of(kind, half, zh, y), t, part] for half in range(2)], axis=1
    )


def hi_rows(w):
    slot = lax.broadcasted_iota(jnp.int32, (RANKS * 2 * SLOTS, 1), 0) % SLOTS
    return slot < 6 - w


GELU_A = math.sqrt(2.0 / math.pi)
GELU_B = 0.044715


def normal_of(hidden):
    centre = jnp.mean(hidden, -1, keepdims=True)
    centred = hidden - centre
    inv_std = lax.rsqrt(jnp.mean(centred * centred, -1, keepdims=True) + norm_eps)
    return centred * inv_std, inv_std


def rows_loop(total, step, body):
    def one(k, carry):
        body(pl.ds(pl.multiple_of(k * step, step), step))
        return carry

    lax.fori_loop(0, total // step, one, 0)


MESH = pl.DeviceIdType.MESH
LANES = 128
MASK_LANE = LANES - 1
VAR_ROW, FIRST_ROW, SECOND_ROW = 124, 123, 122


def greet_all(between=None):
    barrier = pltpu.get_barrier_semaphore()
    me = 2 * RANKS // 2 * lax.axis_index("lat") + lax.axis_index("ma")

    def greet(s, carry):
        other = (me + s) % (2 * RANKS)
        pl.semaphore_signal(
            barrier, inc=1, device_id={"lat": other // RANKS, "ma": other % RANKS}, device_id_type=MESH
        )
        return carry

    lax.fori_loop(1, 2 * RANKS, greet, 0)
    if between is not None:
        between()
    pl.semaphore_wait(barrier, 2 * RANKS - 1)


def remote(src, dst, send_sem, recv_sem, device):
    return pltpu.make_async_remote_copy(
        src_ref=src,
        dst_ref=dst,
        send_sem=send_sem,
        recv_sem=recv_sem,
        device_id=device,
        device_id_type=MESH,
    )


def bytes_wait(ref, sem):
    pltpu.make_async_copy(ref, ref, sem).wait()


def flip(value, bits, span):
    out, unit = 0, 1
    while unit < span:
        digit = (value // unit) % 2
        out = out + unit * (1 - digit if bits // unit % 2 else digit)
        unit *= 2
    return out


def peers_of(zh, q):
    ranks = [flip(q, s, RANKS) for s in range(RANKS - 1, 0, -1)]
    return [(d, device_of(zh, d)) for d in ranks]


def push_blocks(source_of, landing, send_sem, recv_sem, peers, q):
    for d, device in peers:
        remote(source_of(d), landing, send_sem, recv_sem, device).start()
    pltpu.make_async_copy(source_of(q), landing, recv_sem).start()


def exchange_start(send, recv, send_sem, recv_sem, peers, q):
    push_blocks(lambda d: send.at[d], recv.at[q], send_sem, recv_sem, peers, q)


def exchange_wait(send, recv, send_sem, recv_sem):
    bytes_wait(recv, recv_sem)
    bytes_wait(send.at[pl.ds(0, RANKS - 1)], send_sem)


def exchange(send, recv, send_sem, recv_sem, peers, q):
    exchange_start(send, recv, send_sem, recv_sem, peers, q)
    exchange_wait(send, recv, send_sem, recv_sem)


def lane_sums(array):
    return jnp.sum(array.reshape(-1, LANES), axis=0, keepdims=True)


def train(
    xb_chunks, x_chunks, t_chunks, spec_w, spec_m, spec_v, mlp_w, mlp_m, mlp_v, r0, r1, r2, r3, f0, f1, f2, f3,
    small, area,
    g_spec, g_mlp, g_small, scalars,
    pfx, pix, pfxt, pixt, ftx, itx, ftxt, itxt, w_all, mlp_bf, mlp_stage, code_bf,
    x_recv, goals, weight, x_low, misfit, d_state, h_all, hid_low, v_low, u_buf, dv_buf, dh_buf,
    n_send, s_recv, y_recv, w_send, b_recv, a_own, d_mix,
    dwf, dw_send, dw_recv, dw_own, dmlp, rs_send, rs_recv, mir_send, mir_recv, ag_src,
    d_small, d_gain, sm_send, sm_recv, sm_mir_send, sm_mir_recv, sm_src, scal, scal_recv,
    ml_buf, dirs, dirs_recv,
    load_sem, stage_sem, once_send, once_recv, w_send_sem, w_recv_sem, x_send, x_recv_sem,
    g_send_sem, g_recv_sem, rs_sem, mir_send_sem, mir_recv_sem, ag_send_sem, ag_recv_sem, sm_sem,
    lamb_sem, ml_sem,
):
    zh, y, w, q = place()
    peers = peers_of(zh, q)
    ma = lax.axis_index("ma")
    xc = ma % 4
    mirror_ma = 4 * (3 - ma // 4) + xc
    near, far, cross = {"lat": 1 - y, "ma": ma}, {"lat": y, "ma": mirror_ma}, {"lat": 1 - y, "ma": mirror_ma}
    pixels, chans = dh_buf.shape
    spectra = pix.shape[0]
    triples = pfx.shape[0]
    third = 3

    loads = [
        pltpu.make_async_copy(src.at[q], dst, load_sem.at[k])
        for k, (src, dst) in enumerate(((r0, pfx), (r1, pix), (r2, pfxt), (r3, pixt)))
    ] + [
        pltpu.make_async_copy(src, dst, load_sem.at[4 + k])
        for k, (src, dst) in enumerate(((f0, ftx), (f1, itx), (f2, ftxt), (f3, itxt)))
    ]
    stage = dwf

    class SpecLoad:
        def __init__(self, b):
            self.copies = [
                pltpu.make_async_copy(
                    spec_w.at[b, pl.ds(third * k, third)], stage.at[2 * (b % 2) + k], stage_sem.at[2 * b + k]
                )
                for k in range(2)
            ]

        def start(self):
            for copy in self.copies:
                copy.start()

        def wait(self):
            for copy in self.copies:
                copy.wait()

    spec_loads = [SpecLoad(b) for b in range(NB)]
    mlp_loads = [pltpu.make_async_copy(mlp_w.at[b], mlp_stage.at[b % 2], stage_sem.at[2 * NB + b]) for b in range(NB)]
    spec_loads[0].start()
    spec_loads[1].start()
    loads[4].start()
    scal[...] = jnp.zeros_like(scal)
    d_small[...] = jnp.zeros_like(d_small)
    d_gain[...] = jnp.zeros_like(d_gain)
    d_state[...] = jnp.zeros_like(d_state)
    dirs[...] = jnp.zeros_like(dirs)
    kept_rows = lax.broadcasted_iota(jnp.int32, (LANES, 1), 0) < C
    for k in range(2):
        code_bf[k] = jnp.where(kept_rows, small[k], 0.0).astype(BF16)

    def chunk_to(chunks, landing, sems):
        for bits in range(RANKS - 1, 0, -1):
            other = flip(ma, bits, RANKS)
            remote(chunks.at[other], landing, sems[0], sems[1], {"lat": y, "ma": other}).start()
        pltpu.make_async_copy(chunks.at[ma], landing, sems[1]).start()

    def weights_out(b, where, triple):
        source, piece, device = {
            "near": (dw_send, 1, near), "far": (w_all, 2, far), "cross": (dw_send, 3, cross)
        }[where]
        for t in triple:
            remote(source.at[b, 0, t], w_all.at[b, piece, t], w_send_sem.at[b], w_recv_sem.at[b], device).start()

    def cast_weights(b):
        spec_loads[b].wait()
        for t in range(third):
            for own, target in ((y, w_all.at[b, 0]), (1 - y, dw_send.at[b, 0])):
                value = stage[2 * (b % 2) + own, t]
                scal[2 + b : 3 + b] += lane_sums(value * value)
                target[t] = value.astype(BF16)
        if b + 2 < NB:
            spec_loads[b + 2].start()

    def first_weights():
        cast_weights(0)
        loads[0].start()
        mlp_loads[0].start()
        mlp_loads[1].start()
        for k in (1, 2, 3, 5, 6, 7):
            loads[k].start()

    greet_all(first_weights)
    chunk_to(xb_chunks, x_low.at[0, :, ma], (once_send.at[0], once_recv.at[0]))
    weights_out(0, "far", range(third))
    weights_out(0, "cross", range(third))
    weights_out(0, "near", range(third))
    for b in range(1, NB):
        cast_weights(b)
    for b in range(NB):
        mlp_loads[b].wait()
        mlp_bf[b] = mlp_stage[b % 2].astype(BF16)
        if b + 2 < NB:
            mlp_loads[b + 2].start()
    for copy in loads:
        copy.wait()
    share_rows = pl.ds(pl.multiple_of((q % (RANKS // 2)) * ml_buf.shape[2], ml_buf.shape[2]), ml_buf.shape[2])
    ml_loads = [
        pltpu.make_async_copy(array.at[b, q // (RANKS // 2), share_rows], ml_buf.at[k, b], ml_sem)
        for k, array in enumerate((mlp_w, mlp_m, mlp_v))
        for b in range(NB)
    ]
    for copy in ml_loads:
        copy.start()
    bytes_wait(x_low.at[0], once_recv.at[0])
    bytes_wait(xb_chunks.at[pl.ds(0, RANKS - 1)], once_send.at[0])

    hi = hi_rows(w)
    rows_mix = RANKS * 2 * SLOTS

    halves = range(2)

    def cols(half):
        return slice(half * LANES, (half + 1) * LANES)

    def narrow(value):
        return value.astype(BF16).reshape(n_send.shape[1:])

    def broad(value):
        return value.astype(BF16).reshape(w_send.shape[1:])

    def go(phase, half, send, recv):
        exchange_start(send, recv, x_send.at[phase, half], x_recv_sem.at[phase, half], peers, q)

    def come(phase, half, send, recv):
        exchange_wait(send, recv, x_send.at[phase, half], x_recv_sem.at[phase, half])

    def whole(ref, rows):
        return jnp.concatenate([ref[half].reshape(rows, LANES) for half in halves], axis=1)

    def rows_of(ref, t):
        return jnp.concatenate([ref[half, :, t].reshape(rows_mix, LANES) for half in halves], axis=1)

    def swapped(product):
        wide = product.reshape(RANKS, 2, SLOTS, 2 * LANES)
        return wide[..., :LANES], wide[..., LANES:]

    def fwd_block(step, block):
        slot, idx = 4 * step + block, NB * step + block
        gain_row = small[0, pl.ds(LANES - NB + block, 1), :]

        def norm_rows(rows):
            normal, unused = normal_of(h_all[slot, rows, :])
            u_buf[rows, :] = (normal * gain_row).astype(BF16)

        rows_loop(pixels, 256, norm_rows)
        for half in halves:
            n_send[half] = narrow(nn(ftx[...], u_buf[:, cols(half)]))
            go(0, half, n_send.at[half], s_recv.at[half])

        @pl.when(jnp.logical_and(step == 0, block > 0))
        def _():
            weights_out(block, "cross", (2,))
            weights_out(block, "near", (2,))

        @pl.when(jnp.logical_and(step == 1, block == 0))
        def _():
            chunk_to(t_chunks.at[1], goals.at[1, :, ma], (once_send.at[2], once_recv.at[2]))

        for half in halves:
            come(0, half, n_send.at[half], s_recv.at[half])
            w_send[half] = broad(nn(pfx[...], s_recv[half].reshape(spectra, LANES)))
            go(1, half, w_send.at[half], a_own.at[idx, half])

        @pl.when(jnp.logical_and(step == 0, block < NB - 1))
        def _():
            weights_out(block + 1, "far", (0,))

        @pl.when(jnp.logical_and(step == 0, block == NB - 1))
        def _():
            chunk_to(x_chunks, x_recv.at[:, ma], (once_send.at[3], once_recv.at[3]))
            chunk_to(t_chunks.at[0], goals.at[0, :, ma], (once_send.at[1], once_recv.at[1]))

        for half in halves:
            come(1, half, w_send.at[half], a_own.at[idx, half])

        @pl.when(step == 0)
        def _():
            bytes_wait(w_all.at[block, pl.ds(1, 3)], w_recv_sem.at[block])

        for half in halves:
            for t in range(3):
                coef = rows_of(a_own.at[idx], t)

                def mixed_by(kind):
                    piece = piece_of(kind, half, zh, y)
                    return nn(coef, jnp.concatenate([w_all[block, piece, t, 0], w_all[block, piece, t, 1]], axis=1))

                by_real, by_imag = swapped(jnp.where(hi, mixed_by(0), mixed_by(1)))
                mixed = jnp.stack([by_real[:, 0] - by_imag[:, 1], by_real[:, 1] + by_imag[:, 0]], 1)
                w_send[half, :, t] = mixed.reshape(RANKS, 2 * SLOTS, LANES).astype(BF16)
            go(2, half, w_send.at[half], b_recv.at[half])

        @pl.when(jnp.logical_and(step == 0, block < NB - 1))
        def _():
            weights_out(block + 1, "far", (1,))
            weights_out(block + 1, "near", (0,))

        for half in halves:
            come(2, half, w_send.at[half], b_recv.at[half])
            n_send[half] = narrow(nn(pix[...], b_recv[half].reshape(triples, LANES)))
            go(3, half, n_send.at[half], y_recv.at[half])

        @pl.when(jnp.logical_and(step == 0, block < NB - 1))
        def _():
            weights_out(block + 1, "far", (2,))
            weights_out(block + 1, "cross", (0, 1))
            weights_out(block + 1, "near", (1,))

        for half in halves:
            come(3, half, n_send.at[half], y_recv.at[half])
        spectrum = whole(y_recv, spectra)

        def mlp_rows(rows):
            merged = h_all[slot, rows, :] + nn(itx[rows, :], spectrum)
            merged_low = merged.astype(BF16)
            v_low[idx, rows, :] = merged_low
            pre = nn(merged_low, mlp_bf[block, 0])
            act = (0.5 * pre * (1.0 + jnp.tanh(GELU_A * (pre + GELU_B * pre * pre * pre)))).astype(BF16)
            h_all[slot + 1, rows, :] = merged + nt(act, mlp_bf[block, 1])

        rows_loop(pixels, 256, mlp_rows)

    denom = float(pixels * RANKS * C * 2)

    def fwd_step(step, carry):
        h_all[4 * step] = nn(x_low[step].reshape(pixels, LANES), code_bf[0])

        def one(block, inner):
            fwd_block(step, block)
            return inner

        lax.fori_loop(0, NB, one, 0)
        hidden_low = h_all[4 * step + 3].astype(BF16)
        hid_low[step] = hidden_low
        delta = nt(hidden_low, code_bf[1])

        @pl.when(step == 0)
        def _():
            bytes_wait(x_recv, once_recv.at[3])
            bytes_wait(x_chunks.at[pl.ds(0, RANKS - 1)], once_send.at[3])
            bytes_wait(goals.at[0], once_recv.at[1])
            bytes_wait(t_chunks.at[0, pl.ds(0, RANKS - 1)], once_send.at[1])
            for il in range(2):
                valid = goals[0, il].reshape(pixels // 2, LANES)[:, MASK_LANE:]
                rows = slice(il * pixels // 2, (il + 1) * pixels // 2)
                weight[rows, :] = valid * (area[q, il] * small[1, VAR_ROW : VAR_ROW + 1, :LANES])

        @pl.when(step == 1)
        def _():
            bytes_wait(goals.at[1], once_recv.at[2])
            bytes_wait(t_chunks.at[1, pl.ds(0, RANKS - 1)], once_send.at[2])

        prediction = x_recv[...].reshape(pixels, LANES) + delta
        x_recv[...] = prediction.reshape(x_recv.shape)

        @pl.when(step == 0)
        def _():
            x_low[1] = prediction.astype(BF16).reshape(x_low.shape[1:])

        miss = prediction - goals[step].reshape(pixels, LANES)
        weighted = weight[...] * miss
        scal[0:1] += lane_sums(weighted * miss / denom)
        misfit[step] = 2.0 * weighted / denom
        return carry

    lax.fori_loop(0, ROLL, fwd_step, 0)
    for b in range(NB):
        bytes_wait(w_all.at[b, pl.ds(1, 3)], w_send_sem.at[b])

    def settle(block):
        bytes_wait(dw_recv.at[block], g_recv_sem.at[block])
        for t in range(third):
            for own, one, two in (
                (y, dw_own[block, t], dw_recv[block, 1, t]),
                (1 - y, dw_recv[block, 0, t], dw_recv[block, 2, t]),
            ):
                total = one.astype(F32) + two.astype(F32)
                scal[1:2] += lane_sums(total * total)
                g_spec[block, third * own + t] = total

    def shares_start(block):
        rs_send[...] = dmlp[block].astype(BF16).reshape(rs_send.shape)
        exchange_start(rs_send, rs_recv, rs_sem.at[0], rs_sem.at[1], peers, q)

    def shares_finish(block):
        exchange_wait(rs_send, rs_recv, rs_sem.at[0], rs_sem.at[1])
        share = rs_recv[0].astype(F32)
        for k in range(1, RANKS):
            share = share + rs_recv[k].astype(F32)
        mir_send[block] = share
        remote(mir_send.at[block], mir_recv.at[block], mir_send_sem.at[block], mir_recv_sem.at[block], far).start()

    def shares_spread(block):
        bytes_wait(mir_recv.at[block], mir_recv_sem.at[block])
        total = mir_send[block] + mir_recv[block]
        scal[1:2] += 0.5 * lane_sums(total * total)
        ag_src[block] = total.astype(BF16)
        push_blocks(
            lambda d: ag_src.at[block], g_mlp.at[block, q], ag_send_sem.at[block], ag_recv_sem.at[block], peers, q
        )

    def grads_out(b, where, triple):
        piece, device = {"near": (0, near), "far": (1, far), "cross": (2, cross)}[where]
        for t in triple:
            remote(
                dw_send.at[b, piece, t], dw_recv.at[b, piece, t], g_send_sem.at[b], g_recv_sem.at[b], device
            ).start()

    def bwd_block(lap, step, block):
        early = jnp.logical_and(lap == 1, block > 0)
        later = jnp.logical_and(lap == 1, block < NB - 1)
        slot, idx = 4 * step + block, NB * step + block
        gain_row = small[0, pl.ds(LANES - NB + block, 1), :]

        @pl.when(lap == 0)
        def _():
            dmlp[block] = jnp.zeros(dmlp.shape[1:], F32)

        def mlp_rows(rows):
            d_hidden = dh_buf[rows, :]
            d_branch = d_hidden.astype(BF16)
            merged_low = v_low[idx, rows, :]
            pre = nn(merged_low, mlp_bf[block, 0])
            tan = jnp.tanh(GELU_A * (pre + GELU_B * pre * pre * pre))
            act = (0.5 * pre * (1.0 + tan)).astype(BF16)
            slope = 0.5 * (1.0 + tan) + 0.5 * pre * (1.0 - tan * tan) * (
                GELU_A * (1.0 + 3.0 * GELU_B * pre * pre)
            )
            d_pre = (nn(d_branch, mlp_bf[block, 1]) * slope).astype(BF16)
            dmlp[block, 0] += tn(merged_low, d_pre)
            dmlp[block, 1] += tn(d_branch, act)
            d_merged = d_hidden + nt(d_pre, mlp_bf[block, 0])
            dv_buf[rows, :] = d_merged
            u_buf[rows, :] = d_merged.astype(BF16)

        rows_loop(pixels, 256, mlp_rows)
        for half in halves:
            n_send[half] = narrow(nn(itxt[...], u_buf[:, cols(half)]))
            go(4, half, n_send.at[half], s_recv.at[half])

        @pl.when(later)
        def _():
            grads_out(block + 1, "cross", (1,))
            shares_finish(block + 1)

        which = NB * lap + block
        for half in halves:
            come(4, half, n_send.at[half], s_recv.at[half])
            w_send[half] = broad(nn(pixt[...], s_recv[half].reshape(spectra, LANES)))
            go(5, half, w_send.at[half], d_mix.at[which, half])

        @pl.when(later)
        def _():
            grads_out(block + 1, "cross", (2,))
            grads_out(block + 1, "near", (2,))

        for half in halves:
            come(5, half, w_send.at[half], d_mix.at[which, half])

        def turned_of(d_mixed):
            wide = d_mixed.astype(F32).reshape(RANKS, 2, SLOTS, chans)
            return jnp.stack([wide[:, 1], -wide[:, 0]], 1).reshape(rows_mix, chans).astype(BF16)

        for half in halves:
            for t in range(3):
                d_mixed = rows_of(d_mix.at[which], t)

                def mixed_by(kind):
                    parts = [
                        jnp.concatenate(
                            [w_all[block, piece_of(kind, k, zh, y), t, part, cols(half), :] for k in halves], axis=1
                        )
                        for part in range(2)
                    ]
                    return nt(d_mixed, jnp.concatenate(parts, axis=0))

                by_real, by_imag = swapped(jnp.where(hi, mixed_by(0), mixed_by(1)))
                d_coef = jnp.stack([by_real[:, 0] + by_imag[:, 1], by_real[:, 1] - by_imag[:, 0]], 1)
                w_send[half, :, t] = d_coef.reshape(RANKS, 2 * SLOTS, LANES).astype(BF16)
            go(6, half, w_send.at[half], b_recv.at[half])

        @pl.when(jnp.logical_and(lap == 1, block == 0))
        def _():
            shares_start(block)

        @pl.when(lap == 1)
        def _():
            for t in range(3):
                others = []
                for turn in range(ROLL):
                    d_mixed = rows_of(d_mix.at[NB * turn + block], t)
                    others.append((d_mixed, turned_of(d_mixed)))
                for kind in range(2):
                    keep = hi if kind == 0 else jnp.logical_not(hi)
                    kept = [
                        jnp.where(
                            keep, rows_of(a_own.at[NB * (1 - turn) + block], t).astype(F32), 0.0
                        ).astype(BF16)
                        for turn in range(ROLL)
                    ]
                    for part in range(2):
                        grad = tn(kept[0], others[0][part]) + tn(kept[1], others[1][part])
                        for half in range(2):
                            dwf[piece_of(kind, half, zh, y), t, part] = grad[
                                :, half * LANES : (half + 1) * LANES
                            ]
            dw_own[block] = dwf[0]
            for k in range(3):
                dw_send[block, k] = dwf[1 + k].astype(BF16)

            grads_out(block, "far", (0,))

        @pl.when(jnp.logical_and(lap == 1, block == 0))
        def _():
            grads_out(block, "far", (1, 2))

        for half in halves:
            come(6, half, w_send.at[half], b_recv.at[half])
            n_send[half] = narrow(nn(pfxt[...], b_recv[half].reshape(triples, LANES)))
            go(7, half, n_send.at[half], y_recv.at[half])

        @pl.when(early)
        def _():
            grads_out(block, "far", (1, 2))
            grads_out(block, "cross", (0,))
            grads_out(block, "near", (0, 1))

        @pl.when(jnp.logical_and(lap == 1, block == 0))
        def _():
            grads_out(block, "near", range(third))

        for half in halves:
            come(7, half, n_send.at[half], y_recv.at[half])

        @pl.when(early)
        def _():
            shares_start(block)

        @pl.when(jnp.logical_and(lap == 1, block == 0))
        def _():
            shares_finish(block)

        spectrum = whole(y_recv, spectra)

        def norm_rows(rows):
            normal, inv_std = normal_of(h_all[slot, rows, :])
            d_normed = nn(ftxt[rows, :], spectrum)
            scaled = d_normed * gain_row
            d_gain[block] += jnp.sum(d_normed * normal, axis=0, keepdims=True)
            d_norm_in = inv_std * (
                scaled
                - jnp.mean(scaled, -1, keepdims=True)
                - normal * jnp.mean(scaled * normal, -1, keepdims=True)
            )
            dh_buf[rows, :] = dv_buf[rows, :] + d_norm_in

        rows_loop(pixels, 256, norm_rows)

        @pl.when(jnp.logical_and(lap == 1, block < NB - 1))
        def _():
            settle(block + 1)

    def bwd_step(lap, carry):
        step = ROLL - 1 - lap
        d_pred = misfit[step] + d_state[...]
        d_dec = d_pred.astype(BF16)
        d_small[LANES:] += tn(d_dec, hid_low[step])
        dh_buf[...] = nn(d_dec, code_bf[1])

        def one(k, inner):
            bwd_block(lap, step, NB - 1 - k)
            return inner

        lax.fori_loop(0, NB, one, 0)
        d_enc = dh_buf[...].astype(BF16)
        d_small[:LANES] += tn(x_low[step].reshape(pixels, LANES), d_enc)

        @pl.when(lap == 0)
        def _():
            d_state[...] = d_pred + nt(d_enc, code_bf[0])

        return carry

    lax.fori_loop(0, ROLL, bwd_step, 0)

    for b in range(NB):
        d_small[LANES - NB + b : LANES - NB + b + 1] = d_gain[b]
    sm_send[...] = d_small[...].reshape(sm_send.shape)
    exchange_start(sm_send, sm_recv, sm_sem.at[0], sm_sem.at[1], peers, q)
    for b in range(NB - 1, 0, -1):
        shares_spread(b)
    exchange_wait(sm_send, sm_recv, sm_sem.at[0], sm_sem.at[1])
    share = sm_recv[0]
    for k in range(1, RANKS):
        share = share + sm_recv[k]
    sm_mir_send[...] = share
    swap = remote(sm_mir_send, sm_mir_recv, sm_sem.at[2], sm_sem.at[3], far)
    swap.start()
    grads_out(0, "cross", range(third))
    swap.wait()
    total = sm_mir_send[...] + sm_mir_recv[...]
    scal[1:2] += 0.5 * lane_sums(total * total)
    sm_src[...] = total
    push_blocks(lambda d: sm_src, g_small.at[q], sm_sem.at[4], sm_sem.at[5], peers, q)
    shares_spread(0)
    settle(0)

    me = RANKS * y + ma
    sets = ((dwf.at[0], dwf.at[1], dwf.at[2]), (dwf.at[3], dw_own.at[0], dw_own.at[1]))

    def unit_loads(u):
        part = pl.ds(third * (u % 2), third)
        return [
            pltpu.make_async_copy(array.at[u // 2, part], buffer, lamb_sem.at[u % 2, k])
            for k, (array, buffer) in enumerate(zip((spec_w, spec_m, spec_v), sets[u % 2]))
        ]

    for u in range(2):
        for copy in unit_loads(u):
            copy.start()

    def spread_start(value, landing, sems):
        def spread(s, carry):
            other = (me + s) % (2 * RANKS)
            remote(
                value, landing.at[me], sems[0], sems[1], {"lat": other // RANKS, "ma": other % RANKS}
            ).start()
            return carry

        lax.fori_loop(1, 2 * RANKS, spread, 0)
        pltpu.make_async_copy(value, landing.at[me], sems[1]).start()

    def spread_total(landing, sems):
        bytes_wait(landing, sems[1])
        bytes_wait(landing.at[pl.ds(0, 2 * RANKS - 1)], sems[0])
        total = landing[0]
        for k in range(1, 2 * RANKS):
            total = total + landing[k]
        return jnp.broadcast_to(jnp.sum(total, axis=1, keepdims=True), total.shape)

    first_sems, second_sems = (sm_sem.at[6], sm_sem.at[7]), (sm_sem.at[8], sm_sem.at[9])
    spread_start(scal, scal_recv, first_sems)
    for copy in ml_loads:
        copy.wait()
    total = spread_total(scal_recv, first_sems)
    scalars[:8] = total

    scale = clip_norm / jnp.maximum(jnp.sqrt(total[1:2, :1]), clip_norm)
    first_inv = 1.0 / small[1, FIRST_ROW : FIRST_ROW + 1, :1]
    second_inv = 1.0 / small[1, SECOND_ROW : SECOND_ROW + 1, :1]

    def direction_of(weight_old, first, second, grad):
        grad = grad * scale
        first_new = (beta_first * first + (1.0 - beta_first) * grad) * first_inv
        second_new = (beta_second * second + (1.0 - beta_second) * grad * grad) * second_inv
        return first_new / (jnp.sqrt(second_new) + adam_eps) + weight_decay * weight_old

    for u in range(2 * NB):
        for copy in unit_loads(u):
            copy.wait()
        w_buf, m_buf, v_buf = sets[u % 2]

        def one_degree(t, carry, u=u, w_buf=w_buf, m_buf=m_buf, v_buf=v_buf):
            for part in range(2):
                step_dir = direction_of(
                    w_buf[t, part], m_buf[t, part], v_buf[t, part], g_spec[u // 2, third * (u % 2) + t, part]
                )
                dirs[u // 2 : u // 2 + 1] += lane_sums(step_dir * step_dir)
            return carry

        lax.fori_loop(0, third, one_degree, 0)
        if u + 2 < 2 * NB:
            for copy in unit_loads(u + 2):
                copy.start()
    for b in range(NB):
        old = ml_buf[0, b]
        step_dir = direction_of(old, ml_buf[1, b], ml_buf[2, b], ag_src[b].astype(F32))
        row = NB + 2 * b + q // (RANKS // 2)
        for place_row, value in ((row, step_dir), (row + 2 * NB, old)):
            squares = value * value
            lanes = sum(squares[:, k * LANES : (k + 1) * LANES] for k in range(squares.shape[1] // LANES))
            dirs[pl.ds(place_row, 1), :] += 0.5 * jnp.sum(lanes, axis=0, keepdims=True)
    spread_start(dirs, dirs_recv, second_sems)

    bytes_wait(g_small, sm_sem.at[5])
    bytes_wait(g_small.at[pl.ds(0, RANKS - 1)], sm_sem.at[4])
    for b in range(NB):
        bytes_wait(g_mlp.at[b], ag_recv_sem.at[b])
        bytes_wait(g_mlp.at[b, pl.ds(0, RANKS - 1)], ag_send_sem.at[b])
        bytes_wait(mir_send.at[b], mir_send_sem.at[b])
        bytes_wait(dw_send.at[b], g_send_sem.at[b])
    scalars[8:] = spread_total(dirs_recv, second_sems)


def call_train(chunks, weights, tables, small_in, area):
    vmem = pltpu.VMEM
    dma = pltpu.SemaphoreType.DMA
    spec_w, mlp_w = weights[0], weights[3]
    lon = chunks[0].shape[2]
    pixels, chans = 2 * RANKS * lon, small_in.shape[-1]
    third = spec_w.shape[1] // 2
    triple = (third, 2, chans, LANES)
    narrow, wide = (2, RANKS, 4 * ORDS, LANES), (2, RANKS, 3, 2 * SLOTS, LANES)
    triples, spectra = RANKS * 6 * SLOTS, RANKS * 4 * ORDS
    mlp_shape = mlp_w.shape[1:]
    chunk = (mlp_shape[0] * mlp_shape[1] // RANKS, mlp_shape[2])
    small = (2 * LANES // RANKS, chans)
    b16 = lambda *shape: vmem(shape, BF16)
    f32 = lambda *shape: vmem(shape, F32)
    everywhere = pl.BlockSpec(memory_space=pl.ANY)
    inside = pl.BlockSpec(memory_space=vmem)
    return pl.pallas_call(
        train,
        out_shape=(
            jax.ShapeDtypeStruct(spec_w.shape, F32),
            jax.ShapeDtypeStruct((NB, RANKS, *chunk), BF16),
            jax.ShapeDtypeStruct((RANKS, *small), F32),
            jax.ShapeDtypeStruct((24, LANES), F32),
        ),
        in_specs=[everywhere] * 17 + [inside] * 2,
        out_specs=[inside] * 4,
        scratch_shapes=[
            b16(triples, spectra), b16(spectra, triples), b16(spectra, triples), b16(triples, spectra),
            b16(spectra, pixels), b16(pixels, spectra), b16(pixels, spectra), b16(spectra, pixels),
            b16(NB, 4, *triple), b16(*mlp_w.shape), f32(2, *mlp_shape),
            b16(*small_in.shape),
            f32(2, RANKS, lon, LANES), f32(ROLL, 2, RANKS, lon, LANES), f32(pixels, LANES), b16(ROLL, 2, RANKS, lon, LANES),
            f32(ROLL, pixels, LANES), f32(pixels, LANES), f32(4 * ROLL, pixels, chans), b16(ROLL, pixels, chans),
            b16(NB * ROLL, pixels, chans), b16(pixels, chans), f32(pixels, chans), f32(pixels, chans),
            b16(*narrow), b16(*narrow), b16(*narrow), b16(*wide), b16(*wide), b16(NB * ROLL, *wide), b16(NB * ROLL, *wide),
            f32(4, *triple), b16(NB, 3, *triple), b16(NB, 3, *triple), f32(NB, *triple), f32(NB, *mlp_shape),
            b16(RANKS, *chunk), b16(RANKS, *chunk), f32(NB, *chunk), f32(NB, *chunk), b16(NB, *chunk),
            f32(2 * LANES, chans), f32(NB, 1, chans), f32(RANKS, *small), f32(RANKS, *small), f32(*small), f32(*small),
            f32(*small), f32(8, LANES), f32(2 * RANKS, 8, LANES),
            f32(3, NB, *chunk), f32(16, LANES), f32(2 * RANKS, 16, LANES),
            dma((8,)), dma((3 * NB,)), dma((4,)), dma((4,)), dma((NB,)), dma((NB,)), dma((8, 2)), dma((8, 2)),
            dma((NB,)), dma((NB,)), dma((2,)), dma((NB,)), dma((NB,)), dma((NB,)), dma((NB,)), dma((10,)),
            dma((2, 3)), dma,
        ],
        compiler_params=pltpu.CompilerParams(
            collective_id=0, has_side_effects=True, vmem_limit_bytes=61 << 20
        ),
    )(*chunks, *weights, *tables, small_in, area)


def chunks_of(field):
    items, lon, lat, width = field.shape
    pairs = lat // 2
    chunks = jnp.moveaxis(field.reshape(items, lon, pairs, 2, width), 1, 3)
    return jnp.concatenate([chunks[0], jnp.roll(chunks[1], pairs // 2, 0)], 0)


def special(
    inputs,
    targets,
    mask,
    var_weight,
    step_count,
    spec_w,
    spec_m,
    spec_v,
    encdec_w,
    encdec_m,
    encdec_v,
    mlp_w,
    mlp_m,
    mlp_v,
    gain_w,
    gain_m,
    gain_v,
):
    zh, y, w, q = place()
    nlon = inputs.shape[1] * lax.axis_size("ma")
    nlat = inputs.shape[2] * lax.axis_size("lat")
    ranked, common = make_tables(nlat, nlon)
    tables = tuple(jnp.asarray(t) for t in (*ranked, *common))
    spare = LANES - C
    x_chunks = chunks_of(jnp.pad(inputs, ((0, 0),) * 3 + ((0, spare),)))
    masks = jnp.broadcast_to(mask.astype(F32)[None, ..., None], (*targets.shape[:-1], 1))
    goal = jnp.concatenate([targets, jnp.zeros((*targets.shape[:-1], spare - 1), F32), masks], -1)
    t_chunks = jnp.stack([chunks_of(goal[0]), chunks_of(goal[1])], 0)
    sines = np.sin((np.arange(nlat) + 0.5) * (math.pi / nlat))
    area = np.repeat((sines / np.mean(sines)).astype(np.float32).reshape(RANKS, 2, 1, 1), LANES, 3)
    step_float = step_count[0].astype(F32)
    fixes = jnp.stack([1.0 - beta_second**step_float, 1.0 - beta_first**step_float])
    var_row = jnp.pad(var_weight.astype(F32), (0, E - C))[None]
    small_in = jnp.stack(
        [
            jnp.concatenate([encdec_w[0], jnp.zeros((LANES - NB - C, E), F32), gain_w], 0),
            jnp.concatenate(
                [
                    encdec_w[1],
                    jnp.zeros((SECOND_ROW - C, E), F32),
                    jnp.broadcast_to(fixes[:, None], (2, E)),
                    var_row,
                    jnp.zeros((LANES - 1 - VAR_ROW, E), F32),
                ],
                0,
            ),
        ]
    )
    spec_grad, mlp_sum, small_sum, sums = call_train(
        (x_chunks.astype(BF16), x_chunks, t_chunks),
        (spec_w, spec_m, spec_v, mlp_w, mlp_m, mlp_v),
        tables,
        small_in,
        jnp.asarray(area),
    )
    grad_mlp = mlp_sum.reshape(mlp_w.shape).astype(F32)
    small_sum = small_sum.reshape(2, LANES, E)
    grad_encdec = small_sum[:, :C]
    grad_gain = small_sum[0, LANES - NB :]
    sums = sums[:, 0]
    loss_value = sums[0]
    weight_square = sums[2 : 2 + NB]
    grad_norm = jnp.sqrt(sums[1])
    scale = clip_norm / jnp.maximum(grad_norm, clip_norm)
    spec_m_new, spec_v_new, direction = adaptive(
        spec_w, spec_m, spec_v, spec_grad * scale, step_float
    )
    dir_square = sums[8 : 8 + NB]
    weight_norm = jnp.sqrt(weight_square)
    dir_norm = jnp.sqrt(dir_square)
    trust = weight_norm / (dir_norm + 1e-06)
    spec_new = spec_w - learn_rate * trust[:, None, None, None, None] * direction
    encdec_new, encdec_m_new, encdec_v_new, encdec_norms = lamb_dense(
        encdec_w, encdec_m, encdec_v, grad_encdec * scale, step_float, 2
    )
    mlp_m_new, mlp_v_new, mlp_dir = adaptive(mlp_w, mlp_m, mlp_v, grad_mlp * scale, step_float)
    mlp_dir_norm = jnp.sqrt(sums[8 + NB : 8 + 3 * NB])
    mlp_weight_norm = jnp.sqrt(sums[8 + 3 * NB : 8 + 5 * NB])
    mlp_trust = (mlp_weight_norm / (mlp_dir_norm + 1e-06)).reshape(NB, 2, 1, 1)
    mlp_new = mlp_w - learn_rate * mlp_trust * mlp_dir
    mlp_norms = jnp.stack([mlp_weight_norm, mlp_dir_norm], 1)
    gain_new, gain_m_new, gain_v_new, gain_norms = lamb_dense(
        gain_w, gain_m, gain_v, grad_gain * scale, step_float, NB
    )
    matrix_norms = jnp.concatenate(
        [jnp.stack([weight_norm, dir_norm], 1), encdec_norms, mlp_norms, gain_norms], 0
    )
    return (
        loss_value,
        grad_norm,
        matrix_norms,
        spec_new,
        spec_m_new,
        spec_v_new,
        spec_new.astype(jnp.bfloat16),
        encdec_new,
        encdec_m_new,
        encdec_v_new,
        encdec_new.astype(jnp.bfloat16),
        mlp_new,
        mlp_m_new,
        mlp_v_new,
        mlp_new.astype(jnp.bfloat16),
        gain_new,
        gain_m_new,
        gain_v_new,
        gain_new.astype(jnp.bfloat16),
    )


def local(mesh, *args):
    inputs, spec_w = args[0], args[5]
    lat = inputs.shape[2] * mesh.shape["lat"]
    fits = (
        dict(mesh.shape) == {"lat": 2, "ma": RANKS}
        and inputs.shape[0] == 2
        and lat == 2 * RANKS
        and spec_w.shape[1] * RANKS == L
    )
    return (special if fits else general)(*args)


def solution(mesh):
    placed = (
        P(None, "ma", "lat", None),
        P(None, None, "ma", "lat", None),
        P(None, "ma", "lat"),
        P(),
        P(),
        P(None, "ma", None, None, "lat"),
        P(None, "ma", None, None, "lat"),
        P(None, "ma", None, None, "lat"),
        P(),
        P(),
        P(),
        P(),
        P(),
        P(),
        P(),
        P(),
        P(),
    )
    return jax.shard_map(
        functools.partial(local, mesh),
        mesh=mesh,
        in_specs=placed,
        out_specs=(
            P(),
            P(),
            P(),
            P(None, "ma", None, None, "lat"),
            P(None, "ma", None, None, "lat"),
            P(None, "ma", None, None, "lat"),
            P(None, "ma", None, None, "lat"),
            P(),
            P(),
            P(),
            P(),
            P(),
            P(),
            P(),
            P(),
            P(),
            P(),
            P(),
            P(),
        ),
        check_vma=False,
    )
```

```python
import functools
import math

import jax
import jax.numpy as jnp
import ml_dtypes
import numpy as np
from jax import lax
from jax.experimental import pallas as pl
from jax.experimental.pallas import tpu as pltpu
from jax.sharding import PartitionSpec as P

E = 256
C = 73
L = 96
NB = 3
ROLL = 2


beta_first = 0.9
beta_second = 0.999
adam_eps = 1e-08
weight_decay = 0.01
learn_rate = 0.4
clip_norm = 0.05
norm_eps = 1e-05


def legendre(orders, angles):
    cosines = jnp.cos(angles)[None, :]
    sines = jnp.sin(angles)[None, :]
    order_col = orders[:, None]
    log_start = 0.5 * (
        jnp.log((2.0 * order_col + 1.0) / (4.0 * math.pi))
        + lax.lgamma(2.0 * order_col + 1.0)
        - 2.0 * lax.lgamma(order_col + 1.0)
        - order_col * math.log(4.0)
    ) + order_col * jnp.log(sines)
    starting = jnp.exp(log_start)

    def advance(carry, degree):
        previous, earlier = carry
        upper = jnp.maximum(degree * degree - order_col * order_col, 1.0)
        factor = jnp.sqrt(jnp.maximum(4.0 * degree * degree - 1.0, 1.0) / upper)
        lower = jnp.maximum((degree - 1.0) ** 2 - order_col * order_col, 0.0)
        shrink = jnp.sqrt(lower / jnp.maximum(4.0 * (degree - 1.0) ** 2 - 1.0, 1.0))
        stepped = factor * (cosines * previous - shrink * earlier)
        second = jnp.sqrt(2.0 * order_col + 3.0) * cosines * starting
        value = jnp.where(
            degree < order_col,
            0.0,
            jnp.where(
                degree == order_col, starting, jnp.where(degree == order_col + 1.0, second, stepped)
            ),
        )
        return ((value, previous), value)

    zero_rows = jnp.zeros_like(starting)
    unused, table = lax.scan(advance, (zero_rows, zero_rows), jnp.arange(L, dtype=jnp.float32))
    return table


def dft_tables(orders, count_lon):
    phases = orders[:, None] * jnp.arange(count_lon, dtype=jnp.int32)[None, :] % count_lon
    phase = phases.astype(jnp.float32) * (2.0 * math.pi / count_lon)
    cosines = jnp.cos(phase)
    sines = jnp.sin(phase)
    number = orders.shape[0]
    forward = jnp.stack([cosines, -sines], 1).reshape(2 * number, count_lon)
    factor = jnp.where(orders == 0, 1.0, 2.0)[:, None] / math.sqrt(2.0 * math.pi)
    inverse = jnp.stack([factor * cosines, -factor * sines], 1).reshape(2 * number, count_lon).T
    return (forward, inverse)


def adaptive(weight, first, second, grad, step_float):
    first_new = beta_first * first + (1.0 - beta_first) * grad
    second_new = beta_second * second + (1.0 - beta_second) * grad * grad
    direction = (
        first_new
        / (1.0 - beta_first**step_float)
        / (jnp.sqrt(second_new / (1.0 - beta_second**step_float)) + adam_eps)
        + weight_decay * weight
    )
    return (first_new, second_new, direction)


def lamb_dense(weight, first, second, grad, step_float, groups):
    first_new, second_new, direction = adaptive(weight, first, second, grad, step_float)
    flat_weight = weight.reshape(groups, -1)
    flat_dir = direction.reshape(groups, -1)
    weight_norm = jnp.sqrt(jnp.sum(flat_weight * flat_weight, 1))
    dir_norm = jnp.sqrt(jnp.sum(flat_dir * flat_dir, 1))
    trust = weight_norm / (dir_norm + 1e-06)
    new_weight = (flat_weight - learn_rate * trust[:, None] * flat_dir).reshape(weight.shape)
    return (new_weight, first_new, second_new, jnp.stack([weight_norm, dir_norm], 1))


def norm_forward(hidden, gain_vec):
    centre = jnp.mean(hidden, -1, keepdims=True)
    centred = hidden - centre
    inv_std = lax.rsqrt(jnp.mean(centred * centred, -1, keepdims=True) + norm_eps)
    normal = centred * inv_std
    return ((normal * gain_vec).astype(jnp.bfloat16), normal, inv_std)


def norm_backward(d_normed, normal, inv_std, gain_vec):
    scaled = d_normed * gain_vec
    d_gain = jnp.sum(d_normed * normal, axis=(0, 1, 2))
    d_hidden = inv_std * (
        scaled
        - jnp.mean(scaled, -1, keepdims=True)
        - normal * jnp.mean(scaled * normal, -1, keepdims=True)
    )
    return (d_hidden, d_gain)


def mlp_forward(merged, weights):
    merged_low = merged.astype(jnp.bfloat16)
    pre_act = jnp.einsum(
        "jibe,ef->jibf", merged_low, weights[0], preferred_element_type=jnp.float32
    )
    gelu_out = jax.nn.gelu(pre_act).astype(jnp.bfloat16)
    hidden = merged + jnp.einsum(
        "jibf,ef->jibe", gelu_out, weights[1], preferred_element_type=jnp.float32
    )
    return (hidden, (merged_low, pre_act, gelu_out))


def mlp_backward(d_hidden, stored, weights):
    merged_low, pre_act, gelu_out = stored
    d_branch = d_hidden.astype(jnp.bfloat16)
    d_gelu = jnp.einsum("jibe,ef->jibf", d_branch, weights[1], preferred_element_type=jnp.float32)
    unused, pullback = jax.vjp(jax.nn.gelu, pre_act)
    d_pre = pullback(d_gelu)[0].astype(jnp.bfloat16)
    grad_out = jnp.einsum("jibf,jibe->ef", gelu_out, d_branch, preferred_element_type=jnp.float32)
    grad_in = jnp.einsum("jibe,jibf->ef", merged_low, d_pre, preferred_element_type=jnp.float32)
    d_merged = d_hidden + jnp.einsum(
        "jibf,ef->jibe", d_pre, weights[0], preferred_element_type=jnp.float32
    )
    return (d_merged, jnp.stack([grad_in, grad_out], 0))


def general(
    inputs,
    targets,
    mask,
    var_weight,
    step_count,
    spec_w,
    spec_m,
    spec_v,
    encdec_w,
    encdec_m,
    encdec_v,
    mlp_w,
    mlp_m,
    mlp_v,
    gain_w,
    gain_m,
    gain_v,
):
    n_ma = lax.axis_size("ma")
    n_lat = lax.axis_size("lat")
    ma_pos = lax.axis_index("ma")
    lat_pos = lax.axis_index("lat")
    batch = inputs.shape[0]
    lon_loc = inputs.shape[1]
    lat_loc = inputs.shape[2]
    nlon_all = lon_loc * n_ma
    nlat_all = lat_loc * n_lat
    orders_loc = L // n_ma
    angles = (jnp.arange(nlat_all, dtype=jnp.float32) + 0.5) * (math.pi / nlat_all)
    local_orders = ma_pos * orders_loc + jnp.arange(orders_loc, dtype=jnp.int32)
    table = legendre(local_orders.astype(jnp.float32), angles)
    quadrature = jnp.sin(angles) * (math.sqrt(2.0 * math.pi) / nlon_all * math.pi / nlat_all)
    fwd_leg = (table * quadrature[None, None, :]).astype(jnp.bfloat16)
    inv_leg = table.astype(jnp.bfloat16)
    fwd_table, inv_table = dft_tables(jnp.arange(L, dtype=jnp.int32), nlon_all)
    fwd_four = fwd_table.astype(jnp.bfloat16)
    inv_four = inv_table.astype(jnp.bfloat16)
    fwd_back = fwd_four.T
    inv_back = inv_four.T
    sines = jnp.sin(angles)
    area = sines / jnp.mean(sines)
    area_rows = lax.dynamic_slice_in_dim(area, lat_pos * lat_loc, lat_loc)
    mask_grid = jnp.transpose(mask, (1, 2, 0)).astype(jnp.float32)
    pixel_weight = (
        area_rows[None, :, None, None]
        * var_weight.astype(jnp.float32)[None, None, None, :]
        * mask_grid[:, :, :, None]
    )
    grid_targets = jnp.transpose(targets, (0, 2, 3, 1, 4))
    denom = float(batch * nlon_all * nlat_all * C)

    def apply_table(table_full, block_in):
        whole_out = jnp.einsum(
            "ok,kibe->oibe",
            table_full,
            lax.all_to_all(block_in, "ma", split_axis=3, concat_axis=0, tiled=True),
            preferred_element_type=jnp.float32,
        )
        return lax.all_to_all(
            whole_out.astype(jnp.bfloat16), "ma", split_axis=0, concat_axis=3, tiled=True
        ).astype(whole_out.dtype)

    def spectral_backward(d_filtered, owned, weight_blk):
        d_rows = apply_table(inv_back, d_filtered.astype(jnp.bfloat16)).astype(jnp.bfloat16)
        d_spec = lax.all_to_all(d_rows, "lat", split_axis=3, concat_axis=1, tiled=True)
        out_width = d_spec.shape[3]
        d_mixed = jnp.einsum(
            "lmi,mpibo->lmpbo",
            inv_leg,
            d_spec.reshape(orders_loc, 2, nlat_all, batch, out_width),
            preferred_element_type=jnp.float32,
        ).astype(jnp.bfloat16)
        d_own = lax.all_to_all(d_mixed, "ma", split_axis=0, concat_axis=1, tiled=True)
        real_w = weight_blk[:, 0]
        imag_w = weight_blk[:, 1]
        d_real = d_own[:, :, 0]
        d_imag = d_own[:, :, 1]
        d_coef_real = jnp.einsum(
            "lmbo,leo->lmbe", d_real, real_w, preferred_element_type=jnp.float32
        ) + jnp.einsum("lmbo,leo->lmbe", d_imag, imag_w, preferred_element_type=jnp.float32)
        d_coef_imag = jnp.einsum(
            "lmbo,leo->lmbe", d_imag, real_w, preferred_element_type=jnp.float32
        ) - jnp.einsum("lmbo,leo->lmbe", d_real, imag_w, preferred_element_type=jnp.float32)
        grad_real = jnp.einsum(
            "lmbe,lmbo->leo", owned[:, :, 0], d_real, preferred_element_type=jnp.float32
        ) + jnp.einsum("lmbe,lmbo->leo", owned[:, :, 1], d_imag, preferred_element_type=jnp.float32)
        grad_imag = jnp.einsum(
            "lmbe,lmbo->leo", owned[:, :, 0], d_imag, preferred_element_type=jnp.float32
        ) - jnp.einsum("lmbe,lmbo->leo", owned[:, :, 1], d_real, preferred_element_type=jnp.float32)
        d_owned = jnp.stack([d_coef_real, d_coef_imag], 2)
        d_coeffs = lax.all_to_all(
            d_owned.astype(jnp.bfloat16), "ma", split_axis=1, concat_axis=0, tiled=True
        ).astype(d_owned.dtype)
        d_full = jnp.einsum(
            "lmi,lmpbe->mpibe",
            fwd_leg.astype(jnp.float32),
            d_coeffs,
            precision=lax.Precision.HIGHEST,
        ).reshape(2 * orders_loc, nlat_all, batch, E)
        d_spec_rows = lax.psum_scatter(
            d_full.astype(jnp.bfloat16), "lat", scatter_dimension=1, tiled=True
        )
        return (apply_table(fwd_back, d_spec_rows), jnp.stack([grad_real, grad_imag], 1))

    spec_bf = spec_w.astype(jnp.bfloat16)
    encdec_bf = encdec_w.astype(jnp.bfloat16)
    mlp_bf = mlp_w.astype(jnp.bfloat16)

    def model_backward(d_pred, stored):
        state_low, hidden_low, records = stored
        d_dec = d_pred.astype(jnp.bfloat16)
        grad_dec = jnp.einsum(
            "jibe,jibc->ce", hidden_low, d_dec, preferred_element_type=jnp.float32
        )
        d_hidden = jnp.einsum(
            "jibc,ce->jibe", d_dec, encdec_bf[1], preferred_element_type=jnp.float32
        )
        spec_grads = [None] * NB
        mlp_grads = [None] * NB
        gain_grads = [None] * NB
        for block_idx in reversed(range(NB)):
            normal, inv_std, owned, mlp_kept = records[block_idx]
            d_merged, mlp_grads[block_idx] = mlp_backward(d_hidden, mlp_kept, mlp_bf[block_idx])
            d_normed, spec_grads[block_idx] = spectral_backward(d_merged, owned, spec_bf[block_idx])
            d_norm_in, gain_grads[block_idx] = norm_backward(
                d_normed, normal, inv_std, gain_w[block_idx]
            )
            d_hidden = d_merged + d_norm_in
        d_enc = d_hidden.astype(jnp.bfloat16)
        grad_enc = jnp.einsum("jibc,jibe->ce", state_low, d_enc, preferred_element_type=jnp.float32)
        d_state = d_pred + jnp.einsum(
            "jibe,ce->jibc", d_enc, encdec_bf[0], preferred_element_type=jnp.float32
        )
        return (
            d_state,
            (
                jnp.stack([grad_enc, grad_dec], 0),
                jnp.stack(spec_grads, 0),
                jnp.stack(mlp_grads, 0),
                jnp.stack(gain_grads, 0),
            ),
        )

    state = jnp.transpose(inputs, (1, 2, 0, 3))
    history = []
    loss_part = jnp.zeros((), jnp.float32)
    for section_idx in range(ROLL):
        model_state_low = state.astype(jnp.bfloat16)
        hidden = jnp.einsum(
            "jibc,ce->jibe", model_state_low, encdec_bf[0], preferred_element_type=jnp.float32
        )
        model_records = []
        for model_block_idx in range(NB):
            model_normed, model_normal, model_inv_std = norm_forward(
                hidden, gain_w[model_block_idx]
            )
            spectral_weight_blk = spec_bf[model_block_idx]
            spec_rows = apply_table(fwd_four, model_normed).astype(jnp.bfloat16)
            piece = lax.all_gather(spec_rows, "lat", axis=1, tiled=True)
            row_width = piece.shape[1]
            paired = piece.reshape(orders_loc, 2, row_width, piece.shape[2], piece.shape[3])
            coeffs = jnp.einsum(
                "lmi,mpibe->lmpbe", fwd_leg, paired, preferred_element_type=jnp.float32
            ).astype(jnp.bfloat16)
            spectral_owned = lax.all_to_all(coeffs, "ma", split_axis=0, concat_axis=1, tiled=True)
            spectral_real_w = spectral_weight_blk[:, 0]
            spectral_imag_w = spectral_weight_blk[:, 1]
            mixed_real = jnp.einsum(
                "lmbe,leo->lmbo",
                spectral_owned[:, :, 0],
                spectral_real_w,
                preferred_element_type=jnp.float32,
            ) - jnp.einsum(
                "lmbe,leo->lmbo",
                spectral_owned[:, :, 1],
                spectral_imag_w,
                preferred_element_type=jnp.float32,
            )
            mixed_imag = jnp.einsum(
                "lmbe,leo->lmbo",
                spectral_owned[:, :, 0],
                spectral_imag_w,
                preferred_element_type=jnp.float32,
            ) + jnp.einsum(
                "lmbe,leo->lmbo",
                spectral_owned[:, :, 1],
                spectral_real_w,
                preferred_element_type=jnp.float32,
            )
            mixed_owned = jnp.stack([mixed_real, mixed_imag], 2).astype(jnp.bfloat16)
            mixed = lax.all_to_all(mixed_owned, "ma", split_axis=1, concat_axis=0, tiled=True)
            spec_out = jnp.einsum(
                "lmi,lmpbo->mpibo", inv_leg, mixed, preferred_element_type=jnp.float32
            )
            spec_out = spec_out.astype(jnp.bfloat16).reshape(
                2 * orders_loc, nlat_all, batch, mixed.shape[4]
            )
            rows_out = lax.all_to_all(spec_out, "lat", split_axis=1, concat_axis=3, tiled=True)
            filtered = apply_table(inv_four, rows_out)
            hidden, model_mlp_kept = mlp_forward(hidden + filtered, mlp_bf[model_block_idx])
            model_records.append((model_normal, model_inv_std, spectral_owned, model_mlp_kept))
        model_hidden_low = hidden.astype(jnp.bfloat16)
        prediction = state + jnp.einsum(
            "jibe,ce->jibc", model_hidden_low, encdec_bf[1], preferred_element_type=jnp.float32
        )
        prediction, stored = (prediction, (model_state_low, model_hidden_low, model_records))
        misfit = prediction - grid_targets[section_idx]
        loss_part = loss_part + jnp.sum(pixel_weight * misfit * misfit) / denom
        history.append((stored, misfit))
        state = prediction
    d_state = jnp.zeros_like(state)
    totals = None
    for section_idx in reversed(range(ROLL)):
        stored, misfit = history[section_idx]
        d_pred = 2.0 * pixel_weight * misfit / denom + d_state
        d_state, section_grads = model_backward(d_pred, stored)
        totals = section_grads if totals is None else jax.tree.map(jnp.add, totals, section_grads)
    grad_encdec, spec_grad, grad_mlp, grad_gain = totals
    grad_encdec, grad_mlp, grad_gain, loss_value, spec_square, weight_square = lax.psum(
        (
            grad_encdec,
            grad_mlp,
            grad_gain,
            loss_part,
            jnp.sum(spec_grad * spec_grad),
            jnp.sum(spec_w * spec_w, axis=(1, 2, 3, 4)),
        ),
        ("lat", "ma"),
    )
    total_square = (
        spec_square
        + jnp.sum(grad_encdec * grad_encdec)
        + jnp.sum(grad_mlp * grad_mlp)
        + jnp.sum(grad_gain * grad_gain)
    )
    grad_norm = jnp.sqrt(total_square)
    scale = clip_norm / jnp.maximum(grad_norm, clip_norm)
    step_float = step_count[0].astype(jnp.float32)
    spec_m_new, spec_v_new, direction = adaptive(
        spec_w, spec_m, spec_v, spec_grad * scale, step_float
    )
    dir_square = lax.psum(jnp.sum(direction * direction, axis=(1, 2, 3, 4)), ("lat", "ma"))
    weight_norm = jnp.sqrt(weight_square)
    dir_norm = jnp.sqrt(dir_square)
    trust = weight_norm / (dir_norm + 1e-06)
    spec_new = spec_w - learn_rate * trust[:, None, None, None, None] * direction
    encdec_new, encdec_m_new, encdec_v_new, encdec_norms = lamb_dense(
        encdec_w, encdec_m, encdec_v, grad_encdec * scale, step_float, 2
    )
    mlp_new, mlp_m_new, mlp_v_new, mlp_norms = lamb_dense(
        mlp_w, mlp_m, mlp_v, grad_mlp * scale, step_float, 2 * NB
    )
    gain_new, gain_m_new, gain_v_new, gain_norms = lamb_dense(
        gain_w, gain_m, gain_v, grad_gain * scale, step_float, NB
    )
    matrix_norms = jnp.concatenate(
        [jnp.stack([weight_norm, dir_norm], 1), encdec_norms, mlp_norms, gain_norms], 0
    )
    return (
        loss_value,
        grad_norm,
        matrix_norms,
        spec_new,
        spec_m_new,
        spec_v_new,
        spec_new.astype(jnp.bfloat16),
        encdec_new,
        encdec_m_new,
        encdec_v_new,
        encdec_new.astype(jnp.bfloat16),
        mlp_new,
        mlp_m_new,
        mlp_v_new,
        mlp_new.astype(jnp.bfloat16),
        gain_new,
        gain_m_new,
        gain_v_new,
        gain_new.astype(jnp.bfloat16),
    )


RANKS = 16
ORDS = L // RANKS
SLOTS = 8
F32 = jnp.float32
BF16 = jnp.bfloat16


def legendre_f64(nlat):
    theta = (np.arange(nlat) + 0.5) * (math.pi / nlat)
    cosines, sines = np.cos(theta), np.sin(theta)
    table = np.zeros((L, L, nlat))
    for m in range(L):
        log_start = 0.5 * (
            math.log((2.0 * m + 1.0) / (4.0 * math.pi))
            + math.lgamma(2.0 * m + 1.0)
            - 2.0 * math.lgamma(m + 1.0)
            - m * math.log(4.0)
        ) + m * np.log(sines)
        table[m, m] = np.exp(log_start)
        if m + 1 < L:
            table[m + 1, m] = math.sqrt(2.0 * m + 3.0) * cosines * table[m, m]
        for k in range(m + 2, L):
            factor = math.sqrt((4.0 * k * k - 1.0) / (k * k - m * m))
            shrink = math.sqrt(((k - 1.0) ** 2 - m * m) / (4.0 * (k - 1.0) ** 2 - 1.0))
            table[k, m] = factor * (cosines * table[k - 1, m] - shrink * table[k - 2, m])
    return table, sines


def low_np(array):
    return array.astype(np.float32).astype(ml_dtypes.bfloat16)


def slot_map():
    degree = np.full((RANKS, 3, SLOTS), -1)
    order = np.full((RANKS, SLOTS), -1)
    for d in range(RANKS):
        y, w, xc = d // 8, (d // 4) % 2, d % 4
        lo, hi = 4 * w + xc, 4 * (3 - w) + xc
        n_lo, n_hi = (6 * lo + 5) // RANKS + 1, (6 * hi + 5) // RANKS + 1
        for group, first, count in ((hi, 0, n_hi), (lo, SLOTS - n_lo, n_lo)):
            for r in range(count):
                order[d, first + r] = r
                for t in range(3):
                    degree[d, t, first + r] = 6 * group + 3 * y + t
    return degree, order


def make_tables(nlat, nlon):
    table, sines = legendre_f64(nlat)
    quadrature = sines * (math.sqrt(2.0 * math.pi) / nlon * math.pi / nlat)
    fwd_leg = np.asarray(low_np(table * quadrature[None, None, :]))
    inv_leg = np.asarray(low_np(table))
    degree, order = slot_map()
    shape = (RANKS, RANKS, 3, 2, SLOTS, RANKS, ORDS, 2, 2)
    fwd = np.zeros(shape, ml_dtypes.bfloat16)
    inv = np.zeros(shape, ml_dtypes.bfloat16)
    for g in range(RANKS):
        for d in range(RANKS):
            for slot in range(SLOTS):
                r = order[d, slot]
                if r < 0:
                    continue
                for t in range(3):
                    k, m = degree[d, t, slot], g + RANKS * r
                    for p in range(2):
                        fwd[g, d, t, p, slot, :, r, p, :] = fwd_leg[k, m].reshape(RANKS, 2)
                        inv[g, d, t, p, slot, :, r, p, :] = inv_leg[k, m].reshape(RANKS, 2)
    rows = RANKS * 3 * 2 * SLOTS
    cols = RANKS * ORDS * 2 * 2
    fwd = fwd.reshape(RANKS, rows, cols)
    inv = inv.reshape(RANKS, rows, cols)
    phase = 2.0 * math.pi * (np.arange(L)[:, None] * np.arange(nlon)[None, :] % nlon) / nlon
    scale = np.where(np.arange(L) == 0, 1.0, 2.0)[:, None] / math.sqrt(2.0 * math.pi)
    four = low_np(np.stack([np.cos(phase), -np.sin(phase)], 1))
    back = low_np(np.stack([scale * np.cos(phase), -scale * np.sin(phase)], 1))
    def wide(small):
        out = np.zeros((RANKS, ORDS, 2, 2, 2, nlon), ml_dtypes.bfloat16)
        ordered = small.reshape(ORDS, RANKS, 2, nlon).transpose(1, 0, 2, 3)
        for il in range(2):
            out[:, :, :, il, il, :] = ordered
        return out.reshape(cols, 2 * nlon)

    def turn(array):
        return np.ascontiguousarray(np.swapaxes(array, -1, -2))

    four, back = wide(four), wide(back)
    return (fwd, turn(inv), turn(fwd), inv), (four, turn(back), turn(four), back)


def place():
    ma = lax.axis_index("ma")
    y = lax.axis_index("lat")
    z = ma // 4
    zh = z // 2
    w = z + zh * (3 - 2 * z)
    return zh, y, w, 8 * y + 4 * w + ma % 4


def device_of(zh, q):
    w = (q // 4) % 2
    z = w + zh * (3 - 2 * w)
    return {"lat": q // 8, "ma": 4 * z + q % 4}


def nn(a, b):
    return lax.dot_general(a, b, (((1,), (0,)), ((), ())), preferred_element_type=F32)


def nt(a, b):
    return lax.dot_general(a, b, (((1,), (1,)), ((), ())), preferred_element_type=F32)


def tn(a, b):
    return lax.dot_general(a, b, (((0,), (0,)), ((), ())), preferred_element_type=F32)


def piece_of(kind, half, zh, y):
    return 2 - 2 * ((kind + zh) % 2) + (half + y) % 2


def weight_of(w_all, block, kind, t, part, zh, y):
    return jnp.concatenate(
        [w_all[block, piece_of(kind, half, zh, y), t, part] for half in range(2)], axis=1
    )


def hi_rows(w):
    slot = lax.broadcasted_iota(jnp.int32, (RANKS * 2 * SLOTS, 1), 0) % SLOTS
    return slot < 6 - w


GELU_A = math.sqrt(2.0 / math.pi)
GELU_B = 0.044715


def normal_of(hidden):
    centre = jnp.mean(hidden, -1, keepdims=True)
    centred = hidden - centre
    inv_std = lax.rsqrt(jnp.mean(centred * centred, -1, keepdims=True) + norm_eps)
    return centred * inv_std, inv_std


def rows_loop(total, step, body):
    def one(k, carry):
        body(pl.ds(pl.multiple_of(k * step, step), step))
        return carry

    lax.fori_loop(0, total // step, one, 0)


MESH = pl.DeviceIdType.MESH
LANES = 128
MASK_LANE = LANES - 1
VAR_ROW, FIRST_ROW, SECOND_ROW = 124, 123, 122


def greet_all(between=None):
    barrier = pltpu.get_barrier_semaphore()
    me = 2 * RANKS // 2 * lax.axis_index("lat") + lax.axis_index("ma")

    def greet(s, carry):
        other = (me + s) % (2 * RANKS)
        pl.semaphore_signal(
            barrier, inc=1, device_id={"lat": other // RANKS, "ma": other % RANKS}, device_id_type=MESH
        )
        return carry

    lax.fori_loop(1, 2 * RANKS, greet, 0)
    if between is not None:
        between()
    pl.semaphore_wait(barrier, 2 * RANKS - 1)


def remote(src, dst, send_sem, recv_sem, device):
    return pltpu.make_async_remote_copy(
        src_ref=src,
        dst_ref=dst,
        send_sem=send_sem,
        recv_sem=recv_sem,
        device_id=device,
        device_id_type=MESH,
    )


def bytes_wait(ref, sem):
    pltpu.make_async_copy(ref, ref, sem).wait()


def flip(value, bits, span):
    out, unit = 0, 1
    while unit < span:
        digit = (value // unit) % 2
        out = out + unit * (1 - digit if bits // unit % 2 else digit)
        unit *= 2
    return out


def peers_of(zh, q):
    ranks = [flip(q, s, RANKS) for s in range(RANKS - 1, 0, -1)]
    return [(d, device_of(zh, d)) for d in ranks]


def push_blocks(source_of, landing, send_sem, recv_sem, peers, q):
    for d, device in peers:
        remote(source_of(d), landing, send_sem, recv_sem, device).start()
    pltpu.make_async_copy(source_of(q), landing, recv_sem).start()


def exchange_start(send, recv, send_sem, recv_sem, peers, q):
    push_blocks(lambda d: send.at[d], recv.at[q], send_sem, recv_sem, peers, q)


def exchange_wait(send, recv, send_sem, recv_sem):
    bytes_wait(recv, recv_sem)
    bytes_wait(send.at[pl.ds(0, RANKS - 1)], send_sem)


def exchange(send, recv, send_sem, recv_sem, peers, q):
    exchange_start(send, recv, send_sem, recv_sem, peers, q)
    exchange_wait(send, recv, send_sem, recv_sem)


def lane_sums(array):
    return jnp.sum(array.reshape(-1, LANES), axis=0, keepdims=True)


def train(
    xb_chunks, x_chunks, t_chunks, spec_w, spec_m, spec_v, mlp_w, mlp_m, mlp_v, r0, r1, r2, r3, f0, f1, f2, f3,
    small, area,
    g_spec, g_mlp, g_small, scalars,
    pfx, pix, pfxt, pixt, ftx, itx, ftxt, itxt, w_all, mlp_bf, mlp_stage, code_bf,
    x_recv, goals, weight, x_low, misfit, d_state, h_all, hid_low, v_low, u_buf, dv_buf, dh_buf,
    n_send, s_recv, y_recv, w_send, b_recv, a_own, d_mix,
    dwf, dw_send, dw_recv, dw_own, dmlp, rs_send, rs_recv, mir_send, mir_recv, ag_src,
    d_small, d_gain, sm_send, sm_recv, sm_mir_send, sm_mir_recv, sm_src, scal, scal_recv,
    ml_buf, dirs, dirs_recv,
    load_sem, stage_sem, once_send, once_recv, w_send_sem, w_recv_sem, x_send, x_recv_sem,
    g_send_sem, g_recv_sem, rs_sem, mir_send_sem, mir_recv_sem, ag_send_sem, ag_recv_sem, sm_sem,
    lamb_sem, ml_sem,
):
    zh, y, w, q = place()
    peers = peers_of(zh, q)
    ma = lax.axis_index("ma")
    xc = ma % 4
    mirror_ma = 4 * (3 - ma // 4) + xc
    near, far, cross = {"lat": 1 - y, "ma": ma}, {"lat": y, "ma": mirror_ma}, {"lat": 1 - y, "ma": mirror_ma}
    pixels, chans = dh_buf.shape
    spectra = pix.shape[0]
    triples = pfx.shape[0]
    third = 3

    loads = [
        pltpu.make_async_copy(src.at[q], dst, load_sem.at[k])
        for k, (src, dst) in enumerate(((r0, pfx), (r1, pix), (r2, pfxt), (r3, pixt)))
    ] + [
        pltpu.make_async_copy(src, dst, load_sem.at[4 + k])
        for k, (src, dst) in enumerate(((f0, ftx), (f1, itx), (f2, ftxt), (f3, itxt)))
    ]
    stage = dwf

    class SpecLoad:
        def __init__(self, b):
            self.copies = [
                pltpu.make_async_copy(
                    spec_w.at[b, pl.ds(third * k, third)], stage.at[2 * (b % 2) + k], stage_sem.at[2 * b + k]
                )
                for k in range(2)
            ]

        def start(self):
            for copy in self.copies:
                copy.start()

        def wait(self):
            for copy in self.copies:
                copy.wait()

    spec_loads = [SpecLoad(b) for b in range(NB)]
    mlp_loads = [pltpu.make_async_copy(mlp_w.at[b], mlp_stage.at[b % 2], stage_sem.at[2 * NB + b]) for b in range(NB)]
    spec_loads[0].start()
    spec_loads[1].start()
    loads[4].start()
    scal[...] = jnp.zeros_like(scal)
    d_small[...] = jnp.zeros_like(d_small)
    d_gain[...] = jnp.zeros_like(d_gain)
    d_state[...] = jnp.zeros_like(d_state)
    dirs[...] = jnp.zeros_like(dirs)
    kept_rows = lax.broadcasted_iota(jnp.int32, (LANES, 1), 0) < C
    for k in range(2):
        code_bf[k] = jnp.where(kept_rows, small[k], 0.0).astype(BF16)

    def chunk_to(chunks, landing, sems):
        for bits in range(RANKS - 1, 0, -1):
            other = flip(ma, bits, RANKS)
            remote(chunks.at[other], landing, sems[0], sems[1], {"lat": y, "ma": other}).start()
        pltpu.make_async_copy(chunks.at[ma], landing, sems[1]).start()

    def weights_out(b, where, triple):
        source, piece, device = {
            "near": (dw_send, 1, near), "far": (w_all, 2, far), "cross": (dw_send, 3, cross)
        }[where]
        for t in triple:
            remote(source.at[b, 0, t], w_all.at[b, piece, t], w_send_sem.at[b], w_recv_sem.at[b], device).start()

    def cast_weights(b):
        spec_loads[b].wait()
        for t in range(third):
            for own, target in ((y, w_all.at[b, 0]), (1 - y, dw_send.at[b, 0])):
                value = stage[2 * (b % 2) + own, t]
                scal[2 + b : 3 + b] += lane_sums(value * value)
                target[t] = value.astype(BF16)
        if b + 2 < NB:
            spec_loads[b + 2].start()

    def first_weights():
        cast_weights(0)
        loads[0].start()
        mlp_loads[0].start()
        mlp_loads[1].start()
        for k in (1, 2, 3, 5, 6, 7):
            loads[k].start()

    greet_all(first_weights)
    chunk_to(xb_chunks, x_low.at[0, :, ma], (once_send.at[0], once_recv.at[0]))
    weights_out(0, "far", range(third))
    weights_out(0, "cross", range(third))
    weights_out(0, "near", range(third))
    for b in range(1, NB):
        cast_weights(b)
    for b in range(NB):
        mlp_loads[b].wait()
        mlp_bf[b] = mlp_stage[b % 2].astype(BF16)
        if b + 2 < NB:
            mlp_loads[b + 2].start()
    for copy in loads:
        copy.wait()
    share_rows = pl.ds(pl.multiple_of((q % (RANKS // 2)) * ml_buf.shape[2], ml_buf.shape[2]), ml_buf.shape[2])
    ml_loads = [
        pltpu.make_async_copy(array.at[b, q // (RANKS // 2), share_rows], ml_buf.at[k, b], ml_sem)
        for k, array in enumerate((mlp_w, mlp_m, mlp_v))
        for b in range(NB)
    ]
    for copy in ml_loads:
        copy.start()
    bytes_wait(x_low.at[0], once_recv.at[0])
    bytes_wait(xb_chunks.at[pl.ds(0, RANKS - 1)], once_send.at[0])

    hi = hi_rows(w)
    rows_mix = RANKS * 2 * SLOTS

    halves = range(2)

    def cols(half):
        return slice(half * LANES, (half + 1) * LANES)

    def narrow(value):
        return value.astype(BF16).reshape(n_send.shape[1:])

    def broad(value):
        return value.astype(BF16).reshape(w_send.shape[1:])

    def go(phase, half, send, recv):
        exchange_start(send, recv, x_send.at[phase, half], x_recv_sem.at[phase, half], peers, q)

    def come(phase, half, send, recv):
        exchange_wait(send, recv, x_send.at[phase, half], x_recv_sem.at[phase, half])

    def whole(ref, rows):
        return jnp.concatenate([ref[half].reshape(rows, LANES) for half in halves], axis=1)

    def rows_of(ref, t):
        return jnp.concatenate([ref[half, :, t].reshape(rows_mix, LANES) for half in halves], axis=1)

    def swapped(product):
        wide = product.reshape(RANKS, 2, SLOTS, 2 * LANES)
        return wide[..., :LANES], wide[..., LANES:]

    def fwd_block(step, block):
        slot, idx = 4 * step + block, NB * step + block
        gain_row = small[0, pl.ds(LANES - NB + block, 1), :]

        def norm_rows(rows):
            normal, unused = normal_of(h_all[slot, rows, :])
            u_buf[rows, :] = (normal * gain_row).astype(BF16)

        rows_loop(pixels, 256, norm_rows)
        for half in halves:
            n_send[half] = narrow(nn(ftx[...], u_buf[:, cols(half)]))
            go(0, half, n_send.at[half], s_recv.at[half])

        @pl.when(jnp.logical_and(step == 0, block > 0))
        def _():
            weights_out(block, "cross", (2,))
            weights_out(block, "near", (2,))

        @pl.when(jnp.logical_and(step == 1, block == 0))
        def _():
            chunk_to(t_chunks.at[1], goals.at[1, :, ma], (once_send.at[2], once_recv.at[2]))

        for half in halves:
            come(0, half, n_send.at[half], s_recv.at[half])
            w_send[half] = broad(nn(pfx[...], s_recv[half].reshape(spectra, LANES)))
            go(1, half, w_send.at[half], a_own.at[idx, half])

        @pl.when(jnp.logical_and(step == 0, block < NB - 1))
        def _():
            weights_out(block + 1, "far", (0,))

        @pl.when(jnp.logical_and(step == 0, block == NB - 1))
        def _():
            chunk_to(x_chunks, x_recv.at[:, ma], (once_send.at[3], once_recv.at[3]))
            chunk_to(t_chunks.at[0], goals.at[0, :, ma], (once_send.at[1], once_recv.at[1]))

        for half in halves:
            come(1, half, w_send.at[half], a_own.at[idx, half])

        @pl.when(step == 0)
        def _():
            bytes_wait(w_all.at[block, pl.ds(1, 3)], w_recv_sem.at[block])

        for half in halves:
            for t in range(3):
                coef = rows_of(a_own.at[idx], t)

                def mixed_by(kind):
                    piece = piece_of(kind, half, zh, y)
                    return nn(coef, jnp.concatenate([w_all[block, piece, t, 0], w_all[block, piece, t, 1]], axis=1))

                by_real, by_imag = swapped(jnp.where(hi, mixed_by(0), mixed_by(1)))
                mixed = jnp.stack([by_real[:, 0] - by_imag[:, 1], by_real[:, 1] + by_imag[:, 0]], 1)
                w_send[half, :, t] = mixed.reshape(RANKS, 2 * SLOTS, LANES).astype(BF16)
            go(2, half, w_send.at[half], b_recv.at[half])

        @pl.when(jnp.logical_and(step == 0, block < NB - 1))
        def _():
            weights_out(block + 1, "far", (1,))
            weights_out(block + 1, "near", (0,))

        for half in halves:
            come(2, half, w_send.at[half], b_recv.at[half])
            n_send[half] = narrow(nn(pix[...], b_recv[half].reshape(triples, LANES)))
            go(3, half, n_send.at[half], y_recv.at[half])

        @pl.when(jnp.logical_and(step == 0, block < NB - 1))
        def _():
            weights_out(block + 1, "far", (2,))
            weights_out(block + 1, "cross", (0, 1))
            weights_out(block + 1, "near", (1,))

        for half in halves:
            come(3, half, n_send.at[half], y_recv.at[half])
        spectrum = whole(y_recv, spectra)

        def mlp_rows(rows):
            merged = h_all[slot, rows, :] + nn(itx[rows, :], spectrum)
            merged_low = merged.astype(BF16)
            v_low[idx, rows, :] = merged_low
            pre = nn(merged_low, mlp_bf[block, 0])
            act = (0.5 * pre * (1.0 + jnp.tanh(GELU_A * (pre + GELU_B * pre * pre * pre)))).astype(BF16)
            h_all[slot + 1, rows, :] = merged + nt(act, mlp_bf[block, 1])

        rows_loop(pixels, 256, mlp_rows)

    denom = float(pixels * RANKS * C * 2)

    def fwd_step(step, carry):
        h_all[4 * step] = nn(x_low[step].reshape(pixels, LANES), code_bf[0])

        def one(block, inner):
            fwd_block(step, block)
            return inner

        lax.fori_loop(0, NB, one, 0)
        hidden_low = h_all[4 * step + 3].astype(BF16)
        hid_low[step] = hidden_low
        delta = nt(hidden_low, code_bf[1])

        @pl.when(step == 0)
        def _():
            bytes_wait(x_recv, once_recv.at[3])
            bytes_wait(x_chunks.at[pl.ds(0, RANKS - 1)], once_send.at[3])
            bytes_wait(goals.at[0], once_recv.at[1])
            bytes_wait(t_chunks.at[0, pl.ds(0, RANKS - 1)], once_send.at[1])
            for il in range(2):
                valid = goals[0, il].reshape(pixels // 2, LANES)[:, MASK_LANE:]
                rows = slice(il * pixels // 2, (il + 1) * pixels // 2)
                weight[rows, :] = valid * (area[q, il] * small[1, VAR_ROW : VAR_ROW + 1, :LANES])

        @pl.when(step == 1)
        def _():
            bytes_wait(goals.at[1], once_recv.at[2])
            bytes_wait(t_chunks.at[1, pl.ds(0, RANKS - 1)], once_send.at[2])

        prediction = x_recv[...].reshape(pixels, LANES) + delta
        x_recv[...] = prediction.reshape(x_recv.shape)

        @pl.when(step == 0)
        def _():
            x_low[1] = prediction.astype(BF16).reshape(x_low.shape[1:])

        miss = prediction - goals[step].reshape(pixels, LANES)
        weighted = weight[...] * miss
        scal[0:1] += lane_sums(weighted * miss / denom)
        misfit[step] = 2.0 * weighted / denom
        return carry

    lax.fori_loop(0, ROLL, fwd_step, 0)
    for b in range(NB):
        bytes_wait(w_all.at[b, pl.ds(1, 3)], w_send_sem.at[b])

    def settle(block):
        bytes_wait(dw_recv.at[block], g_recv_sem.at[block])
        for t in range(third):
            for own, one, two in (
                (y, dw_own[block, t], dw_recv[block, 1, t]),
                (1 - y, dw_recv[block, 0, t], dw_recv[block, 2, t]),
            ):
                total = one.astype(F32) + two.astype(F32)
                scal[1:2] += lane_sums(total * total)
                g_spec[block, third * own + t] = total

    def shares_start(block):
        rs_send[...] = dmlp[block].astype(BF16).reshape(rs_send.shape)
        exchange_start(rs_send, rs_recv, rs_sem.at[0], rs_sem.at[1], peers, q)

    def shares_finish(block):
        exchange_wait(rs_send, rs_recv, rs_sem.at[0], rs_sem.at[1])
        share = rs_recv[0].astype(F32)
        for k in range(1, RANKS):
            share = share + rs_recv[k].astype(F32)
        mir_send[block] = share
        remote(mir_send.at[block], mir_recv.at[block], mir_send_sem.at[block], mir_recv_sem.at[block], far).start()

    def shares_spread(block):
        bytes_wait(mir_recv.at[block], mir_recv_sem.at[block])
        total = mir_send[block] + mir_recv[block]
        scal[1:2] += 0.5 * lane_sums(total * total)
        ag_src[block] = total.astype(BF16)
        landing = g_mlp.at[block, q // (RANKS // 2), share_rows]
        push_blocks(lambda d: ag_src.at[block], landing, ag_send_sem.at[block], ag_recv_sem.at[block], peers, q)

    def grads_out(b, where, triple):
        piece, device = {"near": (0, near), "far": (1, far), "cross": (2, cross)}[where]
        for t in triple:
            remote(
                dw_send.at[b, piece, t], dw_recv.at[b, piece, t], g_send_sem.at[b], g_recv_sem.at[b], device
            ).start()

    def bwd_block(lap, step, block):
        early = jnp.logical_and(lap == 1, block > 0)
        later = jnp.logical_and(lap == 1, block < NB - 1)
        slot, idx = 4 * step + block, NB * step + block
        gain_row = small[0, pl.ds(LANES - NB + block, 1), :]

        @pl.when(lap == 0)
        def _():
            dmlp[block] = jnp.zeros(dmlp.shape[1:], F32)

        def mlp_rows(rows):
            d_hidden = dh_buf[rows, :]
            d_branch = d_hidden.astype(BF16)
            merged_low = v_low[idx, rows, :]
            pre = nn(merged_low, mlp_bf[block, 0])
            tan = jnp.tanh(GELU_A * (pre + GELU_B * pre * pre * pre))
            act = (0.5 * pre * (1.0 + tan)).astype(BF16)
            slope = 0.5 * (1.0 + tan) + 0.5 * pre * (1.0 - tan * tan) * (
                GELU_A * (1.0 + 3.0 * GELU_B * pre * pre)
            )
            d_pre = (nn(d_branch, mlp_bf[block, 1]) * slope).astype(BF16)
            dmlp[block, 0] += tn(merged_low, d_pre)
            dmlp[block, 1] += tn(d_branch, act)
            d_merged = d_hidden + nt(d_pre, mlp_bf[block, 0])
            dv_buf[rows, :] = d_merged
            u_buf[rows, :] = d_merged.astype(BF16)

        rows_loop(pixels, 256, mlp_rows)
        for half in halves:
            n_send[half] = narrow(nn(itxt[...], u_buf[:, cols(half)]))
            go(4, half, n_send.at[half], s_recv.at[half])

        @pl.when(later)
        def _():
            grads_out(block + 1, "near", (1,))
            shares_finish(block + 1)

        which = NB * lap + block
        for half in halves:
            come(4, half, n_send.at[half], s_recv.at[half])
            w_send[half] = broad(nn(pixt[...], s_recv[half].reshape(spectra, LANES)))
            go(5, half, w_send.at[half], d_mix.at[which, half])

        @pl.when(later)
        def _():
            grads_out(block + 1, "cross", (2,))
            grads_out(block + 1, "near", (2,))

        for half in halves:
            come(5, half, w_send.at[half], d_mix.at[which, half])

        def turned_of(d_mixed):
            wide = d_mixed.astype(F32).reshape(RANKS, 2, SLOTS, chans)
            return jnp.stack([wide[:, 1], -wide[:, 0]], 1).reshape(rows_mix, chans).astype(BF16)

        for half in halves:
            for t in range(3):
                d_mixed = rows_of(d_mix.at[which], t)

                def mixed_by(kind):
                    parts = [
                        jnp.concatenate(
                            [w_all[block, piece_of(kind, k, zh, y), t, part, cols(half), :] for k in halves], axis=1
                        )
                        for part in range(2)
                    ]
                    return nt(d_mixed, jnp.concatenate(parts, axis=0))

                by_real, by_imag = swapped(jnp.where(hi, mixed_by(0), mixed_by(1)))
                d_coef = jnp.stack([by_real[:, 0] + by_imag[:, 1], by_real[:, 1] - by_imag[:, 0]], 1)
                w_send[half, :, t] = d_coef.reshape(RANKS, 2 * SLOTS, LANES).astype(BF16)
            go(6, half, w_send.at[half], b_recv.at[half])

        @pl.when(jnp.logical_and(lap == 1, block == 0))
        def _():
            shares_start(block)

        @pl.when(lap == 1)
        def _():
            for t in range(3):
                others = []
                for turn in range(ROLL):
                    d_mixed = rows_of(d_mix.at[NB * turn + block], t)
                    others.append((d_mixed, turned_of(d_mixed)))
                for kind in range(2):
                    keep = hi if kind == 0 else jnp.logical_not(hi)
                    kept = [
                        jnp.where(
                            keep, rows_of(a_own.at[NB * (1 - turn) + block], t).astype(F32), 0.0
                        ).astype(BF16)
                        for turn in range(ROLL)
                    ]
                    for part in range(2):
                        grad = tn(kept[0], others[0][part]) + tn(kept[1], others[1][part])
                        for half in range(2):
                            dwf[piece_of(kind, half, zh, y), t, part] = grad[
                                :, half * LANES : (half + 1) * LANES
                            ]
            dw_own[block] = dwf[0]
            for k in range(3):
                dw_send[block, k] = dwf[1 + k].astype(BF16)

            grads_out(block, "far", (0,))

        @pl.when(jnp.logical_and(lap == 1, block == 0))
        def _():
            grads_out(block, "far", (1, 2))

        for half in halves:
            come(6, half, w_send.at[half], b_recv.at[half])
            n_send[half] = narrow(nn(pfxt[...], b_recv[half].reshape(triples, LANES)))
            go(7, half, n_send.at[half], y_recv.at[half])

        @pl.when(early)
        def _():
            grads_out(block, "far", (1, 2))
            grads_out(block, "cross", (0, 1))
            grads_out(block, "near", (0,))

        @pl.when(jnp.logical_and(lap == 1, block == 0))
        def _():
            grads_out(block, "near", range(third))

        for half in halves:
            come(7, half, n_send.at[half], y_recv.at[half])

        @pl.when(early)
        def _():
            shares_start(block)

        @pl.when(jnp.logical_and(lap == 1, block == 0))
        def _():
            shares_finish(block)

        spectrum = whole(y_recv, spectra)

        def norm_rows(rows):
            normal, inv_std = normal_of(h_all[slot, rows, :])
            d_normed = nn(ftxt[rows, :], spectrum)
            scaled = d_normed * gain_row
            d_gain[block] += jnp.sum(d_normed * normal, axis=0, keepdims=True)
            d_norm_in = inv_std * (
                scaled
                - jnp.mean(scaled, -1, keepdims=True)
                - normal * jnp.mean(scaled * normal, -1, keepdims=True)
            )
            dh_buf[rows, :] = dv_buf[rows, :] + d_norm_in

        rows_loop(pixels, 256, norm_rows)

        @pl.when(jnp.logical_and(lap == 1, block < NB - 1))
        def _():
            settle(block + 1)

    def bwd_step(lap, carry):
        step = ROLL - 1 - lap
        d_pred = misfit[step] + d_state[...]
        d_dec = d_pred.astype(BF16)
        d_small[LANES:] += tn(d_dec, hid_low[step])
        dh_buf[...] = nn(d_dec, code_bf[1])

        def one(k, inner):
            bwd_block(lap, step, NB - 1 - k)
            return inner

        lax.fori_loop(0, NB, one, 0)
        d_enc = dh_buf[...].astype(BF16)
        d_small[:LANES] += tn(x_low[step].reshape(pixels, LANES), d_enc)

        @pl.when(lap == 0)
        def _():
            d_state[...] = d_pred + nt(d_enc, code_bf[0])

        return carry

    lax.fori_loop(0, ROLL, bwd_step, 0)

    for b in range(NB):
        d_small[LANES - NB + b : LANES - NB + b + 1] = d_gain[b]
    sm_send[...] = d_small[...].reshape(sm_send.shape)
    exchange_start(sm_send, sm_recv, sm_sem.at[0], sm_sem.at[1], peers, q)
    for b in range(NB - 1, 0, -1):
        shares_spread(b)
    exchange_wait(sm_send, sm_recv, sm_sem.at[0], sm_sem.at[1])
    share = sm_recv[0]
    for k in range(1, RANKS):
        share = share + sm_recv[k]
    sm_mir_send[...] = share
    swap = remote(sm_mir_send, sm_mir_recv, sm_sem.at[2], sm_sem.at[3], far)
    swap.start()
    grads_out(0, "cross", range(third))
    swap.wait()
    total = sm_mir_send[...] + sm_mir_recv[...]
    scal[1:2] += 0.5 * lane_sums(total * total)
    sm_src[...] = total
    push_blocks(lambda d: sm_src, g_small.at[q], sm_sem.at[4], sm_sem.at[5], peers, q)
    shares_spread(0)
    settle(0)

    me = RANKS * y + ma
    sets = ((dwf.at[0], dwf.at[1], dwf.at[2]), (dwf.at[3], dw_own.at[0], dw_own.at[1]))

    def unit_loads(u):
        part = pl.ds(third * (u % 2), third)
        return [
            pltpu.make_async_copy(array.at[u // 2, part], buffer, lamb_sem.at[u % 2, k])
            for k, (array, buffer) in enumerate(zip((spec_w, spec_m, spec_v), sets[u % 2]))
        ]

    for u in range(2):
        for copy in unit_loads(u):
            copy.start()

    def spread_start(value, landing, sems):
        for bits in range(2 * RANKS - 1, 0, -1):
            other = {"lat": flip(y, bits // RANKS, 2), "ma": flip(ma, bits % RANKS, RANKS)}
            remote(value, landing.at[me], sems[0], sems[1], other).start()
        pltpu.make_async_copy(value, landing.at[me], sems[1]).start()

    def spread_total(landing, sems):
        bytes_wait(landing, sems[1])
        bytes_wait(landing.at[pl.ds(0, 2 * RANKS - 1)], sems[0])
        total = landing[0]
        for k in range(1, 2 * RANKS):
            total = total + landing[k]
        return jnp.broadcast_to(jnp.sum(total, axis=1, keepdims=True), total.shape)

    first_sems, second_sems = (sm_sem.at[6], sm_sem.at[7]), (sm_sem.at[8], sm_sem.at[9])
    spread_start(scal, scal_recv, first_sems)
    for copy in ml_loads:
        copy.wait()
    total = spread_total(scal_recv, first_sems)
    scalars[:8] = total

    scale = clip_norm / jnp.maximum(jnp.sqrt(total[1:2, :1]), clip_norm)
    first_inv = 1.0 / small[1, FIRST_ROW : FIRST_ROW + 1, :1]
    second_inv = 1.0 / small[1, SECOND_ROW : SECOND_ROW + 1, :1]

    def direction_of(weight_old, first, second, grad):
        grad = grad * scale
        first_new = (beta_first * first + (1.0 - beta_first) * grad) * first_inv
        second_new = (beta_second * second + (1.0 - beta_second) * grad * grad) * second_inv
        return first_new / (jnp.sqrt(second_new) + adam_eps) + weight_decay * weight_old

    for u in range(2 * NB):
        for copy in unit_loads(u):
            copy.wait()
        w_buf, m_buf, v_buf = sets[u % 2]

        def one_degree(t, carry, u=u, w_buf=w_buf, m_buf=m_buf, v_buf=v_buf):
            for part in range(2):
                step_dir = direction_of(
                    w_buf[t, part], m_buf[t, part], v_buf[t, part], g_spec[u // 2, third * (u % 2) + t, part]
                )
                dirs[u // 2 : u // 2 + 1] += lane_sums(step_dir * step_dir)
            return carry

        lax.fori_loop(0, third, one_degree, 0)
        if u + 2 < 2 * NB:
            for copy in unit_loads(u + 2):
                copy.start()
    for b in range(NB):
        old = ml_buf[0, b]
        step_dir = direction_of(old, ml_buf[1, b], ml_buf[2, b], ag_src[b].astype(F32))
        row = NB + 2 * b + q // (RANKS // 2)
        for place_row, value in ((row, step_dir), (row + 2 * NB, old)):
            squares = value * value
            lanes = sum(squares[:, k * LANES : (k + 1) * LANES] for k in range(squares.shape[1] // LANES))
            dirs[pl.ds(place_row, 1), :] += 0.5 * jnp.sum(lanes, axis=0, keepdims=True)
    spread_start(dirs, dirs_recv, second_sems)

    bytes_wait(g_small, sm_sem.at[5])
    bytes_wait(g_small.at[pl.ds(0, RANKS - 1)], sm_sem.at[4])
    for b in range(NB):
        bytes_wait(g_mlp.at[b], ag_recv_sem.at[b])
        bytes_wait(rs_send.at[pl.ds(0, RANKS - 1)], ag_send_sem.at[b])
        bytes_wait(mir_send.at[b], mir_send_sem.at[b])
        bytes_wait(dw_send.at[b], g_send_sem.at[b])
    scalars[8:] = spread_total(dirs_recv, second_sems)


def call_train(chunks, weights, tables, small_in, area):
    vmem = pltpu.VMEM
    dma = pltpu.SemaphoreType.DMA
    spec_w, mlp_w = weights[0], weights[3]
    lon = chunks[0].shape[2]
    pixels, chans = 2 * RANKS * lon, small_in.shape[-1]
    third = spec_w.shape[1] // 2
    triple = (third, 2, chans, LANES)
    narrow, wide = (2, RANKS, 4 * ORDS, LANES), (2, RANKS, 3, 2 * SLOTS, LANES)
    triples, spectra = RANKS * 6 * SLOTS, RANKS * 4 * ORDS
    mlp_shape = mlp_w.shape[1:]
    chunk = (mlp_shape[0] * mlp_shape[1] // RANKS, mlp_shape[2])
    small = (2 * LANES // RANKS, chans)
    b16 = lambda *shape: vmem(shape, BF16)
    f32 = lambda *shape: vmem(shape, F32)
    everywhere = pl.BlockSpec(memory_space=pl.ANY)
    inside = pl.BlockSpec(memory_space=vmem)
    return pl.pallas_call(
        train,
        out_shape=(
            jax.ShapeDtypeStruct(spec_w.shape, F32),
            jax.ShapeDtypeStruct(mlp_w.shape, BF16),
            jax.ShapeDtypeStruct((RANKS, *small), F32),
            jax.ShapeDtypeStruct((24, LANES), F32),
        ),
        in_specs=[everywhere] * 17 + [inside] * 2,
        out_specs=[inside] * 4,
        scratch_shapes=[
            b16(triples, spectra), b16(spectra, triples), b16(spectra, triples), b16(triples, spectra),
            b16(spectra, pixels), b16(pixels, spectra), b16(pixels, spectra), b16(spectra, pixels),
            b16(NB, 4, *triple), b16(*mlp_w.shape), f32(2, *mlp_shape),
            b16(*small_in.shape),
            f32(2, RANKS, lon, LANES), f32(ROLL, 2, RANKS, lon, LANES), f32(pixels, LANES), b16(ROLL, 2, RANKS, lon, LANES),
            f32(ROLL, pixels, LANES), f32(pixels, LANES), f32(4 * ROLL, pixels, chans), b16(ROLL, pixels, chans),
            b16(NB * ROLL, pixels, chans), b16(pixels, chans), f32(pixels, chans), f32(pixels, chans),
            b16(*narrow), b16(*narrow), b16(*narrow), b16(*wide), b16(*wide), b16(NB * ROLL, *wide), b16(NB * ROLL, *wide),
            f32(4, *triple), b16(NB, 3, *triple), b16(NB, 3, *triple), f32(NB, *triple), f32(NB, *mlp_shape),
            b16(RANKS, *chunk), b16(RANKS, *chunk), f32(NB, *chunk), f32(NB, *chunk), b16(NB, *chunk),
            f32(2 * LANES, chans), f32(NB, 1, chans), f32(RANKS, *small), f32(RANKS, *small), f32(*small), f32(*small),
            f32(*small), f32(8, LANES), f32(2 * RANKS, 8, LANES),
            f32(3, NB, *chunk), f32(16, LANES), f32(2 * RANKS, 16, LANES),
            dma((8,)), dma((3 * NB,)), dma((4,)), dma((4,)), dma((NB,)), dma((NB,)), dma((8, 2)), dma((8, 2)),
            dma((NB,)), dma((NB,)), dma((2,)), dma((NB,)), dma((NB,)), dma((NB,)), dma((NB,)), dma((10,)),
            dma((2, 3)), dma,
        ],
        compiler_params=pltpu.CompilerParams(
            collective_id=0, has_side_effects=True, vmem_limit_bytes=61 << 20
        ),
    )(*chunks, *weights, *tables, small_in, area)


def chunks_of(field):
    items, lon, lat, width = field.shape
    pairs = lat // 2
    chunks = jnp.moveaxis(field.reshape(items, lon, pairs, 2, width), 1, 3)
    return jnp.concatenate([chunks[0], jnp.roll(chunks[1], pairs // 2, 0)], 0)


def special(
    inputs,
    targets,
    mask,
    var_weight,
    step_count,
    spec_w,
    spec_m,
    spec_v,
    encdec_w,
    encdec_m,
    encdec_v,
    mlp_w,
    mlp_m,
    mlp_v,
    gain_w,
    gain_m,
    gain_v,
):
    zh, y, w, q = place()
    nlon = inputs.shape[1] * lax.axis_size("ma")
    nlat = inputs.shape[2] * lax.axis_size("lat")
    ranked, common = make_tables(nlat, nlon)
    tables = tuple(jnp.asarray(t) for t in (*ranked, *common))
    spare = LANES - C
    x_chunks = chunks_of(jnp.pad(inputs, ((0, 0),) * 3 + ((0, spare),)))
    masks = jnp.broadcast_to(mask.astype(F32)[None, ..., None], (*targets.shape[:-1], 1))
    goal = jnp.concatenate([targets, jnp.zeros((*targets.shape[:-1], spare - 1), F32), masks], -1)
    t_chunks = jnp.stack([chunks_of(goal[0]), chunks_of(goal[1])], 0)
    sines = np.sin((np.arange(nlat) + 0.5) * (math.pi / nlat))
    area = np.repeat((sines / np.mean(sines)).astype(np.float32).reshape(RANKS, 2, 1, 1), LANES, 3)
    step_float = step_count[0].astype(F32)
    fixes = jnp.stack([1.0 - beta_second**step_float, 1.0 - beta_first**step_float])
    var_row = jnp.pad(var_weight.astype(F32), (0, E - C))[None]
    small_in = jnp.stack(
        [
            jnp.concatenate([encdec_w[0], jnp.zeros((LANES - NB - C, E), F32), gain_w], 0),
            jnp.concatenate(
                [
                    encdec_w[1],
                    jnp.zeros((SECOND_ROW - C, E), F32),
                    jnp.broadcast_to(fixes[:, None], (2, E)),
                    var_row,
                    jnp.zeros((LANES - 1 - VAR_ROW, E), F32),
                ],
                0,
            ),
        ]
    )
    spec_grad, mlp_sum, small_sum, sums = call_train(
        (x_chunks.astype(BF16), x_chunks, t_chunks),
        (spec_w, spec_m, spec_v, mlp_w, mlp_m, mlp_v),
        tables,
        small_in,
        jnp.asarray(area),
    )
    grad_mlp = mlp_sum.astype(F32)
    small_sum = small_sum.reshape(2, LANES, E)
    grad_encdec = small_sum[:, :C]
    grad_gain = small_sum[0, LANES - NB :]
    sums = sums[:, 0]
    loss_value = sums[0]
    weight_square = sums[2 : 2 + NB]
    grad_norm = jnp.sqrt(sums[1])
    scale = clip_norm / jnp.maximum(grad_norm, clip_norm)
    spec_m_new, spec_v_new, direction = adaptive(
        spec_w, spec_m, spec_v, spec_grad * scale, step_float
    )
    dir_square = sums[8 : 8 + NB]
    weight_norm = jnp.sqrt(weight_square)
    dir_norm = jnp.sqrt(dir_square)
    trust = weight_norm / (dir_norm + 1e-06)
    spec_new = spec_w - learn_rate * trust[:, None, None, None, None] * direction
    encdec_new, encdec_m_new, encdec_v_new, encdec_norms = lamb_dense(
        encdec_w, encdec_m, encdec_v, grad_encdec * scale, step_float, 2
    )
    mlp_m_new, mlp_v_new, mlp_dir = adaptive(mlp_w, mlp_m, mlp_v, grad_mlp * scale, step_float)
    mlp_dir_norm = jnp.sqrt(sums[8 + NB : 8 + 3 * NB])
    mlp_weight_norm = jnp.sqrt(sums[8 + 3 * NB : 8 + 5 * NB])
    mlp_trust = (mlp_weight_norm / (mlp_dir_norm + 1e-06)).reshape(NB, 2, 1, 1)
    mlp_new = mlp_w - learn_rate * mlp_trust * mlp_dir
    mlp_norms = jnp.stack([mlp_weight_norm, mlp_dir_norm], 1)
    gain_new, gain_m_new, gain_v_new, gain_norms = lamb_dense(
        gain_w, gain_m, gain_v, grad_gain * scale, step_float, NB
    )
    matrix_norms = jnp.concatenate(
        [jnp.stack([weight_norm, dir_norm], 1), encdec_norms, mlp_norms, gain_norms], 0
    )
    return (
        loss_value,
        grad_norm,
        matrix_norms,
        spec_new,
        spec_m_new,
        spec_v_new,
        spec_new.astype(jnp.bfloat16),
        encdec_new,
        encdec_m_new,
        encdec_v_new,
        encdec_new.astype(jnp.bfloat16),
        mlp_new,
        mlp_m_new,
        mlp_v_new,
        mlp_new.astype(jnp.bfloat16),
        gain_new,
        gain_m_new,
        gain_v_new,
        gain_new.astype(jnp.bfloat16),
    )


def local(mesh, *args):
    inputs, spec_w = args[0], args[5]
    lat = inputs.shape[2] * mesh.shape["lat"]
    fits = (
        dict(mesh.shape) == {"lat": 2, "ma": RANKS}
        and inputs.shape[0] == 2
        and lat == 2 * RANKS
        and spec_w.shape[1] * RANKS == L
    )
    return (special if fits else general)(*args)


def solution(mesh):
    placed = (
        P(None, "ma", "lat", None),
        P(None, None, "ma", "lat", None),
        P(None, "ma", "lat"),
        P(),
        P(),
        P(None, "ma", None, None, "lat"),
        P(None, "ma", None, None, "lat"),
        P(None, "ma", None, None, "lat"),
        P(),
        P(),
        P(),
        P(),
        P(),
        P(),
        P(),
        P(),
        P(),
    )
    return jax.shard_map(
        functools.partial(local, mesh),
        mesh=mesh,
        in_specs=placed,
        out_specs=(
            P(),
            P(),
            P(),
            P(None, "ma", None, None, "lat"),
            P(None, "ma", None, None, "lat"),
            P(None, "ma", None, None, "lat"),
            P(None, "ma", None, None, "lat"),
            P(),
            P(),
            P(),
            P(),
            P(),
            P(),
            P(),
            P(),
            P(),
            P(),
            P(),
            P(),
        ),
        check_vma=False,
    )
```

```python
import functools
import math

import jax
import jax.numpy as jnp
import ml_dtypes
import numpy as np
from jax import lax
from jax.experimental import pallas as pl
from jax.experimental.pallas import tpu as pltpu
from jax.sharding import PartitionSpec as P

E = 256
C = 73
L = 96
NB = 3
ROLL = 2


beta_first = 0.9
beta_second = 0.999
adam_eps = 1e-08
weight_decay = 0.01
learn_rate = 0.4
clip_norm = 0.05
norm_eps = 1e-05


def legendre(orders, angles):
    cosines = jnp.cos(angles)[None, :]
    sines = jnp.sin(angles)[None, :]
    order_col = orders[:, None]
    log_start = 0.5 * (
        jnp.log((2.0 * order_col + 1.0) / (4.0 * math.pi))
        + lax.lgamma(2.0 * order_col + 1.0)
        - 2.0 * lax.lgamma(order_col + 1.0)
        - order_col * math.log(4.0)
    ) + order_col * jnp.log(sines)
    starting = jnp.exp(log_start)

    def advance(carry, degree):
        previous, earlier = carry
        upper = jnp.maximum(degree * degree - order_col * order_col, 1.0)
        factor = jnp.sqrt(jnp.maximum(4.0 * degree * degree - 1.0, 1.0) / upper)
        lower = jnp.maximum((degree - 1.0) ** 2 - order_col * order_col, 0.0)
        shrink = jnp.sqrt(lower / jnp.maximum(4.0 * (degree - 1.0) ** 2 - 1.0, 1.0))
        stepped = factor * (cosines * previous - shrink * earlier)
        second = jnp.sqrt(2.0 * order_col + 3.0) * cosines * starting
        value = jnp.where(
            degree < order_col,
            0.0,
            jnp.where(
                degree == order_col, starting, jnp.where(degree == order_col + 1.0, second, stepped)
            ),
        )
        return ((value, previous), value)

    zero_rows = jnp.zeros_like(starting)
    unused, table = lax.scan(advance, (zero_rows, zero_rows), jnp.arange(L, dtype=jnp.float32))
    return table


def dft_tables(orders, count_lon):
    phases = orders[:, None] * jnp.arange(count_lon, dtype=jnp.int32)[None, :] % count_lon
    phase = phases.astype(jnp.float32) * (2.0 * math.pi / count_lon)
    cosines = jnp.cos(phase)
    sines = jnp.sin(phase)
    number = orders.shape[0]
    forward = jnp.stack([cosines, -sines], 1).reshape(2 * number, count_lon)
    factor = jnp.where(orders == 0, 1.0, 2.0)[:, None] / math.sqrt(2.0 * math.pi)
    inverse = jnp.stack([factor * cosines, -factor * sines], 1).reshape(2 * number, count_lon).T
    return (forward, inverse)


def adaptive(weight, first, second, grad, step_float):
    first_new = beta_first * first + (1.0 - beta_first) * grad
    second_new = beta_second * second + (1.0 - beta_second) * grad * grad
    direction = (
        first_new
        / (1.0 - beta_first**step_float)
        / (jnp.sqrt(second_new / (1.0 - beta_second**step_float)) + adam_eps)
        + weight_decay * weight
    )
    return (first_new, second_new, direction)


def lamb_dense(weight, first, second, grad, step_float, groups):
    first_new, second_new, direction = adaptive(weight, first, second, grad, step_float)
    flat_weight = weight.reshape(groups, -1)
    flat_dir = direction.reshape(groups, -1)
    weight_norm = jnp.sqrt(jnp.sum(flat_weight * flat_weight, 1))
    dir_norm = jnp.sqrt(jnp.sum(flat_dir * flat_dir, 1))
    trust = weight_norm / (dir_norm + 1e-06)
    new_weight = (flat_weight - learn_rate * trust[:, None] * flat_dir).reshape(weight.shape)
    return (new_weight, first_new, second_new, jnp.stack([weight_norm, dir_norm], 1))


def norm_forward(hidden, gain_vec):
    centre = jnp.mean(hidden, -1, keepdims=True)
    centred = hidden - centre
    inv_std = lax.rsqrt(jnp.mean(centred * centred, -1, keepdims=True) + norm_eps)
    normal = centred * inv_std
    return ((normal * gain_vec).astype(jnp.bfloat16), normal, inv_std)


def norm_backward(d_normed, normal, inv_std, gain_vec):
    scaled = d_normed * gain_vec
    d_gain = jnp.sum(d_normed * normal, axis=(0, 1, 2))
    d_hidden = inv_std * (
        scaled
        - jnp.mean(scaled, -1, keepdims=True)
        - normal * jnp.mean(scaled * normal, -1, keepdims=True)
    )
    return (d_hidden, d_gain)


def mlp_forward(merged, weights):
    merged_low = merged.astype(jnp.bfloat16)
    pre_act = jnp.einsum(
        "jibe,ef->jibf", merged_low, weights[0], preferred_element_type=jnp.float32
    )
    gelu_out = jax.nn.gelu(pre_act).astype(jnp.bfloat16)
    hidden = merged + jnp.einsum(
        "jibf,ef->jibe", gelu_out, weights[1], preferred_element_type=jnp.float32
    )
    return (hidden, (merged_low, pre_act, gelu_out))


def mlp_backward(d_hidden, stored, weights):
    merged_low, pre_act, gelu_out = stored
    d_branch = d_hidden.astype(jnp.bfloat16)
    d_gelu = jnp.einsum("jibe,ef->jibf", d_branch, weights[1], preferred_element_type=jnp.float32)
    unused, pullback = jax.vjp(jax.nn.gelu, pre_act)
    d_pre = pullback(d_gelu)[0].astype(jnp.bfloat16)
    grad_out = jnp.einsum("jibf,jibe->ef", gelu_out, d_branch, preferred_element_type=jnp.float32)
    grad_in = jnp.einsum("jibe,jibf->ef", merged_low, d_pre, preferred_element_type=jnp.float32)
    d_merged = d_hidden + jnp.einsum(
        "jibf,ef->jibe", d_pre, weights[0], preferred_element_type=jnp.float32
    )
    return (d_merged, jnp.stack([grad_in, grad_out], 0))


def general(
    inputs,
    targets,
    mask,
    var_weight,
    step_count,
    spec_w,
    spec_m,
    spec_v,
    encdec_w,
    encdec_m,
    encdec_v,
    mlp_w,
    mlp_m,
    mlp_v,
    gain_w,
    gain_m,
    gain_v,
):
    n_ma = lax.axis_size("ma")
    n_lat = lax.axis_size("lat")
    ma_pos = lax.axis_index("ma")
    lat_pos = lax.axis_index("lat")
    batch = inputs.shape[0]
    lon_loc = inputs.shape[1]
    lat_loc = inputs.shape[2]
    nlon_all = lon_loc * n_ma
    nlat_all = lat_loc * n_lat
    orders_loc = L // n_ma
    angles = (jnp.arange(nlat_all, dtype=jnp.float32) + 0.5) * (math.pi / nlat_all)
    local_orders = ma_pos * orders_loc + jnp.arange(orders_loc, dtype=jnp.int32)
    table = legendre(local_orders.astype(jnp.float32), angles)
    quadrature = jnp.sin(angles) * (math.sqrt(2.0 * math.pi) / nlon_all * math.pi / nlat_all)
    fwd_leg = (table * quadrature[None, None, :]).astype(jnp.bfloat16)
    inv_leg = table.astype(jnp.bfloat16)
    fwd_table, inv_table = dft_tables(jnp.arange(L, dtype=jnp.int32), nlon_all)
    fwd_four = fwd_table.astype(jnp.bfloat16)
    inv_four = inv_table.astype(jnp.bfloat16)
    fwd_back = fwd_four.T
    inv_back = inv_four.T
    sines = jnp.sin(angles)
    area = sines / jnp.mean(sines)
    area_rows = lax.dynamic_slice_in_dim(area, lat_pos * lat_loc, lat_loc)
    mask_grid = jnp.transpose(mask, (1, 2, 0)).astype(jnp.float32)
    pixel_weight = (
        area_rows[None, :, None, None]
        * var_weight.astype(jnp.float32)[None, None, None, :]
        * mask_grid[:, :, :, None]
    )
    grid_targets = jnp.transpose(targets, (0, 2, 3, 1, 4))
    denom = float(batch * nlon_all * nlat_all * C)

    def apply_table(table_full, block_in):
        whole_out = jnp.einsum(
            "ok,kibe->oibe",
            table_full,
            lax.all_to_all(block_in, "ma", split_axis=3, concat_axis=0, tiled=True),
            preferred_element_type=jnp.float32,
        )
        return lax.all_to_all(
            whole_out.astype(jnp.bfloat16), "ma", split_axis=0, concat_axis=3, tiled=True
        ).astype(whole_out.dtype)

    def spectral_backward(d_filtered, owned, weight_blk):
        d_rows = apply_table(inv_back, d_filtered.astype(jnp.bfloat16)).astype(jnp.bfloat16)
        d_spec = lax.all_to_all(d_rows, "lat", split_axis=3, concat_axis=1, tiled=True)
        out_width = d_spec.shape[3]
        d_mixed = jnp.einsum(
            "lmi,mpibo->lmpbo",
            inv_leg,
            d_spec.reshape(orders_loc, 2, nlat_all, batch, out_width),
            preferred_element_type=jnp.float32,
        ).astype(jnp.bfloat16)
        d_own = lax.all_to_all(d_mixed, "ma", split_axis=0, concat_axis=1, tiled=True)
        real_w = weight_blk[:, 0]
        imag_w = weight_blk[:, 1]
        d_real = d_own[:, :, 0]
        d_imag = d_own[:, :, 1]
        d_coef_real = jnp.einsum(
            "lmbo,leo->lmbe", d_real, real_w, preferred_element_type=jnp.float32
        ) + jnp.einsum("lmbo,leo->lmbe", d_imag, imag_w, preferred_element_type=jnp.float32)
        d_coef_imag = jnp.einsum(
            "lmbo,leo->lmbe", d_imag, real_w, preferred_element_type=jnp.float32
        ) - jnp.einsum("lmbo,leo->lmbe", d_real, imag_w, preferred_element_type=jnp.float32)
        grad_real = jnp.einsum(
            "lmbe,lmbo->leo", owned[:, :, 0], d_real, preferred_element_type=jnp.float32
        ) + jnp.einsum("lmbe,lmbo->leo", owned[:, :, 1], d_imag, preferred_element_type=jnp.float32)
        grad_imag = jnp.einsum(
            "lmbe,lmbo->leo", owned[:, :, 0], d_imag, preferred_element_type=jnp.float32
        ) - jnp.einsum("lmbe,lmbo->leo", owned[:, :, 1], d_real, preferred_element_type=jnp.float32)
        d_owned = jnp.stack([d_coef_real, d_coef_imag], 2)
        d_coeffs = lax.all_to_all(
            d_owned.astype(jnp.bfloat16), "ma", split_axis=1, concat_axis=0, tiled=True
        ).astype(d_owned.dtype)
        d_full = jnp.einsum(
            "lmi,lmpbe->mpibe",
            fwd_leg.astype(jnp.float32),
            d_coeffs,
            precision=lax.Precision.HIGHEST,
        ).reshape(2 * orders_loc, nlat_all, batch, E)
        d_spec_rows = lax.psum_scatter(
            d_full.astype(jnp.bfloat16), "lat", scatter_dimension=1, tiled=True
        )
        return (apply_table(fwd_back, d_spec_rows), jnp.stack([grad_real, grad_imag], 1))

    spec_bf = spec_w.astype(jnp.bfloat16)
    encdec_bf = encdec_w.astype(jnp.bfloat16)
    mlp_bf = mlp_w.astype(jnp.bfloat16)

    def model_backward(d_pred, stored):
        state_low, hidden_low, records = stored
        d_dec = d_pred.astype(jnp.bfloat16)
        grad_dec = jnp.einsum(
            "jibe,jibc->ce", hidden_low, d_dec, preferred_element_type=jnp.float32
        )
        d_hidden = jnp.einsum(
            "jibc,ce->jibe", d_dec, encdec_bf[1], preferred_element_type=jnp.float32
        )
        spec_grads = [None] * NB
        mlp_grads = [None] * NB
        gain_grads = [None] * NB
        for block_idx in reversed(range(NB)):
            normal, inv_std, owned, mlp_kept = records[block_idx]
            d_merged, mlp_grads[block_idx] = mlp_backward(d_hidden, mlp_kept, mlp_bf[block_idx])
            d_normed, spec_grads[block_idx] = spectral_backward(d_merged, owned, spec_bf[block_idx])
            d_norm_in, gain_grads[block_idx] = norm_backward(
                d_normed, normal, inv_std, gain_w[block_idx]
            )
            d_hidden = d_merged + d_norm_in
        d_enc = d_hidden.astype(jnp.bfloat16)
        grad_enc = jnp.einsum("jibc,jibe->ce", state_low, d_enc, preferred_element_type=jnp.float32)
        d_state = d_pred + jnp.einsum(
            "jibe,ce->jibc", d_enc, encdec_bf[0], preferred_element_type=jnp.float32
        )
        return (
            d_state,
            (
                jnp.stack([grad_enc, grad_dec], 0),
                jnp.stack(spec_grads, 0),
                jnp.stack(mlp_grads, 0),
                jnp.stack(gain_grads, 0),
            ),
        )

    state = jnp.transpose(inputs, (1, 2, 0, 3))
    history = []
    loss_part = jnp.zeros((), jnp.float32)
    for section_idx in range(ROLL):
        model_state_low = state.astype(jnp.bfloat16)
        hidden = jnp.einsum(
            "jibc,ce->jibe", model_state_low, encdec_bf[0], preferred_element_type=jnp.float32
        )
        model_records = []
        for model_block_idx in range(NB):
            model_normed, model_normal, model_inv_std = norm_forward(
                hidden, gain_w[model_block_idx]
            )
            spectral_weight_blk = spec_bf[model_block_idx]
            spec_rows = apply_table(fwd_four, model_normed).astype(jnp.bfloat16)
            piece = lax.all_gather(spec_rows, "lat", axis=1, tiled=True)
            row_width = piece.shape[1]
            paired = piece.reshape(orders_loc, 2, row_width, piece.shape[2], piece.shape[3])
            coeffs = jnp.einsum(
                "lmi,mpibe->lmpbe", fwd_leg, paired, preferred_element_type=jnp.float32
            ).astype(jnp.bfloat16)
            spectral_owned = lax.all_to_all(coeffs, "ma", split_axis=0, concat_axis=1, tiled=True)
            spectral_real_w = spectral_weight_blk[:, 0]
            spectral_imag_w = spectral_weight_blk[:, 1]
            mixed_real = jnp.einsum(
                "lmbe,leo->lmbo",
                spectral_owned[:, :, 0],
                spectral_real_w,
                preferred_element_type=jnp.float32,
            ) - jnp.einsum(
                "lmbe,leo->lmbo",
                spectral_owned[:, :, 1],
                spectral_imag_w,
                preferred_element_type=jnp.float32,
            )
            mixed_imag = jnp.einsum(
                "lmbe,leo->lmbo",
                spectral_owned[:, :, 0],
                spectral_imag_w,
                preferred_element_type=jnp.float32,
            ) + jnp.einsum(
                "lmbe,leo->lmbo",
                spectral_owned[:, :, 1],
                spectral_real_w,
                preferred_element_type=jnp.float32,
            )
            mixed_owned = jnp.stack([mixed_real, mixed_imag], 2).astype(jnp.bfloat16)
            mixed = lax.all_to_all(mixed_owned, "ma", split_axis=1, concat_axis=0, tiled=True)
            spec_out = jnp.einsum(
                "lmi,lmpbo->mpibo", inv_leg, mixed, preferred_element_type=jnp.float32
            )
            spec_out = spec_out.astype(jnp.bfloat16).reshape(
                2 * orders_loc, nlat_all, batch, mixed.shape[4]
            )
            rows_out = lax.all_to_all(spec_out, "lat", split_axis=1, concat_axis=3, tiled=True)
            filtered = apply_table(inv_four, rows_out)
            hidden, model_mlp_kept = mlp_forward(hidden + filtered, mlp_bf[model_block_idx])
            model_records.append((model_normal, model_inv_std, spectral_owned, model_mlp_kept))
        model_hidden_low = hidden.astype(jnp.bfloat16)
        prediction = state + jnp.einsum(
            "jibe,ce->jibc", model_hidden_low, encdec_bf[1], preferred_element_type=jnp.float32
        )
        prediction, stored = (prediction, (model_state_low, model_hidden_low, model_records))
        misfit = prediction - grid_targets[section_idx]
        loss_part = loss_part + jnp.sum(pixel_weight * misfit * misfit) / denom
        history.append((stored, misfit))
        state = prediction
    d_state = jnp.zeros_like(state)
    totals = None
    for section_idx in reversed(range(ROLL)):
        stored, misfit = history[section_idx]
        d_pred = 2.0 * pixel_weight * misfit / denom + d_state
        d_state, section_grads = model_backward(d_pred, stored)
        totals = section_grads if totals is None else jax.tree.map(jnp.add, totals, section_grads)
    grad_encdec, spec_grad, grad_mlp, grad_gain = totals
    grad_encdec, grad_mlp, grad_gain, loss_value, spec_square, weight_square = lax.psum(
        (
            grad_encdec,
            grad_mlp,
            grad_gain,
            loss_part,
            jnp.sum(spec_grad * spec_grad),
            jnp.sum(spec_w * spec_w, axis=(1, 2, 3, 4)),
        ),
        ("lat", "ma"),
    )
    total_square = (
        spec_square
        + jnp.sum(grad_encdec * grad_encdec)
        + jnp.sum(grad_mlp * grad_mlp)
        + jnp.sum(grad_gain * grad_gain)
    )
    grad_norm = jnp.sqrt(total_square)
    scale = clip_norm / jnp.maximum(grad_norm, clip_norm)
    step_float = step_count[0].astype(jnp.float32)
    spec_m_new, spec_v_new, direction = adaptive(
        spec_w, spec_m, spec_v, spec_grad * scale, step_float
    )
    dir_square = lax.psum(jnp.sum(direction * direction, axis=(1, 2, 3, 4)), ("lat", "ma"))
    weight_norm = jnp.sqrt(weight_square)
    dir_norm = jnp.sqrt(dir_square)
    trust = weight_norm / (dir_norm + 1e-06)
    spec_new = spec_w - learn_rate * trust[:, None, None, None, None] * direction
    encdec_new, encdec_m_new, encdec_v_new, encdec_norms = lamb_dense(
        encdec_w, encdec_m, encdec_v, grad_encdec * scale, step_float, 2
    )
    mlp_new, mlp_m_new, mlp_v_new, mlp_norms = lamb_dense(
        mlp_w, mlp_m, mlp_v, grad_mlp * scale, step_float, 2 * NB
    )
    gain_new, gain_m_new, gain_v_new, gain_norms = lamb_dense(
        gain_w, gain_m, gain_v, grad_gain * scale, step_float, NB
    )
    matrix_norms = jnp.concatenate(
        [jnp.stack([weight_norm, dir_norm], 1), encdec_norms, mlp_norms, gain_norms], 0
    )
    return (
        loss_value,
        grad_norm,
        matrix_norms,
        spec_new,
        spec_m_new,
        spec_v_new,
        spec_new.astype(jnp.bfloat16),
        encdec_new,
        encdec_m_new,
        encdec_v_new,
        encdec_new.astype(jnp.bfloat16),
        mlp_new,
        mlp_m_new,
        mlp_v_new,
        mlp_new.astype(jnp.bfloat16),
        gain_new,
        gain_m_new,
        gain_v_new,
        gain_new.astype(jnp.bfloat16),
    )


RANKS = 16
ORDS = L // RANKS
SLOTS = 8
F32 = jnp.float32
BF16 = jnp.bfloat16


def legendre_f64(nlat):
    theta = (np.arange(nlat) + 0.5) * (math.pi / nlat)
    cosines, sines = np.cos(theta), np.sin(theta)
    table = np.zeros((L, L, nlat))
    for m in range(L):
        log_start = 0.5 * (
            math.log((2.0 * m + 1.0) / (4.0 * math.pi))
            + math.lgamma(2.0 * m + 1.0)
            - 2.0 * math.lgamma(m + 1.0)
            - m * math.log(4.0)
        ) + m * np.log(sines)
        table[m, m] = np.exp(log_start)
        if m + 1 < L:
            table[m + 1, m] = math.sqrt(2.0 * m + 3.0) * cosines * table[m, m]
        for k in range(m + 2, L):
            factor = math.sqrt((4.0 * k * k - 1.0) / (k * k - m * m))
            shrink = math.sqrt(((k - 1.0) ** 2 - m * m) / (4.0 * (k - 1.0) ** 2 - 1.0))
            table[k, m] = factor * (cosines * table[k - 1, m] - shrink * table[k - 2, m])
    return table, sines


def low_np(array):
    return array.astype(np.float32).astype(ml_dtypes.bfloat16)


def slot_map():
    degree = np.full((RANKS, 3, SLOTS), -1)
    order = np.full((RANKS, SLOTS), -1)
    for d in range(RANKS):
        y, w, xc = d // 8, (d // 4) % 2, d % 4
        lo, hi = 4 * w + xc, 4 * (3 - w) + xc
        n_lo, n_hi = (6 * lo + 5) // RANKS + 1, (6 * hi + 5) // RANKS + 1
        for group, first, count in ((hi, 0, n_hi), (lo, SLOTS - n_lo, n_lo)):
            for r in range(count):
                order[d, first + r] = r
                for t in range(3):
                    degree[d, t, first + r] = 6 * group + 3 * y + t
    return degree, order


def make_tables(nlat, nlon):
    table, sines = legendre_f64(nlat)
    quadrature = sines * (math.sqrt(2.0 * math.pi) / nlon * math.pi / nlat)
    fwd_leg = np.asarray(low_np(table * quadrature[None, None, :]))
    inv_leg = np.asarray(low_np(table))
    degree, order = slot_map()
    shape = (RANKS, RANKS, 3, 2, SLOTS, RANKS, ORDS, 2, 2)
    fwd = np.zeros(shape, ml_dtypes.bfloat16)
    inv = np.zeros(shape, ml_dtypes.bfloat16)
    for g in range(RANKS):
        for d in range(RANKS):
            for slot in range(SLOTS):
                r = order[d, slot]
                if r < 0:
                    continue
                for t in range(3):
                    k, m = degree[d, t, slot], g + RANKS * r
                    for p in range(2):
                        fwd[g, d, t, p, slot, :, r, p, :] = fwd_leg[k, m].reshape(RANKS, 2)
                        inv[g, d, t, p, slot, :, r, p, :] = inv_leg[k, m].reshape(RANKS, 2)
    rows = RANKS * 3 * 2 * SLOTS
    cols = RANKS * ORDS * 2 * 2
    fwd = fwd.reshape(RANKS, rows, cols)
    inv = inv.reshape(RANKS, rows, cols)
    phase = 2.0 * math.pi * (np.arange(L)[:, None] * np.arange(nlon)[None, :] % nlon) / nlon
    scale = np.where(np.arange(L) == 0, 1.0, 2.0)[:, None] / math.sqrt(2.0 * math.pi)
    four = low_np(np.stack([np.cos(phase), -np.sin(phase)], 1))
    back = low_np(np.stack([scale * np.cos(phase), -scale * np.sin(phase)], 1))
    def wide(small):
        out = np.zeros((RANKS, ORDS, 2, 2, 2, nlon), ml_dtypes.bfloat16)
        ordered = small.reshape(ORDS, RANKS, 2, nlon).transpose(1, 0, 2, 3)
        for il in range(2):
            out[:, :, :, il, il, :] = ordered
        return out.reshape(cols, 2 * nlon)

    def turn(array):
        return np.ascontiguousarray(np.swapaxes(array, -1, -2))

    four, back = wide(four), wide(back)
    return (fwd, turn(inv), turn(fwd), inv), (four, turn(back), turn(four), back)


def place():
    ma = lax.axis_index("ma")
    y = lax.axis_index("lat")
    z = ma // 4
    zh = z // 2
    w = z + zh * (3 - 2 * z)
    return zh, y, w, 8 * y + 4 * w + ma % 4


def device_of(zh, q):
    w = (q // 4) % 2
    z = w + zh * (3 - 2 * w)
    return {"lat": q // 8, "ma": 4 * z + q % 4}


def nn(a, b):
    return lax.dot_general(a, b, (((1,), (0,)), ((), ())), preferred_element_type=F32)


def nt(a, b):
    return lax.dot_general(a, b, (((1,), (1,)), ((), ())), preferred_element_type=F32)


def tn(a, b):
    return lax.dot_general(a, b, (((0,), (0,)), ((), ())), preferred_element_type=F32)


def piece_of(kind, half, zh, y):
    return 2 - 2 * ((kind + zh) % 2) + (half + y) % 2


def weight_of(w_all, block, kind, t, part, zh, y):
    return jnp.concatenate(
        [w_all[block, piece_of(kind, half, zh, y), t, part] for half in range(2)], axis=1
    )


def hi_rows(w):
    slot = lax.broadcasted_iota(jnp.int32, (RANKS * 2 * SLOTS, 1), 0) % SLOTS
    return slot < 6 - w


GELU_A = math.sqrt(2.0 / math.pi)
GELU_B = 0.044715


def normal_of(hidden):
    centre = jnp.mean(hidden, -1, keepdims=True)
    centred = hidden - centre
    inv_std = lax.rsqrt(jnp.mean(centred * centred, -1, keepdims=True) + norm_eps)
    return centred * inv_std, inv_std


def rows_loop(total, step, body):
    def one(k, carry):
        body(pl.ds(pl.multiple_of(k * step, step), step))
        return carry

    lax.fori_loop(0, total // step, one, 0)


MESH = pl.DeviceIdType.MESH
LANES = 128
MASK_LANE = LANES - 1
VAR_ROW, FIRST_ROW, SECOND_ROW = 124, 123, 122


def greet_all(between=None):
    barrier = pltpu.get_barrier_semaphore()
    me = 2 * RANKS // 2 * lax.axis_index("lat") + lax.axis_index("ma")

    def greet(s, carry):
        other = (me + s) % (2 * RANKS)
        pl.semaphore_signal(
            barrier, inc=1, device_id={"lat": other // RANKS, "ma": other % RANKS}, device_id_type=MESH
        )
        return carry

    lax.fori_loop(1, 2 * RANKS, greet, 0)
    if between is not None:
        between()
    pl.semaphore_wait(barrier, 2 * RANKS - 1)


def remote(src, dst, send_sem, recv_sem, device):
    return pltpu.make_async_remote_copy(
        src_ref=src,
        dst_ref=dst,
        send_sem=send_sem,
        recv_sem=recv_sem,
        device_id=device,
        device_id_type=MESH,
    )


def bytes_wait(ref, sem):
    pltpu.make_async_copy(ref, ref, sem).wait()


def flip(value, bits, span):
    out, unit = 0, 1
    while unit < span:
        digit = (value // unit) % 2
        out = out + unit * (1 - digit if bits // unit % 2 else digit)
        unit *= 2
    return out


def peers_of(zh, q):
    ranks = [flip(q, s, RANKS) for s in range(RANKS - 1, 0, -1)]
    return [(d, device_of(zh, d)) for d in ranks]


def push_blocks(source_of, landing, send_sem, recv_sem, peers, q):
    for d, device in peers:
        remote(source_of(d), landing, send_sem, recv_sem, device).start()
    pltpu.make_async_copy(source_of(q), landing, recv_sem).start()


def exchange_start(send, recv, send_sem, recv_sem, peers, q):
    push_blocks(lambda d: send.at[d], recv.at[q], send_sem, recv_sem, peers, q)


def exchange_wait(send, recv, send_sem, recv_sem):
    bytes_wait(recv, recv_sem)
    bytes_wait(send.at[pl.ds(0, RANKS - 1)], send_sem)


def exchange(send, recv, send_sem, recv_sem, peers, q):
    exchange_start(send, recv, send_sem, recv_sem, peers, q)
    exchange_wait(send, recv, send_sem, recv_sem)


def lane_sums(array):
    return jnp.sum(array.reshape(-1, LANES), axis=0, keepdims=True)


def train(
    xb_chunks, x_chunks, t_chunks, spec_w, spec_m, spec_v, mlp_w, mlp_m, mlp_v, r0, r1, r2, r3, f0, f1, f2, f3,
    small, area,
    g_spec, g_mlp, g_small, scalars,
    pfx, pix, pfxt, pixt, ftx, itx, ftxt, itxt, w_all, mlp_bf, mlp_stage, code_bf,
    x_recv, goals, weight, x_low, misfit, d_state, h_all, hid_low, v_low, u_buf, dv_buf, dh_buf,
    n_send, s_recv, y_recv, w_send, b_recv, a_own, d_mix,
    dwf, dw_send, dw_recv, dw_own, dmlp, rs_send, rs_recv, mir_send, mir_recv, ag_src,
    d_small, d_gain, sm_send, sm_recv, sm_mir_send, sm_mir_recv, sm_src, scal, scal_recv,
    ml_buf, dirs, dirs_recv,
    load_sem, stage_sem, once_send, once_recv, w_send_sem, w_recv_sem, x_send, x_recv_sem,
    g_send_sem, g_recv_sem, rs_sem, mir_send_sem, mir_recv_sem, ag_send_sem, ag_recv_sem, sm_sem,
    lamb_sem, ml_sem,
):
    zh, y, w, q = place()
    peers = peers_of(zh, q)
    ma = lax.axis_index("ma")
    xc = ma % 4
    mirror_ma = 4 * (3 - ma // 4) + xc
    near, far, cross = {"lat": 1 - y, "ma": ma}, {"lat": y, "ma": mirror_ma}, {"lat": 1 - y, "ma": mirror_ma}
    pixels, chans = dh_buf.shape
    spectra = pix.shape[0]
    triples = pfx.shape[0]
    third = 3

    loads = [
        pltpu.make_async_copy(src.at[q], dst, load_sem.at[k])
        for k, (src, dst) in enumerate(((r0, pfx), (r1, pix), (r2, pfxt), (r3, pixt)))
    ] + [
        pltpu.make_async_copy(src, dst, load_sem.at[4 + k])
        for k, (src, dst) in enumerate(((f0, ftx), (f1, itx), (f2, ftxt), (f3, itxt)))
    ]
    stage = dwf

    class SpecLoad:
        def __init__(self, b):
            self.copies = [
                pltpu.make_async_copy(
                    spec_w.at[b, pl.ds(third * k, third)], stage.at[2 * (b % 2) + k], stage_sem.at[2 * b + k]
                )
                for k in range(2)
            ]

        def start(self):
            for copy in self.copies:
                copy.start()

        def wait(self):
            for copy in self.copies:
                copy.wait()

    spec_loads = [SpecLoad(b) for b in range(NB)]
    mlp_loads = [pltpu.make_async_copy(mlp_w.at[b], mlp_stage.at[b % 2], stage_sem.at[2 * NB + b]) for b in range(NB)]
    spec_loads[0].start()
    spec_loads[1].start()
    loads[4].start()
    scal[...] = jnp.zeros_like(scal)
    d_small[...] = jnp.zeros_like(d_small)
    d_gain[...] = jnp.zeros_like(d_gain)
    d_state[...] = jnp.zeros_like(d_state)
    dirs[...] = jnp.zeros_like(dirs)
    kept_rows = lax.broadcasted_iota(jnp.int32, (LANES, 1), 0) < C
    for k in range(2):
        code_bf[k] = jnp.where(kept_rows, small[k], 0.0).astype(BF16)

    def chunk_to(chunks, landing, sems):
        for bits in range(RANKS - 1, 0, -1):
            other = flip(ma, bits, RANKS)
            remote(chunks.at[other], landing, sems[0], sems[1], {"lat": y, "ma": other}).start()
        pltpu.make_async_copy(chunks.at[ma], landing, sems[1]).start()

    def weights_out(b, where, triple):
        source, piece, device = {
            "near": (dw_send, 1, near), "far": (w_all, 2, far), "cross": (dw_send, 3, cross)
        }[where]
        for t in triple:
            remote(source.at[b, 0, t], w_all.at[b, piece, t], w_send_sem.at[b], w_recv_sem.at[b], device).start()

    def cast_weights(b):
        spec_loads[b].wait()
        for t in range(third):
            for own, target in ((y, w_all.at[b, 0]), (1 - y, dw_send.at[b, 0])):
                value = stage[2 * (b % 2) + own, t]
                scal[2 + b : 3 + b] += lane_sums(value * value)
                target[t] = value.astype(BF16)
        if b + 2 < NB:
            spec_loads[b + 2].start()

    def first_weights():
        cast_weights(0)
        loads[0].start()
        mlp_loads[0].start()
        mlp_loads[1].start()
        for k in (1, 2, 3, 5, 6, 7):
            loads[k].start()

    greet_all(first_weights)
    chunk_to(xb_chunks, x_low.at[0, :, ma], (once_send.at[0], once_recv.at[0]))
    weights_out(0, "far", range(third))
    weights_out(0, "cross", range(third))
    weights_out(0, "near", range(third))
    for b in range(1, NB):
        cast_weights(b)
    for b in range(NB):
        mlp_loads[b].wait()
        mlp_bf[b] = mlp_stage[b % 2].astype(BF16)
        if b + 2 < NB:
            mlp_loads[b + 2].start()
    for copy in loads:
        copy.wait()
    share_rows = pl.ds(pl.multiple_of((q % (RANKS // 2)) * ml_buf.shape[2], ml_buf.shape[2]), ml_buf.shape[2])
    ml_loads = [
        pltpu.make_async_copy(array.at[b, q // (RANKS // 2), share_rows], ml_buf.at[k, b], ml_sem)
        for k, array in enumerate((mlp_w, mlp_m, mlp_v))
        for b in range(NB)
    ]
    for copy in ml_loads:
        copy.start()
    bytes_wait(x_low.at[0], once_recv.at[0])
    bytes_wait(xb_chunks.at[pl.ds(0, RANKS - 1)], once_send.at[0])

    hi = hi_rows(w)
    rows_mix = RANKS * 2 * SLOTS

    halves = range(2)

    def cols(half):
        return slice(half * LANES, (half + 1) * LANES)

    def narrow(value):
        return value.astype(BF16).reshape(n_send.shape[1:])

    def broad(value):
        return value.astype(BF16).reshape(w_send.shape[1:])

    def go(phase, half, send, recv):
        exchange_start(send, recv, x_send.at[phase, half], x_recv_sem.at[phase, half], peers, q)

    def come(phase, half, send, recv):
        exchange_wait(send, recv, x_send.at[phase, half], x_recv_sem.at[phase, half])

    def whole(ref, rows):
        return jnp.concatenate([ref[half].reshape(rows, LANES) for half in halves], axis=1)

    def rows_of(ref, t):
        return jnp.concatenate([ref[half, :, t].reshape(rows_mix, LANES) for half in halves], axis=1)

    def swapped(product):
        wide = product.reshape(RANKS, 2, SLOTS, 2 * LANES)
        return wide[..., :LANES], wide[..., LANES:]

    def fwd_block(step, block):
        slot, idx = 4 * step + block, NB * step + block
        gain_row = small[0, pl.ds(LANES - NB + block, 1), :]

        def norm_rows(rows):
            normal, unused = normal_of(h_all[slot, rows, :])
            u_buf[rows, :] = (normal * gain_row).astype(BF16)

        rows_loop(pixels, 256, norm_rows)
        for half in halves:
            n_send[half] = narrow(nn(ftx[...], u_buf[:, cols(half)]))
            go(0, half, n_send.at[half], s_recv.at[half])

        @pl.when(jnp.logical_and(step == 0, block > 0))
        def _():
            weights_out(block, "cross", (2,))
            weights_out(block, "near", (2,))

        @pl.when(jnp.logical_and(step == 1, block < ROLL))
        def _():
            sems = (once_send.at[1 + block], once_recv.at[1 + block])
            chunk_to(t_chunks.at[block], goals.at[block, :, ma], sems)

        for half in halves:
            come(0, half, n_send.at[half], s_recv.at[half])
            w_send[half] = broad(nn(pfx[...], s_recv[half].reshape(spectra, LANES)))
            go(1, half, w_send.at[half], a_own.at[idx, half])

        @pl.when(jnp.logical_and(step == 0, block < NB - 1))
        def _():
            weights_out(block + 1, "far", (0,))

        @pl.when(jnp.logical_and(step == 0, block == NB - 1))
        def _():
            chunk_to(x_chunks, x_recv.at[:, ma], (once_send.at[3], once_recv.at[3]))

        for half in halves:
            come(1, half, w_send.at[half], a_own.at[idx, half])

        @pl.when(step == 0)
        def _():
            bytes_wait(w_all.at[block, pl.ds(1, 3)], w_recv_sem.at[block])

        for half in halves:
            for t in range(3):
                coef = rows_of(a_own.at[idx], t)

                def mixed_by(kind):
                    piece = piece_of(kind, half, zh, y)
                    return nn(coef, jnp.concatenate([w_all[block, piece, t, 0], w_all[block, piece, t, 1]], axis=1))

                by_real, by_imag = swapped(jnp.where(hi, mixed_by(0), mixed_by(1)))
                mixed = jnp.stack([by_real[:, 0] - by_imag[:, 1], by_real[:, 1] + by_imag[:, 0]], 1)
                w_send[half, :, t] = mixed.reshape(RANKS, 2 * SLOTS, LANES).astype(BF16)
            go(2, half, w_send.at[half], b_recv.at[half])

        @pl.when(jnp.logical_and(step == 0, block < NB - 1))
        def _():
            weights_out(block + 1, "far", (1,))
            weights_out(block + 1, "near", (0,))

        for half in halves:
            come(2, half, w_send.at[half], b_recv.at[half])
            n_send[half] = narrow(nn(pix[...], b_recv[half].reshape(triples, LANES)))
            go(3, half, n_send.at[half], y_recv.at[half])

        @pl.when(jnp.logical_and(step == 0, block < NB - 1))
        def _():
            weights_out(block + 1, "far", (2,))
            weights_out(block + 1, "cross", (0, 1))
            weights_out(block + 1, "near", (1,))

        for half in halves:
            come(3, half, n_send.at[half], y_recv.at[half])
        spectrum = whole(y_recv, spectra)

        def mlp_rows(rows):
            merged = h_all[slot, rows, :] + nn(itx[rows, :], spectrum)
            merged_low = merged.astype(BF16)
            v_low[idx, rows, :] = merged_low
            pre = nn(merged_low, mlp_bf[block, 0])
            act = (0.5 * pre * (1.0 + jnp.tanh(GELU_A * (pre + GELU_B * pre * pre * pre)))).astype(BF16)
            h_all[slot + 1, rows, :] = merged + nt(act, mlp_bf[block, 1])

        rows_loop(pixels, 256, mlp_rows)

    denom = float(pixels * RANKS * C * 2)

    def fwd_step(step, carry):
        h_all[4 * step] = nn(x_low[step].reshape(pixels, LANES), code_bf[0])

        def one(block, inner):
            fwd_block(step, block)
            return inner

        lax.fori_loop(0, NB, one, 0)
        hidden_low = h_all[4 * step + 3].astype(BF16)
        hid_low[step] = hidden_low
        delta = nt(hidden_low, code_bf[1])

        @pl.when(step == 0)
        def _():
            bytes_wait(x_recv, once_recv.at[3])
            bytes_wait(x_chunks.at[pl.ds(0, RANKS - 1)], once_send.at[3])

        prediction = x_recv[...].reshape(pixels, LANES) + delta
        x_recv[...] = prediction.reshape(x_recv.shape)
        misfit[step] = prediction

        @pl.when(step == 0)
        def _():
            x_low[1] = prediction.astype(BF16).reshape(x_low.shape[1:])

        @pl.when(step == 1)
        def _():
            for k in range(ROLL):
                bytes_wait(goals.at[k], once_recv.at[1 + k])
                bytes_wait(t_chunks.at[k, pl.ds(0, RANKS - 1)], once_send.at[1 + k])
            for il in range(2):
                valid = goals[0, il].reshape(pixels // 2, LANES)[:, MASK_LANE:]
                rows = slice(il * pixels // 2, (il + 1) * pixels // 2)
                weight[rows, :] = valid * (area[q, il] * small[1, VAR_ROW : VAR_ROW + 1, :LANES])
            for k in range(ROLL):
                miss = misfit[k] - goals[k].reshape(pixels, LANES)
                weighted = weight[...] * miss
                scal[0:1] += lane_sums(weighted * miss / denom)
                misfit[k] = 2.0 * weighted / denom

        return carry

    lax.fori_loop(0, ROLL, fwd_step, 0)
    for b in range(NB):
        bytes_wait(w_all.at[b, pl.ds(1, 3)], w_send_sem.at[b])

    def settle(block):
        bytes_wait(dw_recv.at[block], g_recv_sem.at[block])
        for t in range(third):
            for own, one, two in (
                (y, dw_own[block, t], dw_recv[block, 1, t]),
                (1 - y, dw_recv[block, 0, t], dw_recv[block, 2, t]),
            ):
                total = one.astype(F32) + two.astype(F32)
                scal[1:2] += lane_sums(total * total)
                g_spec[block, third * own + t] = total

    def shares_start(block):
        rs_send[...] = dmlp[block].astype(BF16).reshape(rs_send.shape)
        exchange_start(rs_send, rs_recv, rs_sem.at[0], rs_sem.at[1], peers, q)

    def shares_finish(block):
        exchange_wait(rs_send, rs_recv, rs_sem.at[0], rs_sem.at[1])
        share = rs_recv[0].astype(F32)
        for k in range(1, RANKS):
            share = share + rs_recv[k].astype(F32)
        mir_send[block] = share
        remote(mir_send.at[block], mir_recv.at[block], mir_send_sem.at[block], mir_recv_sem.at[block], far).start()

    def shares_spread(block):
        bytes_wait(mir_recv.at[block], mir_recv_sem.at[block])
        total = mir_send[block] + mir_recv[block]
        scal[1:2] += 0.5 * lane_sums(total * total)
        ag_src[block] = total.astype(BF16)
        landing = g_mlp.at[block, q // (RANKS // 2), share_rows]
        push_blocks(lambda d: ag_src.at[block], landing, ag_send_sem.at[block], ag_recv_sem.at[block], peers, q)

    def grads_out(b, where, triple):
        piece, device = {"near": (0, near), "far": (1, far), "cross": (2, cross)}[where]
        for t in triple:
            remote(
                dw_send.at[b, piece, t], dw_recv.at[b, piece, t], g_send_sem.at[b], g_recv_sem.at[b], device
            ).start()

    def bwd_block(lap, step, block):
        early = jnp.logical_and(lap == 1, block > 0)
        later = jnp.logical_and(lap == 1, block < NB - 1)
        slot, idx = 4 * step + block, NB * step + block
        gain_row = small[0, pl.ds(LANES - NB + block, 1), :]

        @pl.when(lap == 0)
        def _():
            dmlp[block] = jnp.zeros(dmlp.shape[1:], F32)

        def mlp_rows(rows):
            d_hidden = dh_buf[rows, :]
            d_branch = d_hidden.astype(BF16)
            merged_low = v_low[idx, rows, :]
            pre = nn(merged_low, mlp_bf[block, 0])
            tan = jnp.tanh(GELU_A * (pre + GELU_B * pre * pre * pre))
            act = (0.5 * pre * (1.0 + tan)).astype(BF16)
            slope = 0.5 * (1.0 + tan) + 0.5 * pre * (1.0 - tan * tan) * (
                GELU_A * (1.0 + 3.0 * GELU_B * pre * pre)
            )
            d_pre = (nn(d_branch, mlp_bf[block, 1]) * slope).astype(BF16)
            dmlp[block, 0] += tn(merged_low, d_pre)
            dmlp[block, 1] += tn(d_branch, act)
            d_merged = d_hidden + nt(d_pre, mlp_bf[block, 0])
            dv_buf[rows, :] = d_merged
            u_buf[rows, :] = d_merged.astype(BF16)

        rows_loop(pixels, 256, mlp_rows)
        for half in halves:
            n_send[half] = narrow(nn(itxt[...], u_buf[:, cols(half)]))
            go(4, half, n_send.at[half], s_recv.at[half])

        @pl.when(later)
        def _():
            grads_out(block + 1, "near", (1,))
            shares_finish(block + 1)

        which = NB * lap + block
        for half in halves:
            come(4, half, n_send.at[half], s_recv.at[half])
            w_send[half] = broad(nn(pixt[...], s_recv[half].reshape(spectra, LANES)))
            go(5, half, w_send.at[half], d_mix.at[which, half])

        @pl.when(later)
        def _():
            grads_out(block + 1, "cross", (2,))
            grads_out(block + 1, "near", (2,))

        for half in halves:
            come(5, half, w_send.at[half], d_mix.at[which, half])

        def turned_of(d_mixed):
            wide = d_mixed.astype(F32).reshape(RANKS, 2, SLOTS, chans)
            return jnp.stack([wide[:, 1], -wide[:, 0]], 1).reshape(rows_mix, chans).astype(BF16)

        for half in halves:
            for t in range(3):
                d_mixed = rows_of(d_mix.at[which], t)

                def mixed_by(kind):
                    parts = [
                        jnp.concatenate(
                            [w_all[block, piece_of(kind, k, zh, y), t, part, cols(half), :] for k in halves], axis=1
                        )
                        for part in range(2)
                    ]
                    return nt(d_mixed, jnp.concatenate(parts, axis=0))

                by_real, by_imag = swapped(jnp.where(hi, mixed_by(0), mixed_by(1)))
                d_coef = jnp.stack([by_real[:, 0] + by_imag[:, 1], by_real[:, 1] - by_imag[:, 0]], 1)
                w_send[half, :, t] = d_coef.reshape(RANKS, 2 * SLOTS, LANES).astype(BF16)
            go(6, half, w_send.at[half], b_recv.at[half])

        @pl.when(jnp.logical_and(lap == 1, block == 0))
        def _():
            shares_start(block)

        @pl.when(lap == 1)
        def _():
            for t in range(3):
                others = []
                for turn in range(ROLL):
                    d_mixed = rows_of(d_mix.at[NB * turn + block], t)
                    others.append((d_mixed, turned_of(d_mixed)))
                for kind in range(2):
                    keep = hi if kind == 0 else jnp.logical_not(hi)
                    kept = [
                        jnp.where(
                            keep, rows_of(a_own.at[NB * (1 - turn) + block], t).astype(F32), 0.0
                        ).astype(BF16)
                        for turn in range(ROLL)
                    ]
                    for part in range(2):
                        grad = tn(kept[0], others[0][part]) + tn(kept[1], others[1][part])
                        for half in range(2):
                            dwf[piece_of(kind, half, zh, y), t, part] = grad[
                                :, half * LANES : (half + 1) * LANES
                            ]
            dw_own[block] = dwf[0]
            for k in range(3):
                dw_send[block, k] = dwf[1 + k].astype(BF16)

            grads_out(block, "far", (0,))

        @pl.when(jnp.logical_and(lap == 1, block == 0))
        def _():
            grads_out(block, "far", (1, 2))

        for half in halves:
            come(6, half, w_send.at[half], b_recv.at[half])
            n_send[half] = narrow(nn(pfxt[...], b_recv[half].reshape(triples, LANES)))
            go(7, half, n_send.at[half], y_recv.at[half])

        @pl.when(early)
        def _():
            grads_out(block, "far", (1, 2))
            grads_out(block, "cross", (0, 1))
            grads_out(block, "near", (0,))

        @pl.when(jnp.logical_and(lap == 1, block == 0))
        def _():
            grads_out(block, "near", range(third))

        for half in halves:
            come(7, half, n_send.at[half], y_recv.at[half])

        @pl.when(early)
        def _():
            shares_start(block)

        @pl.when(jnp.logical_and(lap == 1, block == 0))
        def _():
            shares_finish(block)

        spectrum = whole(y_recv, spectra)

        def norm_rows(rows):
            normal, inv_std = normal_of(h_all[slot, rows, :])
            d_normed = nn(ftxt[rows, :], spectrum)
            scaled = d_normed * gain_row
            d_gain[block] += jnp.sum(d_normed * normal, axis=0, keepdims=True)
            d_norm_in = inv_std * (
                scaled
                - jnp.mean(scaled, -1, keepdims=True)
                - normal * jnp.mean(scaled * normal, -1, keepdims=True)
            )
            dh_buf[rows, :] = dv_buf[rows, :] + d_norm_in

        rows_loop(pixels, 256, norm_rows)

        @pl.when(jnp.logical_and(lap == 1, block < NB - 1))
        def _():
            settle(block + 1)

    def bwd_step(lap, carry):
        step = ROLL - 1 - lap
        d_pred = misfit[step] + d_state[...]
        d_dec = d_pred.astype(BF16)
        d_small[LANES:] += tn(d_dec, hid_low[step])
        dh_buf[...] = nn(d_dec, code_bf[1])

        def one(k, inner):
            bwd_block(lap, step, NB - 1 - k)
            return inner

        lax.fori_loop(0, NB, one, 0)
        d_enc = dh_buf[...].astype(BF16)
        d_small[:LANES] += tn(x_low[step].reshape(pixels, LANES), d_enc)

        @pl.when(lap == 0)
        def _():
            d_state[...] = d_pred + nt(d_enc, code_bf[0])

        return carry

    lax.fori_loop(0, ROLL, bwd_step, 0)

    for b in range(NB):
        d_small[LANES - NB + b : LANES - NB + b + 1] = d_gain[b]
    sm_send[...] = d_small[...].reshape(sm_send.shape)
    exchange_start(sm_send, sm_recv, sm_sem.at[0], sm_sem.at[1], peers, q)
    for b in range(NB - 1, 0, -1):
        shares_spread(b)
    exchange_wait(sm_send, sm_recv, sm_sem.at[0], sm_sem.at[1])
    share = sm_recv[0]
    for k in range(1, RANKS):
        share = share + sm_recv[k]
    sm_mir_send[...] = share
    swap = remote(sm_mir_send, sm_mir_recv, sm_sem.at[2], sm_sem.at[3], far)
    swap.start()
    grads_out(0, "cross", range(third))
    swap.wait()
    total = sm_mir_send[...] + sm_mir_recv[...]
    scal[1:2] += 0.5 * lane_sums(total * total)
    sm_src[...] = total
    push_blocks(lambda d: sm_src, g_small.at[q], sm_sem.at[4], sm_sem.at[5], peers, q)
    shares_spread(0)
    settle(0)

    me = RANKS * y + ma
    sets = ((dwf.at[0], dwf.at[1], dwf.at[2]), (dwf.at[3], dw_own.at[0], dw_own.at[1]))

    def unit_loads(u):
        part = pl.ds(third * (u % 2), third)
        return [
            pltpu.make_async_copy(array.at[u // 2, part], buffer, lamb_sem.at[u % 2, k])
            for k, (array, buffer) in enumerate(zip((spec_w, spec_m, spec_v), sets[u % 2]))
        ]

    for u in range(2):
        for copy in unit_loads(u):
            copy.start()

    def spread_start(value, landing, sems):
        for bits in range(2 * RANKS - 1, 0, -1):
            other = {"lat": flip(y, bits // RANKS, 2), "ma": flip(ma, bits % RANKS, RANKS)}
            remote(value, landing.at[me], sems[0], sems[1], other).start()
        pltpu.make_async_copy(value, landing.at[me], sems[1]).start()

    def spread_total(landing, sems):
        bytes_wait(landing, sems[1])
        bytes_wait(landing.at[pl.ds(0, 2 * RANKS - 1)], sems[0])
        total = landing[0]
        for k in range(1, 2 * RANKS):
            total = total + landing[k]
        return jnp.broadcast_to(jnp.sum(total, axis=1, keepdims=True), total.shape)

    first_sems, second_sems = (sm_sem.at[6], sm_sem.at[7]), (sm_sem.at[8], sm_sem.at[9])
    spread_start(scal, scal_recv, first_sems)
    for copy in ml_loads:
        copy.wait()
    total = spread_total(scal_recv, first_sems)
    scalars[:8] = total

    scale = clip_norm / jnp.maximum(jnp.sqrt(total[1:2, :1]), clip_norm)
    first_inv = 1.0 / small[1, FIRST_ROW : FIRST_ROW + 1, :1]
    second_inv = 1.0 / small[1, SECOND_ROW : SECOND_ROW + 1, :1]

    def direction_of(weight_old, first, second, grad):
        grad = grad * scale
        first_new = (beta_first * first + (1.0 - beta_first) * grad) * first_inv
        second_new = (beta_second * second + (1.0 - beta_second) * grad * grad) * second_inv
        return first_new / (jnp.sqrt(second_new) + adam_eps) + weight_decay * weight_old

    for u in range(2 * NB):
        for copy in unit_loads(u):
            copy.wait()
        w_buf, m_buf, v_buf = sets[u % 2]

        def one_degree(t, carry, u=u, w_buf=w_buf, m_buf=m_buf, v_buf=v_buf):
            for part in range(2):
                step_dir = direction_of(
                    w_buf[t, part], m_buf[t, part], v_buf[t, part], g_spec[u // 2, third * (u % 2) + t, part]
                )
                dirs[u // 2 : u // 2 + 1] += lane_sums(step_dir * step_dir)
            return carry

        lax.fori_loop(0, third, one_degree, 0)
        if u + 2 < 2 * NB:
            for copy in unit_loads(u + 2):
                copy.start()
    for b in range(NB):
        old = ml_buf[0, b]
        step_dir = direction_of(old, ml_buf[1, b], ml_buf[2, b], ag_src[b].astype(F32))
        row = NB + 2 * b + q // (RANKS // 2)
        for place_row, value in ((row, step_dir), (row + 2 * NB, old)):
            squares = value * value
            lanes = sum(squares[:, k * LANES : (k + 1) * LANES] for k in range(squares.shape[1] // LANES))
            dirs[pl.ds(place_row, 1), :] += 0.5 * jnp.sum(lanes, axis=0, keepdims=True)
    spread_start(dirs, dirs_recv, second_sems)

    bytes_wait(g_small, sm_sem.at[5])
    bytes_wait(g_small.at[pl.ds(0, RANKS - 1)], sm_sem.at[4])
    for b in range(NB):
        bytes_wait(g_mlp.at[b], ag_recv_sem.at[b])
        bytes_wait(rs_send.at[pl.ds(0, RANKS - 1)], ag_send_sem.at[b])
        bytes_wait(mir_send.at[b], mir_send_sem.at[b])
        bytes_wait(dw_send.at[b], g_send_sem.at[b])
    scalars[8:] = spread_total(dirs_recv, second_sems)


def call_train(chunks, weights, tables, small_in, area):
    vmem = pltpu.VMEM
    dma = pltpu.SemaphoreType.DMA
    spec_w, mlp_w = weights[0], weights[3]
    lon = chunks[0].shape[2]
    pixels, chans = 2 * RANKS * lon, small_in.shape[-1]
    third = spec_w.shape[1] // 2
    triple = (third, 2, chans, LANES)
    narrow, wide = (2, RANKS, 4 * ORDS, LANES), (2, RANKS, 3, 2 * SLOTS, LANES)
    triples, spectra = RANKS * 6 * SLOTS, RANKS * 4 * ORDS
    mlp_shape = mlp_w.shape[1:]
    chunk = (mlp_shape[0] * mlp_shape[1] // RANKS, mlp_shape[2])
    small = (2 * LANES // RANKS, chans)
    b16 = lambda *shape: vmem(shape, BF16)
    f32 = lambda *shape: vmem(shape, F32)
    everywhere = pl.BlockSpec(memory_space=pl.ANY)
    inside = pl.BlockSpec(memory_space=vmem)
    return pl.pallas_call(
        train,
        out_shape=(
            jax.ShapeDtypeStruct(spec_w.shape, F32),
            jax.ShapeDtypeStruct(mlp_w.shape, BF16),
            jax.ShapeDtypeStruct((RANKS, *small), F32),
            jax.ShapeDtypeStruct((24, LANES), F32),
        ),
        in_specs=[everywhere] * 17 + [inside] * 2,
        out_specs=[inside] * 4,
        scratch_shapes=[
            b16(triples, spectra), b16(spectra, triples), b16(spectra, triples), b16(triples, spectra),
            b16(spectra, pixels), b16(pixels, spectra), b16(pixels, spectra), b16(spectra, pixels),
            b16(NB, 4, *triple), b16(*mlp_w.shape), f32(2, *mlp_shape),
            b16(*small_in.shape),
            f32(2, RANKS, lon, LANES), f32(ROLL, 2, RANKS, lon, LANES), f32(pixels, LANES), b16(ROLL, 2, RANKS, lon, LANES),
            f32(ROLL, pixels, LANES), f32(pixels, LANES), f32(4 * ROLL, pixels, chans), b16(ROLL, pixels, chans),
            b16(NB * ROLL, pixels, chans), b16(pixels, chans), f32(pixels, chans), f32(pixels, chans),
            b16(*narrow), b16(*narrow), b16(*narrow), b16(*wide), b16(*wide), b16(NB * ROLL, *wide), b16(NB * ROLL, *wide),
            f32(4, *triple), b16(NB, 3, *triple), b16(NB, 3, *triple), f32(NB, *triple), f32(NB, *mlp_shape),
            b16(RANKS, *chunk), b16(RANKS, *chunk), f32(NB, *chunk), f32(NB, *chunk), b16(NB, *chunk),
            f32(2 * LANES, chans), f32(NB, 1, chans), f32(RANKS, *small), f32(RANKS, *small), f32(*small), f32(*small),
            f32(*small), f32(8, LANES), f32(2 * RANKS, 8, LANES),
            f32(3, NB, *chunk), f32(16, LANES), f32(2 * RANKS, 16, LANES),
            dma((8,)), dma((3 * NB,)), dma((4,)), dma((4,)), dma((NB,)), dma((NB,)), dma((8, 2)), dma((8, 2)),
            dma((NB,)), dma((NB,)), dma((2,)), dma((NB,)), dma((NB,)), dma((NB,)), dma((NB,)), dma((10,)),
            dma((2, 3)), dma,
        ],
        compiler_params=pltpu.CompilerParams(
            collective_id=0, has_side_effects=True, vmem_limit_bytes=61 << 20
        ),
    )(*chunks, *weights, *tables, small_in, area)


def chunks_of(field):
    items, lon, lat, width = field.shape
    pairs = lat // 2
    chunks = jnp.moveaxis(field.reshape(items, lon, pairs, 2, width), 1, 3)
    return jnp.concatenate([chunks[0], jnp.roll(chunks[1], pairs // 2, 0)], 0)


def special(
    inputs,
    targets,
    mask,
    var_weight,
    step_count,
    spec_w,
    spec_m,
    spec_v,
    encdec_w,
    encdec_m,
    encdec_v,
    mlp_w,
    mlp_m,
    mlp_v,
    gain_w,
    gain_m,
    gain_v,
):
    zh, y, w, q = place()
    nlon = inputs.shape[1] * lax.axis_size("ma")
    nlat = inputs.shape[2] * lax.axis_size("lat")
    ranked, common = make_tables(nlat, nlon)
    tables = tuple(jnp.asarray(t) for t in (*ranked, *common))
    spare = LANES - C
    x_chunks = chunks_of(jnp.pad(inputs, ((0, 0),) * 3 + ((0, spare),)))
    masks = jnp.broadcast_to(mask.astype(F32)[None, ..., None], (*targets.shape[:-1], 1))
    goal = jnp.concatenate([targets, jnp.zeros((*targets.shape[:-1], spare - 1), F32), masks], -1)
    t_chunks = jnp.stack([chunks_of(goal[0]), chunks_of(goal[1])], 0)
    sines = np.sin((np.arange(nlat) + 0.5) * (math.pi / nlat))
    area = np.repeat((sines / np.mean(sines)).astype(np.float32).reshape(RANKS, 2, 1, 1), LANES, 3)
    step_float = step_count[0].astype(F32)
    fixes = jnp.stack([1.0 - beta_second**step_float, 1.0 - beta_first**step_float])
    var_row = jnp.pad(var_weight.astype(F32), (0, E - C))[None]
    small_in = jnp.stack(
        [
            jnp.concatenate([encdec_w[0], jnp.zeros((LANES - NB - C, E), F32), gain_w], 0),
            jnp.concatenate(
                [
                    encdec_w[1],
                    jnp.zeros((SECOND_ROW - C, E), F32),
                    jnp.broadcast_to(fixes[:, None], (2, E)),
                    var_row,
                    jnp.zeros((LANES - 1 - VAR_ROW, E), F32),
                ],
                0,
            ),
        ]
    )
    spec_grad, mlp_sum, small_sum, sums = call_train(
        (x_chunks.astype(BF16), x_chunks, t_chunks),
        (spec_w, spec_m, spec_v, mlp_w, mlp_m, mlp_v),
        tables,
        small_in,
        jnp.asarray(area),
    )
    grad_mlp = mlp_sum.astype(F32)
    small_sum = small_sum.reshape(2, LANES, E)
    grad_encdec = small_sum[:, :C]
    grad_gain = small_sum[0, LANES - NB :]
    sums = sums[:, 0]
    loss_value = sums[0]
    weight_square = sums[2 : 2 + NB]
    grad_norm = jnp.sqrt(sums[1])
    scale = clip_norm / jnp.maximum(grad_norm, clip_norm)
    spec_m_new, spec_v_new, direction = adaptive(
        spec_w, spec_m, spec_v, spec_grad * scale, step_float
    )
    dir_square = sums[8 : 8 + NB]
    weight_norm = jnp.sqrt(weight_square)
    dir_norm = jnp.sqrt(dir_square)
    trust = weight_norm / (dir_norm + 1e-06)
    spec_new = spec_w - learn_rate * trust[:, None, None, None, None] * direction
    encdec_new, encdec_m_new, encdec_v_new, encdec_norms = lamb_dense(
        encdec_w, encdec_m, encdec_v, grad_encdec * scale, step_float, 2
    )
    mlp_m_new, mlp_v_new, mlp_dir = adaptive(mlp_w, mlp_m, mlp_v, grad_mlp * scale, step_float)
    mlp_dir_norm = jnp.sqrt(sums[8 + NB : 8 + 3 * NB])
    mlp_weight_norm = jnp.sqrt(sums[8 + 3 * NB : 8 + 5 * NB])
    mlp_trust = (mlp_weight_norm / (mlp_dir_norm + 1e-06)).reshape(NB, 2, 1, 1)
    mlp_new = mlp_w - learn_rate * mlp_trust * mlp_dir
    mlp_norms = jnp.stack([mlp_weight_norm, mlp_dir_norm], 1)
    gain_new, gain_m_new, gain_v_new, gain_norms = lamb_dense(
        gain_w, gain_m, gain_v, grad_gain * scale, step_float, NB
    )
    matrix_norms = jnp.concatenate(
        [jnp.stack([weight_norm, dir_norm], 1), encdec_norms, mlp_norms, gain_norms], 0
    )
    return (
        loss_value,
        grad_norm,
        matrix_norms,
        spec_new,
        spec_m_new,
        spec_v_new,
        spec_new.astype(jnp.bfloat16),
        encdec_new,
        encdec_m_new,
        encdec_v_new,
        encdec_new.astype(jnp.bfloat16),
        mlp_new,
        mlp_m_new,
        mlp_v_new,
        mlp_new.astype(jnp.bfloat16),
        gain_new,
        gain_m_new,
        gain_v_new,
        gain_new.astype(jnp.bfloat16),
    )


def local(mesh, *args):
    inputs, spec_w = args[0], args[5]
    lat = inputs.shape[2] * mesh.shape["lat"]
    fits = (
        dict(mesh.shape) == {"lat": 2, "ma": RANKS}
        and inputs.shape[0] == 2
        and lat == 2 * RANKS
        and spec_w.shape[1] * RANKS == L
    )
    return (special if fits else general)(*args)


def solution(mesh):
    placed = (
        P(None, "ma", "lat", None),
        P(None, None, "ma", "lat", None),
        P(None, "ma", "lat"),
        P(),
        P(),
        P(None, "ma", None, None, "lat"),
        P(None, "ma", None, None, "lat"),
        P(None, "ma", None, None, "lat"),
        P(),
        P(),
        P(),
        P(),
        P(),
        P(),
        P(),
        P(),
        P(),
    )
    return jax.shard_map(
        functools.partial(local, mesh),
        mesh=mesh,
        in_specs=placed,
        out_specs=(
            P(),
            P(),
            P(),
            P(None, "ma", None, None, "lat"),
            P(None, "ma", None, None, "lat"),
            P(None, "ma", None, None, "lat"),
            P(None, "ma", None, None, "lat"),
            P(),
            P(),
            P(),
            P(),
            P(),
            P(),
            P(),
            P(),
            P(),
            P(),
            P(),
            P(),
        ),
        check_vma=False,
    )
```
